32 devices in a mesh: sec: 4 (over y, core), gx: 8 (over z, x).
Axes of the slice: x: 2, y: 2, z: 4, core: 2. Of those that a mesh axis runs over, the one named last changes fastest.
Arguments:
- incoming: float32 [4, 32, 64, 256], P('sec', 'gx'), may hold values from 0.5 to 2
- backward: bfloat16 [16, 32, 64, 256], P('sec', 'gx'), may hold values from 0.5 to 2
- fields: float32 [3, 32, 256], P(None, 'gx'), may hold values from -0.4 to 0.4
- block_types: int32 [4, 4], P('sec'), may hold values from 0 to 2
- axial_taps: float32 [3, 64], replicated, may hold values from 0.1 to 0.45
- lateral_taps: float32 [3, 64], replicated, may hold values from 0.1 to 0.45
- depth_taps: float32 [3, 64], replicated, may hold values from 0.1 to 0.45
- bend_diagonal: float32 [64], replicated, may hold values from 0.4 to 0.8
- bend_coupling: float32 [64, 64], replicated, may hold values from 0 to 0.025
Outputs:
- handoff: float32 [4, 32, 64, 256], P('sec', 'gx')
- density: float32 [32, 64, 256], P('gx', 'sec')
The draws below stay inside these ranges and needn't reach their ends.
All inputs are finite; a program needn't handle non-finite values.
Results may differ from the reference program's by a relative error of at most 0.0003.
Values sent between devices are 32-bit elements; how exact they have to be, the bound alone decides.
No kernel may reach another device: no remote copies, remote signals or barrier semaphores. Data moves between devices by JAX's collectives and lax.ppermute only.
A program may use at most 64 MiB of HBM per device.

```python
import math
import jax
import jax.numpy as jnp
from jax import lax

ORIENT = 64
NTYPES = 3
STEPS = 4
TICKS = 3
NX = 32
NY = 4
NZ = 64
CONTOUR = 16
N_SEC = 4


def touch_ends(drawn, own_key, least, largest):
    spot = [jax.random.randint(jax.random.fold_in(own_key, axis), (), 0, length) for axis, length in enumerate(drawn.shape)]
    longest = drawn.shape.index(max(drawn.shape))
    neighbour = spot[:longest] + [(spot[longest] + 1) % drawn.shape[longest]] + spot[longest + 1:]
    return drawn.at[tuple(spot)].set(least).at[tuple(neighbour)].set(largest)


def block_scale(key, dims, pieces, least, largest):
    loudness = 1.0
    for dim, blocks in pieces:
        heights = jax.random.uniform(jax.random.fold_in(jax.random.fold_in(key, 6), dim), (blocks,), jnp.float32, least / len(pieces), largest / len(pieces))
        loudness = loudness * jnp.repeat(jnp.exp(heights), dims[dim] // blocks).reshape((-1,) + (1,) * (len(dims) - 1 - dim))
    return loudness


def setup_inputs(seed: int = 0) -> dict:
    seeds = jax.random.split(jax.random.key(seed), 10)
    return {
        "incoming": jnp.clip(jnp.exp(math.log(2.0) - 1.3862944 * jax.random.uniform(seeds[0], (N_SEC, NX, ORIENT, NY * NZ), jnp.float32) ** block_scale(seeds[0], (N_SEC, NX, ORIENT, NY * NZ), ((0, 4), (1, 8)), -0.2, 0.2)), 0.5, 2.0),
        "backward": jnp.clip(jnp.exp(math.log(2.0) - 1.3862944 * jax.random.uniform(seeds[1], (CONTOUR, NX, ORIENT, NY * NZ), jnp.float32) ** block_scale(seeds[1], (CONTOUR, NX, ORIENT, NY * NZ), ((0, 4), (1, 8)), -0.2, 0.2)), 0.5, 2.0).astype(jnp.bfloat16),
        "fields": jnp.clip(jax.random.uniform(seeds[2], (NTYPES, NX, NY * NZ), jnp.float32, -0.4, 0.4) * block_scale(seeds[2], (NTYPES, NX, NY * NZ), ((1, 8),), -0.4, 0.0), -0.4, 0.4),
        "block_types": touch_ends(jax.random.randint(seeds[3], (N_SEC, STEPS), 0, NTYPES), jax.random.fold_in(seeds[3], 1), 0, NTYPES - 1).astype(jnp.int32),
        "axial_taps": jnp.clip(jax.random.uniform(seeds[4], (3, ORIENT), jnp.float32, 0.1, 0.45), 0.1, 0.45),
        "lateral_taps": jnp.clip(jax.random.uniform(seeds[5], (3, ORIENT), jnp.float32, 0.1, 0.45), 0.1, 0.45),
        "depth_taps": jnp.clip(jax.random.uniform(seeds[6], (3, ORIENT), jnp.float32, 0.1, 0.45), 0.1, 0.45),
        "bend_diagonal": jnp.clip(jax.random.uniform(seeds[7], (ORIENT,), jnp.float32, 0.4, 0.8), 0.4, 0.8),
        "bend_coupling": jnp.clip(jax.random.uniform(seeds[8], (ORIENT, ORIENT), jnp.float32, 0.0, 0.025), 0.0, 0.025),
    }


def boltzmann(fields, kinds):
    selector = kinds == jnp.arange(fields.shape[0], dtype=jnp.int32)
    chosen = jnp.sum(jnp.where(selector[:, None, None], fields, jnp.zeros_like(fields)), axis=0)
    return jnp.exp(-chosen)


def column(taps, which):
    return taps[which][None, :, None, None]


def advance(propagator, factor, axial_taps, lateral_taps, depth_taps, kernel):
    planes = propagator.shape[0]
    orients = propagator.shape[1]
    cube = propagator.reshape(planes, orients, NY, NZ)
    along_x = column(axial_taps, 0) * jnp.roll(cube, 1, axis=0) + column(axial_taps, 1) * cube + column(axial_taps, 2) * jnp.roll(cube, -1, axis=0)
    along_y = column(lateral_taps, 0) * jnp.roll(along_x, 1, axis=2) + column(lateral_taps, 1) * along_x + column(lateral_taps, 2) * jnp.roll(along_x, -1, axis=2)
    along_z = column(depth_taps, 0) * jnp.roll(along_y, 1, axis=3) + column(depth_taps, 1) * along_y + column(depth_taps, 2) * jnp.roll(along_y, -1, axis=3)
    blended = jnp.einsum("uv,xvyz->xuyz", kernel, along_z, precision=lax.Precision.HIGHEST)
    return blended.reshape(propagator.shape) * factor[:, None, :]


def reference(incoming, backward, fields, block_types, axial_taps, lateral_taps, depth_taps, bend_diagonal, bend_coupling):
    kernel = jnp.diag(bend_diagonal) + bend_coupling
    steps_each = block_types.shape[1]
    stored_all = backward.reshape((N_SEC, steps_each) + backward.shape[1:])

    def section(density_part, items):
        propagator, kinds, stored = items
        for position in range(steps_each):
            factor = boltzmann(fields, kinds[position])
            propagator = advance(propagator, factor, axial_taps, lateral_taps, depth_taps, kernel)
            density_part = density_part + propagator * stored[position].astype(jnp.float32)
        return density_part, propagator

    current = incoming
    density_sum = jnp.zeros(incoming.shape[1:], jnp.float32)
    outgoing = incoming
    for tick_index in range(TICKS):
        density_sum, outgoing = lax.scan(section, jnp.zeros(incoming.shape[1:], jnp.float32), (current, block_types, stored_all))
        if tick_index + 1 < TICKS:
            current = jnp.concatenate([incoming[:1], outgoing[:-1]], axis=0)
    density = density_sum / (N_SEC * steps_each)
    return outgoing, density
```

```python
import functools

import jax
import jax.numpy as jnp
from jax import lax
from jax.experimental import pallas as pl
from jax.experimental.pallas import tpu as pltpu
from jax.sharding import PartitionSpec as P

TICKS = 3
CZ = 64
GROUP = 4
FIELD_ROWS = 16
VMEM_BYTES = 48 * 2**20
IN_VMEM = pl.BlockSpec(memory_space=pltpu.VMEM)
IN_SMEM = pl.BlockSpec(memory_space=pltpu.SMEM)


def padded_2(block, sides, width):
    for axis, dim in sides:
        count = lax.axis_size(axis)
        forward = [(i, i + 1) for i in range(count - 1)]
        forward.append((count - 1, 0))
        backward = [(target, source) for source, target in forward]
        low = lax.ppermute(
            lax.slice_in_dim(block, block.shape[dim] - width, None, axis=dim), axis, forward
        )
        high = lax.ppermute(lax.slice_in_dim(block, 0, width, axis=dim), axis, backward)
        block = jnp.concatenate([low, block, high], axis=dim)
    return block


def from_behind(array, axis, by):
    length = lax.axis_size(axis)
    pairs = [(i, i + by) for i in range(length) if 0 <= i + by < length]
    return lax.ppermute(array, axis, pairs)


def boltzmann(fields, kinds):
    selector = kinds == jnp.arange(fields.shape[0], dtype=jnp.int32)
    chosen = jnp.sum(jnp.where(selector[:, None, None], fields, jnp.zeros_like(fields)), axis=0)
    return jnp.exp(-chosen)


def column(taps, which):
    return taps[which][None, :, None]


def advance_padded(padded, factor, axial_taps, lateral_taps, depth_taps, kernel):
    along_x = (
        column(axial_taps, 0) * padded[:-2]
        + column(axial_taps, 1) * padded[1:-1]
        + column(axial_taps, 2) * padded[2:]
    )
    along_y = (
        column(lateral_taps, 0) * jnp.roll(along_x, CZ, axis=2)
        + column(lateral_taps, 1) * along_x
        + column(lateral_taps, 2) * jnp.roll(along_x, -CZ, axis=2)
    )
    depth_pos = (jnp.arange(along_y.shape[2], dtype=jnp.int32) % CZ)[None, None, :]
    behind = jnp.where(
        depth_pos == 0, jnp.roll(along_y, -(CZ - 1), axis=2), jnp.roll(along_y, 1, axis=2)
    )
    ahead = jnp.where(
        depth_pos == CZ - 1, jnp.roll(along_y, CZ - 1, axis=2), jnp.roll(along_y, -1, axis=2)
    )
    along_z = (
        column(depth_taps, 0) * behind
        + column(depth_taps, 1) * along_y
        + column(depth_taps, 2) * ahead
    )
    blended = jnp.einsum(
        "uv,xvc->xuc",
        kernel,
        along_z,
        precision=lax.Precision.HIGHEST,
        preferred_element_type=jnp.float32,
    )
    return blended * factor[:, None, :]


def per_device(
    incoming,
    backward,
    fields,
    block_types,
    axial_taps,
    lateral_taps,
    depth_taps,
    bend_diagonal,
    bend_coupling,
):
    kernel = jnp.diag(bend_diagonal) + bend_coupling
    steps_each = block_types.shape[1]
    planes = incoming.shape[1]
    start = incoming[0]
    first_section = lax.axis_index("sec") == 0
    wide_fields = padded_2(fields, (("gx", 1),), steps_each)
    factors = [boltzmann(wide_fields, block_types[0, position]) for position in range(steps_each)]
    current = start
    outgoing = start
    accumulated = jnp.zeros(start.shape, jnp.float32)
    for tick_index in range(TICKS):
        final_tick = tick_index + 1 == TICKS
        extended = padded_2(current, (("gx", 0),), steps_each)
        for position in range(steps_each):
            margin = steps_each - position - 1
            offset = steps_each - margin
            factor = factors[position][offset : offset + planes + 2 * margin]
            extended = advance_padded(
                extended, factor, axial_taps, lateral_taps, depth_taps, kernel
            )
            if final_tick:
                accumulated = accumulated + extended[margin : margin + planes] * backward[
                    position
                ].astype(jnp.float32)
        outgoing = extended
        if not final_tick:
            shifted = from_behind(outgoing, "sec", 1)
            current = jnp.where(first_section, start, shifted)
    reduced = lax.psum_scatter(accumulated, "sec", scatter_dimension=1, tiled=True)
    density = reduced / (lax.axis_size("sec") * steps_each)
    return (outgoing[None], density)


def to_tile(plane, scratch):
    half = plane.shape[1] // 2
    scratch[...] = jnp.concatenate([plane[:, :half], plane[:, half:]], axis=0).T
    return reorder(scratch)


def reorder(scratch):
    rows = scratch.shape[0]
    return jnp.concatenate(
        [scratch[pl.ds(yl * CZ + zl, 8, stride=8), :] for yl in range(rows // CZ) for zl in range(CZ // 8)], axis=0
    )


def from_tile(tile, scratch):
    rows = tile.shape[0]
    for yl in range(rows // CZ):
        for zl in range(CZ // 8):
            at = (yl * (CZ // 8) + zl) * 8
            scratch[pl.ds(yl * CZ + zl, 8, stride=8), :] = tile[at : at + 8]
    turned = scratch[...].T
    half = turned.shape[0] // 2
    return jnp.concatenate([turned[:half], turned[half:]], axis=1)


def stencil(behind, here, ahead, taps):
    a = here + taps[0] * behind + taps[1] * ahead
    low, high = a[:CZ], a[CZ:]
    low_turned = pltpu.roll(low, a.shape[1] // 2, 1)
    high_turned = pltpu.roll(high, a.shape[1] // 2, 1)
    out = []
    for b in (
        low + taps[2] * high_turned + taps[3] * high,
        high + taps[2] * low + taps[3] * low_turned,
    ):
        back = jnp.concatenate([pltpu.roll(b[-8:], 1, 0), b[:-8]], axis=0)
        front = jnp.concatenate([b[8:], pltpu.roll(b[:8], 7, 0)], axis=0)
        out.append(b + taps[4] * back + taps[5] * front)
    return jnp.concatenate(out, axis=0)


def pack_kernel(info, incoming, moved_high, moved_low, fields, out, scratch):
    sec, odd = info[0], info[1]
    rows = scratch.shape[0]
    pair = incoming.shape[0] // 2

    def fill(source):
        for i in range(pair):
            out[i * rows : (i + 1) * rows] = to_tile(source[i], scratch)

    pl.when(sec == 0)(lambda: fill(incoming))
    pl.when(odd == 1)(lambda: fill(moved_high))
    pl.when((sec > 0) & (odd == 0))(lambda: fill(moved_low))
    out[pair * rows :] = jnp.zeros((FIELD_ROWS, rows), jnp.float32)
    for kind in range(fields.shape[0]):
        for i in range(pair):
            line = fields[kind, pl.ds(pair * odd + i, 1), :]
            at = pair * rows + (kind * pair + i) * 2
            out[at : at + 1] = line[:, :rows]
            out[at + 1 : at + 2] = line[:, rows:]


def turn_kernel(stored, out, scratch):
    for i in range(stored.shape[1]):
        out[0, i] = to_tile(stored[0, i].astype(jnp.float32), scratch)


def turn(stored):
    steps, planes, orients, cells = stored.shape
    return pl.pallas_call(
        turn_kernel,
        grid=(steps,),
        in_specs=[pl.BlockSpec((1, planes, orients, cells), lambda s: (s, 0, 0, 0))],
        out_specs=pl.BlockSpec((1, planes, 2 * orients, cells // 2), lambda s: (s, 0, 0, 0)),
        out_shape=jax.ShapeDtypeStruct((steps, planes, 2 * orients, cells // 2), jnp.float32),
        scratch_shapes=[pltpu.VMEM((2 * orients, cells // 2), jnp.float32)],
        compiler_params=pltpu.CompilerParams(vmem_limit_bytes=VMEM_BYTES),
    )(stored)


def places(odd, pair, reach):
    width = 2 * pair
    far = reach - width
    starts = []
    for core in (odd, 1 - odd):
        starts += [
            reach + pair * core,
            far + pair * core,
            reach + width + pair * core,
            jnp.where(core == 0, reach + 2 * width, 0),
        ]
    return starts


def run_steps(info, taps, weights, kinds_at, count, slab, other, first, second, factor, after):
    tap = [taps[i : i + 1, :] for i in range(6)]
    extent, rows, lanes = slab.shape
    buffers = (slab, other)

    def blend(source, at, packed):
        for i in range(GROUP):
            e = stencil(source[at + i - 1], source[at + i], source[at + i + 1], tap)
            coarse = e.astype(jnp.bfloat16)
            packed[i * rows : (i + 1) * rows, :lanes] = coarse
            packed[i * rows : (i + 1) * rows, lanes:] = (e - coarse.astype(jnp.float32)).astype(jnp.bfloat16)

    def mix(target, at, packed, kind):
        product = jnp.dot(packed[...], weights[...], preferred_element_type=jnp.float32)
        product = product[:, :lanes] + product[:, lanes:]
        for i in range(GROUP):
            target[at + i] = product[i * rows : (i + 1) * rows] * factor[kind, at + i]

    for step in range(count):
        source, target = buffers[step % 2], buffers[1 - step % 2]
        begin, width = step + 1, extent - 2 * step - 2
        groups = -(-width // GROUP)
        kind = info[kinds_at + step]

        def at(i, begin=begin, width=width):
            return jnp.minimum(begin + i * GROUP, begin + width - GROUP)

        blend(source, at(0), first)
        if groups > 1:

            def body(i, carry, source=source, target=target, at=at, kind=kind):
                blend(source, at(2 * i + 1), second)
                mix(target, at(2 * i), first, kind)
                blend(source, at(2 * i + 2), first)
                mix(target, at(2 * i + 1), second, kind)
                return carry

            lax.fori_loop(0, (groups - 1) // 2, body, 0)
        if groups % 2 == 0:
            blend(source, at(groups - 1), second)
            mix(target, at(groups - 2), first, kind)
            mix(target, at(groups - 1), second, kind)
        else:
            mix(target, at(groups - 1), first, kind)
        after(step, target)


def spread_factor(columns, factor, starts, kinds, pair):
    rows, lanes = factor.shape[2:]
    left = lax.broadcasted_iota(jnp.int32, (rows, lanes), 1) < lanes // 2
    for piece, start in enumerate(starts):
        for kind in range(kinds):
            for i in range(pair):
                at = piece * FIELD_ROWS + (kind * pair + i) * 2
                factor[kind, start + i] = jnp.where(left, columns[:, at : at + 1], columns[:, at + 1 : at + 2])


def early_kernel(half, kinds, info, taps, weights, *refs):
    pieces, (stored, next_stored) = refs[:8], refs[8:10]
    middle, half_out, kept, total, columns = refs[10:15]
    slab, other, first, second, factor, scratch = refs[15:]
    sec, odd = info[0], info[1]
    planes, rows = middle.shape[:2]
    pair = planes // 2
    starts = places(odd, pair, half)
    for piece, start in zip(pieces, starts):
        for i in range(pair):
            slab[start + i] = piece[i * rows : (i + 1) * rows]
    scratch[...] = jnp.exp(-jnp.concatenate([piece[pair * rows :] for piece in pieces], axis=0)).T
    columns[...] = reorder(scratch)
    spread_factor(columns, factor, starts, kinds, pair)
    steps = stored.shape[0]
    total[...] = jnp.zeros(total.shape, jnp.float32)

    def after(step, state):
        @pl.when(sec == 0)
        def _():
            source = stored if step < steps else next_stored
            total[...] += state[half : half + planes] * source[step % steps]
            if step + 1 == steps:
                kept[...] = state[half : half + planes]

    run_steps(info, taps, weights, 2, half, slab, other, first, second, factor, after)
    state = (slab, other)[half % 2]
    middle[...] = state[half : half + planes]
    half_out[...] = state[pl.ds(half + pair * odd, pair)]


def late_kernel(half, kinds, last, info, taps, weights, *refs):
    middle, pieces, columns = refs[0], refs[1:7], refs[7]
    kept, total_in, stored, next_stored, last_stored = refs[8:13]
    handoff, share, to_pair, to_across, to_corner = refs[13:18]
    slab, other, first, second, factor, scratch, total, saved, whole = refs[18:]
    sec, odd = info[0], info[1]
    planes, rows = middle.shape[:2]
    pair = planes // 2
    starts = places(odd, pair, half)
    slab[half : half + planes] = middle[...]
    for piece, start in zip(pieces, starts[1:4] + starts[5:8]):
        for i in range(pair):
            slab[start + i] = piece[i]
    spread_factor(columns, factor, starts, kinds, pair)
    steps = stored.shape[0]
    total[...] = total_in[...]
    saved[...] = kept[...]

    def after(step, state):
        step = step + half

        @pl.when(sec == 0)
        def _():
            source = next_stored if step < 2 * steps else last_stored
            total[...] += state[half : half + planes] * source[step % steps]

        if step + 1 == 2 * steps:

            @pl.when(sec == 1)
            def _():
                saved[...] = state[half : half + planes]

        if step >= 2 * steps:

            @pl.when(sec == last)
            def _():
                total[...] += state[half : half + planes] * stored[step % steps]

    run_steps(info, taps, weights, 2 + half, half, slab, other, first, second, factor, after)
    state = (slab, other)[half % 2]

    @pl.when(sec == last)
    def _():
        saved[...] = state[half : half + planes]

    orients = handoff.shape[1]
    count = orients // (last + 1)
    held = planes * count
    to_corner[...] = jnp.zeros(to_corner.shape, jnp.float32)
    for i in range(planes):
        handoff[i] = from_tile(saved[i], scratch)
        whole[...] = from_tile(total[i], scratch)
        for piece, who in (
            (share, sec),
            (to_pair, sec + 1 - 2 * odd),
            (to_across, jnp.where(sec == 0, 2, 1)),
            (to_corner, last - sec),
        ):
            piece[i * count : (i + 1) * count] = whole[pl.ds(pl.multiple_of(who * count, count), count)]
    for i in range(pair):
        to_across[held + i * orients : held + (i + 1) * orients] = from_tile(state[half + pair * odd + i], scratch)

    @pl.when(sec == 1)
    def _():
        to_corner[...] = to_across[held:]


def call(kernel, out_shape, scratch, operands):
    return pl.pallas_call(
        kernel,
        in_specs=[IN_SMEM] + [IN_VMEM] * (len(operands) - 1),
        out_specs=[IN_VMEM] * len(out_shape),
        out_shape=[jax.ShapeDtypeStruct(shape, jnp.float32) for shape in out_shape],
        scratch_shapes=scratch,
        compiler_params=pltpu.CompilerParams(vmem_limit_bytes=VMEM_BYTES),
    )(*operands)


def tables(axial_taps, lateral_taps, depth_taps, bend_diagonal, bend_coupling):
    kernel = jnp.diag(bend_diagonal) + bend_coupling
    kernel = (kernel * (axial_taps[1] * lateral_taps[1] * depth_taps[1])[None, :]).T
    ratios = [each[which] / each[1] for each in (axial_taps, lateral_taps, depth_taps) for which in (0, 2)]
    taps = jnp.tile(jnp.stack(ratios + ratios[:2]), (1, 2))
    coarse = lax.reduce_precision(kernel, 8, 7)
    twice = jnp.eye(2, dtype=jnp.float32)
    coarse, fine = jnp.kron(twice, coarse), jnp.kron(twice, kernel - coarse)
    weights = jnp.block([[coarse, fine], [coarse, jnp.zeros_like(fine)]])
    return taps, weights.astype(jnp.bfloat16)


def paired(incoming, backward, fields, block_types, axial_taps, lateral_taps, depth_taps, bend_diagonal, bend_coupling):
    n_sec, n_gx = lax.axis_size("sec"), lax.axis_size("gx")
    steps, planes, orients, cells = backward.shape
    pair = planes // 2
    half = TICKS * steps // 2
    rows = 2 * orients
    lanes = cells // 2
    sec = lax.axis_index("sec")
    odd = sec % 2
    last = n_sec - 1

    def send(array, by_sec, shift=lambda s: 0):
        pairs = [
            (s * n_gx + g, t * n_gx + (g + shift(s)) % n_gx) for s, t in enumerate(by_sec) for g in range(n_gx)
        ]
        return lax.ppermute(array, ("sec", "gx"), pairs)

    same, beside = (0, 1, 2, 3), (1, 0, 3, 2)
    whole = incoming[0]
    moved_high = send(whole[pair:], (1, 3, 0, 2))
    moved_low = send(whole[:pair], (0, 2, 1, 3))
    taps, weights = tables(axial_taps, lateral_taps, depth_taps, bend_diagonal, bend_coupling)
    kinds = lax.all_gather(block_types[0], "sec")
    kinds = lax.dynamic_slice(kinds, (sec // 2, 0), (TICKS, steps)).reshape(-1)
    place = jnp.stack([sec, odd]).astype(jnp.int32)
    info = jnp.concatenate([place, kinds])
    stored = turn(backward)
    next_stored = send(stored, beside)
    last_stored = send(stored, (2, 3, 0, 1))

    tile = pltpu.VMEM((rows, lanes), jnp.float32)
    slab = pltpu.VMEM((planes + 2 * half, rows, lanes), jnp.float32)
    packed = pltpu.VMEM((GROUP * rows, 2 * lanes), jnp.bfloat16)
    factor = pltpu.VMEM((fields.shape[0], planes + 2 * half, rows, lanes), jnp.float32)
    inner = pltpu.VMEM((planes, rows, lanes), jnp.float32)
    work = [slab, slab, packed, packed, factor, tile]

    def exchange(piece):
        own = [
            send(piece, same, lambda s: 1),
            send(piece, same, lambda s: -1),
            send(piece, same, lambda s: -2 if s % 2 == 0 else 2),
        ]
        return own, [send(each, beside) for each in own]

    (piece,) = call(
        pack_kernel, [(pair * rows + FIELD_ROWS, lanes)], [tile], [place, whole, moved_high, moved_low, fields]
    )
    own, swapped = exchange(piece)
    middle, piece, kept, total, columns = call(
        functools.partial(early_kernel, half, fields.shape[0]),
        [(planes, rows, lanes), (pair, rows, lanes), (planes, rows, lanes), (planes, rows, lanes), (rows, lanes)],
        work,
        [info, taps, weights, piece, *own, send(piece, beside), *swapped, stored, next_stored],
    )
    own, swapped = exchange(piece)
    held = planes * (orients // n_sec)
    handoff, share, to_pair, to_across, to_corner = call(
        functools.partial(late_kernel, half, fields.shape[0], last),
        [(planes, orients, cells)]
        + [(held, cells)] * 2
        + [(held + pair * orients, cells), (pair * orients, cells)],
        work + [inner, inner, pltpu.VMEM((orients, cells), jnp.float32)],
        [info, taps, weights, middle, *own, *swapped, columns, kept, total, stored, next_stored, last_stored],
    )
    to_pair = send(to_pair, beside)
    to_across = send(to_across, (2, 0, 3, 1))
    to_corner = send(to_corner, (3, 2, 1, 0))
    third = sec == 2
    density = share + to_pair + to_across[:held] + jnp.where(third, 0.0, to_corner[:held])
    arrived = jnp.concatenate([to_across[held:], to_corner]).reshape(handoff.shape)
    handoff = jnp.where(third, arrived, handoff)
    return handoff[None], density.reshape(planes, -1, cells) / (n_sec * steps)


def pairs_fit(n_sec, planes, steps, orients, cells, kinds):
    return (
        n_sec == TICKS + 1 == 4
        and planes == steps
        and planes % 2 == 0
        and TICKS * steps == 2 * (planes + planes // 2)
        and 2 * orients == 2 * CZ == cells // 2 == 128
        and kinds * planes <= FIELD_ROWS
        and planes >= GROUP
    )


def solution(mesh):
    in_specs = (
        P("sec", "gx", None, None),
        P("sec", "gx", None, None),
        P(None, "gx", None),
        P("sec", None),
        P(),
        P(),
        P(),
        P(),
        P(),
    )
    out_specs = (P("sec", "gx", None, None), P("gx", "sec", None))

    def body(incoming, backward, fields, *rest):
        steps, planes, orients, cells = backward.shape
        fits = pairs_fit(mesh.shape["sec"], planes, steps, orients, cells, fields.shape[0])
        return (paired if fits else per_device)(incoming, backward, fields, *rest)

    return jax.shard_map(body, mesh=mesh, in_specs=in_specs, out_specs=out_specs, check_vma=False)
```

```python
import functools

import jax
import jax.numpy as jnp
from jax import lax
from jax.experimental import pallas as pl
from jax.experimental.pallas import tpu as pltpu
from jax.sharding import PartitionSpec as P

TICKS = 3
CZ = 64
GROUP = 4
FIELD_ROWS = 16
VMEM_BYTES = 48 * 2**20
IN_VMEM = pl.BlockSpec(memory_space=pltpu.VMEM)
IN_SMEM = pl.BlockSpec(memory_space=pltpu.SMEM)


def padded_2(block, sides, width):
    for axis, dim in sides:
        count = lax.axis_size(axis)
        forward = [(i, i + 1) for i in range(count - 1)]
        forward.append((count - 1, 0))
        backward = [(target, source) for source, target in forward]
        low = lax.ppermute(
            lax.slice_in_dim(block, block.shape[dim] - width, None, axis=dim), axis, forward
        )
        high = lax.ppermute(lax.slice_in_dim(block, 0, width, axis=dim), axis, backward)
        block = jnp.concatenate([low, block, high], axis=dim)
    return block


def from_behind(array, axis, by):
    length = lax.axis_size(axis)
    pairs = [(i, i + by) for i in range(length) if 0 <= i + by < length]
    return lax.ppermute(array, axis, pairs)


def boltzmann(fields, kinds):
    selector = kinds == jnp.arange(fields.shape[0], dtype=jnp.int32)
    chosen = jnp.sum(jnp.where(selector[:, None, None], fields, jnp.zeros_like(fields)), axis=0)
    return jnp.exp(-chosen)


def column(taps, which):
    return taps[which][None, :, None]


def advance_padded(padded, factor, axial_taps, lateral_taps, depth_taps, kernel):
    along_x = (
        column(axial_taps, 0) * padded[:-2]
        + column(axial_taps, 1) * padded[1:-1]
        + column(axial_taps, 2) * padded[2:]
    )
    along_y = (
        column(lateral_taps, 0) * jnp.roll(along_x, CZ, axis=2)
        + column(lateral_taps, 1) * along_x
        + column(lateral_taps, 2) * jnp.roll(along_x, -CZ, axis=2)
    )
    depth_pos = (jnp.arange(along_y.shape[2], dtype=jnp.int32) % CZ)[None, None, :]
    behind = jnp.where(
        depth_pos == 0, jnp.roll(along_y, -(CZ - 1), axis=2), jnp.roll(along_y, 1, axis=2)
    )
    ahead = jnp.where(
        depth_pos == CZ - 1, jnp.roll(along_y, CZ - 1, axis=2), jnp.roll(along_y, -1, axis=2)
    )
    along_z = (
        column(depth_taps, 0) * behind
        + column(depth_taps, 1) * along_y
        + column(depth_taps, 2) * ahead
    )
    blended = jnp.einsum(
        "uv,xvc->xuc",
        kernel,
        along_z,
        precision=lax.Precision.HIGHEST,
        preferred_element_type=jnp.float32,
    )
    return blended * factor[:, None, :]


def per_device(
    incoming,
    backward,
    fields,
    block_types,
    axial_taps,
    lateral_taps,
    depth_taps,
    bend_diagonal,
    bend_coupling,
):
    kernel = jnp.diag(bend_diagonal) + bend_coupling
    steps_each = block_types.shape[1]
    planes = incoming.shape[1]
    start = incoming[0]
    first_section = lax.axis_index("sec") == 0
    wide_fields = padded_2(fields, (("gx", 1),), steps_each)
    factors = [boltzmann(wide_fields, block_types[0, position]) for position in range(steps_each)]
    current = start
    outgoing = start
    accumulated = jnp.zeros(start.shape, jnp.float32)
    for tick_index in range(TICKS):
        final_tick = tick_index + 1 == TICKS
        extended = padded_2(current, (("gx", 0),), steps_each)
        for position in range(steps_each):
            margin = steps_each - position - 1
            offset = steps_each - margin
            factor = factors[position][offset : offset + planes + 2 * margin]
            extended = advance_padded(
                extended, factor, axial_taps, lateral_taps, depth_taps, kernel
            )
            if final_tick:
                accumulated = accumulated + extended[margin : margin + planes] * backward[
                    position
                ].astype(jnp.float32)
        outgoing = extended
        if not final_tick:
            shifted = from_behind(outgoing, "sec", 1)
            current = jnp.where(first_section, start, shifted)
    reduced = lax.psum_scatter(accumulated, "sec", scatter_dimension=1, tiled=True)
    density = reduced / (lax.axis_size("sec") * steps_each)
    return (outgoing[None], density)


def to_tile(plane, scratch):
    half = plane.shape[1] // 2
    scratch[...] = jnp.concatenate([plane[:, :half], plane[:, half:]], axis=0).T
    return reorder(scratch)


def reorder(scratch):
    rows = scratch.shape[0]
    return jnp.concatenate(
        [scratch[pl.ds(yl * CZ + zl, 8, stride=8), :] for yl in range(rows // CZ) for zl in range(CZ // 8)], axis=0
    )


def from_tile(tile, scratch):
    rows = tile.shape[0]
    for yl in range(rows // CZ):
        for zl in range(CZ // 8):
            at = (yl * (CZ // 8) + zl) * 8
            scratch[pl.ds(yl * CZ + zl, 8, stride=8), :] = tile[at : at + 8]
    turned = scratch[...].T
    half = turned.shape[0] // 2
    return jnp.concatenate([turned[:half], turned[half:]], axis=1)


def stencil(behind, here, ahead, taps):
    a = here + taps[0] * behind + taps[1] * ahead
    low, high = a[:CZ], a[CZ:]
    low_turned = pltpu.roll(low, a.shape[1] // 2, 1)
    high_turned = pltpu.roll(high, a.shape[1] // 2, 1)
    out = []
    for b in (
        low + taps[2] * high_turned + taps[3] * high,
        high + taps[2] * low + taps[3] * low_turned,
    ):
        back = jnp.concatenate([pltpu.roll(b[-8:], 1, 0), b[:-8]], axis=0)
        front = jnp.concatenate([b[8:], pltpu.roll(b[:8], 7, 0)], axis=0)
        out.append(b + taps[4] * back + taps[5] * front)
    return jnp.concatenate(out, axis=0)


def position():
    sec = lax.axis_index("sec")
    return sec, lax.rem(sec, 2)


def pack_kernel(incoming, moved_high, moved_low, fields, out, scratch):
    sec, odd = position()
    rows = scratch.shape[0]
    pair = incoming.shape[0] // 2

    def fill(source):
        for i in range(pair):
            out[i * rows : (i + 1) * rows] = to_tile(source[i], scratch)

    pl.when(sec == 0)(lambda: fill(incoming))
    pl.when(odd == 1)(lambda: fill(moved_high))
    pl.when((sec > 0) & (odd == 0))(lambda: fill(moved_low))
    out[pair * rows :] = jnp.zeros((FIELD_ROWS, rows), jnp.float32)
    for kind in range(fields.shape[0]):
        for i in range(pair):
            line = fields[kind, pl.ds(pair * odd + i, 1), :]
            at = pair * rows + (kind * pair + i) * 2
            out[at : at + 1] = line[:, :rows]
            out[at + 1 : at + 2] = line[:, rows:]


def prepare_kernel(backward, axial, lateral, depth, diagonal, coupling, stored, taps, weights, scratch):
    for i in range(backward.shape[1]):
        stored[0, i] = to_tile(backward[0, i].astype(jnp.float32), scratch)

    @pl.when(pl.program_id(0) == 0)
    def _():
        orients = coupling.shape[0]
        ratios = [each[w : w + 1] / each[1:2] for each in (axial, lateral, depth) for w in (0, 2)]
        for i, ratio in enumerate(ratios + ratios[:2]):
            taps[i : i + 1] = jnp.concatenate([ratio, ratio], axis=1)
        square = (orients, orients)
        same = lax.broadcasted_iota(jnp.int32, square, 0) == lax.broadcasted_iota(jnp.int32, square, 1)
        kernel = jnp.where(same, diagonal[...], 0.0) + coupling[...]
        kernel = kernel * (axial[1:2] * lateral[1:2] * depth[1:2])
        upper = jnp.concatenate([kernel, jnp.zeros_like(kernel)], axis=1)
        twice = jnp.concatenate([upper, pltpu.roll(upper, orients, 1)], axis=0).T
        coarse = twice.astype(jnp.bfloat16)
        fine = (twice - coarse.astype(jnp.float32)).astype(jnp.bfloat16)
        weights[...] = jnp.concatenate(
            [jnp.concatenate([coarse, fine], axis=1), jnp.concatenate([coarse, jnp.zeros_like(fine)], axis=1)], axis=0
        )


def prepare(backward, axial, lateral, depth, diagonal, coupling):
    steps, planes, orients, cells = backward.shape
    rows, lanes = 2 * orients, cells // 2
    small = [axial, lateral, depth, diagonal.reshape(1, -1), coupling]
    return pl.pallas_call(
        prepare_kernel,
        grid=(steps,),
        in_specs=[pl.BlockSpec((1, planes, orients, cells), lambda s: (s, 0, 0, 0))]
        + [pl.BlockSpec(each.shape, lambda s: (0, 0)) for each in small],
        out_specs=[
            pl.BlockSpec((1, planes, rows, lanes), lambda s: (s, 0, 0, 0)),
            pl.BlockSpec((8, lanes), lambda s: (0, 0)),
            pl.BlockSpec((2 * rows, 2 * lanes), lambda s: (0, 0)),
        ],
        out_shape=[
            jax.ShapeDtypeStruct((steps, planes, rows, lanes), jnp.float32),
            jax.ShapeDtypeStruct((8, lanes), jnp.float32),
            jax.ShapeDtypeStruct((2 * rows, 2 * lanes), jnp.bfloat16),
        ],
        scratch_shapes=[pltpu.VMEM((rows, lanes), jnp.float32)],
        compiler_params=pltpu.CompilerParams(vmem_limit_bytes=VMEM_BYTES),
    )(backward, *small)


def places(odd, pair, reach):
    width = 2 * pair
    far = reach - width
    starts = []
    for core in (odd, 1 - odd):
        starts += [
            reach + pair * core,
            far + pair * core,
            reach + width + pair * core,
            jnp.where(core == 0, reach + 2 * width, 0),
        ]
    return starts


def kind_of(kinds, step, steps):
    sec = lax.axis_index("sec")
    apart = sec ^ (sec // 2 + step // steps)
    each = [ref[0, step % steps] for ref in kinds]
    return jnp.where(
        apart == 0, each[0], jnp.where(apart == 1, each[1], jnp.where(apart == 2, each[2], each[3]))
    )


def run_steps(kinds, steps, taps, weights, begun, count, slab, other, first, second, factor, after):
    tap = [taps[i : i + 1, :] for i in range(6)]
    extent, rows, lanes = slab.shape
    buffers = (slab, other)

    def blend(source, at, packed):
        for i in range(GROUP):
            e = stencil(source[at + i - 1], source[at + i], source[at + i + 1], tap)
            coarse = e.astype(jnp.bfloat16)
            packed[i * rows : (i + 1) * rows, :lanes] = coarse
            packed[i * rows : (i + 1) * rows, lanes:] = (e - coarse.astype(jnp.float32)).astype(jnp.bfloat16)

    def mix(target, at, packed, kind):
        product = jnp.dot(packed[...], weights[...], preferred_element_type=jnp.float32)
        product = product[:, :lanes] + product[:, lanes:]
        for i in range(GROUP):
            target[at + i] = product[i * rows : (i + 1) * rows] * factor[kind, at + i]

    for step in range(count):
        source, target = buffers[step % 2], buffers[1 - step % 2]
        begin, width = step + 1, extent - 2 * step - 2
        groups = -(-width // GROUP)
        kind = kind_of(kinds, begun + step, steps)

        def at(i, begin=begin, width=width):
            return jnp.minimum(begin + i * GROUP, begin + width - GROUP)

        blend(source, at(0), first)
        if groups > 1:

            def body(i, carry, source=source, target=target, at=at, kind=kind):
                blend(source, at(2 * i + 1), second)
                mix(target, at(2 * i), first, kind)
                blend(source, at(2 * i + 2), first)
                mix(target, at(2 * i + 1), second, kind)
                return carry

            lax.fori_loop(0, (groups - 1) // 2, body, 0)
        if groups % 2 == 0:
            blend(source, at(groups - 1), second)
            mix(target, at(groups - 2), first, kind)
            mix(target, at(groups - 1), second, kind)
        else:
            mix(target, at(groups - 1), first, kind)
        after(step, target)


def spread_factor(columns, factor, starts, kinds, pair):
    rows, lanes = factor.shape[2:]
    left = lax.broadcasted_iota(jnp.int32, (rows, lanes), 1) < lanes // 2
    for piece, start in enumerate(starts):
        for kind in range(kinds):
            for i in range(pair):
                at = piece * FIELD_ROWS + (kind * pair + i) * 2
                factor[kind, start + i] = jnp.where(left, columns[:, at : at + 1], columns[:, at + 1 : at + 2])


def early_kernel(half, *refs):
    kinds, taps, weights, pieces, (stored, next_stored) = refs[:4], refs[4], refs[5], refs[6:14], refs[14:16]
    middle, half_out, kept, total, factor = refs[16:21]
    slab, other, first, second, scratch = refs[21:]
    sec, odd = position()
    planes, rows = middle.shape[:2]
    pair = planes // 2
    starts = places(odd, pair, half)
    for piece, start in zip(pieces, starts):
        for i in range(pair):
            slab[start + i] = piece[i * rows : (i + 1) * rows]
    scratch[...] = jnp.exp(-jnp.concatenate([piece[pair * rows :] for piece in pieces], axis=0)).T
    spread_factor(reorder(scratch), factor, starts, factor.shape[0], pair)
    steps = stored.shape[0]
    total[...] = jnp.zeros(total.shape, jnp.float32)

    def after(step, state):
        @pl.when(sec == 0)
        def _():
            source = stored if step < steps else next_stored
            total[...] += state[half : half + planes] * source[step % steps]
            if step + 1 == steps:
                kept[...] = state[half : half + planes]

    run_steps(kinds, steps, taps, weights, 0, half, slab, other, first, second, factor, after)
    state = (slab, other)[half % 2]
    middle[...] = state[half : half + planes]
    half_out[...] = state[pl.ds(half + pair * odd, pair)]


def late_kernel(half, last, *refs):
    kinds, taps, weights, middle, pieces, factor = refs[:4], refs[4], refs[5], refs[6], refs[7:13], refs[13]
    kept, total_in, stored, next_stored, last_stored = refs[14:19]
    handoff, share, to_pair, to_across, to_corner = refs[19:24]
    slab, other, first, second, scratch, total, saved, whole = refs[24:]
    sec, odd = position()
    planes, rows = middle.shape[:2]
    pair = planes // 2
    starts = places(odd, pair, half)
    slab[half : half + planes] = middle[...]
    for piece, start in zip(pieces, starts[1:4] + starts[5:8]):
        for i in range(pair):
            slab[start + i] = piece[i]
    steps = stored.shape[0]
    total[...] = total_in[...]
    saved[...] = kept[...]

    def after(step, state):
        step = step + half

        @pl.when(sec == 0)
        def _():
            source = next_stored if step < 2 * steps else last_stored
            total[...] += state[half : half + planes] * source[step % steps]

        if step + 1 == 2 * steps:

            @pl.when(sec == 1)
            def _():
                saved[...] = state[half : half + planes]

        if step >= 2 * steps:

            @pl.when(sec == last)
            def _():
                total[...] += state[half : half + planes] * stored[step % steps]

    run_steps(kinds, steps, taps, weights, half, half, slab, other, first, second, factor, after)
    state = (slab, other)[half % 2]

    @pl.when(sec == last)
    def _():
        saved[...] = state[half : half + planes]

    orients = handoff.shape[1]
    count = orients // (last + 1)
    held = planes * count
    to_corner[...] = jnp.zeros(to_corner.shape, jnp.float32)
    for i in range(planes):
        handoff[i] = from_tile(saved[i], scratch)
        whole[...] = from_tile(total[i], scratch)
        for piece, who in (
            (share, sec),
            (to_pair, sec + 1 - 2 * odd),
            (to_across, jnp.where(sec == 0, 2, 1)),
            (to_corner, last - sec),
        ):
            piece[i * count : (i + 1) * count] = whole[pl.ds(pl.multiple_of(who * count, count), count)]
    for i in range(pair):
        to_across[held + i * orients : held + (i + 1) * orients] = from_tile(state[half + pair * odd + i], scratch)

    @pl.when(sec == 1)
    def _():
        to_corner[...] = to_across[held:]


def call(kernel, out_shape, scratch, operands, scalars=()):
    return pl.pallas_call(
        kernel,
        in_specs=[IN_SMEM] * len(scalars) + [IN_VMEM] * len(operands),
        out_specs=[IN_VMEM] * len(out_shape),
        out_shape=[jax.ShapeDtypeStruct(shape, jnp.float32) for shape in out_shape],
        scratch_shapes=scratch,
        compiler_params=pltpu.CompilerParams(vmem_limit_bytes=VMEM_BYTES),
    )(*scalars, *operands)


def paired(incoming, backward, fields, block_types, axial_taps, lateral_taps, depth_taps, bend_diagonal, bend_coupling):
    n_sec, n_gx = lax.axis_size("sec"), lax.axis_size("gx")
    steps, planes, orients, cells = backward.shape
    pair = planes // 2
    half = TICKS * steps // 2
    rows = 2 * orients
    lanes = cells // 2
    sec = lax.axis_index("sec")
    last = n_sec - 1

    def send(array, by_sec, shift=lambda s: 0):
        pairs = [
            (s * n_gx + g, t * n_gx + (g + shift(s)) % n_gx) for s, t in enumerate(by_sec) for g in range(n_gx)
        ]
        return lax.ppermute(array, ("sec", "gx"), pairs)

    same, beside, across = (0, 1, 2, 3), (1, 0, 3, 2), (2, 3, 0, 1)
    whole = incoming[0]
    moved_high = send(whole[pair:], (1, 3, 0, 2))
    moved_low = send(whole[:pair], (0, 2, 1, 3))
    kinds = [block_types, send(block_types, beside), send(block_types, across), send(block_types, (3, 2, 1, 0))]
    stored, taps, weights = prepare(backward, axial_taps, lateral_taps, depth_taps, bend_diagonal, bend_coupling)

    tile = pltpu.VMEM((rows, lanes), jnp.float32)
    slab = pltpu.VMEM((planes + 2 * half, rows, lanes), jnp.float32)
    packed = pltpu.VMEM((GROUP * rows, 2 * lanes), jnp.bfloat16)
    inner = pltpu.VMEM((planes, rows, lanes), jnp.float32)
    work = [slab, slab, packed, packed, tile]

    def exchange(piece):
        own = [
            send(piece, same, lambda s: 1),
            send(piece, same, lambda s: -1),
            send(piece, same, lambda s: -2 if s % 2 == 0 else 2),
        ]
        return own, [send(each, beside) for each in own]

    (piece,) = call(
        pack_kernel, [(pair * rows + FIELD_ROWS, lanes)], [tile], [whole, moved_high, moved_low, fields]
    )
    own, swapped = exchange(piece)
    next_stored = send(lax.optimization_barrier((stored, piece))[0], beside)
    last_stored = send(lax.optimization_barrier((stored, own[0]))[0], across)
    middle, piece, kept, total, factor = call(
        functools.partial(early_kernel, half),
        [(planes, rows, lanes), (pair, rows, lanes), (planes, rows, lanes), (planes, rows, lanes)]
        + [(fields.shape[0], planes + 2 * half, rows, lanes)],
        work,
        [taps, weights, piece, *own, send(piece, beside), *swapped, stored, next_stored],
        kinds,
    )
    own, swapped = exchange(piece)
    held = planes * (orients // n_sec)
    handoff, share, to_pair, to_across, to_corner = call(
        functools.partial(late_kernel, half, last),
        [(planes, orients, cells)]
        + [(held, cells)] * 2
        + [(held + pair * orients, cells), (pair * orients, cells)],
        work + [inner, inner, pltpu.VMEM((orients, cells), jnp.float32)],
        [taps, weights, middle, *own, *swapped, factor, kept, total, stored, next_stored, last_stored],
        kinds,
    )
    to_pair = send(to_pair, beside)
    to_across = send(to_across, (2, 0, 3, 1))
    to_corner = send(to_corner, (3, 2, 1, 0))
    third = sec == 2
    density = share + to_pair + to_across[:held] + jnp.where(third, 0.0, to_corner[:held])
    arrived = jnp.concatenate([to_across[held:], to_corner]).reshape(handoff.shape)
    handoff = jnp.where(third, arrived, handoff)
    return handoff[None], density.reshape(planes, -1, cells) / (n_sec * steps)


def pairs_fit(n_sec, planes, steps, orients, cells, kinds):
    return (
        n_sec == TICKS + 1 == 4
        and planes == steps
        and planes % 2 == 0
        and TICKS * steps == 2 * (planes + planes // 2)
        and 2 * orients == 2 * CZ == cells // 2 == 128
        and kinds * planes <= FIELD_ROWS
        and planes >= GROUP
    )


def solution(mesh):
    in_specs = (
        P("sec", "gx", None, None),
        P("sec", "gx", None, None),
        P(None, "gx", None),
        P("sec", None),
        P(),
        P(),
        P(),
        P(),
        P(),
    )
    out_specs = (P("sec", "gx", None, None), P("gx", "sec", None))

    def body(incoming, backward, fields, *rest):
        steps, planes, orients, cells = backward.shape
        fits = pairs_fit(mesh.shape["sec"], planes, steps, orients, cells, fields.shape[0])
        return (paired if fits else per_device)(incoming, backward, fields, *rest)

    return jax.shard_map(body, mesh=mesh, in_specs=in_specs, out_specs=out_specs, check_vma=False)
```

```python
import functools

import jax
import jax.numpy as jnp
from jax import lax
from jax.experimental import pallas as pl
from jax.experimental.pallas import tpu as pltpu
from jax.sharding import PartitionSpec as P

TICKS = 3
CZ = 64
GROUP = 4
FIELD_ROWS = 16
VMEM_BYTES = 48 * 2**20
IN_VMEM = pl.BlockSpec(memory_space=pltpu.VMEM)
IN_SMEM = pl.BlockSpec(memory_space=pltpu.SMEM)


def padded_2(block, sides, width):
    for axis, dim in sides:
        count = lax.axis_size(axis)
        forward = [(i, i + 1) for i in range(count - 1)]
        forward.append((count - 1, 0))
        backward = [(target, source) for source, target in forward]
        low = lax.ppermute(
            lax.slice_in_dim(block, block.shape[dim] - width, None, axis=dim), axis, forward
        )
        high = lax.ppermute(lax.slice_in_dim(block, 0, width, axis=dim), axis, backward)
        block = jnp.concatenate([low, block, high], axis=dim)
    return block


def from_behind(array, axis, by):
    length = lax.axis_size(axis)
    pairs = [(i, i + by) for i in range(length) if 0 <= i + by < length]
    return lax.ppermute(array, axis, pairs)


def boltzmann(fields, kinds):
    selector = kinds == jnp.arange(fields.shape[0], dtype=jnp.int32)
    chosen = jnp.sum(jnp.where(selector[:, None, None], fields, jnp.zeros_like(fields)), axis=0)
    return jnp.exp(-chosen)


def column(taps, which):
    return taps[which][None, :, None]


def advance_padded(padded, factor, axial_taps, lateral_taps, depth_taps, kernel):
    along_x = (
        column(axial_taps, 0) * padded[:-2]
        + column(axial_taps, 1) * padded[1:-1]
        + column(axial_taps, 2) * padded[2:]
    )
    along_y = (
        column(lateral_taps, 0) * jnp.roll(along_x, CZ, axis=2)
        + column(lateral_taps, 1) * along_x
        + column(lateral_taps, 2) * jnp.roll(along_x, -CZ, axis=2)
    )
    depth_pos = (jnp.arange(along_y.shape[2], dtype=jnp.int32) % CZ)[None, None, :]
    behind = jnp.where(
        depth_pos == 0, jnp.roll(along_y, -(CZ - 1), axis=2), jnp.roll(along_y, 1, axis=2)
    )
    ahead = jnp.where(
        depth_pos == CZ - 1, jnp.roll(along_y, CZ - 1, axis=2), jnp.roll(along_y, -1, axis=2)
    )
    along_z = (
        column(depth_taps, 0) * behind
        + column(depth_taps, 1) * along_y
        + column(depth_taps, 2) * ahead
    )
    blended = jnp.einsum(
        "uv,xvc->xuc",
        kernel,
        along_z,
        precision=lax.Precision.HIGHEST,
        preferred_element_type=jnp.float32,
    )
    return blended * factor[:, None, :]


def per_device(
    incoming,
    backward,
    fields,
    block_types,
    axial_taps,
    lateral_taps,
    depth_taps,
    bend_diagonal,
    bend_coupling,
):
    kernel = jnp.diag(bend_diagonal) + bend_coupling
    steps_each = block_types.shape[1]
    planes = incoming.shape[1]
    start = incoming[0]
    first_section = lax.axis_index("sec") == 0
    wide_fields = padded_2(fields, (("gx", 1),), steps_each)
    factors = [boltzmann(wide_fields, block_types[0, position]) for position in range(steps_each)]
    current = start
    outgoing = start
    accumulated = jnp.zeros(start.shape, jnp.float32)
    for tick_index in range(TICKS):
        final_tick = tick_index + 1 == TICKS
        extended = padded_2(current, (("gx", 0),), steps_each)
        for position in range(steps_each):
            margin = steps_each - position - 1
            offset = steps_each - margin
            factor = factors[position][offset : offset + planes + 2 * margin]
            extended = advance_padded(
                extended, factor, axial_taps, lateral_taps, depth_taps, kernel
            )
            if final_tick:
                accumulated = accumulated + extended[margin : margin + planes] * backward[
                    position
                ].astype(jnp.float32)
        outgoing = extended
        if not final_tick:
            shifted = from_behind(outgoing, "sec", 1)
            current = jnp.where(first_section, start, shifted)
    reduced = lax.psum_scatter(accumulated, "sec", scatter_dimension=1, tiled=True)
    density = reduced / (lax.axis_size("sec") * steps_each)
    return (outgoing[None], density)


def to_tile(plane, scratch):
    half = plane.shape[1] // 2
    scratch[...] = jnp.concatenate([plane[:, :half], plane[:, half:]], axis=0).T
    return reorder(scratch)


def reorder(scratch):
    rows = scratch.shape[0]
    return jnp.concatenate(
        [scratch[pl.ds(yl * CZ + zl, 8, stride=8), :] for yl in range(rows // CZ) for zl in range(CZ // 8)], axis=0
    )


def from_tile(tile, scratch):
    rows = tile.shape[0]
    for yl in range(rows // CZ):
        for zl in range(CZ // 8):
            at = (yl * (CZ // 8) + zl) * 8
            scratch[pl.ds(yl * CZ + zl, 8, stride=8), :] = tile[at : at + 8]
    turned = scratch[...].T
    half = turned.shape[0] // 2
    return jnp.concatenate([turned[:half], turned[half:]], axis=1)


def stencil(behind, here, ahead, taps):
    a = here + taps[0] * behind + taps[1] * ahead
    low, high = a[:CZ], a[CZ:]
    low_turned = pltpu.roll(low, a.shape[1] // 2, 1)
    high_turned = pltpu.roll(high, a.shape[1] // 2, 1)
    out = []
    for b in (
        low + taps[2] * high_turned + taps[3] * high,
        high + taps[2] * low + taps[3] * low_turned,
    ):
        back = jnp.concatenate([pltpu.roll(b[-8:], 1, 0), b[:-8]], axis=0)
        front = jnp.concatenate([b[8:], pltpu.roll(b[:8], 7, 0)], axis=0)
        out.append(b + taps[4] * back + taps[5] * front)
    return jnp.concatenate(out, axis=0)


def position():
    sec = lax.axis_index("sec")
    return sec, lax.rem(sec, 2)


def prepare_kernel(*refs):
    sources, (early, late, start, taps, weights) = refs[:8], refs[8:13]
    scratch, copies, sems = refs[13], refs[14:22], refs[22]
    moves = [pltpu.make_async_copy(s, c, sems.at[i]) for i, (s, c) in enumerate(zip(sources, copies))]
    for move in moves:
        move.start()
    backward, incoming, fields, axial, lateral, depth, diagonal, coupling = copies
    for move in moves[3:]:
        move.wait()
    orients = coupling.shape[0]
    ratios = [each[w : w + 1] / each[1:2] for each in (axial, lateral, depth) for w in (0, 2)]
    for i, ratio in enumerate(ratios + ratios[:2]):
        taps[i : i + 1] = jnp.concatenate([ratio, ratio], axis=1)
    square = (orients, orients)
    same = lax.broadcasted_iota(jnp.int32, square, 0) == lax.broadcasted_iota(jnp.int32, square, 1)
    kernel = jnp.where(same, diagonal[...], 0.0) + coupling[...]
    kernel = kernel * (axial[1:2] * lateral[1:2] * depth[1:2])
    upper = jnp.concatenate([kernel, jnp.zeros_like(kernel)], axis=1)
    twice = jnp.concatenate([upper, pltpu.roll(upper, orients, 1)], axis=0).T
    coarse = twice.astype(jnp.bfloat16)
    fine = (twice - coarse.astype(jnp.float32)).astype(jnp.bfloat16)
    weights[...] = jnp.concatenate(
        [jnp.concatenate([coarse, fine], axis=1), jnp.concatenate([coarse, jnp.zeros_like(fine)], axis=1)], axis=0
    )
    odd = position()[1]
    rows = scratch.shape[0]
    pair = incoming.shape[1] // 2
    moves[1].wait()
    for i in range(pair):
        start[i * rows : (i + 1) * rows] = to_tile(incoming[0, i], scratch)
    moves[2].wait()
    start[pair * rows :] = jnp.zeros((FIELD_ROWS, rows), jnp.float32)
    for kind in range(fields.shape[0]):
        for i in range(pair):
            line = fields[kind, pl.ds(pair * odd + i, 1), :]
            at = pair * rows + (kind * pair + i) * 2
            start[at : at + 1] = line[:, :rows]
            start[at + 1 : at + 2] = line[:, rows:]
    moves[0].wait()
    steps, planes = backward.shape[:2]
    for out, begin in ((early, 0), (late, steps // 2)):
        for step in range(steps // 2):
            for i in range(planes):
                out[step, i] = to_tile(backward[begin + step, i].astype(jnp.float32), scratch)


def prepare(backward, incoming, fields, axial, lateral, depth, diagonal, coupling):
    steps, planes, orients, cells = backward.shape
    rows, lanes = 2 * orients, cells // 2
    operands = [backward, incoming, fields, axial, lateral, depth, diagonal.reshape(1, -1), coupling]
    half = ((steps // 2, planes, rows, lanes), jnp.float32)
    piece = ((planes // 2 * rows + FIELD_ROWS, lanes), jnp.float32)
    return pl.pallas_call(
        prepare_kernel,
        in_specs=[pl.BlockSpec(memory_space=pltpu.HBM)] * len(operands),
        out_specs=[IN_VMEM] * 5,
        out_shape=[
            jax.ShapeDtypeStruct(*each)
            for each in (half, half, piece, ((8, lanes), jnp.float32), ((2 * rows, 2 * lanes), jnp.bfloat16))
        ],
        scratch_shapes=[pltpu.VMEM((rows, lanes), jnp.float32)]
        + [pltpu.VMEM(each.shape, each.dtype) for each in operands]
        + [pltpu.SemaphoreType.DMA((len(operands),))],
        compiler_params=pltpu.CompilerParams(vmem_limit_bytes=VMEM_BYTES),
    )(*operands)


def pack_kernel(start, moved_high, moved_low, out, scratch):
    sec, odd = position()
    rows = scratch.shape[0]
    out[...] = start[...]

    def fill(source):
        for i in range(source.shape[0]):
            out[i * rows : (i + 1) * rows] = to_tile(source[i], scratch)

    pl.when(odd == 1)(lambda: fill(moved_high))
    pl.when((sec > 0) & (odd == 0))(lambda: fill(moved_low))


def places(odd, pair, reach):
    width = 2 * pair
    far = reach - width
    starts = []
    for core in (odd, 1 - odd):
        starts += [
            reach + pair * core,
            far + pair * core,
            reach + width + pair * core,
            jnp.where(core == 0, reach + 2 * width, 0),
        ]
    return starts


def kind_of(kinds, step, steps):
    sec = lax.axis_index("sec")
    apart = sec ^ (sec // 2 + step // steps)
    each = [ref[0, step % steps] for ref in kinds]
    return jnp.where(
        apart == 0, each[0], jnp.where(apart == 1, each[1], jnp.where(apart == 2, each[2], each[3]))
    )


def run_steps(kinds, steps, taps, weights, begun, count, slab, other, first, second, factor, after):
    tap = [taps[i : i + 1, :] for i in range(6)]
    extent, rows, lanes = slab.shape
    buffers = (slab, other)

    def blend(source, at, packed):
        for i in range(GROUP):
            e = stencil(source[at + i - 1], source[at + i], source[at + i + 1], tap)
            coarse = e.astype(jnp.bfloat16)
            packed[i * rows : (i + 1) * rows, :lanes] = coarse
            packed[i * rows : (i + 1) * rows, lanes:] = (e - coarse.astype(jnp.float32)).astype(jnp.bfloat16)

    def mix(target, at, packed, kind):
        product = jnp.dot(packed[...], weights[...], preferred_element_type=jnp.float32)
        product = product[:, :lanes] + product[:, lanes:]
        for i in range(GROUP):
            target[at + i] = product[i * rows : (i + 1) * rows] * factor[kind, at + i]

    for step in range(count):
        source, target = buffers[step % 2], buffers[1 - step % 2]
        begin, width = step + 1, extent - 2 * step - 2
        groups = -(-width // GROUP)
        kind = kind_of(kinds, begun + step, steps)

        def at(i, begin=begin, width=width):
            return jnp.minimum(begin + i * GROUP, begin + width - GROUP)

        blend(source, at(0), first)
        if groups > 1:

            def body(i, carry, source=source, target=target, at=at, kind=kind):
                blend(source, at(2 * i + 1), second)
                mix(target, at(2 * i), first, kind)
                blend(source, at(2 * i + 2), first)
                mix(target, at(2 * i + 1), second, kind)
                return carry

            lax.fori_loop(0, (groups - 1) // 2, body, 0)
        if groups % 2 == 0:
            blend(source, at(groups - 1), second)
            mix(target, at(groups - 2), first, kind)
            mix(target, at(groups - 1), second, kind)
        else:
            mix(target, at(groups - 1), first, kind)
        after(step, target)


def spread_factor(columns, factor, starts, kinds, pair):
    rows, lanes = factor.shape[2:]
    left = lax.broadcasted_iota(jnp.int32, (rows, lanes), 1) < lanes // 2
    for piece, start in enumerate(starts):
        for kind in range(kinds):
            for i in range(pair):
                at = piece * FIELD_ROWS + (kind * pair + i) * 2
                factor[kind, start + i] = jnp.where(left, columns[:, at : at + 1], columns[:, at + 1 : at + 2])


def early_kernel(half, *refs):
    kinds, taps, weights, pieces, series = refs[:4], refs[4], refs[5], refs[6:14], refs[14:17]
    middle, half_out, kept, total, factor = refs[17:22]
    slab, other, first, second, scratch = refs[22:]
    sec, odd = position()
    planes, rows = middle.shape[:2]
    pair = planes // 2
    starts = places(odd, pair, half)
    for piece, start in zip(pieces, starts):
        for i in range(pair):
            slab[start + i] = piece[i * rows : (i + 1) * rows]
    scratch[...] = jnp.exp(-jnp.concatenate([piece[pair * rows :] for piece in pieces], axis=0)).T
    spread_factor(reorder(scratch), factor, starts, factor.shape[0], pair)
    span = series[0].shape[0]
    steps = 2 * span
    total[...] = jnp.zeros(total.shape, jnp.float32)

    def after(step, state):
        @pl.when(sec == 0)
        def _():
            total[...] += state[half : half + planes] * series[step // span][step % span]
            if step + 1 == steps:
                kept[...] = state[half : half + planes]

    run_steps(kinds, steps, taps, weights, 0, half, slab, other, first, second, factor, after)
    state = (slab, other)[half % 2]
    middle[...] = state[half : half + planes]
    half_out[...] = state[pl.ds(half + pair * odd, pair)]


def late_kernel(half, last, *refs):
    kinds, taps, weights, middle, pieces, factor = refs[:4], refs[4], refs[5], refs[6], refs[7:13], refs[13]
    kept, total_in, series, stored = refs[14], refs[15], refs[16:19], refs[19:21]
    handoff, share, to_pair, to_across, to_corner = refs[21:26]
    slab, other, first, second, scratch, total, saved, whole = refs[26:]
    sec, odd = position()
    planes, rows = middle.shape[:2]
    pair = planes // 2
    starts = places(odd, pair, half)
    slab[half : half + planes] = middle[...]
    for piece, start in zip(pieces, starts[1:4] + starts[5:8]):
        for i in range(pair):
            slab[start + i] = piece[i]
    span = series[0].shape[0]
    steps = 2 * span
    total[...] = total_in[...]
    saved[...] = kept[...]

    def after(step, state):
        part = step // span
        step = step + half

        @pl.when(sec == 0)
        def _():
            total[...] += state[half : half + planes] * series[part][step % span]

        if step + 1 == 2 * steps:

            @pl.when(sec == 1)
            def _():
                saved[...] = state[half : half + planes]

        if step >= 2 * steps:

            @pl.when(sec == last)
            def _():
                total[...] += state[half : half + planes] * stored[step % steps // span][step % span]

    run_steps(kinds, steps, taps, weights, half, half, slab, other, first, second, factor, after)
    state = (slab, other)[half % 2]

    @pl.when(sec == last)
    def _():
        saved[...] = state[half : half + planes]

    orients = handoff.shape[1]
    count = orients // (last + 1)
    held = planes * count
    to_corner[...] = jnp.zeros(to_corner.shape, jnp.float32)
    for i in range(planes):
        handoff[i] = from_tile(saved[i], scratch)
        whole[...] = from_tile(total[i], scratch)
        for piece, who in (
            (share, sec),
            (to_pair, sec + 1 - 2 * odd),
            (to_across, jnp.where(sec == 0, 2, 1)),
            (to_corner, last - sec),
        ):
            piece[i * count : (i + 1) * count] = whole[pl.ds(pl.multiple_of(who * count, count), count)]
    for i in range(pair):
        to_across[held + i * orients : held + (i + 1) * orients] = from_tile(state[half + pair * odd + i], scratch)

    @pl.when(sec == 1)
    def _():
        to_corner[...] = to_across[held:]


def call(kernel, out_shape, scratch, operands, scalars=()):
    return pl.pallas_call(
        kernel,
        in_specs=[IN_SMEM] * len(scalars) + [IN_VMEM] * len(operands),
        out_specs=[IN_VMEM] * len(out_shape),
        out_shape=[jax.ShapeDtypeStruct(shape, jnp.float32) for shape in out_shape],
        scratch_shapes=scratch,
        compiler_params=pltpu.CompilerParams(vmem_limit_bytes=VMEM_BYTES),
    )(*scalars, *operands)


def paired(incoming, backward, fields, block_types, axial_taps, lateral_taps, depth_taps, bend_diagonal, bend_coupling):
    n_sec, n_gx = lax.axis_size("sec"), lax.axis_size("gx")
    steps, planes, orients, cells = backward.shape
    pair = planes // 2
    half = TICKS * steps // 2
    rows = 2 * orients
    lanes = cells // 2
    sec = lax.axis_index("sec")
    last = n_sec - 1

    def send(array, by_sec, shift=lambda s: 0):
        pairs = [
            (s * n_gx + g, t * n_gx + (g + shift(s)) % n_gx) for s, t in enumerate(by_sec) for g in range(n_gx)
        ]
        return lax.ppermute(array, ("sec", "gx"), pairs)

    same, beside, across, crossing = (0, 1, 2, 3), (1, 0, 3, 2), (2, 3, 0, 1), (2, 1, 0, 3)
    whole = incoming[0]
    backward, moved = lax.optimization_barrier((backward, whole[pair:]))
    moved_high = send(moved, (1, 3, 0, 2))
    moved_low = send(whole[:pair], (0, 2, 1, 3))
    kinds = [block_types, send(block_types, beside), send(block_types, across), send(block_types, (3, 2, 1, 0))]
    early_stored, late_stored, start, taps, weights = prepare(
        backward, incoming, fields, axial_taps, lateral_taps, depth_taps, bend_diagonal, bend_coupling
    )
    early_next, early_last = send(early_stored, beside), send(early_stored, crossing)

    tile = pltpu.VMEM((rows, lanes), jnp.float32)
    slab = pltpu.VMEM((planes + 2 * half, rows, lanes), jnp.float32)
    packed = pltpu.VMEM((GROUP * rows, 2 * lanes), jnp.bfloat16)
    inner = pltpu.VMEM((planes, rows, lanes), jnp.float32)
    work = [slab, slab, packed, packed, tile]

    def exchange(piece):
        own = [
            send(piece, same, lambda s: 1),
            send(piece, same, lambda s: -1),
            send(piece, same, lambda s: -2 if s % 2 == 0 else 2),
        ]
        return own, [send(each, beside) for each in own]

    (piece,) = call(
        pack_kernel, [(pair * rows + FIELD_ROWS, lanes)], [tile], [start, moved_high, moved_low]
    )
    own, swapped = exchange(piece)
    late_stored, *swapped = lax.optimization_barrier((late_stored, *swapped))
    late_next, late_last = send(late_stored, beside), send(late_stored, crossing)
    middle, piece, kept, total, factor = call(
        functools.partial(early_kernel, half),
        [(planes, rows, lanes), (pair, rows, lanes), (planes, rows, lanes), (planes, rows, lanes)]
        + [(fields.shape[0], planes + 2 * half, rows, lanes)],
        work,
        [taps, weights, piece, *own, send(piece, beside), *swapped, early_stored, late_stored, early_next],
        kinds,
    )
    own, swapped = exchange(piece)
    held = planes * (orients // n_sec)
    handoff, share, to_pair, to_across, to_corner = call(
        functools.partial(late_kernel, half, last),
        [(planes, orients, cells)]
        + [(held, cells)] * 2
        + [(held + pair * orients, cells), (pair * orients, cells)],
        work + [inner, inner, pltpu.VMEM((orients, cells), jnp.float32)],
        [taps, weights, middle, *own, *swapped, factor, kept, total]
        + [late_next, early_last, late_last, early_stored, late_stored],
        kinds,
    )
    to_pair = send(to_pair, beside)
    to_across = send(to_across, (2, 0, 3, 1))
    to_corner = send(to_corner, (3, 2, 1, 0))
    third = sec == 2
    density = share + to_pair + to_across[:held] + jnp.where(third, 0.0, to_corner[:held])
    arrived = jnp.concatenate([to_across[held:], to_corner]).reshape(handoff.shape)
    handoff = jnp.where(third, arrived, handoff)
    return handoff[None], density.reshape(planes, -1, cells) / (n_sec * steps)


def pairs_fit(n_sec, planes, steps, orients, cells, kinds):
    return (
        n_sec == TICKS + 1 == 4
        and planes == steps
        and planes % 2 == 0
        and TICKS * steps == 2 * (planes + planes // 2)
        and 2 * orients == 2 * CZ == cells // 2 == 128
        and kinds * planes <= FIELD_ROWS
        and planes >= GROUP
    )


def solution(mesh):
    in_specs = (
        P("sec", "gx", None, None),
        P("sec", "gx", None, None),
        P(None, "gx", None),
        P("sec", None),
        P(),
        P(),
        P(),
        P(),
        P(),
    )
    out_specs = (P("sec", "gx", None, None), P("gx", "sec", None))

    def body(incoming, backward, fields, *rest):
        steps, planes, orients, cells = backward.shape
        fits = pairs_fit(mesh.shape["sec"], planes, steps, orients, cells, fields.shape[0])
        return (paired if fits else per_device)(incoming, backward, fields, *rest)

    return jax.shard_map(body, mesh=mesh, in_specs=in_specs, out_specs=out_specs, check_vma=False)
```

```python
import functools

import jax
import jax.numpy as jnp
from jax import lax
from jax.experimental import pallas as pl
from jax.experimental.pallas import tpu as pltpu
from jax.sharding import PartitionSpec as P

TICKS = 3
CZ = 64
GROUP = 4
FIELD_ROWS = 16
VMEM_BYTES = 16 * 2**20
WHOLE_VMEM_BYTES = 62 * 2**20
IN_VMEM = pl.BlockSpec(memory_space=pltpu.VMEM)
IN_SMEM = pl.BlockSpec(memory_space=pltpu.SMEM)


def padded_2(block, sides, width):
    for axis, dim in sides:
        count = lax.axis_size(axis)
        forward = [(i, i + 1) for i in range(count - 1)]
        forward.append((count - 1, 0))
        backward = [(target, source) for source, target in forward]
        low = lax.ppermute(
            lax.slice_in_dim(block, block.shape[dim] - width, None, axis=dim), axis, forward
        )
        high = lax.ppermute(lax.slice_in_dim(block, 0, width, axis=dim), axis, backward)
        block = jnp.concatenate([low, block, high], axis=dim)
    return block


def from_behind(array, axis, by):
    length = lax.axis_size(axis)
    pairs = [(i, i + by) for i in range(length) if 0 <= i + by < length]
    return lax.ppermute(array, axis, pairs)


def boltzmann(fields, kinds):
    selector = kinds == jnp.arange(fields.shape[0], dtype=jnp.int32)
    chosen = jnp.sum(jnp.where(selector[:, None, None], fields, jnp.zeros_like(fields)), axis=0)
    return jnp.exp(-chosen)


def column(taps, which):
    return taps[which][None, :, None]


def advance_padded(padded, factor, axial_taps, lateral_taps, depth_taps, kernel):
    along_x = (
        column(axial_taps, 0) * padded[:-2]
        + column(axial_taps, 1) * padded[1:-1]
        + column(axial_taps, 2) * padded[2:]
    )
    along_y = (
        column(lateral_taps, 0) * jnp.roll(along_x, CZ, axis=2)
        + column(lateral_taps, 1) * along_x
        + column(lateral_taps, 2) * jnp.roll(along_x, -CZ, axis=2)
    )
    depth_pos = (jnp.arange(along_y.shape[2], dtype=jnp.int32) % CZ)[None, None, :]
    behind = jnp.where(
        depth_pos == 0, jnp.roll(along_y, -(CZ - 1), axis=2), jnp.roll(along_y, 1, axis=2)
    )
    ahead = jnp.where(
        depth_pos == CZ - 1, jnp.roll(along_y, CZ - 1, axis=2), jnp.roll(along_y, -1, axis=2)
    )
    along_z = (
        column(depth_taps, 0) * behind
        + column(depth_taps, 1) * along_y
        + column(depth_taps, 2) * ahead
    )
    blended = jnp.einsum(
        "uv,xvc->xuc",
        kernel,
        along_z,
        precision=lax.Precision.HIGHEST,
        preferred_element_type=jnp.float32,
    )
    return blended * factor[:, None, :]


def per_device(
    incoming,
    backward,
    fields,
    block_types,
    axial_taps,
    lateral_taps,
    depth_taps,
    bend_diagonal,
    bend_coupling,
):
    kernel = jnp.diag(bend_diagonal) + bend_coupling
    steps_each = block_types.shape[1]
    planes = incoming.shape[1]
    start = incoming[0]
    first_section = lax.axis_index("sec") == 0
    wide_fields = padded_2(fields, (("gx", 1),), steps_each)
    factors = [boltzmann(wide_fields, block_types[0, position]) for position in range(steps_each)]
    current = start
    outgoing = start
    accumulated = jnp.zeros(start.shape, jnp.float32)
    for tick_index in range(TICKS):
        final_tick = tick_index + 1 == TICKS
        extended = padded_2(current, (("gx", 0),), steps_each)
        for position in range(steps_each):
            margin = steps_each - position - 1
            offset = steps_each - margin
            factor = factors[position][offset : offset + planes + 2 * margin]
            extended = advance_padded(
                extended, factor, axial_taps, lateral_taps, depth_taps, kernel
            )
            if final_tick:
                accumulated = accumulated + extended[margin : margin + planes] * backward[
                    position
                ].astype(jnp.float32)
        outgoing = extended
        if not final_tick:
            shifted = from_behind(outgoing, "sec", 1)
            current = jnp.where(first_section, start, shifted)
    reduced = lax.psum_scatter(accumulated, "sec", scatter_dimension=1, tiled=True)
    density = reduced / (lax.axis_size("sec") * steps_each)
    return (outgoing[None], density)


def to_tile(plane, scratch):
    half = plane.shape[1] // 2
    scratch[...] = jnp.concatenate([plane[:, :half], plane[:, half:]], axis=0).T
    return reorder(scratch)


def reorder(scratch):
    rows = scratch.shape[0]
    return jnp.concatenate(
        [scratch[pl.ds(yl * CZ + zl, 8, stride=8), :] for yl in range(rows // CZ) for zl in range(CZ // 8)], axis=0
    )


def from_tile(tile, scratch):
    rows = tile.shape[0]
    for yl in range(rows // CZ):
        for zl in range(CZ // 8):
            at = (yl * (CZ // 8) + zl) * 8
            scratch[pl.ds(yl * CZ + zl, 8, stride=8), :] = tile[at : at + 8]
    turned = scratch[...].T
    half = turned.shape[0] // 2
    return jnp.concatenate([turned[:half], turned[half:]], axis=1)


def stencil(behind, here, ahead, taps):
    a = here + taps[0] * behind + taps[1] * ahead
    low, high = a[:CZ], a[CZ:]
    low_turned = pltpu.roll(low, a.shape[1] // 2, 1)
    high_turned = pltpu.roll(high, a.shape[1] // 2, 1)
    out = []
    for b in (
        low + taps[2] * high_turned + taps[3] * high,
        high + taps[2] * low + taps[3] * low_turned,
    ):
        back = jnp.concatenate([pltpu.roll(b[-8:], 1, 0), b[:-8]], axis=0)
        front = jnp.concatenate([b[8:], pltpu.roll(b[:8], 7, 0)], axis=0)
        out.append(b + taps[4] * back + taps[5] * front)
    return jnp.concatenate(out, axis=0)


def position():
    sec = lax.axis_index("sec")
    return sec, lax.rem(sec, 2)


def prepare_kernel(*refs):
    sources, (early, late, start, taps, weights) = refs[:8], refs[8:13]
    scratch, copies, sems = refs[13], refs[14:22], refs[22]
    moves = [pltpu.make_async_copy(s, c, sems.at[i]) for i, (s, c) in enumerate(zip(sources, copies))]
    for move in moves:
        move.start()
    backward, incoming, fields, axial, lateral, depth, diagonal, coupling = copies
    for move in moves[3:]:
        move.wait()
    orients = coupling.shape[0]
    ratios = [each[w : w + 1] / each[1:2] for each in (axial, lateral, depth) for w in (0, 2)]
    for i, ratio in enumerate(ratios + ratios[:2]):
        taps[i : i + 1] = jnp.concatenate([ratio, ratio], axis=1)
    square = (orients, orients)
    same = lax.broadcasted_iota(jnp.int32, square, 0) == lax.broadcasted_iota(jnp.int32, square, 1)
    kernel = jnp.where(same, diagonal[...], 0.0) + coupling[...]
    kernel = kernel * (axial[1:2] * lateral[1:2] * depth[1:2])
    upper = jnp.concatenate([kernel, jnp.zeros_like(kernel)], axis=1)
    twice = jnp.concatenate([upper, pltpu.roll(upper, orients, 1)], axis=0).T
    coarse = twice.astype(jnp.bfloat16)
    fine = (twice - coarse.astype(jnp.float32)).astype(jnp.bfloat16)
    weights[...] = jnp.concatenate(
        [jnp.concatenate([coarse, fine], axis=1), jnp.concatenate([coarse, jnp.zeros_like(fine)], axis=1)], axis=0
    )
    odd = position()[1]
    rows = scratch.shape[0]
    pair = incoming.shape[1] // 2
    moves[1].wait()
    for i in range(pair):
        start[i * rows : (i + 1) * rows] = to_tile(incoming[0, i], scratch)
    moves[2].wait()
    start[pair * rows :] = jnp.zeros((FIELD_ROWS, rows), jnp.float32)
    for kind in range(fields.shape[0]):
        for i in range(pair):
            line = fields[kind, pl.ds(pair * odd + i, 1), :]
            at = pair * rows + (kind * pair + i) * 2
            start[at : at + 1] = line[:, :rows]
            start[at + 1 : at + 2] = line[:, rows:]
    moves[0].wait()
    steps, planes = backward.shape[:2]
    for out, begin in ((early, 0), (late, steps // 2)):
        for step in range(steps // 2):
            for i in range(planes):
                out[step, i] = to_tile(backward[begin + step, i].astype(jnp.float32), scratch)


def prepare(backward, incoming, fields, axial, lateral, depth, diagonal, coupling):
    steps, planes, orients, cells = backward.shape
    rows, lanes = 2 * orients, cells // 2
    operands = [backward, incoming, fields, axial, lateral, depth, diagonal.reshape(1, -1), coupling]
    half = ((steps // 2, planes, rows, lanes), jnp.float32)
    piece = ((planes // 2 * rows + FIELD_ROWS, lanes), jnp.float32)
    return pl.pallas_call(
        prepare_kernel,
        in_specs=[pl.BlockSpec(memory_space=pltpu.HBM)] * len(operands),
        out_specs=[IN_VMEM] * 5,
        out_shape=[
            jax.ShapeDtypeStruct(*each)
            for each in (half, half, piece, ((8, lanes), jnp.float32), ((2 * rows, 2 * lanes), jnp.bfloat16))
        ],
        scratch_shapes=[pltpu.VMEM((rows, lanes), jnp.float32)]
        + [pltpu.VMEM(each.shape, each.dtype) for each in operands]
        + [pltpu.SemaphoreType.DMA((len(operands),))],
        compiler_params=pltpu.CompilerParams(vmem_limit_bytes=WHOLE_VMEM_BYTES),
    )(*operands)


def pack_kernel(*refs):
    kinds, start, moved_high, moved_low, out, info, scratch = refs[:4], *refs[4:]
    sec, odd = position()
    rows = scratch.shape[0]
    out[...] = start[...]
    steps = kinds[0].shape[1]
    for step in range(info.shape[1]):
        info[0, step] = kind_of(kinds, step, steps)

    def fill(source):
        for i in range(source.shape[0]):
            out[i * rows : (i + 1) * rows] = to_tile(source[i], scratch)

    pl.when(odd == 1)(lambda: fill(moved_high))
    pl.when((sec > 0) & (odd == 0))(lambda: fill(moved_low))


def places(odd, pair, reach):
    width = 2 * pair
    far = reach - width
    starts = []
    for core in (odd, 1 - odd):
        starts += [
            reach + pair * core,
            far + pair * core,
            reach + width + pair * core,
            jnp.where(core == 0, reach + 2 * width, 0),
        ]
    return starts


def kind_of(kinds, step, steps):
    sec = lax.axis_index("sec")
    apart = sec ^ (sec // 2 + step // steps)
    each = [ref[0, step % steps] for ref in kinds]
    return jnp.where(
        apart == 0, each[0], jnp.where(apart == 1, each[1], jnp.where(apart == 2, each[2], each[3]))
    )


def run_steps(info, taps, weights, begun, count, slab, other, first, second, factor, after):
    tap = [taps[i : i + 1, :] for i in range(6)]
    extent, rows, lanes = slab.shape
    buffers = (slab, other)

    def blend(source, at, packed):
        for i in range(GROUP):
            e = stencil(source[at + i - 1], source[at + i], source[at + i + 1], tap)
            coarse = e.astype(jnp.bfloat16)
            packed[i * rows : (i + 1) * rows, :lanes] = coarse
            packed[i * rows : (i + 1) * rows, lanes:] = (e - coarse.astype(jnp.float32)).astype(jnp.bfloat16)

    def mix(target, at, packed, kind):
        product = jnp.dot(packed[...], weights[...], preferred_element_type=jnp.float32)
        product = product[:, :lanes] + product[:, lanes:]
        for i in range(GROUP):
            target[at + i] = product[i * rows : (i + 1) * rows] * factor[kind, at + i]

    for step in range(count):
        source, target = buffers[step % 2], buffers[1 - step % 2]
        begin, width = step + 1, extent - 2 * step - 2
        groups = -(-width // GROUP)
        kind = info[0, begun + step]

        def at(i, begin=begin, width=width):
            return jnp.minimum(begin + i * GROUP, begin + width - GROUP)

        blend(source, at(0), first)
        if groups > 1:

            def body(i, carry, source=source, target=target, at=at, kind=kind):
                blend(source, at(2 * i + 1), second)
                mix(target, at(2 * i), first, kind)
                blend(source, at(2 * i + 2), first)
                mix(target, at(2 * i + 1), second, kind)
                return carry

            lax.fori_loop(0, (groups - 1) // 2, body, 0)
        if groups % 2 == 0:
            blend(source, at(groups - 1), second)
            mix(target, at(groups - 2), first, kind)
            mix(target, at(groups - 1), second, kind)
        else:
            mix(target, at(groups - 1), first, kind)
        after(step, target)


def spread_factor(columns, factor, starts, kinds, pair):
    rows, lanes = factor.shape[2:]
    left = lax.broadcasted_iota(jnp.int32, (rows, lanes), 1) < lanes // 2
    for piece, start in enumerate(starts):
        for kind in range(kinds):
            for i in range(pair):
                at = piece * FIELD_ROWS + (kind * pair + i) * 2
                factor[kind, start + i] = jnp.where(left, columns[:, at : at + 1], columns[:, at + 1 : at + 2])


def early_kernel(half, *refs):
    info, taps, weights, pieces, stored = refs[0], refs[1], refs[2], refs[3:11], refs[11:13]
    middle, half_out, kept, total, factor = refs[13:18]
    slab, other, first, second, scratch = refs[18:]
    sec, odd = position()
    planes, rows = middle.shape[:2]
    pair = planes // 2
    starts = places(odd, pair, half)
    for piece, start in zip(pieces, starts):
        for i in range(pair):
            slab[start + i] = piece[i * rows : (i + 1) * rows]
    scratch[...] = jnp.exp(-jnp.concatenate([piece[pair * rows :] for piece in pieces], axis=0)).T
    spread_factor(reorder(scratch), factor, starts, factor.shape[0], pair)
    span = stored[0].shape[0]
    steps = 2 * span
    total[...] = jnp.zeros(total.shape, jnp.float32)

    def after(step, state):
        @pl.when(sec == step // steps)
        def _():
            total[...] += state[half : half + planes] * stored[step % steps // span][step % span]
            if step + 1 == steps:
                kept[...] = state[half : half + planes]

    run_steps(info, taps, weights, 0, half, slab, other, first, second, factor, after)
    state = (slab, other)[half % 2]
    middle[...] = state[half : half + planes]
    half_out[...] = state[pl.ds(half + pair * odd, pair)]


def late_kernel(half, last, *refs):
    info, taps, weights, middle, pieces, factor = refs[0], refs[1], refs[2], refs[3], refs[4:10], refs[10]
    kept, total_in, total_beside, series, stored = refs[11], refs[12], refs[13], refs[14:17], refs[17:19]
    handoff, share, to_pair, to_across, to_corner = refs[19:24]
    slab, other, first, second, scratch, total, saved, whole = refs[24:]
    sec, odd = position()
    planes, rows = middle.shape[:2]
    pair = planes // 2
    starts = places(odd, pair, half)
    slab[half : half + planes] = middle[...]
    for piece, start in zip(pieces, starts[1:4] + starts[5:8]):
        for i in range(pair):
            slab[start + i] = piece[i]
    span = series[0].shape[0]
    steps = 2 * span
    total[...] = jnp.zeros(total.shape, jnp.float32)

    @pl.when(sec == 0)
    def _():
        total[...] = total_in[...] + total_beside[...]

    saved[...] = kept[...]

    def after(step, state):
        part = step // span
        step = step + half

        @pl.when(sec == 0)
        def _():
            total[...] += state[half : half + planes] * series[part][step % span]

        if step + 1 == 2 * steps:

            @pl.when(sec == 1)
            def _():
                saved[...] = state[half : half + planes]

        if step >= 2 * steps:

            @pl.when(sec == last)
            def _():
                total[...] += state[half : half + planes] * stored[step % steps // span][step % span]

    run_steps(info, taps, weights, half, half, slab, other, first, second, factor, after)
    state = (slab, other)[half % 2]

    @pl.when(sec == last)
    def _():
        saved[...] = state[half : half + planes]

    orients = handoff.shape[1]
    count = orients // (last + 1)
    held = planes * count
    to_corner[...] = jnp.zeros(to_corner.shape, jnp.float32)
    for i in range(planes):
        handoff[i] = from_tile(saved[i], scratch)
        whole[...] = from_tile(total[i], scratch)
        for piece, who in (
            (share, sec),
            (to_pair, sec + 1 - 2 * odd),
            (to_across, jnp.where(sec == 0, 2, 1)),
            (to_corner, last - sec),
        ):
            piece[i * count : (i + 1) * count] = whole[pl.ds(pl.multiple_of(who * count, count), count)]
    for i in range(pair):
        to_across[held + i * orients : held + (i + 1) * orients] = from_tile(state[half + pair * odd + i], scratch)

    @pl.when(sec == 1)
    def _():
        to_corner[...] = to_across[held:]


def call(kernel, out_shape, scratch, operands, scalars=()):
    return pl.pallas_call(
        kernel,
        in_specs=[IN_SMEM] * len(scalars) + [IN_VMEM] * len(operands),
        out_specs=[IN_VMEM] * len(out_shape),
        out_shape=[jax.ShapeDtypeStruct(shape, jnp.float32) for shape in out_shape],
        scratch_shapes=scratch,
        compiler_params=pltpu.CompilerParams(vmem_limit_bytes=VMEM_BYTES),
    )(*scalars, *operands)


def paired(incoming, backward, fields, block_types, axial_taps, lateral_taps, depth_taps, bend_diagonal, bend_coupling):
    n_sec, n_gx = lax.axis_size("sec"), lax.axis_size("gx")
    steps, planes, orients, cells = backward.shape
    pair = planes // 2
    half = TICKS * steps // 2
    rows = 2 * orients
    lanes = cells // 2
    sec = lax.axis_index("sec")
    last = n_sec - 1

    def send(array, by_sec, shift=lambda s: 0):
        pairs = [
            (s * n_gx + g, t * n_gx + (g + shift(s)) % n_gx) for s, t in enumerate(by_sec) for g in range(n_gx)
        ]
        return lax.ppermute(array, ("sec", "gx"), pairs)

    same, beside, across, crossing = (0, 1, 2, 3), (1, 0, 3, 2), (2, 3, 0, 1), (2, 1, 0, 3)
    whole = incoming[0]
    backward, moved = lax.optimization_barrier((backward, whole[pair:]))
    moved_high = send(moved, (1, 3, 0, 2))
    moved_low = send(whole[:pair], (0, 2, 1, 3))
    kinds = [block_types, send(block_types, beside), send(block_types, across), send(block_types, (3, 2, 1, 0))]
    early_stored, late_stored, start, taps, weights = prepare(
        backward, incoming, fields, axial_taps, lateral_taps, depth_taps, bend_diagonal, bend_coupling
    )
    early_last = send(early_stored, crossing)

    tile = pltpu.VMEM((rows, lanes), jnp.float32)
    slab = pltpu.VMEM((planes + 2 * half, rows, lanes), jnp.float32)
    packed = pltpu.VMEM((GROUP * rows, 2 * lanes), jnp.bfloat16)
    inner = pltpu.VMEM((planes, rows, lanes), jnp.float32)
    work = [slab, slab, packed, packed, tile]

    def exchange(piece):
        own = [
            send(piece, same, lambda s: 1),
            send(piece, same, lambda s: -1),
            send(piece, same, lambda s: -2 if s % 2 == 0 else 2),
        ]
        return own, [send(each, beside) for each in own]

    piece, info = pl.pallas_call(
        pack_kernel,
        in_specs=[IN_SMEM] * 4 + [IN_VMEM] * 3,
        out_specs=[IN_VMEM, IN_SMEM],
        out_shape=[
            jax.ShapeDtypeStruct(start.shape, jnp.float32),
            jax.ShapeDtypeStruct((1, TICKS * steps), jnp.int32),
        ],
        scratch_shapes=[tile],
        compiler_params=pltpu.CompilerParams(vmem_limit_bytes=VMEM_BYTES),
    )(*kinds, start, moved_high, moved_low)
    own, swapped = exchange(piece)
    late_stored, *swapped = lax.optimization_barrier((late_stored, *swapped))
    late_next, late_last = send(late_stored, beside), send(late_stored, crossing)
    middle, piece, kept, total, factor = call(
        functools.partial(early_kernel, half),
        [(planes, rows, lanes), (pair, rows, lanes), (planes, rows, lanes), (planes, rows, lanes)]
        + [(fields.shape[0], planes + 2 * half, rows, lanes)],
        work,
        [taps, weights, piece, *own, send(piece, beside), *swapped, early_stored, late_stored],
        [info],
    )
    own, swapped = exchange(piece)
    held = planes * (orients // n_sec)
    handoff, share, to_pair, to_across, to_corner = call(
        functools.partial(late_kernel, half, last),
        [(planes, orients, cells)]
        + [(held, cells)] * 2
        + [(held + pair * orients, cells), (pair * orients, cells)],
        work + [inner, inner, pltpu.VMEM((orients, cells), jnp.float32)],
        [taps, weights, middle, *own, *swapped, factor, kept, total, send(total, beside)]
        + [late_next, early_last, late_last, early_stored, late_stored],
        [info],
    )
    to_pair = send(to_pair, beside)
    to_across = send(to_across, (2, 0, 3, 1))
    to_corner = send(to_corner, (3, 2, 1, 0))
    third = sec == 2
    density = share + to_pair + to_across[:held] + jnp.where(third, 0.0, to_corner[:held])
    arrived = jnp.concatenate([to_across[held:], to_corner]).reshape(handoff.shape)
    handoff = jnp.where(third, arrived, handoff)
    return handoff[None], density.reshape(planes, -1, cells) / (n_sec * steps)


def pairs_fit(n_sec, planes, steps, orients, cells, kinds):
    return (
        n_sec == TICKS + 1 == 4
        and planes == steps
        and planes % 2 == 0
        and TICKS * steps == 2 * (planes + planes // 2)
        and 2 * orients == 2 * CZ == cells // 2 == 128
        and kinds * planes <= FIELD_ROWS
        and planes >= GROUP
    )


def solution(mesh):
    in_specs = (
        P("sec", "gx", None, None),
        P("sec", "gx", None, None),
        P(None, "gx", None),
        P("sec", None),
        P(),
        P(),
        P(),
        P(),
        P(),
    )
    out_specs = (P("sec", "gx", None, None), P("gx", "sec", None))

    def body(incoming, backward, fields, *rest):
        steps, planes, orients, cells = backward.shape
        fits = pairs_fit(mesh.shape["sec"], planes, steps, orients, cells, fields.shape[0])
        return (paired if fits else per_device)(incoming, backward, fields, *rest)

    return jax.shard_map(body, mesh=mesh, in_specs=in_specs, out_specs=out_specs, check_vma=False)
```

```python
import functools

import jax
import jax.numpy as jnp
from jax import lax
from jax.experimental import pallas as pl
from jax.experimental.pallas import tpu as pltpu
from jax.sharding import PartitionSpec as P

TICKS = 3
CZ = 64
GROUP = 4
FIELD_ROWS = 16
OWN_KINDS, FIRST_KINDS, ACROSS_KINDS = 12, 13, 14
LEAD = 1
VMEM_BYTES = 16 * 2**20
WHOLE_VMEM_BYTES = 62 * 2**20
IN_VMEM = pl.BlockSpec(memory_space=pltpu.VMEM)


def padded_2(block, sides, width):
    for axis, dim in sides:
        count = lax.axis_size(axis)
        forward = [(i, i + 1) for i in range(count - 1)]
        forward.append((count - 1, 0))
        backward = [(target, source) for source, target in forward]
        low = lax.ppermute(
            lax.slice_in_dim(block, block.shape[dim] - width, None, axis=dim), axis, forward
        )
        high = lax.ppermute(lax.slice_in_dim(block, 0, width, axis=dim), axis, backward)
        block = jnp.concatenate([low, block, high], axis=dim)
    return block


def from_behind(array, axis, by):
    length = lax.axis_size(axis)
    pairs = [(i, i + by) for i in range(length) if 0 <= i + by < length]
    return lax.ppermute(array, axis, pairs)


def boltzmann(fields, kinds):
    selector = kinds == jnp.arange(fields.shape[0], dtype=jnp.int32)
    chosen = jnp.sum(jnp.where(selector[:, None, None], fields, jnp.zeros_like(fields)), axis=0)
    return jnp.exp(-chosen)


def column(taps, which):
    return taps[which][None, :, None]


def advance_padded(padded, factor, axial_taps, lateral_taps, depth_taps, kernel):
    along_x = (
        column(axial_taps, 0) * padded[:-2]
        + column(axial_taps, 1) * padded[1:-1]
        + column(axial_taps, 2) * padded[2:]
    )
    along_y = (
        column(lateral_taps, 0) * jnp.roll(along_x, CZ, axis=2)
        + column(lateral_taps, 1) * along_x
        + column(lateral_taps, 2) * jnp.roll(along_x, -CZ, axis=2)
    )
    depth_pos = (jnp.arange(along_y.shape[2], dtype=jnp.int32) % CZ)[None, None, :]
    behind = jnp.where(
        depth_pos == 0, jnp.roll(along_y, -(CZ - 1), axis=2), jnp.roll(along_y, 1, axis=2)
    )
    ahead = jnp.where(
        depth_pos == CZ - 1, jnp.roll(along_y, CZ - 1, axis=2), jnp.roll(along_y, -1, axis=2)
    )
    along_z = (
        column(depth_taps, 0) * behind
        + column(depth_taps, 1) * along_y
        + column(depth_taps, 2) * ahead
    )
    blended = jnp.einsum(
        "uv,xvc->xuc",
        kernel,
        along_z,
        precision=lax.Precision.HIGHEST,
        preferred_element_type=jnp.float32,
    )
    return blended * factor[:, None, :]


def per_device(
    incoming,
    backward,
    fields,
    block_types,
    axial_taps,
    lateral_taps,
    depth_taps,
    bend_diagonal,
    bend_coupling,
):
    kernel = jnp.diag(bend_diagonal) + bend_coupling
    steps_each = block_types.shape[1]
    planes = incoming.shape[1]
    start = incoming[0]
    first_section = lax.axis_index("sec") == 0
    wide_fields = padded_2(fields, (("gx", 1),), steps_each)
    factors = [boltzmann(wide_fields, block_types[0, position]) for position in range(steps_each)]
    current = start
    outgoing = start
    accumulated = jnp.zeros(start.shape, jnp.float32)
    for tick_index in range(TICKS):
        final_tick = tick_index + 1 == TICKS
        extended = padded_2(current, (("gx", 0),), steps_each)
        for position in range(steps_each):
            margin = steps_each - position - 1
            offset = steps_each - margin
            factor = factors[position][offset : offset + planes + 2 * margin]
            extended = advance_padded(
                extended, factor, axial_taps, lateral_taps, depth_taps, kernel
            )
            if final_tick:
                accumulated = accumulated + extended[margin : margin + planes] * backward[
                    position
                ].astype(jnp.float32)
        outgoing = extended
        if not final_tick:
            shifted = from_behind(outgoing, "sec", 1)
            current = jnp.where(first_section, start, shifted)
    reduced = lax.psum_scatter(accumulated, "sec", scatter_dimension=1, tiled=True)
    density = reduced / (lax.axis_size("sec") * steps_each)
    return (outgoing[None], density)


def to_tile(plane, scratch):
    half = plane.shape[1] // 2
    scratch[...] = jnp.concatenate([plane[:, :half], plane[:, half:]], axis=0).T
    return reorder(scratch)


def reorder(scratch):
    rows = scratch.shape[0]
    return jnp.concatenate(
        [scratch[pl.ds(yl * CZ + zl, 8, stride=8), :] for yl in range(rows // CZ) for zl in range(CZ // 8)], axis=0
    )


def from_tile(tile, scratch):
    rows = tile.shape[0]
    for yl in range(rows // CZ):
        for zl in range(CZ // 8):
            at = (yl * (CZ // 8) + zl) * 8
            scratch[pl.ds(yl * CZ + zl, 8, stride=8), :] = tile[at : at + 8]
    turned = scratch[...].T
    half = turned.shape[0] // 2
    return jnp.concatenate([turned[:half], turned[half:]], axis=1)


def stencil(behind, here, ahead, taps):
    a = here + taps[0] * behind + taps[1] * ahead
    low, high = a[:CZ], a[CZ:]
    low_turned = pltpu.roll(low, a.shape[1] // 2, 1)
    high_turned = pltpu.roll(high, a.shape[1] // 2, 1)
    out = []
    for b in (
        low + taps[2] * high_turned + taps[3] * high,
        high + taps[2] * low + taps[3] * low_turned,
    ):
        back = jnp.concatenate([pltpu.roll(b[-8:], 1, 0), b[:-8]], axis=0)
        front = jnp.concatenate([b[8:], pltpu.roll(b[:8], 7, 0)], axis=0)
        out.append(b + taps[4] * back + taps[5] * front)
    return jnp.concatenate(out, axis=0)


def position():
    sec = lax.axis_index("sec")
    return sec, lax.rem(sec, 2)


def prepare_kernel(*refs):
    sources, (early, late, taps, weights) = refs[:6], refs[6:10]
    scratch, copies, sems = refs[10], refs[11:17], refs[17]
    moves = [pltpu.make_async_copy(s, c, sems.at[i]) for i, (s, c) in enumerate(zip(sources, copies))]
    for move in moves:
        move.start()
    backward, axial, lateral, depth, diagonal, coupling = copies
    for move in moves[1:]:
        move.wait()
    orients = coupling.shape[0]
    ratios = [each[w : w + 1] / each[1:2] for each in (axial, lateral, depth) for w in (0, 2)]
    for i, ratio in enumerate(ratios + ratios[:2]):
        taps[i : i + 1] = jnp.concatenate([ratio, ratio], axis=1)
    square = (orients, orients)
    same = lax.broadcasted_iota(jnp.int32, square, 0) == lax.broadcasted_iota(jnp.int32, square, 1)
    kernel = jnp.where(same, diagonal[...], 0.0) + coupling[...]
    kernel = kernel * (axial[1:2] * lateral[1:2] * depth[1:2])
    upper = jnp.concatenate([kernel, jnp.zeros_like(kernel)], axis=1)
    twice = jnp.concatenate([upper, pltpu.roll(upper, orients, 1)], axis=0).T
    coarse = twice.astype(jnp.bfloat16)
    fine = (twice - coarse.astype(jnp.float32)).astype(jnp.bfloat16)
    weights[...] = jnp.concatenate(
        [jnp.concatenate([coarse, fine], axis=1), jnp.concatenate([coarse, jnp.zeros_like(fine)], axis=1)], axis=0
    )
    moves[0].wait()
    for out, begin in ((early, 0), (late, LEAD)):
        for step in range(out.shape[0]):
            for i in range(out.shape[1]):
                out[step, i] = to_tile(backward[begin + step, i].astype(jnp.float32), scratch)


def prepare(backward, axial, lateral, depth, diagonal, coupling):
    steps, planes, orients, cells = backward.shape
    rows, lanes = 2 * orients, cells // 2
    operands = [backward, axial, lateral, depth, diagonal.reshape(1, -1), coupling]
    first, rest = (((count, planes, rows, lanes), jnp.float32) for count in (LEAD, steps - LEAD))
    return pl.pallas_call(
        prepare_kernel,
        in_specs=[pl.BlockSpec(memory_space=pltpu.HBM)] * len(operands),
        out_specs=[IN_VMEM] * 4,
        out_shape=[
            jax.ShapeDtypeStruct(*each)
            for each in (first, rest, ((8, lanes), jnp.float32), ((2 * rows, 2 * lanes), jnp.bfloat16))
        ],
        scratch_shapes=[pltpu.VMEM((rows, lanes), jnp.float32)]
        + [pltpu.VMEM(each.shape, each.dtype) for each in operands]
        + [pltpu.SemaphoreType.DMA((len(operands),))],
        compiler_params=pltpu.CompilerParams(vmem_limit_bytes=WHOLE_VMEM_BYTES),
    )(*operands)


def settle_kernel(*refs):
    for source, out in zip(refs[: len(refs) // 2], refs[len(refs) // 2 :]):
        out[...] = source[...]


def pack_kernel(low, moved_high, moved_low, across, fields, out, scratch):
    sec, odd = position()
    rows = scratch.shape[0]
    orients = rows // 2
    pair = low.shape[0] // orients
    count = fields.shape[0]
    out[pair * rows :] = jnp.zeros((FIELD_ROWS, rows), jnp.float32)
    for i in range(count):
        out[pair * rows + 2 * i : pair * rows + 2 * i + 1] = fields[i : i + 1, :rows]
        out[pair * rows + 2 * i + 1 : pair * rows + 2 * i + 2] = fields[i : i + 1, rows:]
    out[OWN_KINDS + pair * rows : OWN_KINDS + pair * rows + 1] = low[pair * orients : pair * orients + 1, :rows]
    out[ACROSS_KINDS + pair * rows : ACROSS_KINDS + pair * rows + 1] = across[:1, :rows]

    def fill(source):
        for i in range(pair):
            out[i * rows : (i + 1) * rows] = to_tile(source[i * orients : (i + 1) * orients], scratch)
        out[FIRST_KINDS + pair * rows : FIRST_KINDS + pair * rows + 1] = source[pair * orients : pair * orients + 1, :rows]

    pl.when(sec == 0)(lambda: fill(low))
    pl.when(odd == 1)(lambda: fill(moved_high))
    pl.when((sec > 0) & (odd == 0))(lambda: fill(moved_low))


def scalars_of(row, count):
    lane = lax.broadcasted_iota(jnp.int32, row.shape, 1)
    return [jnp.sum(jnp.where(lane == i, row, 0.0)).astype(jnp.int32) for i in range(count)]


def places(odd, planes, reach, blocks):
    return [reach + block * planes + planes // 2 * core for core in (odd, 1 - odd) for block in blocks]


def run_steps(kinds, taps, weights, count, slab, other, first, second, factor, offset, after):
    tap = [taps[i : i + 1, :] for i in range(6)]
    extent, rows, lanes = slab.shape
    buffers = (slab, other)

    def blend(source, at, packed):
        for i in range(GROUP):
            e = stencil(source[at + i - 1], source[at + i], source[at + i + 1], tap)
            coarse = e.astype(jnp.bfloat16)
            packed[i * rows : (i + 1) * rows, :lanes] = coarse
            packed[i * rows : (i + 1) * rows, lanes:] = (e - coarse.astype(jnp.float32)).astype(jnp.bfloat16)

    def mix(target, at, packed, kind):
        product = jnp.dot(packed[...], weights[...], preferred_element_type=jnp.float32)
        product = product[:, :lanes] + product[:, lanes:]
        for i in range(GROUP):
            target[at + i] = product[i * rows : (i + 1) * rows] * factor[kind, at + i + offset]

    for step in range(count):
        source, target = buffers[step % 2], buffers[1 - step % 2]
        begin, width = step + 1, extent - 2 * step - 2
        groups = -(-width // GROUP)
        kind = kinds[step]

        def at(i, begin=begin, width=width):
            return jnp.minimum(begin + i * GROUP, begin + width - GROUP)

        blend(source, at(0), first)
        if groups > 1:

            def body(i, carry, source=source, target=target, at=at, kind=kind):
                blend(source, at(2 * i + 1), second)
                mix(target, at(2 * i), first, kind)
                blend(source, at(2 * i + 2), first)
                mix(target, at(2 * i + 1), second, kind)
                return carry

            lax.fori_loop(0, (groups - 1) // 2, body, 0)
        if groups % 2 == 0:
            blend(source, at(groups - 1), second)
            mix(target, at(groups - 2), first, kind)
            mix(target, at(groups - 1), second, kind)
        else:
            mix(target, at(groups - 1), first, kind)
        after(step, target)


def spread_factor(columns, factor, starts, width):
    rows, lanes = factor.shape[2:]
    pair = factor.shape[1] // len(starts)
    right = (lax.broadcasted_iota(jnp.int32, (rows, lanes), 1) >= lanes // 2).astype(jnp.int32)
    for piece, start in enumerate(starts):
        for kind in range(factor.shape[0]):
            for i in range(pair):
                at = piece * width + (kind * pair + i) * 2
                factor[kind, start + i] = jnp.take_along_axis(columns, right + at, axis=1, mode="promise_in_bounds")


def early_kernel(blocks, taps, weights, *refs):
    pieces, refs = refs[: 2 * len(blocks)], refs[2 * len(blocks) :]
    stored, (middle, half_out, kept, total, factor) = refs[:2], refs[2:7]
    slab, other, first, second, scratch = refs[7:]
    sec, odd = position()
    planes, rows = middle.shape[:2]
    pair = planes // 2
    reach = (slab.shape[0] - planes) // 2
    starts = places(odd, planes, reach, blocks)
    for piece, start in zip(pieces, starts):
        for i in range(pair):
            slab[start + i] = piece[i * rows : (i + 1) * rows]
    at = pair * rows
    mine, others = (piece[at + OWN_KINDS : at + OWN_KINDS + 1] for piece in (pieces[0], pieces[len(blocks)]))
    steps = LEAD + stored[1].shape[0]
    second_kinds = jnp.where((sec == 1) | (sec == 2), mine, others)
    kinds = scalars_of(pieces[0][at + FIRST_KINDS : at + FIRST_KINDS + 1], steps) + scalars_of(second_kinds, steps)
    width = 2 * pair * factor.shape[0]
    lines = [piece[pair * rows : pair * rows + width] for piece in pieces]
    lines.append(jnp.zeros((rows - width * len(pieces), rows), jnp.float32))
    scratch[...] = jnp.exp(-jnp.concatenate(lines, axis=0)).T
    spread_factor(reorder(scratch), factor, starts, width)
    total[...] = jnp.zeros(total.shape, jnp.float32)
    kept[...] = jnp.zeros(kept.shape, jnp.float32)

    def after(step, state):
        @pl.when(sec == step // steps)
        def _():
            j = step % steps
            source = stored[0][j] if j < LEAD else stored[1][j - LEAD]
            total[...] += state[reach : reach + planes] * source
            if j + 1 == steps:
                kept[...] = state[reach : reach + planes]

    run_steps(kinds, taps, weights, reach, slab, other, first, second, factor, 0, after)
    state = (slab, other)[reach % 2]
    middle[...] = state[reach : reach + planes]
    half_out[...] = state[pl.ds(reach + pair * odd, pair)]


def late_kernel(blocks, last, taps, weights, first_own, first_swapped, middle, *refs):
    pieces, refs = refs[: 2 * len(blocks)], refs[2 * len(blocks) :]
    factor, kept, total_in, total_beside, series, stored = refs[0], refs[1], refs[2], refs[3], refs[4:6], refs[6:8]
    handoff, share, to_pair, to_across, to_corner = refs[8:13]
    slab, other, first, second, scratch, total, saved, whole = refs[13:]
    sec, odd = position()
    planes, rows = middle.shape[:2]
    pair = planes // 2
    reach = (slab.shape[0] - planes) // 2
    begun = (factor.shape[1] - planes) // 2
    own, others = (
        [each[pair * rows + at : pair * rows + at + 1] for at in (OWN_KINDS, ACROSS_KINDS)]
        for each in (first_own, first_swapped)
    )
    row = jnp.where(sec < 2, jnp.where(odd == 0, own[1], others[1]), jnp.where(odd == 0, others[0], own[0]))
    kinds = scalars_of(row, reach)
    slab[reach : reach + planes] = middle[...]
    for piece, start in zip(pieces, places(odd, planes, reach, blocks)):
        for i in range(pair):
            slab[start + i] = piece[i]
    total[...] = jnp.zeros(total.shape, jnp.float32)

    @pl.when(sec == 0)
    def _():
        total[...] = total_in[...] + total_beside[...]

    saved[...] = kept[...]

    def after(step, state):
        for where, source in ((sec == 0, series), (sec == last, stored)):

            @pl.when(where)
            def _(source=source):
                part = source[0][step] if step < LEAD else source[1][step - LEAD]
                total[...] += state[reach : reach + planes] * part

    run_steps(kinds, taps, weights, reach, slab, other, first, second, factor, begun - reach, after)
    state = (slab, other)[reach % 2]

    @pl.when(sec == last)
    def _():
        saved[...] = state[reach : reach + planes]

    orients = handoff.shape[1]
    count = orients // (last + 1)
    held = planes * count
    to_corner[...] = jnp.zeros(to_corner.shape, jnp.float32)
    for i in range(planes):
        handoff[i] = from_tile(saved[i], scratch)
        whole[...] = from_tile(total[i], scratch)
        for piece, who in (
            (share, sec),
            (to_pair, sec + 1 - 2 * odd),
            (to_across, jnp.where(sec == 0, 2, 1)),
            (to_corner, last - sec),
        ):
            piece[i * count : (i + 1) * count] = whole[pl.ds(pl.multiple_of(who * count, count), count)]
    for i in range(pair):
        to_across[held + i * orients : held + (i + 1) * orients] = from_tile(state[reach + pair * odd + i], scratch)

    @pl.when(sec == 1)
    def _():
        to_corner[...] = to_across[held:]


def call(kernel, out_shape, scratch, operands):
    return pl.pallas_call(
        kernel,
        in_specs=[IN_VMEM] * len(operands),
        out_specs=[IN_VMEM] * len(out_shape),
        out_shape=[jax.ShapeDtypeStruct(shape, jnp.float32) for shape in out_shape],
        scratch_shapes=scratch,
        compiler_params=pltpu.CompilerParams(vmem_limit_bytes=VMEM_BYTES),
    )(*operands)


def paired(incoming, backward, fields, block_types, axial_taps, lateral_taps, depth_taps, bend_diagonal, bend_coupling):
    n_sec, n_gx = lax.axis_size("sec"), lax.axis_size("gx")
    steps, planes, orients, cells = backward.shape
    pair = planes // 2
    reach = (TICKS - 1) * steps, steps
    near, far = (1, -1), (1, -1, 2, -2)
    rows = 2 * orients
    lanes = cells // 2
    sec = lax.axis_index("sec")
    last = n_sec - 1

    def send(array, by_sec, shift=lambda s: 0):
        pairs = [
            (s * n_gx + g, t * n_gx + (g + shift(s)) % n_gx) for s, t in enumerate(by_sec) for g in range(n_gx)
        ]
        return lax.ppermute(array, ("sec", "gx"), pairs)

    same, beside, across, crossing = (0, 1, 2, 3), (1, 0, 3, 2), (2, 3, 0, 1), (2, 1, 0, 3)
    whole = incoming[0]
    types = jnp.pad(block_types.astype(jnp.float32), ((0, 7), (0, cells - steps)))
    low, high = (jnp.concatenate([each.reshape(-1, cells), types]) for each in (whole[:pair], whole[pair:]))
    backward, high, low = lax.optimization_barrier((backward, high, low))
    moved_high = send(high, (1, 3, 0, 2))
    moved_low = send(low, (0, 2, 1, 3))
    across_types = send(types, across)
    lines = lax.dynamic_slice_in_dim(fields, sec % 2 * pair, pair, axis=1).reshape(-1, cells)
    settled = prepare(backward, axial_taps, lateral_taps, depth_taps, bend_diagonal, bend_coupling)
    early_stored, late_stored = settled[:2]

    tile = pltpu.VMEM((rows, lanes), jnp.float32)
    packed = pltpu.VMEM((GROUP * rows, 2 * lanes), jnp.bfloat16)
    inner = pltpu.VMEM((planes, rows, lanes), jnp.float32)

    def work(extent):
        slab = pltpu.VMEM((planes + 2 * extent, rows, lanes), jnp.float32)
        return [slab, slab, packed, packed, tile]

    (piece,) = call(
        pack_kernel, [(pair * rows + FIELD_ROWS, lanes)], [tile], [low, moved_high, moved_low, across_types, lines]
    )
    own = [send(piece, same, lambda s: shift) for shift in far]
    early_last = send(early_stored, crossing)
    settled = pl.pallas_call(
        settle_kernel,
        in_specs=[IN_VMEM] * len(settled),
        out_specs=[IN_VMEM] * len(settled),
        out_shape=[jax.ShapeDtypeStruct(each.shape, each.dtype) for each in settled],
        compiler_params=pltpu.CompilerParams(vmem_limit_bytes=VMEM_BYTES),
    )(*settled)
    own[-1], *settled = lax.optimization_barrier((own[-1], *settled))
    stored, (taps, weights) = settled[:2], settled[2:]
    swapped = [send(each, beside) for each in [piece] + own]
    late_stored, *swapped = lax.optimization_barrier((late_stored, *swapped))
    late_last = send(late_stored, crossing)
    firsts = [piece, swapped[0]]
    middle, piece, kept, total, factor = call(
        functools.partial(early_kernel, tuple(-shift for shift in (0,) + far)),
        [(planes, rows, lanes), (pair, rows, lanes), (planes, rows, lanes), (planes, rows, lanes)]
        + [(fields.shape[0], planes + 2 * reach[0], rows, lanes)],
        work(reach[0]),
        [taps, weights, piece, *own, *swapped, *stored],
    )
    own = [send(piece, same, lambda s: shift) for shift in near]
    beside_total = send(total, beside)
    swapped = [send(each, beside) for each in own]
    held = planes * (orients // n_sec)
    handoff, share, to_pair, to_across, to_corner = call(
        functools.partial(late_kernel, tuple(-shift for shift in near), last),
        [(planes, orients, cells)]
        + [(held, cells)] * 2
        + [(held + pair * orients, cells), (pair * orients, cells)],
        work(reach[1]) + [inner, inner, pltpu.VMEM((orients, cells), jnp.float32)],
        [taps, weights, *firsts, middle, *own, *swapped, factor, kept, total, beside_total]
        + [early_last, late_last, *stored],
    )
    to_pair = send(to_pair, beside)
    to_across = send(to_across, (2, 0, 3, 1))
    to_corner = send(to_corner, (3, 2, 1, 0))
    third = sec == 2
    density = share + to_pair + to_across[:held] + jnp.where(third, 0.0, to_corner[:held])
    arrived = jnp.concatenate([to_across[held:], to_corner]).reshape(handoff.shape)
    handoff = jnp.where(third, arrived, handoff)
    return handoff[None], density.reshape(planes, -1, cells) / (n_sec * steps)


def pairs_fit(n_sec, planes, steps, orients, cells, kinds):
    return (
        n_sec == TICKS + 1 == 4
        and planes == steps
        and planes % 2 == 0
        and 2 * orients == 2 * CZ == cells // 2 == 128
        and kinds * planes <= FIELD_ROWS and 10 * kinds * planes <= 2 * orients
        and planes >= GROUP
    )


def solution(mesh):
    in_specs = (
        P("sec", "gx", None, None),
        P("sec", "gx", None, None),
        P(None, "gx", None),
        P("sec", None),
        P(),
        P(),
        P(),
        P(),
        P(),
    )
    out_specs = (P("sec", "gx", None, None), P("gx", "sec", None))

    def body(incoming, backward, fields, *rest):
        steps, planes, orients, cells = backward.shape
        fits = pairs_fit(mesh.shape["sec"], planes, steps, orients, cells, fields.shape[0])
        return (paired if fits else per_device)(incoming, backward, fields, *rest)

    return jax.shard_map(body, mesh=mesh, in_specs=in_specs, out_specs=out_specs, check_vma=False)
```

```python
import functools

import jax
import jax.numpy as jnp
from jax import lax
from jax.experimental import pallas as pl
from jax.experimental.pallas import tpu as pltpu
from jax.sharding import PartitionSpec as P

TICKS = 3
CZ = 64
GROUP = 6
FIELD_ROWS = 16
OWN_KINDS, FIRST_KINDS, ACROSS_KINDS = 12, 13, 14
LEAD = 1
VMEM_BYTES = 16 * 2**20
WHOLE_VMEM_BYTES = 62 * 2**20
IN_VMEM = pl.BlockSpec(memory_space=pltpu.VMEM)


def padded_2(block, sides, width):
    for axis, dim in sides:
        count = lax.axis_size(axis)
        forward = [(i, i + 1) for i in range(count - 1)]
        forward.append((count - 1, 0))
        backward = [(target, source) for source, target in forward]
        low = lax.ppermute(
            lax.slice_in_dim(block, block.shape[dim] - width, None, axis=dim), axis, forward
        )
        high = lax.ppermute(lax.slice_in_dim(block, 0, width, axis=dim), axis, backward)
        block = jnp.concatenate([low, block, high], axis=dim)
    return block


def from_behind(array, axis, by):
    length = lax.axis_size(axis)
    pairs = [(i, i + by) for i in range(length) if 0 <= i + by < length]
    return lax.ppermute(array, axis, pairs)


def boltzmann(fields, kinds):
    selector = kinds == jnp.arange(fields.shape[0], dtype=jnp.int32)
    chosen = jnp.sum(jnp.where(selector[:, None, None], fields, jnp.zeros_like(fields)), axis=0)
    return jnp.exp(-chosen)


def column(taps, which):
    return taps[which][None, :, None]


def advance_padded(padded, factor, axial_taps, lateral_taps, depth_taps, kernel):
    along_x = (
        column(axial_taps, 0) * padded[:-2]
        + column(axial_taps, 1) * padded[1:-1]
        + column(axial_taps, 2) * padded[2:]
    )
    along_y = (
        column(lateral_taps, 0) * jnp.roll(along_x, CZ, axis=2)
        + column(lateral_taps, 1) * along_x
        + column(lateral_taps, 2) * jnp.roll(along_x, -CZ, axis=2)
    )
    depth_pos = (jnp.arange(along_y.shape[2], dtype=jnp.int32) % CZ)[None, None, :]
    behind = jnp.where(
        depth_pos == 0, jnp.roll(along_y, -(CZ - 1), axis=2), jnp.roll(along_y, 1, axis=2)
    )
    ahead = jnp.where(
        depth_pos == CZ - 1, jnp.roll(along_y, CZ - 1, axis=2), jnp.roll(along_y, -1, axis=2)
    )
    along_z = (
        column(depth_taps, 0) * behind
        + column(depth_taps, 1) * along_y
        + column(depth_taps, 2) * ahead
    )
    blended = jnp.einsum(
        "uv,xvc->xuc",
        kernel,
        along_z,
        precision=lax.Precision.HIGHEST,
        preferred_element_type=jnp.float32,
    )
    return blended * factor[:, None, :]


def per_device(
    incoming,
    backward,
    fields,
    block_types,
    axial_taps,
    lateral_taps,
    depth_taps,
    bend_diagonal,
    bend_coupling,
):
    kernel = jnp.diag(bend_diagonal) + bend_coupling
    steps_each = block_types.shape[1]
    planes = incoming.shape[1]
    start = incoming[0]
    first_section = lax.axis_index("sec") == 0
    wide_fields = padded_2(fields, (("gx", 1),), steps_each)
    factors = [boltzmann(wide_fields, block_types[0, position]) for position in range(steps_each)]
    current = start
    outgoing = start
    accumulated = jnp.zeros(start.shape, jnp.float32)
    for tick_index in range(TICKS):
        final_tick = tick_index + 1 == TICKS
        extended = padded_2(current, (("gx", 0),), steps_each)
        for position in range(steps_each):
            margin = steps_each - position - 1
            offset = steps_each - margin
            factor = factors[position][offset : offset + planes + 2 * margin]
            extended = advance_padded(
                extended, factor, axial_taps, lateral_taps, depth_taps, kernel
            )
            if final_tick:
                accumulated = accumulated + extended[margin : margin + planes] * backward[
                    position
                ].astype(jnp.float32)
        outgoing = extended
        if not final_tick:
            shifted = from_behind(outgoing, "sec", 1)
            current = jnp.where(first_section, start, shifted)
    reduced = lax.psum_scatter(accumulated, "sec", scatter_dimension=1, tiled=True)
    density = reduced / (lax.axis_size("sec") * steps_each)
    return (outgoing[None], density)


def to_tile(plane, scratch):
    half = plane.shape[1] // 2
    scratch[...] = jnp.concatenate([plane[:, :half], plane[:, half:]], axis=0).T
    return reorder(scratch)


def reorder(scratch):
    rows = scratch.shape[0]
    return jnp.concatenate(
        [scratch[pl.ds(yl * CZ + zl, 8, stride=8), :] for yl in range(rows // CZ) for zl in range(CZ // 8)], axis=0
    )


def from_tile(tile, scratch):
    rows = tile.shape[0]
    for yl in range(rows // CZ):
        for zl in range(CZ // 8):
            at = (yl * (CZ // 8) + zl) * 8
            scratch[pl.ds(yl * CZ + zl, 8, stride=8), :] = tile[at : at + 8]
    turned = scratch[...].T
    half = turned.shape[0] // 2
    return jnp.concatenate([turned[:half], turned[half:]], axis=1)


def stencil(behind, here, ahead, taps):
    a = here + taps[0] * behind + taps[1] * ahead
    low, high = a[:CZ], a[CZ:]
    low_turned = pltpu.roll(low, a.shape[1] // 2, 1)
    high_turned = pltpu.roll(high, a.shape[1] // 2, 1)
    out = []
    for b in (
        low + taps[2] * high_turned + taps[3] * high,
        high + taps[2] * low + taps[3] * low_turned,
    ):
        back = jnp.concatenate([pltpu.roll(b[-8:], 1, 0), b[:-8]], axis=0)
        front = jnp.concatenate([b[8:], pltpu.roll(b[:8], 7, 0)], axis=0)
        out.append(b + taps[4] * back + taps[5] * front)
    return jnp.concatenate(out, axis=0)


def position():
    sec = lax.axis_index("sec")
    return sec, lax.rem(sec, 2)


def prepare_kernel(*refs):
    sources, (early, late, taps, weights) = refs[:6], refs[6:10]
    scratch, copies, sems = refs[10], refs[11:17], refs[17]
    moves = [pltpu.make_async_copy(s, c, sems.at[i]) for i, (s, c) in enumerate(zip(sources, copies))]
    for move in moves:
        move.start()
    backward, axial, lateral, depth, diagonal, coupling = copies
    for move in moves[1:]:
        move.wait()
    orients = coupling.shape[0]
    ratios = [each[w : w + 1] / each[1:2] for each in (axial, lateral, depth) for w in (0, 2)]
    for i, ratio in enumerate(ratios + ratios[:2]):
        taps[i : i + 1] = jnp.concatenate([ratio, ratio], axis=1)
    square = (orients, orients)
    same = lax.broadcasted_iota(jnp.int32, square, 0) == lax.broadcasted_iota(jnp.int32, square, 1)
    kernel = jnp.where(same, diagonal[...], 0.0) + coupling[...]
    kernel = kernel * (axial[1:2] * lateral[1:2] * depth[1:2])
    upper = jnp.concatenate([kernel, jnp.zeros_like(kernel)], axis=1)
    twice = jnp.concatenate([upper, pltpu.roll(upper, orients, 1)], axis=0).T
    coarse = twice.astype(jnp.bfloat16)
    fine = (twice - coarse.astype(jnp.float32)).astype(jnp.bfloat16)
    weights[...] = jnp.concatenate(
        [jnp.concatenate([coarse, fine], axis=1), jnp.concatenate([coarse, jnp.zeros_like(fine)], axis=1)], axis=0
    )
    moves[0].wait()
    for out, begin in ((early, 0), (late, LEAD)):
        for step in range(out.shape[0]):
            for i in range(out.shape[1]):
                out[step, i] = to_tile(backward[begin + step, i].astype(jnp.float32), scratch)


def prepare(backward, axial, lateral, depth, diagonal, coupling):
    steps, planes, orients, cells = backward.shape
    rows, lanes = 2 * orients, cells // 2
    operands = [backward, axial, lateral, depth, diagonal.reshape(1, -1), coupling]
    first, rest = (((count, planes, rows, lanes), jnp.float32) for count in (LEAD, steps - LEAD))
    return pl.pallas_call(
        prepare_kernel,
        in_specs=[pl.BlockSpec(memory_space=pltpu.HBM)] * len(operands),
        out_specs=[IN_VMEM] * 4,
        out_shape=[
            jax.ShapeDtypeStruct(*each)
            for each in (first, rest, ((8, lanes), jnp.float32), ((2 * rows, 2 * lanes), jnp.bfloat16))
        ],
        scratch_shapes=[pltpu.VMEM((rows, lanes), jnp.float32)]
        + [pltpu.VMEM(each.shape, each.dtype) for each in operands]
        + [pltpu.SemaphoreType.DMA((len(operands),))],
        compiler_params=pltpu.CompilerParams(vmem_limit_bytes=WHOLE_VMEM_BYTES),
    )(*operands)


def settle_kernel(*refs):
    for source, out in zip(refs[: len(refs) // 2], refs[len(refs) // 2 :]):
        out[...] = source[...]


def pack_kernel(low, moved_high, moved_low, across, fields, out, scratch):
    sec, odd = position()
    rows = scratch.shape[0]
    orients = rows // 2
    pair = low.shape[0] // orients
    count = fields.shape[0]
    out[pair * rows :] = jnp.zeros((FIELD_ROWS, rows), jnp.float32)
    for i in range(count):
        out[pair * rows + 2 * i : pair * rows + 2 * i + 1] = fields[i : i + 1, :rows]
        out[pair * rows + 2 * i + 1 : pair * rows + 2 * i + 2] = fields[i : i + 1, rows:]
    out[OWN_KINDS + pair * rows : OWN_KINDS + pair * rows + 1] = low[pair * orients : pair * orients + 1, :rows]
    out[ACROSS_KINDS + pair * rows : ACROSS_KINDS + pair * rows + 1] = across[:1, :rows]

    def fill(source):
        for i in range(pair):
            out[i * rows : (i + 1) * rows] = to_tile(source[i * orients : (i + 1) * orients], scratch)
        out[FIRST_KINDS + pair * rows : FIRST_KINDS + pair * rows + 1] = source[pair * orients : pair * orients + 1, :rows]

    pl.when(sec == 0)(lambda: fill(low))
    pl.when(odd == 1)(lambda: fill(moved_high))
    pl.when((sec > 0) & (odd == 0))(lambda: fill(moved_low))


def scalars_of(row, count):
    lane = lax.broadcasted_iota(jnp.int32, row.shape, 1)
    return [jnp.sum(jnp.where(lane == i, row, 0.0)).astype(jnp.int32) for i in range(count)]


def places(odd, planes, reach, blocks):
    return [reach + block * planes + planes // 2 * core for core in (odd, 1 - odd) for block in blocks]


def run_steps(kinds, taps, weights, count, slab, other, first, second, factor, offset, after):
    tap = [taps[i : i + 1, :] for i in range(6)]
    extent, rows, lanes = slab.shape
    buffers = (slab, other)

    def blend(source, at, packed):
        for i in range(GROUP):
            e = stencil(source[at + i - 1], source[at + i], source[at + i + 1], tap)
            coarse = e.astype(jnp.bfloat16)
            packed[i * rows : (i + 1) * rows, :lanes] = coarse
            packed[i * rows : (i + 1) * rows, lanes:] = (e - coarse.astype(jnp.float32)).astype(jnp.bfloat16)

    def mix(target, at, packed, kind):
        product = jnp.dot(packed[...], weights[...], preferred_element_type=jnp.float32)
        product = product[:, :lanes] + product[:, lanes:]
        for i in range(GROUP):
            target[at + i] = product[i * rows : (i + 1) * rows] * factor[kind, at + i + offset]

    for step in range(count):
        source, target = buffers[step % 2], buffers[1 - step % 2]
        begin, width = step + 1, extent - 2 * step - 2
        groups = -(-width // GROUP)
        kind = kinds[step]

        def at(i, begin=begin, width=width):
            return jnp.minimum(begin + i * GROUP, begin + width - GROUP)

        blend(source, at(0), first)
        if groups > 1:

            def body(i, carry, source=source, target=target, at=at, kind=kind):
                blend(source, at(2 * i + 1), second)
                mix(target, at(2 * i), first, kind)
                blend(source, at(2 * i + 2), first)
                mix(target, at(2 * i + 1), second, kind)
                return carry

            lax.fori_loop(0, (groups - 1) // 2, body, 0)
        if groups % 2 == 0:
            blend(source, at(groups - 1), second)
            mix(target, at(groups - 2), first, kind)
            mix(target, at(groups - 1), second, kind)
        else:
            mix(target, at(groups - 1), first, kind)
        after(step, target)


def spread_factor(columns, factor, starts, width):
    rows, lanes = factor.shape[2:]
    pair = factor.shape[1] // len(starts)
    right = (lax.broadcasted_iota(jnp.int32, (rows, lanes), 1) >= lanes // 2).astype(jnp.int32)
    for piece, start in enumerate(starts):
        for kind in range(factor.shape[0]):
            for i in range(pair):
                at = piece * width + (kind * pair + i) * 2
                factor[kind, start + i] = jnp.take_along_axis(columns, right + at, axis=1, mode="promise_in_bounds")


def early_kernel(blocks, taps, weights, *refs):
    pieces, refs = refs[: 2 * len(blocks)], refs[2 * len(blocks) :]
    stored, (middle, half_out, kept, total, factor) = refs[:2], refs[2:7]
    slab, other, first, second, scratch = refs[7:]
    sec, odd = position()
    planes, rows = middle.shape[:2]
    pair = planes // 2
    reach = (slab.shape[0] - planes) // 2
    starts = places(odd, planes, reach, blocks)
    for piece, start in zip(pieces, starts):
        for i in range(pair):
            slab[start + i] = piece[i * rows : (i + 1) * rows]
    at = pair * rows
    mine, others = (piece[at + OWN_KINDS : at + OWN_KINDS + 1] for piece in (pieces[0], pieces[len(blocks)]))
    steps = LEAD + stored[1].shape[0]
    second_kinds = jnp.where((sec == 1) | (sec == 2), mine, others)
    kinds = scalars_of(pieces[0][at + FIRST_KINDS : at + FIRST_KINDS + 1], steps) + scalars_of(second_kinds, steps)
    width = 2 * pair * factor.shape[0]
    lines = [piece[pair * rows : pair * rows + width] for piece in pieces]
    lines.append(jnp.zeros((rows - width * len(pieces), rows), jnp.float32))
    scratch[...] = jnp.exp(-jnp.concatenate(lines, axis=0)).T
    spread_factor(reorder(scratch), factor, starts, width)
    total[...] = jnp.zeros(total.shape, jnp.float32)
    kept[...] = jnp.zeros(kept.shape, jnp.float32)

    def after(step, state):
        @pl.when(sec == step // steps)
        def _():
            j = step % steps
            source = stored[0][j] if j < LEAD else stored[1][j - LEAD]
            total[...] += state[reach : reach + planes] * source
            if j + 1 == steps:
                kept[...] = state[reach : reach + planes]

    run_steps(kinds, taps, weights, reach, slab, other, first, second, factor, 0, after)
    state = (slab, other)[reach % 2]
    middle[...] = state[reach : reach + planes]
    half_out[...] = state[pl.ds(reach + pair * odd, pair)]


def late_kernel(blocks, last, taps, weights, first_own, first_swapped, middle, *refs):
    pieces, refs = refs[: 2 * len(blocks)], refs[2 * len(blocks) :]
    factor, kept, total_in, total_beside, series, stored = refs[0], refs[1], refs[2], refs[3], refs[4:6], refs[6:8]
    handoff, share, to_pair, to_across, to_corner = refs[8:13]
    slab, other, first, second, scratch, total, saved, whole = refs[13:]
    sec, odd = position()
    planes, rows = middle.shape[:2]
    pair = planes // 2
    reach = (slab.shape[0] - planes) // 2
    begun = (factor.shape[1] - planes) // 2
    own, others = (
        [each[pair * rows + at : pair * rows + at + 1] for at in (OWN_KINDS, ACROSS_KINDS)]
        for each in (first_own, first_swapped)
    )
    row = jnp.where(sec < 2, jnp.where(odd == 0, own[1], others[1]), jnp.where(odd == 0, others[0], own[0]))
    kinds = scalars_of(row, reach)
    slab[reach : reach + planes] = middle[...]
    for piece, start in zip(pieces, places(odd, planes, reach, blocks)):
        for i in range(pair):
            slab[start + i] = piece[i]
    total[...] = jnp.zeros(total.shape, jnp.float32)

    @pl.when(sec == 0)
    def _():
        total[...] = total_in[...] + total_beside[...]

    saved[...] = kept[...]

    def after(step, state):
        @pl.when(sec == 0)
        def _():
            for i in range(planes):
                part = series[1][step - LEAD, i] if step >= LEAD else to_tile(series[0][step, i], scratch)
                total[i] += state[reach + i] * part

        @pl.when(sec == last)
        def _():
            part = stored[0][step] if step < LEAD else stored[1][step - LEAD]
            total[...] += state[reach : reach + planes] * part

    run_steps(kinds, taps, weights, reach, slab, other, first, second, factor, begun - reach, after)
    state = (slab, other)[reach % 2]

    @pl.when(sec == last)
    def _():
        saved[...] = state[reach : reach + planes]

    orients = handoff.shape[1]
    count = orients // (last + 1)
    held = planes * count
    to_corner[...] = jnp.zeros(to_corner.shape, jnp.float32)
    for i in range(planes):
        handoff[i] = from_tile(saved[i], scratch)
        whole[...] = from_tile(total[i], scratch)
        for piece, who in (
            (share, sec),
            (to_pair, sec + 1 - 2 * odd),
            (to_across, jnp.where(sec == 0, 2, 1)),
            (to_corner, last - sec),
        ):
            piece[i * count : (i + 1) * count] = whole[pl.ds(pl.multiple_of(who * count, count), count)]
    for i in range(pair):
        to_across[held + i * orients : held + (i + 1) * orients] = from_tile(state[reach + pair * odd + i], scratch)

    @pl.when(sec == 1)
    def _():
        to_corner[...] = to_across[held:]


def call(kernel, out_shape, scratch, operands):
    return pl.pallas_call(
        kernel,
        in_specs=[IN_VMEM] * len(operands),
        out_specs=[IN_VMEM] * len(out_shape),
        out_shape=[jax.ShapeDtypeStruct(shape, jnp.float32) for shape in out_shape],
        scratch_shapes=scratch,
        compiler_params=pltpu.CompilerParams(vmem_limit_bytes=VMEM_BYTES),
    )(*operands)


def paired(incoming, backward, fields, block_types, axial_taps, lateral_taps, depth_taps, bend_diagonal, bend_coupling):
    n_sec, n_gx = lax.axis_size("sec"), lax.axis_size("gx")
    steps, planes, orients, cells = backward.shape
    pair = planes // 2
    reach = (TICKS - 1) * steps, steps
    near, far = (1, -1), (1, -1, 2, -2)
    rows = 2 * orients
    lanes = cells // 2
    sec = lax.axis_index("sec")
    last = n_sec - 1

    def send(array, by_sec, shift=0):
        by_sec = by_sec.items() if isinstance(by_sec, dict) else enumerate(by_sec)
        pairs = [(s * n_gx + g, t * n_gx + (g + shift) % n_gx) for s, t in by_sec for g in range(n_gx)]
        return lax.ppermute(array, ("sec", "gx"), pairs)

    same, beside, across = (0, 1, 2, 3), (1, 0, 3, 2), (2, 3, 0, 1)
    whole = incoming[0]
    types = jnp.pad(block_types.astype(jnp.float32), ((0, 7), (0, cells - steps)))
    low, high = (jnp.concatenate([each.reshape(-1, cells), types]) for each in (whole[:pair], whole[pair:]))
    lead = backward[:LEAD]
    backward, lead, high, low = lax.optimization_barrier((backward, lead, high, low))
    moved_high = send(high, (1, 3, 0, 2))
    moved_low = send(low, (0, 2, 1, 3))
    across_types = send(high[pair * orients :], across)
    early_last = send(lead.astype(jnp.float32), {2: 0})
    lines = lax.dynamic_slice_in_dim(fields, sec % 2 * pair, pair, axis=1).reshape(-1, cells)
    settled = prepare(backward, axial_taps, lateral_taps, depth_taps, bend_diagonal, bend_coupling)
    lines, early_last, *settled = lax.optimization_barrier((lines, early_last, *settled))

    tile = pltpu.VMEM((rows, lanes), jnp.float32)
    packed = pltpu.VMEM((GROUP * rows, 2 * lanes), jnp.bfloat16)
    inner = pltpu.VMEM((planes, rows, lanes), jnp.float32)

    def work(extent):
        slab = pltpu.VMEM((planes + 2 * extent, rows, lanes), jnp.float32)
        return [slab, slab, packed, packed, tile]

    (piece,) = call(
        pack_kernel, [(pair * rows + FIELD_ROWS, lanes)], [tile], [low, moved_high, moved_low, across_types, lines]
    )
    own = [send(piece, same, shift) for shift in far]
    settled = pl.pallas_call(
        settle_kernel,
        in_specs=[IN_VMEM] * len(settled),
        out_specs=[IN_VMEM] * len(settled),
        out_shape=[jax.ShapeDtypeStruct(each.shape, each.dtype) for each in settled],
        compiler_params=pltpu.CompilerParams(vmem_limit_bytes=VMEM_BYTES),
    )(*settled)
    own[-1], *settled = lax.optimization_barrier((own[-1], *settled))
    stored, (taps, weights) = settled[:2], settled[2:]
    swapped = [send(each, beside) for each in [piece] + own]
    late_stored, *swapped = lax.optimization_barrier((stored[1], *swapped))
    late_last = send(late_stored, {2: 0})
    firsts = [piece, swapped[0]]
    middle, piece, kept, total, factor = call(
        functools.partial(early_kernel, tuple(-shift for shift in (0,) + far)),
        [(planes, rows, lanes), (pair, rows, lanes), (planes, rows, lanes), (planes, rows, lanes)]
        + [(fields.shape[0], planes + 2 * reach[0], rows, lanes)],
        work(reach[0]),
        [taps, weights, piece, *own, *swapped, *stored],
    )
    own = [send(piece, same, shift) for shift in near]
    beside_total = send(total, beside)
    swapped = [send(each, beside) for each in own]
    held = planes * (orients // n_sec)
    handoff, share, to_pair, to_across, to_corner = call(
        functools.partial(late_kernel, tuple(-shift for shift in near), last),
        [(planes, orients, cells)]
        + [(held, cells)] * 2
        + [(held + pair * orients, cells), (pair * orients, cells)],
        work(reach[1]) + [inner, inner, pltpu.VMEM((orients, cells), jnp.float32)],
        [taps, weights, *firsts, middle, *own, *swapped, factor, kept, total, beside_total]
        + [early_last, late_last, *stored],
    )
    to_pair = send(to_pair, beside)
    to_across = send(to_across, (2, 0, 3, 1))
    to_corner = send(to_corner, (3, 2, 1, 0))
    third = sec == 2
    density = share + to_pair + to_across[:held] + jnp.where(third, 0.0, to_corner[:held])
    arrived = jnp.concatenate([to_across[held:], to_corner]).reshape(handoff.shape)
    handoff = jnp.where(third, arrived, handoff)
    return handoff[None], density.reshape(planes, -1, cells) / (n_sec * steps)


def pairs_fit(n_sec, planes, steps, orients, cells, kinds):
    return (
        n_sec == TICKS + 1 == 4
        and planes == steps
        and planes % 2 == 0
        and 2 * orients == 2 * CZ == cells // 2 == 128
        and kinds * planes <= FIELD_ROWS and 10 * kinds * planes <= 2 * orients
        and GROUP < 2 * planes
    )


def solution(mesh):
    in_specs = (
        P("sec", "gx", None, None),
        P("sec", "gx", None, None),
        P(None, "gx", None),
        P("sec", None),
        P(),
        P(),
        P(),
        P(),
        P(),
    )
    out_specs = (P("sec", "gx", None, None), P("gx", "sec", None))

    def body(incoming, backward, fields, *rest):
        steps, planes, orients, cells = backward.shape
        fits = pairs_fit(mesh.shape["sec"], planes, steps, orients, cells, fields.shape[0])
        return (paired if fits else per_device)(incoming, backward, fields, *rest)

    return jax.shard_map(body, mesh=mesh, in_specs=in_specs, out_specs=out_specs, check_vma=False)
```

```python
import functools

import jax
import jax.numpy as jnp
from jax import lax
from jax.experimental import pallas as pl
from jax.experimental.pallas import tpu as pltpu
from jax.sharding import PartitionSpec as P

TICKS = 3
CZ = 64
GROUP = 6
FIELD_ROWS = 16
OWN_KINDS, ACROSS_KINDS = 12, 13
LEAD = 1
VMEM_BYTES = 16 * 2**20
IN_VMEM = pl.BlockSpec(memory_space=pltpu.VMEM)


def padded_2(block, sides, width):
    for axis, dim in sides:
        count = lax.axis_size(axis)
        forward = [(i, i + 1) for i in range(count - 1)]
        forward.append((count - 1, 0))
        backward = [(target, source) for source, target in forward]
        low = lax.ppermute(
            lax.slice_in_dim(block, block.shape[dim] - width, None, axis=dim), axis, forward
        )
        high = lax.ppermute(lax.slice_in_dim(block, 0, width, axis=dim), axis, backward)
        block = jnp.concatenate([low, block, high], axis=dim)
    return block


def from_behind(array, axis, by):
    length = lax.axis_size(axis)
    pairs = [(i, i + by) for i in range(length) if 0 <= i + by < length]
    return lax.ppermute(array, axis, pairs)


def boltzmann(fields, kinds):
    selector = kinds == jnp.arange(fields.shape[0], dtype=jnp.int32)
    chosen = jnp.sum(jnp.where(selector[:, None, None], fields, jnp.zeros_like(fields)), axis=0)
    return jnp.exp(-chosen)


def column(taps, which):
    return taps[which][None, :, None]


def advance_padded(padded, factor, axial_taps, lateral_taps, depth_taps, kernel):
    along_x = (
        column(axial_taps, 0) * padded[:-2]
        + column(axial_taps, 1) * padded[1:-1]
        + column(axial_taps, 2) * padded[2:]
    )
    along_y = (
        column(lateral_taps, 0) * jnp.roll(along_x, CZ, axis=2)
        + column(lateral_taps, 1) * along_x
        + column(lateral_taps, 2) * jnp.roll(along_x, -CZ, axis=2)
    )
    depth_pos = (jnp.arange(along_y.shape[2], dtype=jnp.int32) % CZ)[None, None, :]
    behind = jnp.where(
        depth_pos == 0, jnp.roll(along_y, -(CZ - 1), axis=2), jnp.roll(along_y, 1, axis=2)
    )
    ahead = jnp.where(
        depth_pos == CZ - 1, jnp.roll(along_y, CZ - 1, axis=2), jnp.roll(along_y, -1, axis=2)
    )
    along_z = (
        column(depth_taps, 0) * behind
        + column(depth_taps, 1) * along_y
        + column(depth_taps, 2) * ahead
    )
    blended = jnp.einsum(
        "uv,xvc->xuc",
        kernel,
        along_z,
        precision=lax.Precision.HIGHEST,
        preferred_element_type=jnp.float32,
    )
    return blended * factor[:, None, :]


def per_device(
    incoming,
    backward,
    fields,
    block_types,
    axial_taps,
    lateral_taps,
    depth_taps,
    bend_diagonal,
    bend_coupling,
):
    kernel = jnp.diag(bend_diagonal) + bend_coupling
    steps_each = block_types.shape[1]
    planes = incoming.shape[1]
    start = incoming[0]
    first_section = lax.axis_index("sec") == 0
    wide_fields = padded_2(fields, (("gx", 1),), steps_each)
    factors = [boltzmann(wide_fields, block_types[0, position]) for position in range(steps_each)]
    current = start
    outgoing = start
    accumulated = jnp.zeros(start.shape, jnp.float32)
    for tick_index in range(TICKS):
        final_tick = tick_index + 1 == TICKS
        extended = padded_2(current, (("gx", 0),), steps_each)
        for position in range(steps_each):
            margin = steps_each - position - 1
            offset = steps_each - margin
            factor = factors[position][offset : offset + planes + 2 * margin]
            extended = advance_padded(
                extended, factor, axial_taps, lateral_taps, depth_taps, kernel
            )
            if final_tick:
                accumulated = accumulated + extended[margin : margin + planes] * backward[
                    position
                ].astype(jnp.float32)
        outgoing = extended
        if not final_tick:
            shifted = from_behind(outgoing, "sec", 1)
            current = jnp.where(first_section, start, shifted)
    reduced = lax.psum_scatter(accumulated, "sec", scatter_dimension=1, tiled=True)
    density = reduced / (lax.axis_size("sec") * steps_each)
    return (outgoing[None], density)


def to_tile(plane, scratch):
    half = plane.shape[1] // 2
    scratch[...] = jnp.concatenate([plane[:, :half], plane[:, half:]], axis=0).T
    return reorder(scratch)


def reorder(scratch):
    rows = scratch.shape[0]
    return jnp.concatenate(
        [scratch[pl.ds(yl * CZ + zl, 8, stride=8), :] for yl in range(rows // CZ) for zl in range(CZ // 8)], axis=0
    )


def from_tile(tile, scratch):
    rows = tile.shape[0]
    for yl in range(rows // CZ):
        for zl in range(CZ // 8):
            at = (yl * (CZ // 8) + zl) * 8
            scratch[pl.ds(yl * CZ + zl, 8, stride=8), :] = tile[at : at + 8]
    turned = scratch[...].T
    half = turned.shape[0] // 2
    return jnp.concatenate([turned[:half], turned[half:]], axis=1)


def stencil(behind, here, ahead, taps):
    a = here + taps[0] * behind + taps[1] * ahead
    low, high = a[:CZ], a[CZ:]
    low_turned = pltpu.roll(low, a.shape[1] // 2, 1)
    high_turned = pltpu.roll(high, a.shape[1] // 2, 1)
    out = []
    for b in (
        low + taps[2] * high_turned + taps[3] * high,
        high + taps[2] * low + taps[3] * low_turned,
    ):
        back = jnp.concatenate([pltpu.roll(b[-8:], 1, 0), b[:-8]], axis=0)
        front = jnp.concatenate([b[8:], pltpu.roll(b[:8], 7, 0)], axis=0)
        out.append(b + taps[4] * back + taps[5] * front)
    return jnp.concatenate(out, axis=0)


def position():
    sec = lax.axis_index("sec")
    return sec, lax.rem(sec, 2)


def prepare_kernel(backward, table, early, late, taps, weights, scratch):
    orients = table.shape[1]
    axial, lateral, depth, diagonal, coupling = (table[i : i + n] for i, n in ((0, 3), (3, 3), (6, 3), (9, 1), (16, orients)))
    ratios = [each[w : w + 1] / each[1:2] for each in (axial, lateral, depth) for w in (0, 2)]
    for i, ratio in enumerate(ratios + ratios[:2]):
        taps[i : i + 1] = jnp.concatenate([ratio, ratio], axis=1)
    square = (orients, orients)
    same = lax.broadcasted_iota(jnp.int32, square, 0) == lax.broadcasted_iota(jnp.int32, square, 1)
    kernel = jnp.where(same, diagonal, 0.0) + coupling
    kernel = kernel * (axial[1:2] * lateral[1:2] * depth[1:2])
    upper = jnp.concatenate([kernel, jnp.zeros_like(kernel)], axis=1)
    twice = jnp.concatenate([upper, pltpu.roll(upper, orients, 1)], axis=0).T
    coarse = twice.astype(jnp.bfloat16)
    fine = (twice - coarse.astype(jnp.float32)).astype(jnp.bfloat16)
    weights[...] = jnp.concatenate(
        [jnp.concatenate([coarse, fine], axis=1), jnp.concatenate([coarse, jnp.zeros_like(fine)], axis=1)], axis=0
    )
    for out, begin in ((early, 0), (late, LEAD)):
        for step in range(out.shape[0]):
            for i in range(out.shape[1]):
                out[step, i] = to_tile(backward[begin + step, i].astype(jnp.float32), scratch)


def prepare(backward, axial, lateral, depth, diagonal, coupling):
    steps, planes, orients, cells = backward.shape
    rows, lanes = 2 * orients, cells // 2
    table = jnp.concatenate([axial, lateral, depth, jnp.broadcast_to(diagonal, (7, orients)), coupling])
    first, rest = (((count, planes, rows, lanes), jnp.float32) for count in (LEAD, steps - LEAD))
    return pl.pallas_call(
        prepare_kernel,
        in_specs=[IN_VMEM] * 2,
        out_specs=[IN_VMEM] * 4,
        out_shape=[
            jax.ShapeDtypeStruct(*each)
            for each in (first, rest, ((8, lanes), jnp.float32), ((2 * rows, 2 * lanes), jnp.bfloat16))
        ],
        scratch_shapes=[pltpu.VMEM((rows, lanes), jnp.float32)],
        compiler_params=pltpu.CompilerParams(vmem_limit_bytes=VMEM_BYTES),
    )(backward, table)


def pack_kernel(low, moved_high, moved_low, kinds, across, fields, out, scratch):
    sec, odd = position()
    rows = scratch.shape[0]
    at = low.shape[0] * rows
    count = fields.shape[0]
    out[at:] = jnp.zeros((FIELD_ROWS, rows), jnp.float32)
    for i in range(count):
        out[at + 2 * i : at + 2 * i + 1] = fields[i : i + 1, :rows]
        out[at + 2 * i + 1 : at + 2 * i + 2] = fields[i : i + 1, rows:]
    out[at + OWN_KINDS : at + OWN_KINDS + 1] = kinds[:1]
    out[at + ACROSS_KINDS : at + ACROSS_KINDS + 1] = across[:1]

    def fill(source):
        for i in range(source.shape[0]):
            out[i * rows : (i + 1) * rows] = to_tile(source[i], scratch)

    pl.when(sec == 0)(lambda: fill(low))
    pl.when(odd == 1)(lambda: fill(moved_high))
    pl.when((sec > 0) & (odd == 0))(lambda: fill(moved_low))


def kinds_at(pieces, at, which):
    sec, odd = position()
    own, others = ([each[at + i : at + i + 1] for i in (OWN_KINDS, ACROSS_KINDS)] for each in pieces)
    even_core, odd_core = (
        [jnp.where(odd == core, mine, theirs) for mine, theirs in zip(own, others)] for core in (0, 1)
    )
    row = jnp.where(
        sec < 2,
        (even_core[0], odd_core[0], even_core[1])[which],
        (odd_core[1], even_core[0], odd_core[0])[which],
    )
    lane = lax.broadcasted_iota(jnp.int32, row.shape, 1)
    return lambda count: [jnp.sum(jnp.where(lane == i, row, 0.0)).astype(jnp.int32) for i in range(count)]


def places(odd, planes, reach, blocks):
    return [reach + block * planes + planes // 2 * core for core in (odd, 1 - odd) for block in blocks]


def run_steps(kinds, taps, weights, count, slab, other, first, second, factor, offset, after):
    tap = [taps[i : i + 1, :] for i in range(6)]
    extent, rows, lanes = slab.shape
    buffers = (slab, other)

    def blend(source, at, packed):
        for i in range(GROUP):
            e = stencil(source[at + i - 1], source[at + i], source[at + i + 1], tap)
            coarse = e.astype(jnp.bfloat16)
            packed[i * rows : (i + 1) * rows, :lanes] = coarse
            packed[i * rows : (i + 1) * rows, lanes:] = (e - coarse.astype(jnp.float32)).astype(jnp.bfloat16)

    def mix(target, at, packed, kind):
        product = jnp.dot(packed[...], weights[...], preferred_element_type=jnp.float32)
        product = product[:, :lanes] + product[:, lanes:]
        for i in range(GROUP):
            target[at + i] = product[i * rows : (i + 1) * rows] * factor[kind, at + i + offset]

    for step in range(count):
        source, target = buffers[step % 2], buffers[1 - step % 2]
        begin, width = step + 1, extent - 2 * step - 2
        groups = -(-width // GROUP)
        kind = kinds[step]

        def at(i, begin=begin, width=width):
            return jnp.minimum(begin + i * GROUP, begin + width - GROUP)

        blend(source, at(0), first)
        if groups > 1:

            def body(i, carry, source=source, target=target, at=at, kind=kind):
                blend(source, at(2 * i + 1), second)
                mix(target, at(2 * i), first, kind)
                blend(source, at(2 * i + 2), first)
                mix(target, at(2 * i + 1), second, kind)
                return carry

            lax.fori_loop(0, (groups - 1) // 2, body, 0)
        if groups % 2 == 0:
            blend(source, at(groups - 1), second)
            mix(target, at(groups - 2), first, kind)
            mix(target, at(groups - 1), second, kind)
        else:
            mix(target, at(groups - 1), first, kind)
        after(step, target)


def spread_factor(columns, factor, starts, width):
    rows, lanes = factor.shape[2:]
    pair = factor.shape[1] // len(starts)
    right = (lax.broadcasted_iota(jnp.int32, (rows, lanes), 1) >= lanes // 2).astype(jnp.int32)
    for piece, start in enumerate(starts):
        for kind in range(factor.shape[0]):
            for i in range(pair):
                at = piece * width + (kind * pair + i) * 2
                factor[kind, start + i] = jnp.take_along_axis(columns, right + at, axis=1, mode="promise_in_bounds")


def early_kernel(blocks, taps, weights, *refs):
    pieces, refs = refs[: 2 * len(blocks)], refs[2 * len(blocks) :]
    stored, (middle, half_out, kept, total, factor) = refs[:2], refs[2:7]
    slab, other, first, second, scratch = refs[7:]
    sec, odd = position()
    planes, rows = middle.shape[:2]
    pair = planes // 2
    reach = (slab.shape[0] - planes) // 2
    starts = places(odd, planes, reach, blocks)
    for piece, start in zip(pieces, starts):
        for i in range(pair):
            slab[start + i] = piece[i * rows : (i + 1) * rows]
    steps = LEAD + stored[1].shape[0]
    centre = (pieces[0], pieces[len(blocks)])
    kinds = [kind for which in (0, 1) for kind in kinds_at(centre, pair * rows, which)(steps)]
    width = 2 * pair * factor.shape[0]
    lines = [piece[pair * rows : pair * rows + width] for piece in pieces]
    lines.append(jnp.zeros((rows - width * len(pieces), rows), jnp.float32))
    scratch[...] = jnp.exp(-jnp.concatenate(lines, axis=0)).T
    spread_factor(reorder(scratch), factor, starts, width)
    total[...] = jnp.zeros(total.shape, jnp.float32)
    kept[...] = jnp.zeros(kept.shape, jnp.float32)

    def after(step, state):
        @pl.when(sec == step // steps)
        def _():
            j = step % steps
            source = stored[0][j] if j < LEAD else stored[1][j - LEAD]
            total[...] += state[reach : reach + planes] * source
            if j + 1 == steps:
                kept[...] = state[reach : reach + planes]

    run_steps(kinds, taps, weights, reach, slab, other, first, second, factor, 0, after)
    state = (slab, other)[reach % 2]
    middle[...] = state[reach : reach + planes]
    half_out[...] = state[pl.ds(reach + pair * odd, pair)]


def late_kernel(blocks, last, taps, weights, first_own, first_swapped, middle, *refs):
    pieces, refs = refs[: 2 * len(blocks)], refs[2 * len(blocks) :]
    factor, kept, total_in, total_beside, series, stored = refs[0], refs[1], refs[2], refs[3], refs[4:6], refs[6:8]
    handoff, share, to_pair, to_across, to_corner = refs[8:13]
    slab, other, first, second, scratch, total, saved, whole = refs[13:]
    sec, odd = position()
    planes, rows = middle.shape[:2]
    pair = planes // 2
    reach = (slab.shape[0] - planes) // 2
    begun = (factor.shape[1] - planes) // 2
    kinds = kinds_at((first_own, first_swapped), pair * rows, 2)(reach)
    slab[reach : reach + planes] = middle[...]
    for piece, start in zip(pieces, places(odd, planes, reach, blocks)):
        for i in range(pair):
            slab[start + i] = piece[i]
    total[...] = jnp.zeros(total.shape, jnp.float32)

    @pl.when(sec == 0)
    def _():
        total[...] = total_in[...] + total_beside[...]

    saved[...] = kept[...]

    def after(step, state):
        @pl.when(sec == 0)
        def _():
            for i in range(planes):
                part = series[1][step - LEAD, i] if step >= LEAD else to_tile(series[0][step, i], scratch)
                total[i] += state[reach + i] * part

        @pl.when(sec == last)
        def _():
            part = stored[0][step] if step < LEAD else stored[1][step - LEAD]
            total[...] += state[reach : reach + planes] * part

    run_steps(kinds, taps, weights, reach, slab, other, first, second, factor, begun - reach, after)
    state = (slab, other)[reach % 2]

    @pl.when(sec == last)
    def _():
        saved[...] = state[reach : reach + planes]

    orients = handoff.shape[1]
    count = orients // (last + 1)
    held = planes * count
    to_corner[...] = jnp.zeros(to_corner.shape, jnp.float32)
    for i in range(planes):
        handoff[i] = from_tile(saved[i], scratch)
        whole[...] = from_tile(total[i], scratch)
        for piece, who in (
            (share, sec),
            (to_pair, sec + 1 - 2 * odd),
            (to_across, jnp.where(sec == 0, 2, 1)),
            (to_corner, last - sec),
        ):
            piece[i * count : (i + 1) * count] = whole[pl.ds(pl.multiple_of(who * count, count), count)]
    for i in range(pair):
        to_across[held + i * orients : held + (i + 1) * orients] = from_tile(state[reach + pair * odd + i], scratch)

    @pl.when(sec == 1)
    def _():
        to_corner[...] = to_across[held:]


def call(kernel, out_shape, scratch, operands):
    return pl.pallas_call(
        kernel,
        in_specs=[IN_VMEM] * len(operands),
        out_specs=[IN_VMEM] * len(out_shape),
        out_shape=[jax.ShapeDtypeStruct(shape, jnp.float32) for shape in out_shape],
        scratch_shapes=scratch,
        compiler_params=pltpu.CompilerParams(vmem_limit_bytes=VMEM_BYTES),
    )(*operands)


def paired(incoming, backward, fields, block_types, axial_taps, lateral_taps, depth_taps, bend_diagonal, bend_coupling):
    n_sec, n_gx = lax.axis_size("sec"), lax.axis_size("gx")
    steps, planes, orients, cells = backward.shape
    pair = planes // 2
    reach = (TICKS - 1) * steps, steps
    near, far = (1, -1), (1, -1, 2, -2)
    rows = 2 * orients
    lanes = cells // 2
    sec = lax.axis_index("sec")
    last = n_sec - 1

    def send(array, by_sec, shift=0):
        by_sec = by_sec.items() if isinstance(by_sec, dict) else enumerate(by_sec)
        pairs = [(s * n_gx + g, t * n_gx + (g + shift) % n_gx) for s, t in by_sec for g in range(n_gx)]
        return lax.ppermute(array, ("sec", "gx"), pairs)

    same, beside, across = (0, 1, 2, 3), (1, 0, 3, 2), (2, 3, 0, 1)
    whole = incoming[0]
    backward, fields, block_types, high, low = lax.optimization_barrier(
        (backward, fields, block_types, whole[pair:], whole[:pair])
    )
    moved_high = send(high, (1, 3, 0, 2))
    moved_low = send(low, (0, 2, 1, 3))
    types = jnp.pad(block_types.astype(jnp.float32), ((0, 7), (0, lanes - steps)))
    across_types = send(types, across)
    lines = lax.dynamic_slice_in_dim(fields, sec % 2 * pair, pair, axis=1).reshape(-1, cells)
    lines, backward = lax.optimization_barrier((lines, backward))
    early_last = send(backward[:LEAD].astype(jnp.float32), {2: 0})
    settled = prepare(backward, axial_taps, lateral_taps, depth_taps, bend_diagonal, bend_coupling)
    lines, early_last, *settled = lax.optimization_barrier((lines, early_last, *settled))
    stored, (taps, weights) = settled[:2], settled[2:]

    tile = pltpu.VMEM((rows, lanes), jnp.float32)
    packed = pltpu.VMEM((GROUP * rows, 2 * lanes), jnp.bfloat16)
    inner = pltpu.VMEM((planes, rows, lanes), jnp.float32)

    def work(extent):
        slab = pltpu.VMEM((planes + 2 * extent, rows, lanes), jnp.float32)
        return [slab, slab, packed, packed, tile]

    (piece,) = call(
        pack_kernel, [(pair * rows + FIELD_ROWS, lanes)], [tile], [low, moved_high, moved_low, types, across_types, lines]
    )
    own = [send(piece, same, shift) for shift in far]
    swapped = [send(each, beside) for each in [piece] + own]
    late_stored, *swapped = lax.optimization_barrier((stored[1], *swapped))
    late_last = send(late_stored, {2: 0})
    firsts = [piece, swapped[0]]
    middle, piece, kept, total, factor = call(
        functools.partial(early_kernel, tuple(-shift for shift in (0,) + far)),
        [(planes, rows, lanes), (pair, rows, lanes), (planes, rows, lanes), (planes, rows, lanes)]
        + [(fields.shape[0], planes + 2 * reach[0], rows, lanes)],
        work(reach[0]),
        [taps, weights, piece, *own, *swapped, *stored],
    )
    own = [send(piece, same, shift) for shift in near]
    beside_total = send(total, beside)
    swapped = [send(each, beside) for each in own]
    held = planes * (orients // n_sec)
    handoff, share, to_pair, to_across, to_corner = call(
        functools.partial(late_kernel, tuple(-shift for shift in near), last),
        [(planes, orients, cells)]
        + [(held, cells)] * 2
        + [(held + pair * orients, cells), (pair * orients, cells)],
        work(reach[1]) + [inner, inner, pltpu.VMEM((orients, cells), jnp.float32)],
        [taps, weights, *firsts, middle, *own, *swapped, factor, kept, total, beside_total]
        + [early_last, late_last, *stored],
    )
    to_pair = send(to_pair, beside)
    to_across = send(to_across, (2, 0, 3, 1))
    to_corner = send(to_corner, (3, 2, 1, 0))
    third = sec == 2
    density = share + to_pair + to_across[:held] + jnp.where(third, 0.0, to_corner[:held])
    arrived = jnp.concatenate([to_across[held:], to_corner]).reshape(handoff.shape)
    handoff = jnp.where(third, arrived, handoff)
    return handoff[None], density.reshape(planes, -1, cells) / (n_sec * steps)


def pairs_fit(n_sec, planes, steps, orients, cells, kinds):
    return (
        n_sec == TICKS + 1 == 4
        and planes == steps
        and planes % 2 == 0
        and 2 * orients == 2 * CZ == cells // 2 == 128
        and kinds * planes <= FIELD_ROWS and 10 * kinds * planes <= 2 * orients
        and GROUP < 2 * planes
    )


def solution(mesh):
    in_specs = (
        P("sec", "gx", None, None),
        P("sec", "gx", None, None),
        P(None, "gx", None),
        P("sec", None),
        P(),
        P(),
        P(),
        P(),
        P(),
    )
    out_specs = (P("sec", "gx", None, None), P("gx", "sec", None))

    def body(incoming, backward, fields, *rest):
        steps, planes, orients, cells = backward.shape
        fits = pairs_fit(mesh.shape["sec"], planes, steps, orients, cells, fields.shape[0])
        return (paired if fits else per_device)(incoming, backward, fields, *rest)

    return jax.shard_map(body, mesh=mesh, in_specs=in_specs, out_specs=out_specs, check_vma=False)
```

```python
import functools

import jax
import jax.numpy as jnp
from jax import lax
from jax.experimental import pallas as pl
from jax.experimental.pallas import tpu as pltpu
from jax.sharding import PartitionSpec as P

TICKS = 3
CZ = 64
GROUP = 6
FIELD_ROWS = 16
TAP_ROWS = 8
OWN_KINDS, FIRST_KINDS, ACROSS_KINDS = 12, 13, 14
LEAD = 1
VMEM_BYTES = 16 * 2**20
WHOLE_VMEM_BYTES = 62 * 2**20
IN_VMEM = pl.BlockSpec(memory_space=pltpu.VMEM)


def padded_2(block, sides, width):
    for axis, dim in sides:
        count = lax.axis_size(axis)
        forward = [(i, i + 1) for i in range(count - 1)]
        forward.append((count - 1, 0))
        backward = [(target, source) for source, target in forward]
        low = lax.ppermute(
            lax.slice_in_dim(block, block.shape[dim] - width, None, axis=dim), axis, forward
        )
        high = lax.ppermute(lax.slice_in_dim(block, 0, width, axis=dim), axis, backward)
        block = jnp.concatenate([low, block, high], axis=dim)
    return block


def from_behind(array, axis, by):
    length = lax.axis_size(axis)
    pairs = [(i, i + by) for i in range(length) if 0 <= i + by < length]
    return lax.ppermute(array, axis, pairs)


def boltzmann(fields, kinds):
    selector = kinds == jnp.arange(fields.shape[0], dtype=jnp.int32)
    chosen = jnp.sum(jnp.where(selector[:, None, None], fields, jnp.zeros_like(fields)), axis=0)
    return jnp.exp(-chosen)


def column(taps, which):
    return taps[which][None, :, None]


def advance_padded(padded, factor, axial_taps, lateral_taps, depth_taps, kernel):
    along_x = (
        column(axial_taps, 0) * padded[:-2]
        + column(axial_taps, 1) * padded[1:-1]
        + column(axial_taps, 2) * padded[2:]
    )
    along_y = (
        column(lateral_taps, 0) * jnp.roll(along_x, CZ, axis=2)
        + column(lateral_taps, 1) * along_x
        + column(lateral_taps, 2) * jnp.roll(along_x, -CZ, axis=2)
    )
    depth_pos = (jnp.arange(along_y.shape[2], dtype=jnp.int32) % CZ)[None, None, :]
    behind = jnp.where(
        depth_pos == 0, jnp.roll(along_y, -(CZ - 1), axis=2), jnp.roll(along_y, 1, axis=2)
    )
    ahead = jnp.where(
        depth_pos == CZ - 1, jnp.roll(along_y, CZ - 1, axis=2), jnp.roll(along_y, -1, axis=2)
    )
    along_z = (
        column(depth_taps, 0) * behind
        + column(depth_taps, 1) * along_y
        + column(depth_taps, 2) * ahead
    )
    blended = jnp.einsum(
        "uv,xvc->xuc",
        kernel,
        along_z,
        precision=lax.Precision.HIGHEST,
        preferred_element_type=jnp.float32,
    )
    return blended * factor[:, None, :]


def per_device(
    incoming,
    backward,
    fields,
    block_types,
    axial_taps,
    lateral_taps,
    depth_taps,
    bend_diagonal,
    bend_coupling,
):
    kernel = jnp.diag(bend_diagonal) + bend_coupling
    steps_each = block_types.shape[1]
    planes = incoming.shape[1]
    start = incoming[0]
    first_section = lax.axis_index("sec") == 0
    wide_fields = padded_2(fields, (("gx", 1),), steps_each)
    factors = [boltzmann(wide_fields, block_types[0, position]) for position in range(steps_each)]
    current = start
    outgoing = start
    accumulated = jnp.zeros(start.shape, jnp.float32)
    for tick_index in range(TICKS):
        final_tick = tick_index + 1 == TICKS
        extended = padded_2(current, (("gx", 0),), steps_each)
        for position in range(steps_each):
            margin = steps_each - position - 1
            offset = steps_each - margin
            factor = factors[position][offset : offset + planes + 2 * margin]
            extended = advance_padded(
                extended, factor, axial_taps, lateral_taps, depth_taps, kernel
            )
            if final_tick:
                accumulated = accumulated + extended[margin : margin + planes] * backward[
                    position
                ].astype(jnp.float32)
        outgoing = extended
        if not final_tick:
            shifted = from_behind(outgoing, "sec", 1)
            current = jnp.where(first_section, start, shifted)
    reduced = lax.psum_scatter(accumulated, "sec", scatter_dimension=1, tiled=True)
    density = reduced / (lax.axis_size("sec") * steps_each)
    return (outgoing[None], density)


def to_tile(plane, scratch):
    half = plane.shape[1] // 2
    scratch[...] = jnp.concatenate([plane[:, :half], plane[:, half:]], axis=0).T
    return reorder(scratch)


def reorder(scratch):
    rows = scratch.shape[0]
    return jnp.concatenate(
        [scratch[pl.ds(yl * CZ + zl, 8, stride=8), :] for yl in range(rows // CZ) for zl in range(CZ // 8)], axis=0
    )


def from_tile(tile, scratch):
    rows = tile.shape[0]
    for yl in range(rows // CZ):
        for zl in range(CZ // 8):
            at = (yl * (CZ // 8) + zl) * 8
            scratch[pl.ds(yl * CZ + zl, 8, stride=8), :] = tile[at : at + 8]
    turned = scratch[...].T
    half = turned.shape[0] // 2
    return jnp.concatenate([turned[:half], turned[half:]], axis=1)


def stencil(behind, here, ahead, taps):
    a = here + taps[0] * behind + taps[1] * ahead
    low, high = a[:CZ], a[CZ:]
    low_turned = pltpu.roll(low, a.shape[1] // 2, 1)
    high_turned = pltpu.roll(high, a.shape[1] // 2, 1)
    out = []
    for b in (
        low + taps[2] * high_turned + taps[3] * high,
        high + taps[2] * low + taps[3] * low_turned,
    ):
        back = jnp.concatenate([pltpu.roll(b[-8:], 1, 0), b[:-8]], axis=0)
        front = jnp.concatenate([b[8:], pltpu.roll(b[:8], 7, 0)], axis=0)
        out.append(b + taps[4] * back + taps[5] * front)
    return jnp.concatenate(out, axis=0)


def position():
    sec = lax.axis_index("sec")
    return sec, lax.rem(sec, 2)


def launch_kernel(*refs):
    sources, (high, low, lead, bundle) = refs[:9], refs[9:13]
    scratch, copies, sems = refs[13], refs[14:23], refs[23]
    moves = [
        pltpu.make_async_copy(source.at[pl.ds(0, copy.shape[0])], copy, sems.at[i])
        for i, (source, copy) in enumerate(zip(sources, copies))
    ]
    for move in moves:
        move.start()
    incoming, stored, fields, kinds, axial, lateral, depth, diagonal, coupling = copies
    for move in moves[2:]:
        move.wait()
    rows, cells = scratch.shape[0], high.shape[1]
    orients = rows // 2
    ratios = [each[w : w + 1] / each[1:2] for each in (axial, lateral, depth) for w in (0, 2)]
    for i, ratio in enumerate(ratios + ratios[:2]):
        bundle[i : i + 1] = jnp.concatenate([ratio, ratio], axis=1)
    square = (orients, orients)
    same = lax.broadcasted_iota(jnp.int32, square, 0) == lax.broadcasted_iota(jnp.int32, square, 1)
    kernel = jnp.where(same, diagonal[...], 0.0) + coupling[...]
    kernel = kernel * (axial[1:2] * lateral[1:2] * depth[1:2])
    upper = jnp.concatenate([kernel, jnp.zeros_like(kernel)], axis=1)
    bundle[TAP_ROWS : TAP_ROWS + rows] = jnp.concatenate([upper, pltpu.roll(upper, orients, 1)], axis=0).T
    types = kinds[...].astype(jnp.float32)
    types = jnp.concatenate([types, jnp.zeros((1, cells - types.shape[1]), jnp.float32)], axis=1)
    odd = position()[1]
    pair = incoming.shape[1] // 2
    at = TAP_ROWS + rows
    bundle[at : at + FIELD_ROWS] = jnp.zeros((FIELD_ROWS, rows), jnp.float32)
    for kind in range(fields.shape[0]):
        for i in range(pair):
            line = fields[kind, pl.ds(pair * odd + i, 1), :]
            here = at + (kind * pair + i) * 2
            bundle[here : here + 1] = line[:, :rows]
            bundle[here + 1 : here + 2] = line[:, rows:]
    bundle[at + OWN_KINDS : at + OWN_KINDS + 1] = types[:, :rows]
    moves[0].wait()
    for i in range(pair):
        low[i * orients : (i + 1) * orients] = incoming[0, i]
        high[i * orients : (i + 1) * orients] = incoming[0, pair + i]
        here = at + FIELD_ROWS + i * rows
        bundle[here : here + rows] = to_tile(incoming[0, i], scratch)
    moves[1].wait()
    planes = stored.shape[1]
    for step in range(LEAD):
        for i in range(planes):
            here = (step * planes + i) * orients
            lead[here : here + orients] = stored[step, i].astype(jnp.float32)
    for out in (high, low, lead):
        out[out.shape[0] - 8 :] = jnp.broadcast_to(types, (8, cells))


def launch(incoming, backward, fields, kinds, axial, lateral, depth, diagonal, coupling):
    planes, orients, cells = backward.shape[1:]
    rows = 2 * orients
    operands = [incoming, backward, fields, kinds, axial, lateral, depth, diagonal.reshape(1, -1), coupling]
    half = (planes // 2 * orients + 8, cells)
    shapes = [half, half, (LEAD * planes * orients + 8, cells), (TAP_ROWS + rows + FIELD_ROWS + planes // 2 * rows, rows)]
    taken = [(LEAD,) + each.shape[1:] if i == 1 else each.shape for i, each in enumerate(operands)]
    return pl.pallas_call(
        launch_kernel,
        in_specs=[pl.BlockSpec(memory_space=pltpu.HBM)] * len(operands),
        out_specs=[IN_VMEM] * len(shapes),
        out_shape=[jax.ShapeDtypeStruct(shape, jnp.float32) for shape in shapes],
        scratch_shapes=[pltpu.VMEM((rows, rows), jnp.float32)]
        + [pltpu.VMEM(shape, each.dtype) for shape, each in zip(taken, operands)]
        + [pltpu.SemaphoreType.DMA((len(operands),))],
        compiler_params=pltpu.CompilerParams(vmem_limit_bytes=WHOLE_VMEM_BYTES),
    )(*operands)


def turn_kernel(backward, early, late, scratch):
    for out, begin in ((early, 0), (late, LEAD)):
        for step in range(out.shape[0]):
            for i in range(out.shape[1]):
                out[step, i] = to_tile(backward[begin + step, i].astype(jnp.float32), scratch)


def pack_kernel(bundle, moved_high, moved_low, lead, out, taps, weights, scratch):
    sec, odd = position()
    rows = scratch.shape[0]
    orients = rows // 2
    taps[...] = bundle[:TAP_ROWS]
    twice = bundle[TAP_ROWS : TAP_ROWS + rows]
    coarse = twice.astype(jnp.bfloat16)
    fine = (twice - coarse.astype(jnp.float32)).astype(jnp.bfloat16)
    weights[...] = jnp.concatenate(
        [jnp.concatenate([coarse, fine], axis=1), jnp.concatenate([coarse, jnp.zeros_like(fine)], axis=1)], axis=0
    )
    at = out.shape[0] - FIELD_ROWS
    lines = TAP_ROWS + rows
    out[at:] = bundle[lines : lines + FIELD_ROWS]
    out[at + ACROSS_KINDS : at + ACROSS_KINDS + 1] = lead[lead.shape[0] - 8 : lead.shape[0] - 7, :rows]

    @pl.when(sec == 0)
    def _():
        out[:at] = bundle[lines + FIELD_ROWS :]
        out[at + FIRST_KINDS : at + FIRST_KINDS + 1] = out[at + OWN_KINDS : at + OWN_KINDS + 1]

    def fill(source):
        for i in range(at // rows):
            out[i * rows : (i + 1) * rows] = to_tile(source[i * orients : (i + 1) * orients], scratch)
        here = source.shape[0] - 8
        out[at + FIRST_KINDS : at + FIRST_KINDS + 1] = source[here : here + 1, :rows]

    pl.when(odd == 1)(lambda: fill(moved_high))
    pl.when((sec > 0) & (odd == 0))(lambda: fill(moved_low))


def kinds_at(pieces, at, which):
    sec, odd = position()
    own, others = ([each[at + i : at + i + 1] for i in (OWN_KINDS, FIRST_KINDS, ACROSS_KINDS)] for each in pieces)
    even_core, odd_core = (
        [jnp.where(odd == core, mine, theirs) for mine, theirs in zip(own, others)] for core in (0, 1)
    )
    row = own[1]
    if which > 0:
        row = jnp.where(sec < 2, (odd_core[0], even_core[2])[which - 1], (even_core[0], odd_core[0])[which - 1])
    lane = lax.broadcasted_iota(jnp.int32, row.shape, 1)
    return lambda count: [jnp.sum(jnp.where(lane == i, row, 0.0)).astype(jnp.int32) for i in range(count)]


def places(odd, planes, reach, blocks):
    return [reach + block * planes + planes // 2 * core for core in (odd, 1 - odd) for block in blocks]


def run_steps(kinds, taps, weights, count, slab, other, first, second, factor, offset, after):
    tap = [taps[i : i + 1, :] for i in range(6)]
    extent, rows, lanes = slab.shape
    buffers = (slab, other)

    def blend(source, at, packed):
        for i in range(GROUP):
            e = stencil(source[at + i - 1], source[at + i], source[at + i + 1], tap)
            coarse = e.astype(jnp.bfloat16)
            packed[i * rows : (i + 1) * rows, :lanes] = coarse
            packed[i * rows : (i + 1) * rows, lanes:] = (e - coarse.astype(jnp.float32)).astype(jnp.bfloat16)

    def mix(target, at, packed, kind):
        product = jnp.dot(packed[...], weights[...], preferred_element_type=jnp.float32)
        product = product[:, :lanes] + product[:, lanes:]
        for i in range(GROUP):
            target[at + i] = product[i * rows : (i + 1) * rows] * factor[kind, at + i + offset]

    for step in range(count):
        source, target = buffers[step % 2], buffers[1 - step % 2]
        begin, width = step + 1, extent - 2 * step - 2
        groups = -(-width // GROUP)
        kind = kinds[step]

        def at(i, begin=begin, width=width):
            return jnp.minimum(begin + i * GROUP, begin + width - GROUP)

        blend(source, at(0), first)
        if groups > 1:

            def body(i, carry, source=source, target=target, at=at, kind=kind):
                blend(source, at(2 * i + 1), second)
                mix(target, at(2 * i), first, kind)
                blend(source, at(2 * i + 2), first)
                mix(target, at(2 * i + 1), second, kind)
                return carry

            lax.fori_loop(0, (groups - 1) // 2, body, 0)
        if groups % 2 == 0:
            blend(source, at(groups - 1), second)
            mix(target, at(groups - 2), first, kind)
            mix(target, at(groups - 1), second, kind)
        else:
            mix(target, at(groups - 1), first, kind)
        after(step, target)


def spread_factor(columns, factor, starts, width):
    rows, lanes = factor.shape[2:]
    pair = factor.shape[1] // len(starts)
    right = (lax.broadcasted_iota(jnp.int32, (rows, lanes), 1) >= lanes // 2).astype(jnp.int32)
    for piece, start in enumerate(starts):
        for kind in range(factor.shape[0]):
            for i in range(pair):
                at = piece * width + (kind * pair + i) * 2
                factor[kind, start + i] = jnp.take_along_axis(columns, right + at, axis=1, mode="promise_in_bounds")


def early_kernel(blocks, taps, weights, *refs):
    pieces, refs = refs[: 2 * len(blocks)], refs[2 * len(blocks) :]
    stored, (middle, half_out, kept, total, factor) = refs[:2], refs[2:7]
    slab, other, first, second, scratch = refs[7:]
    sec, odd = position()
    planes, rows = middle.shape[:2]
    pair = planes // 2
    reach = (slab.shape[0] - planes) // 2
    starts = places(odd, planes, reach, blocks)
    for piece, start in zip(pieces, starts):
        for i in range(pair):
            slab[start + i] = piece[i * rows : (i + 1) * rows]
    steps = LEAD + stored[1].shape[0]
    centre = (pieces[0], pieces[len(blocks)])
    kinds = [kind for which in (0, 1) for kind in kinds_at(centre, pair * rows, which)(steps)]
    width = 2 * pair * factor.shape[0]
    lines = [piece[pair * rows : pair * rows + width] for piece in pieces]
    lines.append(jnp.zeros((rows - width * len(pieces), rows), jnp.float32))
    scratch[...] = jnp.exp(-jnp.concatenate(lines, axis=0)).T
    spread_factor(reorder(scratch), factor, starts, width)
    total[...] = jnp.zeros(total.shape, jnp.float32)
    kept[...] = jnp.zeros(kept.shape, jnp.float32)

    def after(step, state):
        @pl.when(sec == step // steps)
        def _():
            j = step % steps
            source = stored[0][j] if j < LEAD else stored[1][j - LEAD]
            total[...] += state[reach : reach + planes] * source
            if j + 1 == steps:
                kept[...] = state[reach : reach + planes]

    run_steps(kinds, taps, weights, reach, slab, other, first, second, factor, 0, after)
    state = (slab, other)[reach % 2]
    middle[...] = state[reach : reach + planes]
    half_out[...] = state[pl.ds(reach + pair * odd, pair)]


def late_kernel(blocks, last, taps, weights, first_own, first_swapped, middle, *refs):
    pieces, refs = refs[: 2 * len(blocks)], refs[2 * len(blocks) :]
    factor, kept, total_in, total_beside, series, stored = refs[0], refs[1], refs[2], refs[3], refs[4:6], refs[6:8]
    handoff, share, to_pair, to_across, to_corner = refs[8:13]
    slab, other, first, second, scratch, total, saved, whole = refs[13:]
    sec, odd = position()
    planes, rows = middle.shape[:2]
    pair = planes // 2
    reach = (slab.shape[0] - planes) // 2
    begun = (factor.shape[1] - planes) // 2
    kinds = kinds_at((first_own, first_swapped), pair * rows, 2)(reach)
    slab[reach : reach + planes] = middle[...]
    for piece, start in zip(pieces, places(odd, planes, reach, blocks)):
        for i in range(pair):
            slab[start + i] = piece[i]
    total[...] = jnp.zeros(total.shape, jnp.float32)

    @pl.when(sec == 0)
    def _():
        total[...] = total_in[...] + total_beside[...]

    saved[...] = kept[...]

    def lead_plane(i):
        return series[0][i * rows // 2 : (i + 1) * rows // 2]

    def after(step, state):
        @pl.when(sec == 0)
        def _():
            for i in range(planes):
                part = series[1][step - LEAD, i] if step >= LEAD else to_tile(lead_plane(step * planes + i), scratch)
                total[i] += state[reach + i] * part

        @pl.when(sec == last)
        def _():
            part = stored[0][step] if step < LEAD else stored[1][step - LEAD]
            total[...] += state[reach : reach + planes] * part

    run_steps(kinds, taps, weights, reach, slab, other, first, second, factor, begun - reach, after)
    state = (slab, other)[reach % 2]

    @pl.when(sec == last)
    def _():
        saved[...] = state[reach : reach + planes]

    orients = handoff.shape[1]
    count = orients // (last + 1)
    held = planes * count
    to_corner[...] = jnp.zeros(to_corner.shape, jnp.float32)
    for i in range(planes):
        handoff[i] = from_tile(saved[i], scratch)
        whole[...] = from_tile(total[i], scratch)
        for piece, who in (
            (share, sec),
            (to_pair, sec + 1 - 2 * odd),
            (to_across, jnp.where(sec == 0, 2, 1)),
            (to_corner, last - sec),
        ):
            piece[i * count : (i + 1) * count] = whole[pl.ds(pl.multiple_of(who * count, count), count)]
    for i in range(pair):
        to_across[held + i * orients : held + (i + 1) * orients] = from_tile(state[reach + pair * odd + i], scratch)

    @pl.when(sec == 1)
    def _():
        to_corner[...] = to_across[held:]


def finish_kernel(contour, handoff_in, share, to_pair, to_across, to_corner, handoff, density):
    sec = lax.axis_index("sec")
    planes, count = density.shape[:2]
    held = planes * count
    corner = jnp.where(sec == 2, 0.0, to_corner[:held])
    total = (share[...] + to_pair[...] + to_across[:held] + corner) / contour
    for i in range(planes):
        density[i] = total[i * count : (i + 1) * count]
    handoff[0] = handoff_in[...]

    @pl.when(sec == 2)
    def _():
        orients = handoff.shape[2]
        pair = planes // 2
        for i in range(pair):
            handoff[0, i] = to_across[held + i * orients : held + (i + 1) * orients]
            handoff[0, pair + i] = to_corner[i * orients : (i + 1) * orients]


def call(kernel, out_shape, scratch, operands, dtypes=None):
    return pl.pallas_call(
        kernel,
        in_specs=[IN_VMEM] * len(operands),
        out_specs=[IN_VMEM] * len(out_shape),
        out_shape=[jax.ShapeDtypeStruct(shape, (dtypes or {}).get(i, jnp.float32)) for i, shape in enumerate(out_shape)],
        scratch_shapes=scratch,
        compiler_params=pltpu.CompilerParams(vmem_limit_bytes=VMEM_BYTES),
    )(*operands)


def paired(incoming, backward, fields, block_types, axial_taps, lateral_taps, depth_taps, bend_diagonal, bend_coupling):
    n_sec, n_gx = lax.axis_size("sec"), lax.axis_size("gx")
    steps, planes, orients, cells = backward.shape
    pair = planes // 2
    reach = (TICKS - 1) * steps, steps
    near, far = (1, -1), (1, -1, 2, -2)
    rows = 2 * orients
    lanes = cells // 2
    last = n_sec - 1

    def send(array, by_sec, shift=0):
        by_sec = by_sec.items() if isinstance(by_sec, dict) else enumerate(by_sec)
        pairs = [(s * n_gx + g, t * n_gx + (g + shift) % n_gx) for s, t in by_sec for g in range(n_gx)]
        return lax.ppermute(array, ("sec", "gx"), pairs)

    same, beside = (0, 1, 2, 3), (1, 0, 3, 2)
    high, low, lead, bundle = launch(
        incoming, backward, fields, block_types, axial_taps, lateral_taps, depth_taps, bend_diagonal, bend_coupling
    )
    moved_high = send(high, {0: 1, 1: 3})
    moved_low = send(low, {1: 2})
    early_last = send(lead, {2: 0})

    tile = pltpu.VMEM((rows, lanes), jnp.float32)
    packed = pltpu.VMEM((GROUP * rows, 2 * lanes), jnp.bfloat16)
    inner = pltpu.VMEM((planes, rows, lanes), jnp.float32)

    def work(extent):
        slab = pltpu.VMEM((planes + 2 * extent, rows, lanes), jnp.float32)
        return [slab, slab, packed, packed, tile]

    piece, taps, weights = call(
        pack_kernel,
        [(pair * rows + FIELD_ROWS, lanes), (TAP_ROWS, lanes), (2 * rows, 2 * lanes)],
        [tile],
        [bundle, moved_high, moved_low, early_last],
        {2: jnp.bfloat16},
    )
    own = [send(piece, same, shift) for shift in far]
    backward, _ = lax.optimization_barrier((backward, piece))
    stored = call(turn_kernel, [(count, planes, rows, lanes) for count in (LEAD, steps - LEAD)], [tile], [backward])
    own[-1], *stored = lax.optimization_barrier((own[-1], *stored))
    swapped = [send(each, beside) for each in [piece] + own]
    late_stored, *swapped = lax.optimization_barrier((stored[1], *swapped))
    late_last = send(late_stored, {2: 0})
    firsts = [piece, swapped[0]]
    middle, piece, kept, total, factor = call(
        functools.partial(early_kernel, tuple(-shift for shift in (0,) + far)),
        [(planes, rows, lanes), (pair, rows, lanes), (planes, rows, lanes), (planes, rows, lanes)]
        + [(fields.shape[0], planes + 2 * reach[0], rows, lanes)],
        work(reach[0]),
        [taps, weights, piece, *own, *swapped, *stored],
    )
    own = [send(piece, same, shift) for shift in near]
    beside_total = send(total, beside)
    swapped = [send(each, beside) for each in own]
    held = planes * (orients // n_sec)
    handoff, share, to_pair, to_across, to_corner = call(
        functools.partial(late_kernel, tuple(-shift for shift in near), last),
        [(planes, orients, cells)]
        + [(held, cells)] * 2
        + [(held + pair * orients, cells), (pair * orients, cells)],
        work(reach[1]) + [inner, inner, pltpu.VMEM((orients, cells), jnp.float32)],
        [taps, weights, *firsts, middle, *own, *swapped, factor, kept, total, beside_total]
        + [early_last, late_last, *stored],
    )
    to_pair = send(to_pair, beside)
    to_across = send(to_across, (2, 0, 3, 1))
    to_corner = send(to_corner, (3, 2, 1, 0))
    handoff, density = call(
        functools.partial(finish_kernel, n_sec * steps),
        [(1,) + handoff.shape, (planes, orients // n_sec, cells)],
        [],
        [handoff, share, to_pair, to_across, to_corner],
    )
    return handoff, density


def pairs_fit(n_sec, planes, steps, orients, cells, kinds):
    return (
        n_sec == TICKS + 1 == 4
        and planes == steps
        and planes % 2 == 0
        and 2 * orients == 2 * CZ == cells // 2 == 128
        and kinds * planes <= FIELD_ROWS and 10 * kinds * planes <= 2 * orients
        and GROUP < 2 * planes
    )


def solution(mesh):
    in_specs = (
        P("sec", "gx", None, None),
        P("sec", "gx", None, None),
        P(None, "gx", None),
        P("sec", None),
        P(),
        P(),
        P(),
        P(),
        P(),
    )
    out_specs = (P("sec", "gx", None, None), P("gx", "sec", None))

    def body(incoming, backward, fields, *rest):
        steps, planes, orients, cells = backward.shape
        fits = pairs_fit(mesh.shape["sec"], planes, steps, orients, cells, fields.shape[0])
        return (paired if fits else per_device)(incoming, backward, fields, *rest)

    return jax.shard_map(body, mesh=mesh, in_specs=in_specs, out_specs=out_specs, check_vma=False)
```

```python
import functools

import jax
import jax.numpy as jnp
from jax import lax
from jax.experimental import pallas as pl
from jax.experimental.pallas import tpu as pltpu
from jax.sharding import PartitionSpec as P

TICKS = 3
CZ = 64
GROUP = 6
FIELD_ROWS = 32
TAP_ROWS = 8
OWN_KINDS, FIRST_KINDS = 24, 25
LEAD = 1
VMEM_BYTES = 16 * 2**20
WHOLE_VMEM_BYTES = 62 * 2**20
IN_VMEM = pl.BlockSpec(memory_space=pltpu.VMEM)


def padded_2(block, sides, width):
    for axis, dim in sides:
        count = lax.axis_size(axis)
        forward = [(i, i + 1) for i in range(count - 1)]
        forward.append((count - 1, 0))
        backward = [(target, source) for source, target in forward]
        low = lax.ppermute(
            lax.slice_in_dim(block, block.shape[dim] - width, None, axis=dim), axis, forward
        )
        high = lax.ppermute(lax.slice_in_dim(block, 0, width, axis=dim), axis, backward)
        block = jnp.concatenate([low, block, high], axis=dim)
    return block


def from_behind(array, axis, by):
    length = lax.axis_size(axis)
    pairs = [(i, i + by) for i in range(length) if 0 <= i + by < length]
    return lax.ppermute(array, axis, pairs)


def boltzmann(fields, kinds):
    selector = kinds == jnp.arange(fields.shape[0], dtype=jnp.int32)
    chosen = jnp.sum(jnp.where(selector[:, None, None], fields, jnp.zeros_like(fields)), axis=0)
    return jnp.exp(-chosen)


def column(taps, which):
    return taps[which][None, :, None]


def advance_padded(padded, factor, axial_taps, lateral_taps, depth_taps, kernel):
    along_x = (
        column(axial_taps, 0) * padded[:-2]
        + column(axial_taps, 1) * padded[1:-1]
        + column(axial_taps, 2) * padded[2:]
    )
    along_y = (
        column(lateral_taps, 0) * jnp.roll(along_x, CZ, axis=2)
        + column(lateral_taps, 1) * along_x
        + column(lateral_taps, 2) * jnp.roll(along_x, -CZ, axis=2)
    )
    depth_pos = (jnp.arange(along_y.shape[2], dtype=jnp.int32) % CZ)[None, None, :]
    behind = jnp.where(
        depth_pos == 0, jnp.roll(along_y, -(CZ - 1), axis=2), jnp.roll(along_y, 1, axis=2)
    )
    ahead = jnp.where(
        depth_pos == CZ - 1, jnp.roll(along_y, CZ - 1, axis=2), jnp.roll(along_y, -1, axis=2)
    )
    along_z = (
        column(depth_taps, 0) * behind
        + column(depth_taps, 1) * along_y
        + column(depth_taps, 2) * ahead
    )
    blended = jnp.einsum(
        "uv,xvc->xuc",
        kernel,
        along_z,
        precision=lax.Precision.HIGHEST,
        preferred_element_type=jnp.float32,
    )
    return blended * factor[:, None, :]


def per_device(
    incoming,
    backward,
    fields,
    block_types,
    axial_taps,
    lateral_taps,
    depth_taps,
    bend_diagonal,
    bend_coupling,
):
    kernel = jnp.diag(bend_diagonal) + bend_coupling
    steps_each = block_types.shape[1]
    planes = incoming.shape[1]
    start = incoming[0]
    first_section = lax.axis_index("sec") == 0
    wide_fields = padded_2(fields, (("gx", 1),), steps_each)
    factors = [boltzmann(wide_fields, block_types[0, position]) for position in range(steps_each)]
    current = start
    outgoing = start
    accumulated = jnp.zeros(start.shape, jnp.float32)
    for tick_index in range(TICKS):
        final_tick = tick_index + 1 == TICKS
        extended = padded_2(current, (("gx", 0),), steps_each)
        for position in range(steps_each):
            margin = steps_each - position - 1
            offset = steps_each - margin
            factor = factors[position][offset : offset + planes + 2 * margin]
            extended = advance_padded(
                extended, factor, axial_taps, lateral_taps, depth_taps, kernel
            )
            if final_tick:
                accumulated = accumulated + extended[margin : margin + planes] * backward[
                    position
                ].astype(jnp.float32)
        outgoing = extended
        if not final_tick:
            shifted = from_behind(outgoing, "sec", 1)
            current = jnp.where(first_section, start, shifted)
    reduced = lax.psum_scatter(accumulated, "sec", scatter_dimension=1, tiled=True)
    density = reduced / (lax.axis_size("sec") * steps_each)
    return (outgoing[None], density)


def to_tile(plane, scratch):
    half = plane.shape[1] // 2
    scratch[...] = jnp.concatenate([plane[:, :half], plane[:, half:]], axis=0).T
    return reorder(scratch)


def reorder(scratch):
    rows = scratch.shape[0]
    return jnp.concatenate(
        [scratch[pl.ds(yl * CZ + zl, 8, stride=8), :] for yl in range(rows // CZ) for zl in range(CZ // 8)], axis=0
    )


def from_tile(tile, scratch):
    rows = tile.shape[0]
    for yl in range(rows // CZ):
        for zl in range(CZ // 8):
            at = (yl * (CZ // 8) + zl) * 8
            scratch[pl.ds(yl * CZ + zl, 8, stride=8), :] = tile[at : at + 8]
    turned = scratch[...].T
    half = turned.shape[0] // 2
    return jnp.concatenate([turned[:half], turned[half:]], axis=1)


def stencil(behind, here, ahead, taps):
    a = here + taps[0] * behind + taps[1] * ahead
    low, high = a[:CZ], a[CZ:]
    low_turned = pltpu.roll(low, a.shape[1] // 2, 1)
    high_turned = pltpu.roll(high, a.shape[1] // 2, 1)
    out = []
    for b in (
        low + taps[2] * high_turned + taps[3] * high,
        high + taps[2] * low + taps[3] * low_turned,
    ):
        back = jnp.concatenate([pltpu.roll(b[-8:], 1, 0), b[:-8]], axis=0)
        front = jnp.concatenate([b[8:], pltpu.roll(b[:8], 7, 0)], axis=0)
        out.append(b + taps[4] * back + taps[5] * front)
    return jnp.concatenate(out, axis=0)


def position():
    sec = lax.axis_index("sec")
    return sec, lax.rem(sec, 2)


def launch_kernel(*refs):
    sources, (full, lead, bundle) = refs[:9], refs[9:12]
    scratch, copies, sems = refs[12], refs[13:22], refs[22]
    moves = [
        pltpu.make_async_copy(source.at[pl.ds(0, copy.shape[0])], copy, sems.at[i])
        for i, (source, copy) in enumerate(zip(sources, copies))
    ]
    for move in moves:
        move.start()
    incoming, stored, fields, kinds, axial, lateral, depth, diagonal, coupling = copies
    for move in moves[2:]:
        move.wait()
    rows, cells = scratch.shape[0], full.shape[1]
    orients = rows // 2
    ratios = [each[w : w + 1] / each[1:2] for each in (axial, lateral, depth) for w in (0, 2)]
    for i, ratio in enumerate(ratios + ratios[:2]):
        bundle[i : i + 1] = jnp.concatenate([ratio, ratio], axis=1)
    square = (orients, orients)
    same = lax.broadcasted_iota(jnp.int32, square, 0) == lax.broadcasted_iota(jnp.int32, square, 1)
    kernel = jnp.where(same, diagonal[...], 0.0) + coupling[...]
    kernel = kernel * (axial[1:2] * lateral[1:2] * depth[1:2])
    upper = jnp.concatenate([kernel, jnp.zeros_like(kernel)], axis=1)
    bundle[TAP_ROWS : TAP_ROWS + rows] = jnp.concatenate([upper, pltpu.roll(upper, orients, 1)], axis=0).T
    types = kinds[...].astype(jnp.float32)
    types = jnp.concatenate([types, jnp.zeros((1, cells - types.shape[1]), jnp.float32)], axis=1)
    planes = incoming.shape[1]
    at = TAP_ROWS + rows
    bundle[at : at + FIELD_ROWS] = jnp.zeros((FIELD_ROWS, rows), jnp.float32)
    for kind in range(fields.shape[0]):
        for i in range(planes):
            line = fields[kind, i : i + 1, :]
            here = at + (kind * planes + i) * 2
            bundle[here : here + 1] = line[:, :rows]
            bundle[here + 1 : here + 2] = line[:, rows:]
    bundle[at + OWN_KINDS : at + OWN_KINDS + 1] = types[:, :rows]
    moves[0].wait()
    for i in range(planes):
        full[i * orients : (i + 1) * orients] = incoming[0, i]
        here = at + FIELD_ROWS + i * rows
        bundle[here : here + rows] = to_tile(incoming[0, i], scratch)
    moves[1].wait()
    for step in range(LEAD):
        for i in range(planes):
            here = (step * planes + i) * orients
            lead[here : here + orients] = stored[step, i].astype(jnp.float32)
    for out in (full, lead):
        out[out.shape[0] - 8 :] = jnp.broadcast_to(types, (8, cells))


def launch(incoming, backward, fields, kinds, axial, lateral, depth, diagonal, coupling):
    planes, orients, cells = backward.shape[1:]
    rows = 2 * orients
    operands = [incoming, backward, fields, kinds, axial, lateral, depth, diagonal.reshape(1, -1), coupling]
    shapes = [(count * planes * orients + 8, cells) for count in (1, LEAD)]
    shapes.append((TAP_ROWS + rows + FIELD_ROWS + planes * rows, rows))
    taken = [(LEAD,) + each.shape[1:] if i == 1 else each.shape for i, each in enumerate(operands)]
    return pl.pallas_call(
        launch_kernel,
        in_specs=[pl.BlockSpec(memory_space=pltpu.HBM)] * len(operands),
        out_specs=[IN_VMEM] * len(shapes),
        out_shape=[jax.ShapeDtypeStruct(shape, jnp.float32) for shape in shapes],
        scratch_shapes=[pltpu.VMEM((rows, rows), jnp.float32)]
        + [pltpu.VMEM(shape, each.dtype) for shape, each in zip(taken, operands)]
        + [pltpu.SemaphoreType.DMA((len(operands),))],
        compiler_params=pltpu.CompilerParams(vmem_limit_bytes=WHOLE_VMEM_BYTES),
    )(*operands)


def turn_kernel(backward, early, late, scratch):
    for out, begin in ((early, 0), (late, LEAD)):
        for step in range(out.shape[0]):
            for i in range(out.shape[1]):
                out[step, i] = to_tile(backward[begin + step, i].astype(jnp.float32), scratch)


def pack_kernel(bundle, moved, passed, out, taps, weights, scratch):
    sec, odd = position()
    rows = scratch.shape[0]
    orients = rows // 2
    taps[...] = bundle[:TAP_ROWS]
    twice = bundle[TAP_ROWS : TAP_ROWS + rows]
    coarse = twice.astype(jnp.bfloat16)
    fine = (twice - coarse.astype(jnp.float32)).astype(jnp.bfloat16)
    weights[...] = jnp.concatenate(
        [jnp.concatenate([coarse, fine], axis=1), jnp.concatenate([coarse, jnp.zeros_like(fine)], axis=1)], axis=0
    )
    at = out.shape[0] - FIELD_ROWS
    lines = TAP_ROWS + rows
    out[at:] = bundle[lines : lines + FIELD_ROWS]

    @pl.when(sec == 0)
    def _():
        out[:at] = bundle[lines + FIELD_ROWS :]
        out[at + FIRST_KINDS : at + FIRST_KINDS + 1] = out[at + OWN_KINDS : at + OWN_KINDS + 1]

    def fill(source):
        for i in range(at // rows):
            out[i * rows : (i + 1) * rows] = to_tile(source[i * orients : (i + 1) * orients], scratch)
        here = source.shape[0] - 8
        out[at + FIRST_KINDS : at + FIRST_KINDS + 1] = source[here : here + 1, :rows]

    pl.when(odd == 1)(lambda: fill(moved))
    pl.when((sec > 0) & (odd == 0))(lambda: fill(passed))


def scalars_of(row, count):
    lane = lax.broadcasted_iota(jnp.int32, row.shape, 1)
    return [jnp.sum(jnp.where(lane == i, row, 0.0)).astype(jnp.int32) for i in range(count)]


def places(odd, planes, reach, blocks):
    return [reach + block * planes + planes // 2 * core for core in (odd, 1 - odd) for block in blocks]


def run_steps(kinds, taps, weights, count, slab, other, first, second, factor, offset, after):
    tap = [taps[i : i + 1, :] for i in range(6)]
    extent, rows, lanes = slab.shape
    buffers = (slab, other)

    def blend(source, at, packed):
        for i in range(GROUP):
            e = stencil(source[at + i - 1], source[at + i], source[at + i + 1], tap)
            coarse = e.astype(jnp.bfloat16)
            packed[i * rows : (i + 1) * rows, :lanes] = coarse
            packed[i * rows : (i + 1) * rows, lanes:] = (e - coarse.astype(jnp.float32)).astype(jnp.bfloat16)

    def mix(target, at, packed, kind):
        product = jnp.dot(packed[...], weights[...], preferred_element_type=jnp.float32)
        product = product[:, :lanes] + product[:, lanes:]
        for i in range(GROUP):
            target[at + i] = product[i * rows : (i + 1) * rows] * factor[kind, at + i + offset]

    for step in range(count):
        source, target = buffers[step % 2], buffers[1 - step % 2]
        begin, width = step + 1, extent - 2 * step - 2
        groups = -(-width // GROUP)
        kind = kinds[step]

        def at(i, begin=begin, width=width):
            return jnp.minimum(begin + i * GROUP, begin + width - GROUP)

        blend(source, at(0), first)
        if groups > 1:

            def body(i, carry, source=source, target=target, at=at, kind=kind):
                blend(source, at(2 * i + 1), second)
                mix(target, at(2 * i), first, kind)
                blend(source, at(2 * i + 2), first)
                mix(target, at(2 * i + 1), second, kind)
                return carry

            lax.fori_loop(0, (groups - 1) // 2, body, 0)
        if groups % 2 == 0:
            blend(source, at(groups - 1), second)
            mix(target, at(groups - 2), first, kind)
            mix(target, at(groups - 1), second, kind)
        else:
            mix(target, at(groups - 1), first, kind)
        after(step, target)


def spread_factor(columns, factor, starts, width):
    rows, lanes = factor.shape[2:]
    pair = factor.shape[1] // len(starts)
    right = (lax.broadcasted_iota(jnp.int32, (rows, lanes), 1) >= lanes // 2).astype(jnp.int32)
    for piece, start in enumerate(starts):
        for kind in range(factor.shape[0]):
            for i in range(pair):
                at = piece * width + (kind * pair + i) * 2
                factor[kind, start + i] = jnp.take_along_axis(columns, right + at, axis=1, mode="promise_in_bounds")


def early_kernel(taps, weights, lead, *refs):
    pieces, stored, (middle, half_out, kept, total, factor) = refs[:5], refs[5:7], refs[7:12]
    slab, other, first, second, scratch = refs[12:]
    sec, odd = position()
    planes, rows = middle.shape[:2]
    pair = planes // 2
    reach = (slab.shape[0] - planes) // 2
    mine, others = (planes * (1 + core) for core in (odd, 1 - odd))
    starts = [reach, reach - mine, reach + mine, reach - others, reach + others]
    for piece, start in zip(pieces, starts):
        for i in range(planes):
            slab[start + i] = piece[i * rows : (i + 1) * rows]
    at = planes * rows
    steps = LEAD + stored[1].shape[0]
    own_kinds, first_kinds = (pieces[0][at + row : at + row + 1] for row in (OWN_KINDS, FIRST_KINDS))
    beside_kinds = pieces[3][at + OWN_KINDS : at + OWN_KINDS + 1]
    kinds = scalars_of(first_kinds, steps)
    kinds += scalars_of(jnp.where((sec == 1) | (sec == 2), own_kinds, beside_kinds), steps)
    lead_kinds = lead[lead.shape[0] - 8 : lead.shape[0], :rows]
    half_out[pair * rows :] = jnp.where(sec == 0, lead_kinds, jnp.broadcast_to(own_kinds, lead_kinds.shape))
    width = 2 * planes * factor.shape[0]
    lines = [piece[at : at + width] for piece in pieces]
    lines.append(jnp.zeros((rows - width * len(pieces), rows), jnp.float32))
    scratch[...] = jnp.exp(-jnp.concatenate(lines, axis=0)).T
    spread_factor(reorder(scratch), factor, starts, width)
    total[...] = jnp.zeros(total.shape, jnp.float32)
    kept[...] = jnp.zeros(kept.shape, jnp.float32)

    def after(step, state):
        @pl.when(sec == step // steps)
        def _():
            j = step % steps
            source = stored[0][j] if j < LEAD else stored[1][j - LEAD]
            total[...] += state[reach : reach + planes] * source
            if j + 1 == steps:
                kept[...] = state[reach : reach + planes]

    run_steps(kinds, taps, weights, reach, slab, other, first, second, factor, 0, after)
    state = (slab, other)[reach % 2]
    middle[...] = state[reach : reach + planes]
    for i in range(pair):
        half_out[i * rows : (i + 1) * rows] = state[reach + pair * odd + i]


def late_kernel(blocks, last, taps, weights, middle, *refs):
    pieces, refs = refs[: 2 * len(blocks)], refs[2 * len(blocks) :]
    factor, kept, total_in, total_beside, series, stored = refs[0], refs[1], refs[2], refs[3], refs[4:6], refs[6:8]
    handoff, share, to_pair, to_across, to_corner = refs[8:13]
    slab, other, first, second, scratch, total, saved, whole = refs[13:]
    sec, odd = position()
    planes, rows = middle.shape[:2]
    pair = planes // 2
    reach = (slab.shape[0] - planes) // 2
    begun = (factor.shape[1] - planes) // 2
    even, uneven = (jnp.where(odd == core, pieces[0][pair * rows :], pieces[len(blocks)][pair * rows :]) for core in (0, 1))
    kinds = scalars_of(jnp.where(sec < 2, even, uneven)[:1], reach)
    slab[reach : reach + planes] = middle[...]
    for piece, start in zip(pieces, places(odd, planes, reach, blocks)):
        for i in range(pair):
            slab[start + i] = piece[i * rows : (i + 1) * rows]
    total[...] = jnp.zeros(total.shape, jnp.float32)

    @pl.when(sec == 0)
    def _():
        total[...] = total_in[...] + total_beside[...]

    saved[...] = kept[...]

    def lead_plane(i):
        return series[0][i * rows // 2 : (i + 1) * rows // 2]

    def after(step, state):
        @pl.when(sec == 0)
        def _():
            for i in range(planes):
                part = series[1][step - LEAD, i] if step >= LEAD else to_tile(lead_plane(step * planes + i), scratch)
                total[i] += state[reach + i] * part

        @pl.when(sec == last)
        def _():
            part = stored[0][step] if step < LEAD else stored[1][step - LEAD]
            total[...] += state[reach : reach + planes] * part

    run_steps(kinds, taps, weights, reach, slab, other, first, second, factor, begun - reach, after)
    state = (slab, other)[reach % 2]

    @pl.when(sec == last)
    def _():
        saved[...] = state[reach : reach + planes]

    orients = handoff.shape[1]
    count = orients // (last + 1)
    held = planes * count
    to_corner[...] = jnp.zeros(to_corner.shape, jnp.float32)
    for i in range(planes):
        handoff[i] = from_tile(saved[i], scratch)
        whole[...] = from_tile(total[i], scratch)
        for piece, who in (
            (share, sec),
            (to_pair, sec + 1 - 2 * odd),
            (to_across, jnp.where(sec == 0, 2, 1)),
            (to_corner, last - sec),
        ):
            piece[i * count : (i + 1) * count] = whole[pl.ds(pl.multiple_of(who * count, count), count)]
    for i in range(pair):
        to_across[held + i * orients : held + (i + 1) * orients] = from_tile(state[reach + pair * odd + i], scratch)

    @pl.when(sec == 1)
    def _():
        to_corner[...] = to_across[held:]


def finish_kernel(contour, handoff_in, share, to_pair, to_across, to_corner, handoff, density):
    sec = lax.axis_index("sec")
    planes, count = density.shape[:2]
    held = planes * count
    corner = jnp.where(sec == 2, 0.0, to_corner[:held])
    total = (share[...] + to_pair[...] + to_across[:held] + corner) / contour
    for i in range(planes):
        density[i] = total[i * count : (i + 1) * count]
    handoff[0] = handoff_in[...]

    @pl.when(sec == 2)
    def _():
        orients = handoff.shape[2]
        pair = planes // 2
        for i in range(pair):
            handoff[0, i] = to_across[held + i * orients : held + (i + 1) * orients]
            handoff[0, pair + i] = to_corner[i * orients : (i + 1) * orients]


def call(kernel, out_shape, scratch, operands, dtypes=None):
    return pl.pallas_call(
        kernel,
        in_specs=[IN_VMEM] * len(operands),
        out_specs=[IN_VMEM] * len(out_shape),
        out_shape=[jax.ShapeDtypeStruct(shape, (dtypes or {}).get(i, jnp.float32)) for i, shape in enumerate(out_shape)],
        scratch_shapes=scratch,
        compiler_params=pltpu.CompilerParams(vmem_limit_bytes=VMEM_BYTES),
    )(*operands)


def paired(incoming, backward, fields, block_types, axial_taps, lateral_taps, depth_taps, bend_diagonal, bend_coupling):
    n_sec, n_gx = lax.axis_size("sec"), lax.axis_size("gx")
    steps, planes, orients, cells = backward.shape
    pair = planes // 2
    reach = (TICKS - 1) * steps, steps
    near = (1, -1)
    rows = 2 * orients
    lanes = cells // 2
    last = n_sec - 1

    def send(array, by_sec, even=0, odd=0):
        by_sec = by_sec.items() if isinstance(by_sec, dict) else enumerate(by_sec)
        pairs = [
            (s * n_gx + g, t * n_gx + (g + (odd if s % 2 else even)) % n_gx) for s, t in by_sec for g in range(n_gx)
        ]
        return lax.ppermute(array, ("sec", "gx"), pairs)

    same, beside = (0, 1, 2, 3), (1, 0, 3, 2)
    full, lead, bundle = launch(
        incoming, backward, fields, block_types, axial_taps, lateral_taps, depth_taps, bend_diagonal, bend_coupling
    )
    moved = send(full, {0: 1, 1: 3})
    passed = send(moved, {3: 2})
    passed, lead = lax.optimization_barrier((passed, send(lead, {2: 0})))

    tile = pltpu.VMEM((rows, lanes), jnp.float32)
    packed = pltpu.VMEM((GROUP * rows, 2 * lanes), jnp.bfloat16)
    inner = pltpu.VMEM((planes, rows, lanes), jnp.float32)

    def work(extent):
        slab = pltpu.VMEM((planes + 2 * extent, rows, lanes), jnp.float32)
        return [slab, slab, packed, packed, tile]

    piece, taps, weights = call(
        pack_kernel,
        [(planes * rows + FIELD_ROWS, lanes), (TAP_ROWS, lanes), (2 * rows, 2 * lanes)],
        [tile],
        [bundle, moved, passed],
        {2: jnp.bfloat16},
    )
    own = [send(piece, same, shift, 2 * shift) for shift in near]
    backward, _ = lax.optimization_barrier((backward, piece))
    stored = call(turn_kernel, [(count, planes, rows, lanes) for count in (LEAD, steps - LEAD)], [tile], [backward])
    own[-1], *stored = lax.optimization_barrier((own[-1], *stored))
    swapped = [send(each, beside) for each in own]
    late_stored, *swapped = lax.optimization_barrier((stored[1], *swapped))
    late_last = send(late_stored, {2: 0})
    middle, piece, kept, total, factor = call(
        early_kernel,
        [(planes, rows, lanes), (pair * rows + 8, lanes), (planes, rows, lanes), (planes, rows, lanes)]
        + [(fields.shape[0], planes + 2 * reach[0], rows, lanes)],
        work(reach[0]),
        [taps, weights, lead, piece, *own, *swapped, *stored],
    )
    own = [send(piece, same, shift, shift) for shift in near]
    beside_total = send(total, beside)
    swapped = [send(each, beside) for each in own]
    held = planes * (orients // n_sec)
    handoff, share, to_pair, to_across, to_corner = call(
        functools.partial(late_kernel, tuple(-shift for shift in near), last),
        [(planes, orients, cells)]
        + [(held, cells)] * 2
        + [(held + pair * orients, cells), (pair * orients, cells)],
        work(reach[1]) + [inner, inner, pltpu.VMEM((orients, cells), jnp.float32)],
        [taps, weights, middle, *own, *swapped, factor, kept, total, beside_total]
        + [lead, late_last, *stored],
    )
    to_pair = send(to_pair, beside)
    to_across = send(to_across, (2, 0, 3, 1))
    to_corner = send(to_corner, (3, 2, 1, 0))
    handoff, density = call(
        functools.partial(finish_kernel, n_sec * steps),
        [(1,) + handoff.shape, (planes, orients // n_sec, cells)],
        [],
        [handoff, share, to_pair, to_across, to_corner],
    )
    return handoff, density


def pairs_fit(n_sec, planes, steps, orients, cells, kinds):
    return (
        n_sec == TICKS + 1 == 4
        and planes == steps
        and planes % 2 == 0
        and 2 * orients == 2 * CZ == cells // 2 == 128
        and 2 * kinds * planes <= OWN_KINDS and 10 * kinds * planes <= 2 * orients
        and GROUP < 2 * planes
    )


def solution(mesh):
    in_specs = (
        P("sec", "gx", None, None),
        P("sec", "gx", None, None),
        P(None, "gx", None),
        P("sec", None),
        P(),
        P(),
        P(),
        P(),
        P(),
    )
    out_specs = (P("sec", "gx", None, None), P("gx", "sec", None))

    def body(incoming, backward, fields, *rest):
        steps, planes, orients, cells = backward.shape
        fits = pairs_fit(mesh.shape["sec"], planes, steps, orients, cells, fields.shape[0])
        return (paired if fits else per_device)(incoming, backward, fields, *rest)

    return jax.shard_map(body, mesh=mesh, in_specs=in_specs, out_specs=out_specs, check_vma=False)
```

```python
import functools

import jax
import jax.numpy as jnp
from jax import lax
from jax.experimental import pallas as pl
from jax.experimental.pallas import tpu as pltpu
from jax.sharding import PartitionSpec as P

TICKS = 3
CZ = 64
GROUP = 6
FIELD_ROWS = 32
TAP_ROWS = 8
OWN_KINDS, FIRST_KINDS, ACROSS_KINDS = 24, 25, 26
LEAD = 1
VMEM_BYTES = 16 * 2**20
WHOLE_VMEM_BYTES = 62 * 2**20
IN_VMEM = pl.BlockSpec(memory_space=pltpu.VMEM)


def padded_2(block, sides, width):
    for axis, dim in sides:
        count = lax.axis_size(axis)
        forward = [(i, i + 1) for i in range(count - 1)]
        forward.append((count - 1, 0))
        backward = [(target, source) for source, target in forward]
        low = lax.ppermute(
            lax.slice_in_dim(block, block.shape[dim] - width, None, axis=dim), axis, forward
        )
        high = lax.ppermute(lax.slice_in_dim(block, 0, width, axis=dim), axis, backward)
        block = jnp.concatenate([low, block, high], axis=dim)
    return block


def from_behind(array, axis, by):
    length = lax.axis_size(axis)
    pairs = [(i, i + by) for i in range(length) if 0 <= i + by < length]
    return lax.ppermute(array, axis, pairs)


def boltzmann(fields, kinds):
    selector = kinds == jnp.arange(fields.shape[0], dtype=jnp.int32)
    chosen = jnp.sum(jnp.where(selector[:, None, None], fields, jnp.zeros_like(fields)), axis=0)
    return jnp.exp(-chosen)


def column(taps, which):
    return taps[which][None, :, None]


def advance_padded(padded, factor, axial_taps, lateral_taps, depth_taps, kernel):
    along_x = (
        column(axial_taps, 0) * padded[:-2]
        + column(axial_taps, 1) * padded[1:-1]
        + column(axial_taps, 2) * padded[2:]
    )
    along_y = (
        column(lateral_taps, 0) * jnp.roll(along_x, CZ, axis=2)
        + column(lateral_taps, 1) * along_x
        + column(lateral_taps, 2) * jnp.roll(along_x, -CZ, axis=2)
    )
    depth_pos = (jnp.arange(along_y.shape[2], dtype=jnp.int32) % CZ)[None, None, :]
    behind = jnp.where(
        depth_pos == 0, jnp.roll(along_y, -(CZ - 1), axis=2), jnp.roll(along_y, 1, axis=2)
    )
    ahead = jnp.where(
        depth_pos == CZ - 1, jnp.roll(along_y, CZ - 1, axis=2), jnp.roll(along_y, -1, axis=2)
    )
    along_z = (
        column(depth_taps, 0) * behind
        + column(depth_taps, 1) * along_y
        + column(depth_taps, 2) * ahead
    )
    blended = jnp.einsum(
        "uv,xvc->xuc",
        kernel,
        along_z,
        precision=lax.Precision.HIGHEST,
        preferred_element_type=jnp.float32,
    )
    return blended * factor[:, None, :]


def per_device(
    incoming,
    backward,
    fields,
    block_types,
    axial_taps,
    lateral_taps,
    depth_taps,
    bend_diagonal,
    bend_coupling,
):
    kernel = jnp.diag(bend_diagonal) + bend_coupling
    steps_each = block_types.shape[1]
    planes = incoming.shape[1]
    start = incoming[0]
    first_section = lax.axis_index("sec") == 0
    wide_fields = padded_2(fields, (("gx", 1),), steps_each)
    factors = [boltzmann(wide_fields, block_types[0, position]) for position in range(steps_each)]
    current = start
    outgoing = start
    accumulated = jnp.zeros(start.shape, jnp.float32)
    for tick_index in range(TICKS):
        final_tick = tick_index + 1 == TICKS
        extended = padded_2(current, (("gx", 0),), steps_each)
        for position in range(steps_each):
            margin = steps_each - position - 1
            offset = steps_each - margin
            factor = factors[position][offset : offset + planes + 2 * margin]
            extended = advance_padded(
                extended, factor, axial_taps, lateral_taps, depth_taps, kernel
            )
            if final_tick:
                accumulated = accumulated + extended[margin : margin + planes] * backward[
                    position
                ].astype(jnp.float32)
        outgoing = extended
        if not final_tick:
            shifted = from_behind(outgoing, "sec", 1)
            current = jnp.where(first_section, start, shifted)
    reduced = lax.psum_scatter(accumulated, "sec", scatter_dimension=1, tiled=True)
    density = reduced / (lax.axis_size("sec") * steps_each)
    return (outgoing[None], density)


def to_tile(plane, scratch):
    half = plane.shape[1] // 2
    scratch[...] = jnp.concatenate([plane[:, :half], plane[:, half:]], axis=0).T
    return reorder(scratch)


def reorder(scratch):
    rows = scratch.shape[0]
    return jnp.concatenate(
        [scratch[pl.ds(yl * CZ + zl, 8, stride=8), :] for yl in range(rows // CZ) for zl in range(CZ // 8)], axis=0
    )


def from_tile(tile, scratch):
    rows = tile.shape[0]
    for yl in range(rows // CZ):
        for zl in range(CZ // 8):
            at = (yl * (CZ // 8) + zl) * 8
            scratch[pl.ds(yl * CZ + zl, 8, stride=8), :] = tile[at : at + 8]
    turned = scratch[...].T
    half = turned.shape[0] // 2
    return jnp.concatenate([turned[:half], turned[half:]], axis=1)


def stencil(behind, here, ahead, taps):
    a = here + taps[0] * behind + taps[1] * ahead
    low, high = a[:CZ], a[CZ:]
    low_turned = pltpu.roll(low, a.shape[1] // 2, 1)
    high_turned = pltpu.roll(high, a.shape[1] // 2, 1)
    out = []
    for b in (
        low + taps[2] * high_turned + taps[3] * high,
        high + taps[2] * low + taps[3] * low_turned,
    ):
        back = jnp.concatenate([pltpu.roll(b[-8:], 1, 0), b[:-8]], axis=0)
        front = jnp.concatenate([b[8:], pltpu.roll(b[:8], 7, 0)], axis=0)
        out.append(b + taps[4] * back + taps[5] * front)
    return jnp.concatenate(out, axis=0)


def position():
    sec = lax.axis_index("sec")
    return sec, lax.rem(sec, 2)


def launch_kernel(*refs):
    sources, (lead, bundle) = refs[:9], refs[9:11]
    scratch, copies, sems = refs[11], refs[12:21], refs[21]
    moves = [
        pltpu.make_async_copy(source.at[pl.ds(0, copy.shape[0])], copy, sems.at[i])
        for i, (source, copy) in enumerate(zip(sources, copies))
    ]
    for move in moves:
        move.start()
    incoming, stored, fields, kinds, axial, lateral, depth, diagonal, coupling = copies
    for move in moves[2:]:
        move.wait()
    rows = scratch.shape[0]
    orients = rows // 2
    ratios = [each[w : w + 1] / each[1:2] for each in (axial, lateral, depth) for w in (0, 2)]
    for i, ratio in enumerate(ratios + ratios[:2]):
        bundle[i : i + 1] = jnp.concatenate([ratio, ratio], axis=1)
    square = (orients, orients)
    same = lax.broadcasted_iota(jnp.int32, square, 0) == lax.broadcasted_iota(jnp.int32, square, 1)
    kernel = jnp.where(same, diagonal[...], 0.0) + coupling[...]
    kernel = kernel * (axial[1:2] * lateral[1:2] * depth[1:2])
    upper = jnp.concatenate([kernel, jnp.zeros_like(kernel)], axis=1)
    bundle[TAP_ROWS : TAP_ROWS + rows] = jnp.concatenate([upper, pltpu.roll(upper, orients, 1)], axis=0).T
    line = kinds[...].astype(jnp.float32)
    line = jnp.concatenate([line, jnp.zeros((1, rows - line.shape[1]), jnp.float32)], axis=1)
    types = line
    planes = incoming.shape[1]
    at = TAP_ROWS + rows
    bundle[at : at + FIELD_ROWS] = jnp.zeros((FIELD_ROWS, rows), jnp.float32)
    for kind in range(fields.shape[0]):
        for i in range(planes):
            line = fields[kind, i : i + 1, :]
            here = at + (kind * planes + i) * 2
            bundle[here : here + 1] = line[:, :rows]
            bundle[here + 1 : here + 2] = line[:, rows:]
    bundle[at + OWN_KINDS : at + OWN_KINDS + 1] = types
    moves[0].wait()
    for i in range(planes):
        here = at + FIELD_ROWS + i * rows
        bundle[here : here + rows] = to_tile(incoming[0, i], scratch)
    moves[1].wait()
    for step in range(LEAD):
        for i in range(planes):
            here = (step * planes + i) * orients
            lead[here : here + orients] = stored[step, i].astype(jnp.float32)


def launch(incoming, backward, fields, kinds, axial, lateral, depth, diagonal, coupling):
    planes, orients, cells = backward.shape[1:]
    rows = 2 * orients
    operands = [incoming, backward, fields, kinds, axial, lateral, depth, diagonal.reshape(1, -1), coupling]
    shapes = [(LEAD * planes * orients, cells), (TAP_ROWS + rows + FIELD_ROWS + planes * rows, rows)]
    taken = [(LEAD,) + each.shape[1:] if i == 1 else each.shape for i, each in enumerate(operands)]
    return pl.pallas_call(
        launch_kernel,
        in_specs=[pl.BlockSpec(memory_space=pltpu.HBM)] * len(operands),
        out_specs=[IN_VMEM] * len(shapes),
        out_shape=[jax.ShapeDtypeStruct(shape, jnp.float32) for shape in shapes],
        scratch_shapes=[pltpu.VMEM((rows, rows), jnp.float32)]
        + [pltpu.VMEM(shape, each.dtype) for shape, each in zip(taken, operands)]
        + [pltpu.SemaphoreType.DMA((len(operands),))],
        compiler_params=pltpu.CompilerParams(vmem_limit_bytes=WHOLE_VMEM_BYTES),
    )(*operands)


def turn_kernel(backward, lead, early, late, out, scratch):
    orients = scratch.shape[0] // 2
    for target, begin in ((early, 0), (late, LEAD)):
        for step in range(target.shape[0]):
            for i in range(target.shape[1]):
                target[step, i] = to_tile(backward[begin + step, i].astype(jnp.float32), scratch)
    for step in range(out.shape[0]):
        for i in range(out.shape[1]):
            here = (step * out.shape[1] + i) * orients
            out[step, i] = to_tile(lead[here : here + orients], scratch)


def unpack_kernel(bundle, out, taps, weights):
    rows = taps.shape[1]
    taps[...] = bundle[:TAP_ROWS]
    twice = bundle[TAP_ROWS : TAP_ROWS + rows]
    coarse = twice.astype(jnp.bfloat16)
    fine = (twice - coarse.astype(jnp.float32)).astype(jnp.bfloat16)
    weights[...] = jnp.concatenate(
        [jnp.concatenate([coarse, fine], axis=1), jnp.concatenate([coarse, jnp.zeros_like(fine)], axis=1)], axis=0
    )
    at = out.shape[0] - FIELD_ROWS
    lines = TAP_ROWS + rows
    out[at:] = bundle[lines : lines + FIELD_ROWS]
    out[:at] = bundle[lines + FIELD_ROWS :]


def pack_kernel(base, moved, passed, types, out, scratch):
    sec, odd = position()
    rows = scratch.shape[0]
    at = out.shape[0] - FIELD_ROWS
    out[at:] = base[at:]
    out[at + FIRST_KINDS : at + FIRST_KINDS + 1] = jnp.where(
        sec == 0, base[at + OWN_KINDS : at + OWN_KINDS + 1], types[:1]
    )
    out[at + ACROSS_KINDS : at + ACROSS_KINDS + 1] = types[:1]

    @pl.when(sec == 0)
    def _():
        out[:at] = base[:at]

    def fill(source):
        for i in range(source.shape[0]):
            out[i * rows : (i + 1) * rows] = to_tile(source[i], scratch)

    pl.when(odd == 1)(lambda: fill(moved))
    pl.when((sec > 0) & (odd == 0))(lambda: fill(passed))


def scalars_of(row, count):
    lane = lax.broadcasted_iota(jnp.int32, row.shape, 1)
    return [jnp.sum(jnp.where(lane == i, row, 0.0)).astype(jnp.int32) for i in range(count)]


def places(odd, planes, reach, blocks):
    return [reach + block * planes + planes // 2 * core for core in (odd, 1 - odd) for block in blocks]


def run_steps(kinds, taps, weights, count, slab, other, first, second, factor, offset, after):
    tap = [taps[i : i + 1, :] for i in range(6)]
    extent, rows, lanes = slab.shape
    buffers = (slab, other)

    def blend(source, at, packed):
        for i in range(GROUP):
            e = stencil(source[at + i - 1], source[at + i], source[at + i + 1], tap)
            coarse = e.astype(jnp.bfloat16)
            packed[i * rows : (i + 1) * rows, :lanes] = coarse
            packed[i * rows : (i + 1) * rows, lanes:] = (e - coarse.astype(jnp.float32)).astype(jnp.bfloat16)

    def mix(target, at, packed, kind):
        product = jnp.dot(packed[...], weights[...], preferred_element_type=jnp.float32)
        product = product[:, :lanes] + product[:, lanes:]
        for i in range(GROUP):
            target[at + i] = product[i * rows : (i + 1) * rows] * factor[kind, at + i + offset]

    for step in range(count):
        source, target = buffers[step % 2], buffers[1 - step % 2]
        begin, width = step + 1, extent - 2 * step - 2
        groups = -(-width // GROUP)
        kind = kinds[step]

        def at(i, begin=begin, width=width):
            return jnp.minimum(begin + i * GROUP, begin + width - GROUP)

        blend(source, at(0), first)
        if groups > 1:

            def body(i, carry, source=source, target=target, at=at, kind=kind):
                blend(source, at(2 * i + 1), second)
                mix(target, at(2 * i), first, kind)
                blend(source, at(2 * i + 2), first)
                mix(target, at(2 * i + 1), second, kind)
                return carry

            lax.fori_loop(0, (groups - 1) // 2, body, 0)
        if groups % 2 == 0:
            blend(source, at(groups - 1), second)
            mix(target, at(groups - 2), first, kind)
            mix(target, at(groups - 1), second, kind)
        else:
            mix(target, at(groups - 1), first, kind)
        after(step, target)


def spread_factor(columns, factor, starts, width):
    rows, lanes = factor.shape[2:]
    pair = factor.shape[1] // len(starts)
    right = (lax.broadcasted_iota(jnp.int32, (rows, lanes), 1) >= lanes // 2).astype(jnp.int32)
    for piece, start in enumerate(starts):
        for kind in range(factor.shape[0]):
            for i in range(pair):
                at = piece * width + (kind * pair + i) * 2
                factor[kind, start + i] = jnp.take_along_axis(columns, right + at, axis=1, mode="promise_in_bounds")


def early_kernel(taps, weights, *refs):
    pieces, stored, (middle, half_out, kept, total, factor) = refs[:5], refs[5:7], refs[7:12]
    slab, other, first, second, scratch = refs[12:]
    sec, odd = position()
    planes, rows = middle.shape[:2]
    pair = planes // 2
    reach = (slab.shape[0] - planes) // 2
    mine, others = (planes * (1 + core) for core in (odd, 1 - odd))
    starts = [reach, reach - mine, reach + mine, reach - others, reach + others]
    for piece, start in zip(pieces, starts):
        for i in range(planes):
            slab[start + i] = piece[i * rows : (i + 1) * rows]
    at = planes * rows
    steps = LEAD + stored[1].shape[0]
    own_kinds, first_kinds, across_kinds = (
        pieces[0][at + row : at + row + 1] for row in (OWN_KINDS, FIRST_KINDS, ACROSS_KINDS)
    )
    beside_kinds, beside_first = (pieces[3][at + row : at + row + 1] for row in (OWN_KINDS, FIRST_KINDS))
    kinds = scalars_of(jnp.where((sec == 1) | (sec == 2), beside_first, first_kinds), steps)
    kinds += scalars_of(jnp.where((sec == 1) | (sec == 2), own_kinds, beside_kinds), steps)
    last_kinds = jnp.where(sec == 0, across_kinds, own_kinds)
    half_out[pair * rows :] = jnp.broadcast_to(last_kinds, (8, rows))
    width = 2 * planes * factor.shape[0]
    lines = [piece[at : at + width] for piece in pieces]
    lines.append(jnp.zeros((rows - width * len(pieces), rows), jnp.float32))
    scratch[...] = jnp.exp(-jnp.concatenate(lines, axis=0)).T
    spread_factor(reorder(scratch), factor, starts, width)
    total[...] = jnp.zeros(total.shape, jnp.float32)
    kept[...] = jnp.zeros(kept.shape, jnp.float32)

    def after(step, state):
        @pl.when(sec == step // steps)
        def _():
            j = step % steps
            source = stored[0][j] if j < LEAD else stored[1][j - LEAD]
            total[...] += state[reach : reach + planes] * source
            if j + 1 == steps:
                kept[...] = state[reach : reach + planes]

    run_steps(kinds, taps, weights, reach, slab, other, first, second, factor, 0, after)
    state = (slab, other)[reach % 2]
    middle[...] = state[reach : reach + planes]
    for i in range(pair):
        half_out[i * rows : (i + 1) * rows] = state[reach + pair * odd + i]


def late_kernel(blocks, last, taps, weights, middle, *refs):
    pieces, refs = refs[: 2 * len(blocks)], refs[2 * len(blocks) :]
    factor, kept, total_in, total_beside, series, stored = refs[0], refs[1], refs[2], refs[3], refs[4:6], refs[6:8]
    handoff, share, to_pair, to_across, to_corner = refs[8:13]
    slab, other, first, second, scratch, total, saved, whole = refs[13:]
    sec, odd = position()
    planes, rows = middle.shape[:2]
    pair = planes // 2
    reach = (slab.shape[0] - planes) // 2
    begun = (factor.shape[1] - planes) // 2
    even, uneven = (jnp.where(odd == core, pieces[0][pair * rows :], pieces[len(blocks)][pair * rows :]) for core in (0, 1))
    kinds = scalars_of(jnp.where(sec < 2, even, uneven)[:1], reach)
    slab[reach : reach + planes] = middle[...]
    for piece, start in zip(pieces, places(odd, planes, reach, blocks)):
        for i in range(pair):
            slab[start + i] = piece[i * rows : (i + 1) * rows]
    total[...] = jnp.zeros(total.shape, jnp.float32)

    @pl.when(sec == 0)
    def _():
        total[...] = total_in[...] + total_beside[...]

    saved[...] = kept[...]

    def after(step, state):
        for where, source in ((sec == 0, series), (sec == last, stored)):

            @pl.when(where)
            def _(source=source):
                part = source[0][step] if step < LEAD else source[1][step - LEAD]
                total[...] += state[reach : reach + planes] * part

    run_steps(kinds, taps, weights, reach, slab, other, first, second, factor, begun - reach, after)
    state = (slab, other)[reach % 2]

    @pl.when(sec == last)
    def _():
        saved[...] = state[reach : reach + planes]

    orients = handoff.shape[1]
    count = orients // (last + 1)
    held = planes * count
    to_corner[...] = jnp.zeros(to_corner.shape, jnp.float32)
    for i in range(planes):
        handoff[i] = from_tile(saved[i], scratch)
        whole[...] = from_tile(total[i], scratch)
        for piece, who in (
            (share, sec),
            (to_pair, sec + 1 - 2 * odd),
            (to_across, jnp.where(sec == 0, 2, 1)),
            (to_corner, last - sec),
        ):
            piece[i * count : (i + 1) * count] = whole[pl.ds(pl.multiple_of(who * count, count), count)]
    for i in range(pair):
        to_across[held + i * orients : held + (i + 1) * orients] = from_tile(state[reach + pair * odd + i], scratch)

    @pl.when(sec == 1)
    def _():
        to_corner[...] = to_across[held:]


def finish_kernel(contour, handoff_in, share, to_pair, to_across, to_corner, handoff, density):
    sec = lax.axis_index("sec")
    planes, count = density.shape[:2]
    held = planes * count
    corner = jnp.where(sec == 2, 0.0, to_corner[:held])
    total = (share[...] + to_pair[...] + to_across[:held] + corner) / contour
    for i in range(planes):
        density[i] = total[i * count : (i + 1) * count]
    handoff[0] = handoff_in[...]

    @pl.when(sec == 2)
    def _():
        orients = handoff.shape[2]
        pair = planes // 2
        for i in range(pair):
            handoff[0, i] = to_across[held + i * orients : held + (i + 1) * orients]
            handoff[0, pair + i] = to_corner[i * orients : (i + 1) * orients]


def call(kernel, out_shape, scratch, operands, dtypes=None):
    return pl.pallas_call(
        kernel,
        in_specs=[IN_VMEM] * len(operands),
        out_specs=[IN_VMEM] * len(out_shape),
        out_shape=[jax.ShapeDtypeStruct(shape, (dtypes or {}).get(i, jnp.float32)) for i, shape in enumerate(out_shape)],
        scratch_shapes=scratch,
        compiler_params=pltpu.CompilerParams(vmem_limit_bytes=VMEM_BYTES),
    )(*operands)


def paired(incoming, backward, fields, block_types, axial_taps, lateral_taps, depth_taps, bend_diagonal, bend_coupling):
    n_sec, n_gx = lax.axis_size("sec"), lax.axis_size("gx")
    steps, planes, orients, cells = backward.shape
    pair = planes // 2
    reach = (TICKS - 1) * steps, steps
    near = (1, -1)
    rows = 2 * orients
    lanes = cells // 2
    last = n_sec - 1

    def send(array, by_sec, even=0, odd=0):
        by_sec = by_sec.items() if isinstance(by_sec, dict) else enumerate(by_sec)
        pairs = [
            (s * n_gx + g, t * n_gx + (g + (odd if s % 2 else even)) % n_gx) for s, t in by_sec for g in range(n_gx)
        ]
        return lax.ppermute(array, ("sec", "gx"), pairs)

    same, beside = (0, 1, 2, 3), (1, 0, 3, 2)
    moved = send(incoming[0], {0: 1, 1: 3})
    lead, bundle = launch(
        incoming, backward, fields, block_types, axial_taps, lateral_taps, depth_taps, bend_diagonal, bend_coupling
    )
    types = jnp.pad(block_types.astype(jnp.float32), ((0, 7), (0, lanes - steps)))
    types = send(types, {1: 3, 2: 0})
    lead = send(lead, {2: 0})
    size = planes * rows + FIELD_ROWS
    base, taps, weights = call(
        unpack_kernel, [(size, lanes), (TAP_ROWS, lanes), (2 * rows, 2 * lanes)], [], [bundle], {2: jnp.bfloat16}
    )
    moved, base, types = lax.optimization_barrier((moved, base, types))
    passed = send(moved, {3: 2})

    tile = pltpu.VMEM((rows, lanes), jnp.float32)
    packed = pltpu.VMEM((GROUP * rows, 2 * lanes), jnp.bfloat16)
    inner = pltpu.VMEM((planes, rows, lanes), jnp.float32)

    def work(extent):
        slab = pltpu.VMEM((planes + 2 * extent, rows, lanes), jnp.float32)
        return [slab, slab, packed, packed, tile]

    (piece,) = call(pack_kernel, [(size, lanes)], [tile], [base, moved, passed, types])
    own = [send(piece, same, shift, 2 * shift) for shift in near]
    backward, _ = lax.optimization_barrier((backward, piece))
    *stored, lead = call(
        turn_kernel,
        [(count, planes, rows, lanes) for count in (LEAD, steps - LEAD, LEAD)],
        [tile],
        [backward, lead],
    )
    own[-1], *stored = lax.optimization_barrier((own[-1], *stored))
    swapped = [send(each, beside) for each in own]
    late_stored, *swapped = lax.optimization_barrier((stored[1], *swapped))
    late_last = send(late_stored, {2: 0})
    middle, piece, kept, total, factor = call(
        early_kernel,
        [(planes, rows, lanes), (pair * rows + 8, lanes), (planes, rows, lanes), (planes, rows, lanes)]
        + [(fields.shape[0], planes + 2 * reach[0], rows, lanes)],
        work(reach[0]),
        [taps, weights, piece, *own, *swapped, *stored],
    )
    own = [send(piece, same, shift, shift) for shift in near]
    beside_total = send(total, beside)
    swapped = [send(each, beside) for each in own]
    held = planes * (orients // n_sec)
    handoff, share, to_pair, to_across, to_corner = call(
        functools.partial(late_kernel, tuple(-shift for shift in near), last),
        [(planes, orients, cells)]
        + [(held, cells)] * 2
        + [(held + pair * orients, cells), (pair * orients, cells)],
        work(reach[1]) + [inner, inner, pltpu.VMEM((orients, cells), jnp.float32)],
        [taps, weights, middle, *own, *swapped, factor, kept, total, beside_total]
        + [lead, late_last, *stored],
    )
    to_pair = send(to_pair, beside)
    to_across = send(to_across, (2, 0, 3, 1))
    to_corner = send(to_corner, (3, 2, 1, 0))
    handoff, density = call(
        functools.partial(finish_kernel, n_sec * steps),
        [(1,) + handoff.shape, (planes, orients // n_sec, cells)],
        [],
        [handoff, share, to_pair, to_across, to_corner],
    )
    return handoff, density


def pairs_fit(n_sec, planes, steps, orients, cells, kinds):
    return (
        n_sec == TICKS + 1 == 4
        and planes == steps
        and planes % 2 == 0
        and 2 * orients == 2 * CZ == cells // 2 == 128
        and 2 * kinds * planes <= OWN_KINDS and 10 * kinds * planes <= 2 * orients
        and GROUP < 2 * planes
    )


def solution(mesh):
    in_specs = (
        P("sec", "gx", None, None),
        P("sec", "gx", None, None),
        P(None, "gx", None),
        P("sec", None),
        P(),
        P(),
        P(),
        P(),
        P(),
    )
    out_specs = (P("sec", "gx", None, None), P("gx", "sec", None))

    def body(incoming, backward, fields, *rest):
        steps, planes, orients, cells = backward.shape
        fits = pairs_fit(mesh.shape["sec"], planes, steps, orients, cells, fields.shape[0])
        return (paired if fits else per_device)(incoming, backward, fields, *rest)

    return jax.shard_map(body, mesh=mesh, in_specs=in_specs, out_specs=out_specs, check_vma=False)
```

```python
import functools

import jax
import jax.numpy as jnp
from jax import lax
from jax.experimental import pallas as pl
from jax.experimental.pallas import tpu as pltpu
from jax.sharding import PartitionSpec as P

TICKS = 3
CZ = 64
GROUP = 6
FIELD_ROWS = 32
TAP_ROWS = 8
OWN_KINDS, FIRST_KINDS = 24, 25
VMEM_BYTES = 16 * 2**20
WHOLE_VMEM_BYTES = 62 * 2**20
IN_VMEM = pl.BlockSpec(memory_space=pltpu.VMEM)


def padded_2(block, sides, width):
    for axis, dim in sides:
        count = lax.axis_size(axis)
        forward = [(i, i + 1) for i in range(count - 1)]
        forward.append((count - 1, 0))
        backward = [(target, source) for source, target in forward]
        low = lax.ppermute(
            lax.slice_in_dim(block, block.shape[dim] - width, None, axis=dim), axis, forward
        )
        high = lax.ppermute(lax.slice_in_dim(block, 0, width, axis=dim), axis, backward)
        block = jnp.concatenate([low, block, high], axis=dim)
    return block


def from_behind(array, axis, by):
    length = lax.axis_size(axis)
    pairs = [(i, i + by) for i in range(length) if 0 <= i + by < length]
    return lax.ppermute(array, axis, pairs)


def boltzmann(fields, kinds):
    selector = kinds == jnp.arange(fields.shape[0], dtype=jnp.int32)
    chosen = jnp.sum(jnp.where(selector[:, None, None], fields, jnp.zeros_like(fields)), axis=0)
    return jnp.exp(-chosen)


def column(taps, which):
    return taps[which][None, :, None]


def advance_padded(padded, factor, axial_taps, lateral_taps, depth_taps, kernel):
    along_x = (
        column(axial_taps, 0) * padded[:-2]
        + column(axial_taps, 1) * padded[1:-1]
        + column(axial_taps, 2) * padded[2:]
    )
    along_y = (
        column(lateral_taps, 0) * jnp.roll(along_x, CZ, axis=2)
        + column(lateral_taps, 1) * along_x
        + column(lateral_taps, 2) * jnp.roll(along_x, -CZ, axis=2)
    )
    depth_pos = (jnp.arange(along_y.shape[2], dtype=jnp.int32) % CZ)[None, None, :]
    behind = jnp.where(
        depth_pos == 0, jnp.roll(along_y, -(CZ - 1), axis=2), jnp.roll(along_y, 1, axis=2)
    )
    ahead = jnp.where(
        depth_pos == CZ - 1, jnp.roll(along_y, CZ - 1, axis=2), jnp.roll(along_y, -1, axis=2)
    )
    along_z = (
        column(depth_taps, 0) * behind
        + column(depth_taps, 1) * along_y
        + column(depth_taps, 2) * ahead
    )
    blended = jnp.einsum(
        "uv,xvc->xuc",
        kernel,
        along_z,
        precision=lax.Precision.HIGHEST,
        preferred_element_type=jnp.float32,
    )
    return blended * factor[:, None, :]


def per_device(
    incoming,
    backward,
    fields,
    block_types,
    axial_taps,
    lateral_taps,
    depth_taps,
    bend_diagonal,
    bend_coupling,
):
    kernel = jnp.diag(bend_diagonal) + bend_coupling
    steps_each = block_types.shape[1]
    planes = incoming.shape[1]
    start = incoming[0]
    first_section = lax.axis_index("sec") == 0
    wide_fields = padded_2(fields, (("gx", 1),), steps_each)
    factors = [boltzmann(wide_fields, block_types[0, position]) for position in range(steps_each)]
    current = start
    outgoing = start
    accumulated = jnp.zeros(start.shape, jnp.float32)
    for tick_index in range(TICKS):
        final_tick = tick_index + 1 == TICKS
        extended = padded_2(current, (("gx", 0),), steps_each)
        for position in range(steps_each):
            margin = steps_each - position - 1
            offset = steps_each - margin
            factor = factors[position][offset : offset + planes + 2 * margin]
            extended = advance_padded(
                extended, factor, axial_taps, lateral_taps, depth_taps, kernel
            )
            if final_tick:
                accumulated = accumulated + extended[margin : margin + planes] * backward[
                    position
                ].astype(jnp.float32)
        outgoing = extended
        if not final_tick:
            shifted = from_behind(outgoing, "sec", 1)
            current = jnp.where(first_section, start, shifted)
    reduced = lax.psum_scatter(accumulated, "sec", scatter_dimension=1, tiled=True)
    density = reduced / (lax.axis_size("sec") * steps_each)
    return (outgoing[None], density)


def to_tile(plane, scratch):
    half = plane.shape[1] // 2
    scratch[...] = jnp.concatenate([plane[:, :half], plane[:, half:]], axis=0).T
    return reorder(scratch)


def reorder(scratch):
    rows = scratch.shape[0]
    return jnp.concatenate(
        [scratch[pl.ds(yl * CZ + zl, 8, stride=8), :] for yl in range(rows // CZ) for zl in range(CZ // 8)], axis=0
    )


def from_tile(tile, scratch):
    rows = tile.shape[0]
    for yl in range(rows // CZ):
        for zl in range(CZ // 8):
            at = (yl * (CZ // 8) + zl) * 8
            scratch[pl.ds(yl * CZ + zl, 8, stride=8), :] = tile[at : at + 8]
    turned = scratch[...].T
    half = turned.shape[0] // 2
    return jnp.concatenate([turned[:half], turned[half:]], axis=1)


def stencil(behind, here, ahead, taps):
    a = here + taps[0] * behind + taps[1] * ahead
    low, high = a[:CZ], a[CZ:]
    low_turned = pltpu.roll(low, a.shape[1] // 2, 1)
    high_turned = pltpu.roll(high, a.shape[1] // 2, 1)
    out = []
    for b in (
        low + taps[2] * high_turned + taps[3] * high,
        high + taps[2] * low + taps[3] * low_turned,
    ):
        back = jnp.concatenate([pltpu.roll(b[-8:], 1, 0), b[:-8]], axis=0)
        front = jnp.concatenate([b[8:], pltpu.roll(b[:8], 7, 0)], axis=0)
        out.append(b + taps[4] * back + taps[5] * front)
    return jnp.concatenate(out, axis=0)


def position():
    sec = lax.axis_index("sec")
    return sec, lax.rem(sec, 2)


def launch_kernel(*refs):
    sources, bundle, scratch, copies, sems = refs[:8], refs[8], refs[9], refs[10:18], refs[18]
    moves = [pltpu.make_async_copy(s, c, sems.at[i]) for i, (s, c) in enumerate(zip(sources, copies))]
    for move in moves:
        move.start()
    incoming, fields, kinds, axial, lateral, depth, diagonal, coupling = copies
    for move in moves[1:]:
        move.wait()
    rows = scratch.shape[0]
    orients = rows // 2
    ratios = [each[w : w + 1] / each[1:2] for each in (axial, lateral, depth) for w in (0, 2)]
    for i, ratio in enumerate(ratios + ratios[:2]):
        bundle[i : i + 1] = jnp.concatenate([ratio, ratio], axis=1)
    square = (orients, orients)
    same = lax.broadcasted_iota(jnp.int32, square, 0) == lax.broadcasted_iota(jnp.int32, square, 1)
    kernel = jnp.where(same, diagonal[...], 0.0) + coupling[...]
    kernel = kernel * (axial[1:2] * lateral[1:2] * depth[1:2])
    upper = jnp.concatenate([kernel, jnp.zeros_like(kernel)], axis=1)
    bundle[TAP_ROWS : TAP_ROWS + rows] = jnp.concatenate([upper, pltpu.roll(upper, orients, 1)], axis=0).T
    line = kinds[...].astype(jnp.float32)
    line = jnp.concatenate([line, jnp.zeros((1, rows - line.shape[1]), jnp.float32)], axis=1)
    types = line
    planes = incoming.shape[1]
    at = TAP_ROWS + rows
    bundle[at : at + FIELD_ROWS] = jnp.zeros((FIELD_ROWS, rows), jnp.float32)
    for kind in range(fields.shape[0]):
        for i in range(planes):
            line = fields[kind, i : i + 1, :]
            here = at + (kind * planes + i) * 2
            bundle[here : here + 1] = line[:, :rows]
            bundle[here + 1 : here + 2] = line[:, rows:]
    bundle[at + OWN_KINDS : at + OWN_KINDS + 1] = types
    moves[0].wait()
    for i in range(planes):
        here = at + FIELD_ROWS + i * rows
        bundle[here : here + rows] = to_tile(incoming[0, i], scratch)


def launch(incoming, fields, kinds, axial, lateral, depth, diagonal, coupling):
    planes, orients, cells = incoming.shape[1:]
    rows = 2 * orients
    operands = [incoming, fields, kinds, axial, lateral, depth, diagonal.reshape(1, -1), coupling]
    return pl.pallas_call(
        launch_kernel,
        in_specs=[pl.BlockSpec(memory_space=pltpu.HBM)] * len(operands),
        out_specs=IN_VMEM,
        out_shape=jax.ShapeDtypeStruct((TAP_ROWS + rows + FIELD_ROWS + planes * rows, rows), jnp.float32),
        scratch_shapes=[pltpu.VMEM((rows, rows), jnp.float32)]
        + [pltpu.VMEM(each.shape, each.dtype) for each in operands]
        + [pltpu.SemaphoreType.DMA((len(operands),))],
        compiler_params=pltpu.CompilerParams(vmem_limit_bytes=WHOLE_VMEM_BYTES),
    )(*operands)


def turn_kernel(backward, out, scratch):
    for step in range(out.shape[0]):
        for i in range(out.shape[1]):
            out[step, i] = to_tile(backward[step, i].astype(jnp.float32), scratch)


def unpack_kernel(bundle, out, taps, weights):
    rows = taps.shape[1]
    taps[...] = bundle[:TAP_ROWS]
    twice = bundle[TAP_ROWS : TAP_ROWS + rows]
    coarse = twice.astype(jnp.bfloat16)
    fine = (twice - coarse.astype(jnp.float32)).astype(jnp.bfloat16)
    weights[...] = jnp.concatenate(
        [jnp.concatenate([coarse, fine], axis=1), jnp.concatenate([coarse, jnp.zeros_like(fine)], axis=1)], axis=0
    )
    at = out.shape[0] - FIELD_ROWS
    lines = TAP_ROWS + rows
    out[at:] = bundle[lines : lines + FIELD_ROWS]
    out[:at] = bundle[lines + FIELD_ROWS :]


def pack_kernel(base, moved, passed, types, out, scratch):
    sec, odd = position()
    rows = scratch.shape[0]
    at = out.shape[0] - FIELD_ROWS
    out[at:] = base[at:]
    out[at + FIRST_KINDS : at + FIRST_KINDS + 1] = jnp.where(
        sec == 0, base[at + OWN_KINDS : at + OWN_KINDS + 1], types[:1]
    )

    @pl.when(sec == 0)
    def _():
        out[:at] = base[:at]

    def fill(source):
        for i in range(source.shape[0]):
            out[i * rows : (i + 1) * rows] = to_tile(source[i], scratch)

    pl.when(odd == 1)(lambda: fill(moved))
    pl.when((sec > 0) & (odd == 0))(lambda: fill(passed))


def scalars_of(row, count):
    lane = lax.broadcasted_iota(jnp.int32, row.shape, 1)
    return [jnp.sum(jnp.where(lane == i, row, 0.0)).astype(jnp.int32) for i in range(count)]


def places(odd, planes, reach, blocks):
    return [reach + block * planes + planes // 2 * core for core in (odd, 1 - odd) for block in blocks]


def run_steps(kinds, taps, weights, count, slab, other, first, second, factor, offset, after):
    tap = [taps[i : i + 1, :] for i in range(6)]
    extent, rows, lanes = slab.shape
    buffers = (slab, other)

    def blend(source, at, packed):
        for i in range(GROUP):
            e = stencil(source[at + i - 1], source[at + i], source[at + i + 1], tap)
            coarse = e.astype(jnp.bfloat16)
            packed[i * rows : (i + 1) * rows, :lanes] = coarse
            packed[i * rows : (i + 1) * rows, lanes:] = (e - coarse.astype(jnp.float32)).astype(jnp.bfloat16)

    def mix(target, at, packed, kind):
        product = jnp.dot(packed[...], weights[...], preferred_element_type=jnp.float32)
        product = product[:, :lanes] + product[:, lanes:]
        for i in range(GROUP):
            target[at + i] = product[i * rows : (i + 1) * rows] * factor[kind, at + i + offset]

    for step in range(count):
        source, target = buffers[step % 2], buffers[1 - step % 2]
        begin, width = step + 1, extent - 2 * step - 2
        groups = -(-width // GROUP)
        kind = kinds[step]

        def at(i, begin=begin, width=width):
            return jnp.minimum(begin + i * GROUP, begin + width - GROUP)

        blend(source, at(0), first)
        if groups > 1:

            def body(i, carry, source=source, target=target, at=at, kind=kind):
                blend(source, at(2 * i + 1), second)
                mix(target, at(2 * i), first, kind)
                blend(source, at(2 * i + 2), first)
                mix(target, at(2 * i + 1), second, kind)
                return carry

            lax.fori_loop(0, (groups - 1) // 2, body, 0)
        if groups % 2 == 0:
            blend(source, at(groups - 1), second)
            mix(target, at(groups - 2), first, kind)
            mix(target, at(groups - 1), second, kind)
        else:
            mix(target, at(groups - 1), first, kind)
        after(step, target)


def spread_factor(columns, factor, starts, width):
    rows, lanes = factor.shape[2:]
    pair = factor.shape[1] // len(starts)
    right = (lax.broadcasted_iota(jnp.int32, (rows, lanes), 1) >= lanes // 2).astype(jnp.int32)
    for piece, start in enumerate(starts):
        for kind in range(factor.shape[0]):
            for i in range(pair):
                at = piece * width + (kind * pair + i) * 2
                factor[kind, start + i] = jnp.take_along_axis(columns, right + at, axis=1, mode="promise_in_bounds")


def early_kernel(taps, weights, across, *refs):
    pieces, stored, (middle, half_out, kept, total, factor) = refs[:5], refs[5], refs[6:11]
    slab, other, first, second, scratch = refs[11:]
    sec, odd = position()
    planes, rows = middle.shape[:2]
    pair = planes // 2
    reach = (slab.shape[0] - planes) // 2
    mine, others = (planes * (1 + core) for core in (odd, 1 - odd))
    starts = [reach, reach - mine, reach + mine, reach - others, reach + others]
    for piece, start in zip(pieces, starts):
        for i in range(planes):
            slab[start + i] = piece[i * rows : (i + 1) * rows]
    at = planes * rows
    steps = stored.shape[0]
    own_kinds, first_kinds = (pieces[0][at + row : at + row + 1] for row in (OWN_KINDS, FIRST_KINDS))
    beside_kinds, beside_first = (pieces[3][at + row : at + row + 1] for row in (OWN_KINDS, FIRST_KINDS))
    kinds = scalars_of(jnp.where((sec == 1) | (sec == 2), beside_first, first_kinds), steps)
    kinds += scalars_of(jnp.where((sec == 1) | (sec == 2), own_kinds, beside_kinds), steps)
    last_kinds = jnp.where(sec == 0, across[:1], own_kinds)
    half_out[pair * rows :] = jnp.broadcast_to(last_kinds, (8, rows))
    width = 2 * planes * factor.shape[0]
    lines = [piece[at : at + width] for piece in pieces]
    lines.append(jnp.zeros((rows - width * len(pieces), rows), jnp.float32))
    scratch[...] = jnp.exp(-jnp.concatenate(lines, axis=0)).T
    spread_factor(reorder(scratch), factor, starts, width)
    total[...] = jnp.zeros(total.shape, jnp.float32)
    kept[...] = jnp.zeros(kept.shape, jnp.float32)

    def after(step, state):
        @pl.when(sec == step // steps)
        def _():
            total[...] += state[reach : reach + planes] * stored[step % steps]
            if (step + 1) % steps == 0:
                kept[...] = state[reach : reach + planes]

    run_steps(kinds, taps, weights, reach, slab, other, first, second, factor, 0, after)
    state = (slab, other)[reach % 2]
    middle[...] = state[reach : reach + planes]
    for i in range(pair):
        half_out[i * rows : (i + 1) * rows] = state[reach + pair * odd + i]


def late_kernel(blocks, last, taps, weights, middle, *refs):
    pieces, refs = refs[: 2 * len(blocks)], refs[2 * len(blocks) :]
    factor, kept, total_in, total_beside, series, stored = refs[:6]
    handoff, onward, share, to_pair, to_across, to_corner = refs[6:12]
    slab, other, first, second, scratch, total, whole = refs[12:]
    sec, odd = position()
    planes, rows = middle.shape[:2]
    pair = planes // 2
    reach = (slab.shape[0] - planes) // 2
    begun = (factor.shape[1] - planes) // 2
    even, uneven = (jnp.where(odd == core, pieces[0][pair * rows :], pieces[len(blocks)][pair * rows :]) for core in (0, 1))
    kinds = scalars_of(jnp.where(sec < 2, even, uneven)[:1], reach)
    slab[reach : reach + planes] = middle[...]
    for piece, start in zip(pieces, places(odd, planes, reach, blocks)):
        for i in range(pair):
            slab[start + i] = piece[i * rows : (i + 1) * rows]
    total[...] = jnp.zeros(total.shape, jnp.float32)

    @pl.when(sec == 0)
    def _():
        total[...] = total_in[...] + total_beside[...]

    def after(step, state):
        for where, source in ((sec == 0, series), (sec == last, stored)):

            @pl.when(where)
            def _(source=source):
                total[...] += state[reach : reach + planes] * source[step]

    run_steps(kinds, taps, weights, reach, slab, other, first, second, factor, begun - reach, after)
    state = (slab, other)[reach % 2]

    orients = handoff.shape[1]
    count = orients // (last + 1)
    for i in range(planes):
        onward[i] = from_tile(state[reach + i], scratch)

    @pl.when(sec < 2)
    def _():
        for i in range(planes):
            handoff[i] = from_tile(kept[i], scratch)

    @pl.when(sec >= 2)
    def _():
        handoff[...] = onward[...]

    for i in range(planes):
        whole[...] = from_tile(total[i], scratch)
        for piece, who in (
            (share, sec),
            (to_pair, sec + 1 - 2 * odd),
            (to_across, jnp.where(sec == 0, 2, 1)),
            (to_corner, last - sec),
        ):
            piece[i * count : (i + 1) * count] = whole[pl.ds(pl.multiple_of(who * count, count), count)]


def finish_kernel(contour, handoff_in, onward, share, to_pair, to_across, to_corner, handoff, density):
    sec = lax.axis_index("sec")
    planes, count = density.shape[:2]
    total = (share[...] + to_pair[...] + to_across[...] + to_corner[...]) / contour
    for i in range(planes):
        density[i] = total[i * count : (i + 1) * count]

    @pl.when(sec == 2)
    def _():
        handoff[0] = onward[...]

    @pl.when(sec != 2)
    def _():
        handoff[0] = handoff_in[...]


def call(kernel, out_shape, scratch, operands, dtypes=None):
    return pl.pallas_call(
        kernel,
        in_specs=[IN_VMEM] * len(operands),
        out_specs=[IN_VMEM] * len(out_shape),
        out_shape=[jax.ShapeDtypeStruct(shape, (dtypes or {}).get(i, jnp.float32)) for i, shape in enumerate(out_shape)],
        scratch_shapes=scratch,
        compiler_params=pltpu.CompilerParams(vmem_limit_bytes=VMEM_BYTES),
    )(*operands)


def paired(incoming, backward, fields, block_types, axial_taps, lateral_taps, depth_taps, bend_diagonal, bend_coupling):
    n_sec, n_gx = lax.axis_size("sec"), lax.axis_size("gx")
    steps, planes, orients, cells = backward.shape
    pair = planes // 2
    reach = (TICKS - 1) * steps, steps
    near = (1, -1)
    rows = 2 * orients
    lanes = cells // 2
    last = n_sec - 1

    def send(array, by_sec, even=0, odd=0):
        by_sec = by_sec.items() if isinstance(by_sec, dict) else enumerate(by_sec)
        pairs = [
            (s * n_gx + g, t * n_gx + (g + (odd if s % 2 else even)) % n_gx) for s, t in by_sec for g in range(n_gx)
        ]
        return lax.ppermute(array, ("sec", "gx"), pairs)

    same, beside = (0, 1, 2, 3), (1, 0, 3, 2)
    moved = send(incoming[0], {0: 1, 1: 3})
    bundle = launch(
        incoming, fields, block_types, axial_taps, lateral_taps, depth_taps, bend_diagonal, bend_coupling
    )
    own_types = jnp.pad(block_types.astype(jnp.float32), ((0, 7), (0, lanes - steps)))
    types = send(own_types, {1: 3})
    size = planes * rows + FIELD_ROWS
    base, taps, weights = call(
        unpack_kernel, [(size, lanes), (TAP_ROWS, lanes), (2 * rows, 2 * lanes)], [], [bundle], {2: jnp.bfloat16}
    )
    moved, base, types = lax.optimization_barrier((moved, base, types))
    passed = send(moved, {3: 2})

    tile = pltpu.VMEM((rows, lanes), jnp.float32)
    packed = pltpu.VMEM((GROUP * rows, 2 * lanes), jnp.bfloat16)
    inner = pltpu.VMEM((planes, rows, lanes), jnp.float32)

    def work(extent):
        slab = pltpu.VMEM((planes + 2 * extent, rows, lanes), jnp.float32)
        return [slab, slab, packed, packed, tile]

    (piece,) = call(pack_kernel, [(size, lanes)], [tile], [base, moved, passed, types])
    own = [send(piece, same, shift, 2 * shift) for shift in near]
    backward, own_types, _ = lax.optimization_barrier((backward, own_types, piece))
    across_types = send(own_types, {2: 0})
    (stored,) = call(turn_kernel, [(steps, planes, rows, lanes)], [tile], [backward])
    own[-1], stored, across_types = lax.optimization_barrier((own[-1], stored, across_types))
    swapped = [send(each, beside) for each in own]
    leaving, *swapped = lax.optimization_barrier((stored, *swapped))
    arrived = send(leaving, {2: 0})
    middle, piece, kept, total, factor = call(
        early_kernel,
        [(planes, rows, lanes), (pair * rows + 8, lanes), (planes, rows, lanes), (planes, rows, lanes)]
        + [(fields.shape[0], planes + 2 * reach[0], rows, lanes)],
        work(reach[0]),
        [taps, weights, across_types, piece, *own, *swapped, stored],
    )
    own = [send(piece, same, shift, shift) for shift in near]
    beside_total = send(total, beside)
    swapped = [send(each, beside) for each in own]
    held = planes * (orients // n_sec), cells
    handoff, onward, share, to_pair, to_across, to_corner = call(
        functools.partial(late_kernel, tuple(-shift for shift in near), last),
        [(planes, orients, cells)] * 2 + [held] * 4,
        work(reach[1]) + [inner, pltpu.VMEM((orients, cells), jnp.float32)],
        [taps, weights, middle, *own, *swapped, factor, kept, total, beside_total, arrived, stored],
    )
    onward = send(onward, {1: 2})
    to_corner = send(to_corner, (3, 2, 1, 0))
    to_across = send(to_across, (2, 0, 3, 1))
    to_pair = send(to_pair, beside)
    handoff, density = call(
        functools.partial(finish_kernel, n_sec * steps),
        [(1,) + handoff.shape, (planes, orients // n_sec, cells)],
        [],
        [handoff, onward, share, to_pair, to_across, to_corner],
    )
    return handoff, density


def pairs_fit(n_sec, planes, steps, orients, cells, kinds):
    return (
        n_sec == TICKS + 1 == 4
        and planes == steps
        and planes % 2 == 0
        and 2 * orients == 2 * CZ == cells // 2 == 128
        and 2 * kinds * planes <= OWN_KINDS and 10 * kinds * planes <= 2 * orients
        and GROUP < 2 * planes
    )


def solution(mesh):
    in_specs = (
        P("sec", "gx", None, None),
        P("sec", "gx", None, None),
        P(None, "gx", None),
        P("sec", None),
        P(),
        P(),
        P(),
        P(),
        P(),
    )
    out_specs = (P("sec", "gx", None, None), P("gx", "sec", None))

    def body(incoming, backward, fields, *rest):
        steps, planes, orients, cells = backward.shape
        fits = pairs_fit(mesh.shape["sec"], planes, steps, orients, cells, fields.shape[0])
        return (paired if fits else per_device)(incoming, backward, fields, *rest)

    return jax.shard_map(body, mesh=mesh, in_specs=in_specs, out_specs=out_specs, check_vma=False)
```

```python
import functools

import jax
import jax.numpy as jnp
from jax import lax
from jax.experimental import pallas as pl
from jax.experimental.pallas import tpu as pltpu
from jax.sharding import PartitionSpec as P

TICKS = 3
CZ = 64
GROUP = 6
FIELD_ROWS = 32
PIECE_ROWS = 16
TAP_ROWS = 8
OWN_KINDS = 24
PIECE_OWN, PIECE_FIRST = 12, 13
VMEM_BYTES = 16 * 2**20
WHOLE_VMEM_BYTES = 62 * 2**20
IN_VMEM = pl.BlockSpec(memory_space=pltpu.VMEM)


def padded_2(block, sides, width):
    for axis, dim in sides:
        count = lax.axis_size(axis)
        forward = [(i, i + 1) for i in range(count - 1)]
        forward.append((count - 1, 0))
        backward = [(target, source) for source, target in forward]
        low = lax.ppermute(
            lax.slice_in_dim(block, block.shape[dim] - width, None, axis=dim), axis, forward
        )
        high = lax.ppermute(lax.slice_in_dim(block, 0, width, axis=dim), axis, backward)
        block = jnp.concatenate([low, block, high], axis=dim)
    return block


def from_behind(array, axis, by):
    length = lax.axis_size(axis)
    pairs = [(i, i + by) for i in range(length) if 0 <= i + by < length]
    return lax.ppermute(array, axis, pairs)


def boltzmann(fields, kinds):
    selector = kinds == jnp.arange(fields.shape[0], dtype=jnp.int32)
    chosen = jnp.sum(jnp.where(selector[:, None, None], fields, jnp.zeros_like(fields)), axis=0)
    return jnp.exp(-chosen)


def column(taps, which):
    return taps[which][None, :, None]


def advance_padded(padded, factor, axial_taps, lateral_taps, depth_taps, kernel):
    along_x = (
        column(axial_taps, 0) * padded[:-2]
        + column(axial_taps, 1) * padded[1:-1]
        + column(axial_taps, 2) * padded[2:]
    )
    along_y = (
        column(lateral_taps, 0) * jnp.roll(along_x, CZ, axis=2)
        + column(lateral_taps, 1) * along_x
        + column(lateral_taps, 2) * jnp.roll(along_x, -CZ, axis=2)
    )
    depth_pos = (jnp.arange(along_y.shape[2], dtype=jnp.int32) % CZ)[None, None, :]
    behind = jnp.where(
        depth_pos == 0, jnp.roll(along_y, -(CZ - 1), axis=2), jnp.roll(along_y, 1, axis=2)
    )
    ahead = jnp.where(
        depth_pos == CZ - 1, jnp.roll(along_y, CZ - 1, axis=2), jnp.roll(along_y, -1, axis=2)
    )
    along_z = (
        column(depth_taps, 0) * behind
        + column(depth_taps, 1) * along_y
        + column(depth_taps, 2) * ahead
    )
    blended = jnp.einsum(
        "uv,xvc->xuc",
        kernel,
        along_z,
        precision=lax.Precision.HIGHEST,
        preferred_element_type=jnp.float32,
    )
    return blended * factor[:, None, :]


def per_device(
    incoming,
    backward,
    fields,
    block_types,
    axial_taps,
    lateral_taps,
    depth_taps,
    bend_diagonal,
    bend_coupling,
):
    kernel = jnp.diag(bend_diagonal) + bend_coupling
    steps_each = block_types.shape[1]
    planes = incoming.shape[1]
    start = incoming[0]
    first_section = lax.axis_index("sec") == 0
    wide_fields = padded_2(fields, (("gx", 1),), steps_each)
    factors = [boltzmann(wide_fields, block_types[0, position]) for position in range(steps_each)]
    current = start
    outgoing = start
    accumulated = jnp.zeros(start.shape, jnp.float32)
    for tick_index in range(TICKS):
        final_tick = tick_index + 1 == TICKS
        extended = padded_2(current, (("gx", 0),), steps_each)
        for position in range(steps_each):
            margin = steps_each - position - 1
            offset = steps_each - margin
            factor = factors[position][offset : offset + planes + 2 * margin]
            extended = advance_padded(
                extended, factor, axial_taps, lateral_taps, depth_taps, kernel
            )
            if final_tick:
                accumulated = accumulated + extended[margin : margin + planes] * backward[
                    position
                ].astype(jnp.float32)
        outgoing = extended
        if not final_tick:
            shifted = from_behind(outgoing, "sec", 1)
            current = jnp.where(first_section, start, shifted)
    reduced = lax.psum_scatter(accumulated, "sec", scatter_dimension=1, tiled=True)
    density = reduced / (lax.axis_size("sec") * steps_each)
    return (outgoing[None], density)


def to_tile(plane, scratch):
    half = plane.shape[1] // 2
    scratch[...] = jnp.concatenate([plane[:, :half], plane[:, half:]], axis=0).T
    return reorder(scratch)


def reorder(scratch):
    rows = scratch.shape[0]
    return jnp.concatenate(
        [scratch[pl.ds(yl * CZ + zl, 8, stride=8), :] for yl in range(rows // CZ) for zl in range(CZ // 8)], axis=0
    )


def from_tile(tile, scratch):
    rows = tile.shape[0]
    for yl in range(rows // CZ):
        for zl in range(CZ // 8):
            at = (yl * (CZ // 8) + zl) * 8
            scratch[pl.ds(yl * CZ + zl, 8, stride=8), :] = tile[at : at + 8]
    turned = scratch[...].T
    half = turned.shape[0] // 2
    return jnp.concatenate([turned[:half], turned[half:]], axis=1)


def stencil(behind, here, ahead, taps):
    a = here + taps[0] * behind + taps[1] * ahead
    low, high = a[:CZ], a[CZ:]
    low_turned = pltpu.roll(low, a.shape[1] // 2, 1)
    high_turned = pltpu.roll(high, a.shape[1] // 2, 1)
    out = []
    for b in (
        low + taps[2] * high_turned + taps[3] * high,
        high + taps[2] * low + taps[3] * low_turned,
    ):
        back = jnp.concatenate([pltpu.roll(b[-8:], 1, 0), b[:-8]], axis=0)
        front = jnp.concatenate([b[8:], pltpu.roll(b[:8], 7, 0)], axis=0)
        out.append(b + taps[4] * back + taps[5] * front)
    return jnp.concatenate(out, axis=0)


def position():
    sec = lax.axis_index("sec")
    return sec, lax.rem(sec, 2)


def launch_kernel(*refs):
    sources, bundle, scratch, copies, sems = refs[:8], refs[8], refs[9], refs[10:18], refs[18]
    moves = [pltpu.make_async_copy(s, c, sems.at[i]) for i, (s, c) in enumerate(zip(sources, copies))]
    for move in moves:
        move.start()
    incoming, fields, kinds, axial, lateral, depth, diagonal, coupling = copies
    for move in moves[1:]:
        move.wait()
    rows = scratch.shape[0]
    orients = rows // 2
    ratios = [each[w : w + 1] / each[1:2] for each in (axial, lateral, depth) for w in (0, 2)]
    for i, ratio in enumerate(ratios + ratios[:2]):
        bundle[i : i + 1] = jnp.concatenate([ratio, ratio], axis=1)
    square = (orients, orients)
    same = lax.broadcasted_iota(jnp.int32, square, 0) == lax.broadcasted_iota(jnp.int32, square, 1)
    kernel = jnp.where(same, diagonal[...], 0.0) + coupling[...]
    kernel = kernel * (axial[1:2] * lateral[1:2] * depth[1:2])
    upper = jnp.concatenate([kernel, jnp.zeros_like(kernel)], axis=1)
    bundle[TAP_ROWS : TAP_ROWS + rows] = jnp.concatenate([upper, pltpu.roll(upper, orients, 1)], axis=0).T
    line = kinds[...].astype(jnp.float32)
    line = jnp.concatenate([line, jnp.zeros((1, rows - line.shape[1]), jnp.float32)], axis=1)
    types = line
    planes = incoming.shape[1]
    at = TAP_ROWS + rows
    bundle[at : at + FIELD_ROWS] = jnp.zeros((FIELD_ROWS, rows), jnp.float32)
    for kind in range(fields.shape[0]):
        for i in range(planes):
            line = fields[kind, i : i + 1, :]
            here = at + (kind * planes + i) * 2
            bundle[here : here + 1] = line[:, :rows]
            bundle[here + 1 : here + 2] = line[:, rows:]
    bundle[at + OWN_KINDS : at + OWN_KINDS + 1] = types
    moves[0].wait()
    for i in range(planes):
        here = at + FIELD_ROWS + i * rows
        bundle[here : here + rows] = to_tile(incoming[0, i], scratch)


def launch(incoming, fields, kinds, axial, lateral, depth, diagonal, coupling):
    planes, orients, cells = incoming.shape[1:]
    rows = 2 * orients
    operands = [incoming, fields, kinds, axial, lateral, depth, diagonal.reshape(1, -1), coupling]
    return pl.pallas_call(
        launch_kernel,
        in_specs=[pl.BlockSpec(memory_space=pltpu.HBM)] * len(operands),
        out_specs=IN_VMEM,
        out_shape=jax.ShapeDtypeStruct((TAP_ROWS + rows + FIELD_ROWS + planes * rows, rows), jnp.float32),
        scratch_shapes=[pltpu.VMEM((rows, rows), jnp.float32)]
        + [pltpu.VMEM(each.shape, each.dtype) for each in operands]
        + [pltpu.SemaphoreType.DMA((len(operands),))],
        compiler_params=pltpu.CompilerParams(vmem_limit_bytes=WHOLE_VMEM_BYTES),
    )(*operands)


def turn_kernel(backward, early, late, scratch):
    for out, begin in ((early, 0), (late, early.shape[0])):
        for step in range(out.shape[0]):
            for i in range(out.shape[1]):
                out[step, i] = to_tile(backward[begin + step, i].astype(jnp.float32), scratch)


def unpack_kernel(bundle, out, taps, weights):
    rows = taps.shape[1]
    taps[...] = bundle[:TAP_ROWS]
    twice = bundle[TAP_ROWS : TAP_ROWS + rows]
    coarse = twice.astype(jnp.bfloat16)
    fine = (twice - coarse.astype(jnp.float32)).astype(jnp.bfloat16)
    weights[...] = jnp.concatenate(
        [jnp.concatenate([coarse, fine], axis=1), jnp.concatenate([coarse, jnp.zeros_like(fine)], axis=1)], axis=0
    )
    at = out.shape[0] - FIELD_ROWS
    lines = TAP_ROWS + rows
    out[at:] = bundle[lines : lines + FIELD_ROWS]
    out[:at] = bundle[lines + FIELD_ROWS :]


def pack_kernel(base, moved, passed, types, middle, piece, scratch):
    sec, odd = position()
    planes, rows = middle.shape[:2]
    pair = planes // 2
    at = planes * rows

    @pl.when(sec == 0)
    def _():
        for i in range(planes):
            middle[i] = base[i * rows : (i + 1) * rows]

    def fill(source):
        for i in range(planes):
            middle[i] = to_tile(source[i], scratch)

    pl.when(odd == 1)(lambda: fill(moved))
    pl.when((sec > 0) & (odd == 0))(lambda: fill(passed))
    for i in range(pair):
        piece[i * rows : (i + 1) * rows] = middle[pair * odd + i]
    here = pair * rows
    piece[here:] = jnp.zeros((PIECE_ROWS, rows), jnp.float32)
    for kind in range(OWN_KINDS // (2 * planes)):
        for i in range(pair):
            to = here + (kind * pair + i) * 2
            piece[to : to + 2] = base[pl.ds(at + (kind * planes + pair * odd + i) * 2, 2)]
    own = base[at + OWN_KINDS : at + OWN_KINDS + 1]
    piece[here + PIECE_OWN : here + PIECE_OWN + 1] = own
    piece[here + PIECE_FIRST : here + PIECE_FIRST + 1] = jnp.where(sec == 0, own, types[:1])


def scalars_of(row, count):
    lane = lax.broadcasted_iota(jnp.int32, row.shape, 1)
    return [jnp.sum(jnp.where(lane == i, row, 0.0)).astype(jnp.int32) for i in range(count)]


def places(odd, planes, reach, blocks):
    return [reach + block * planes + planes // 2 * core for core in (odd, 1 - odd) for block in blocks]


def run_steps(kinds, taps, weights, count, slab, other, first, second, factor, offset, after):
    tap = [taps[i : i + 1, :] for i in range(6)]
    extent, rows, lanes = slab.shape
    buffers = (slab, other)

    def blend(source, at, packed):
        for i in range(GROUP):
            e = stencil(source[at + i - 1], source[at + i], source[at + i + 1], tap)
            coarse = e.astype(jnp.bfloat16)
            packed[i * rows : (i + 1) * rows, :lanes] = coarse
            packed[i * rows : (i + 1) * rows, lanes:] = (e - coarse.astype(jnp.float32)).astype(jnp.bfloat16)

    def mix(target, at, packed, kind):
        product = jnp.dot(packed[...], weights[...], preferred_element_type=jnp.float32)
        product = product[:, :lanes] + product[:, lanes:]
        for i in range(GROUP):
            target[at + i] = product[i * rows : (i + 1) * rows] * factor[kind, at + i + offset]

    for step in range(count):
        source, target = buffers[step % 2], buffers[1 - step % 2]
        begin, width = step + 1, extent - 2 * step - 2
        groups = -(-width // GROUP)
        kind = kinds[step]

        def at(i, begin=begin, width=width):
            return jnp.minimum(begin + i * GROUP, begin + width - GROUP)

        blend(source, at(0), first)
        if groups > 1:

            def body(i, carry, source=source, target=target, at=at, kind=kind):
                blend(source, at(2 * i + 1), second)
                mix(target, at(2 * i), first, kind)
                blend(source, at(2 * i + 2), first)
                mix(target, at(2 * i + 1), second, kind)
                return carry

            lax.fori_loop(0, (groups - 1) // 2, body, 0)
        if groups % 2 == 0:
            blend(source, at(groups - 1), second)
            mix(target, at(groups - 2), first, kind)
            mix(target, at(groups - 1), second, kind)
        else:
            mix(target, at(groups - 1), first, kind)
        after(step, target)


def spread_factor(columns, factor, begin, start, count):
    rows, lanes = factor.shape[2:]
    right = (lax.broadcasted_iota(jnp.int32, (rows, lanes), 1) >= lanes // 2).astype(jnp.int32)
    for kind in range(factor.shape[0]):
        for i in range(count):
            at = begin + (kind * count + i) * 2
            factor[kind, start + i] = jnp.take_along_axis(columns, right + at, axis=1, mode="promise_in_bounds")


def load_slab(slab, middle, pieces, odd):
    planes, rows = middle.shape[:2]
    pair = planes // 2
    starts = places(odd, planes, planes, (-1, 1))
    slab[planes : 2 * planes] = middle[...]
    for piece, start in zip(pieces, starts):
        for i in range(pair):
            slab[start + i] = piece[i * rows : (i + 1) * rows]
    return starts


def early_kernel(taps, weights, base, middle_in, *refs):
    pieces, stored, (middle, half_out, kept, total, factor) = refs[:4], refs[4:6], refs[6:11]
    slab, other, first, second, scratch = refs[11:]
    sec, odd = position()
    planes, rows = middle.shape[:2]
    pair = planes // 2
    starts = load_slab(slab, middle_in, pieces, odd)
    at = pair * rows
    own_first, beside_first = (each[at + PIECE_FIRST : at + PIECE_FIRST + 1] for each in (pieces[0], pieces[2]))
    kinds = scalars_of(jnp.where((sec == 0) | (sec == 3), own_first, beside_first), planes)
    centre = base.shape[0] - FIELD_ROWS
    lines = [base[centre : centre + OWN_KINDS]] + [piece[at : at + PIECE_OWN] for piece in pieces]
    used = OWN_KINDS + PIECE_OWN * len(pieces)
    lines.append(jnp.zeros((rows - used, rows), jnp.float32))
    scratch[...] = jnp.exp(-jnp.concatenate(lines, axis=0)).T
    columns = reorder(scratch)
    spread_factor(columns, factor, 0, planes, planes)
    for i, start in enumerate(starts):
        spread_factor(columns, factor, OWN_KINDS + PIECE_OWN * i, start, pair)
    finish_round(stored, sec == 0, kinds, taps, weights, factor, refs[6:10], refs[11:15])
    half_out[at:] = jnp.broadcast_to(base[centre + OWN_KINDS : centre + OWN_KINDS + 1], (8, rows))


def mid_kernel(taps, weights, across, middle_in, *refs):
    pieces, factor, stored, (middle, half_out, kept, total) = refs[:4], refs[4], refs[5:7], refs[7:11]
    slab, other, first, second, scratch = refs[11:]
    sec, odd = position()
    planes, rows = middle.shape[:2]
    at = planes // 2 * rows
    load_slab(slab, middle_in, pieces, odd)
    own, beside = (each[at : at + 1] for each in (pieces[0], pieces[2]))
    kinds = scalars_of(jnp.where((sec == 1) | (sec == 2), own, beside), planes)
    finish_round(stored, sec == 1, kinds, taps, weights, factor, refs[7:11], refs[11:15])
    half_out[at:] = jnp.broadcast_to(jnp.where(sec == 0, across[:1], own), (8, rows))


def finish_round(stored, counted, kinds, taps, weights, factor, outs, work):
    middle, half_out, kept, total = outs
    slab, other, first, second = work
    odd = position()[1]
    planes, rows = middle.shape[:2]
    pair = planes // 2
    span = stored[0].shape[0]
    total[...] = jnp.zeros(total.shape, jnp.float32)

    def after(step, state):
        @pl.when(counted)
        def _():
            total[...] += state[planes : 2 * planes] * stored[step // span][step % span]

    run_steps(kinds, taps, weights, planes, slab, other, first, second, factor, 0, after)
    state = (slab, other)[planes % 2]
    middle[...] = state[planes : 2 * planes]
    kept[...] = state[planes : 2 * planes]
    for i in range(pair):
        half_out[i * rows : (i + 1) * rows] = state[planes + pair * odd + i]


def late_kernel(last, taps, weights, middle, *refs):
    pieces, (factor, kept, beside_kept, total_in, total_beside) = refs[:4], refs[4:9]
    series, stored = refs[9:11], refs[11:13]
    handoff, share, to_pair, to_across, to_corner = refs[13:18]
    slab, other, first, second, scratch, total, whole = refs[18:]
    sec, odd = position()
    planes, rows = middle.shape[:2]
    pair = planes // 2
    load_slab(slab, middle, pieces, odd)
    even, uneven = (jnp.where(odd == core, pieces[0][pair * rows :], pieces[2][pair * rows :]) for core in (0, 1))
    kinds = scalars_of(jnp.where(sec < 2, even, uneven)[:1], planes)
    total[...] = jnp.zeros(total.shape, jnp.float32)

    @pl.when(sec == 0)
    def _():
        total[...] = total_in[...] + total_beside[...]

    span = stored[0].shape[0]

    def after(step, state):
        for where, source in ((sec == 0, series), (sec == last, stored)):

            @pl.when(where)
            def _(source=source):
                total[...] += state[planes : 2 * planes] * source[step // span][step % span]

    run_steps(kinds, taps, weights, planes, slab, other, first, second, factor, 0, after)
    state = (slab, other)[planes % 2]
    orients = handoff.shape[1]
    count = orients // (last + 1)
    held = planes * count
    to_corner[...] = jnp.zeros(to_corner.shape, jnp.float32)
    for who, source in ((0, kept), (1, beside_kept), (last, state)):

        @pl.when(sec == who)
        def _(source=source):
            begin = planes if source is state else 0
            for i in range(planes):
                handoff[i] = from_tile(source[begin + i], scratch)

    for i in range(planes):
        whole[...] = from_tile(total[i], scratch)
        for piece, who in (
            (share, sec),
            (to_pair, sec + 1 - 2 * odd),
            (to_across, jnp.where(sec == 0, 2, 1)),
            (to_corner, last - sec),
        ):
            piece[i * count : (i + 1) * count] = whole[pl.ds(pl.multiple_of(who * count, count), count)]
    for i in range(pair):
        to_across[held + i * orients : held + (i + 1) * orients] = from_tile(
            state[planes + pair * odd + i], scratch
        )

    @pl.when(sec == 1)
    def _():
        to_corner[...] = to_across[held:]


def finish_kernel(contour, handoff_in, share, to_pair, to_across, to_corner, handoff, density):
    sec = lax.axis_index("sec")
    planes, count = density.shape[:2]
    held = planes * count
    corner = jnp.where(sec == 2, 0.0, to_corner[:held])
    total = (share[...] + to_pair[...] + to_across[:held] + corner) / contour
    for i in range(planes):
        density[i] = total[i * count : (i + 1) * count]
    handoff[0] = handoff_in[...]

    @pl.when(sec == 2)
    def _():
        orients = handoff.shape[2]
        pair = planes // 2
        for i in range(pair):
            handoff[0, i] = to_across[held + i * orients : held + (i + 1) * orients]
            handoff[0, pair + i] = to_corner[i * orients : (i + 1) * orients]


def call(kernel, out_shape, scratch, operands, dtypes=None):
    return pl.pallas_call(
        kernel,
        in_specs=[IN_VMEM] * len(operands),
        out_specs=[IN_VMEM] * len(out_shape),
        out_shape=[jax.ShapeDtypeStruct(shape, (dtypes or {}).get(i, jnp.float32)) for i, shape in enumerate(out_shape)],
        scratch_shapes=scratch,
        compiler_params=pltpu.CompilerParams(vmem_limit_bytes=VMEM_BYTES),
    )(*operands)


def paired(incoming, backward, fields, block_types, axial_taps, lateral_taps, depth_taps, bend_diagonal, bend_coupling):
    n_sec, n_gx = lax.axis_size("sec"), lax.axis_size("gx")
    steps, planes, orients, cells = backward.shape
    pair = planes // 2
    rows = 2 * orients
    lanes = cells // 2
    last = n_sec - 1

    def send(array, by_sec, shift=0):
        by_sec = by_sec.items() if isinstance(by_sec, dict) else enumerate(by_sec)
        pairs = [(s * n_gx + g, t * n_gx + (g + shift) % n_gx) for s, t in by_sec for g in range(n_gx)]
        return lax.ppermute(array, ("sec", "gx"), pairs)

    same, beside = (0, 1, 2, 3), (1, 0, 3, 2)
    moved = send(incoming[0], {0: 1, 1: 3})
    bundle = launch(
        incoming, fields, block_types, axial_taps, lateral_taps, depth_taps, bend_diagonal, bend_coupling
    )
    own_types = jnp.pad(block_types.astype(jnp.float32), ((0, 7), (0, lanes - steps)))
    types = send(own_types, {1: 3})
    size = planes * rows + FIELD_ROWS
    base, taps, weights = call(
        unpack_kernel, [(size, lanes), (TAP_ROWS, lanes), (2 * rows, 2 * lanes)], [], [bundle], {2: jnp.bfloat16}
    )
    moved, base, types = lax.optimization_barrier((moved, base, types))
    passed = send(moved, {3: 2})

    tile = pltpu.VMEM((rows, lanes), jnp.float32)
    packed = pltpu.VMEM((GROUP * rows, 2 * lanes), jnp.bfloat16)
    inner = pltpu.VMEM((planes, rows, lanes), jnp.float32)

    slab = pltpu.VMEM((3 * planes, rows, lanes), jnp.float32)
    work = [slab, slab, packed, packed, tile]
    block, half = (planes, rows, lanes), (pair * rows + 8, lanes)

    def exchange(piece, *others):
        own = [send(piece, same, shift) for shift in (1, -1)]
        own[-1], *others = lax.optimization_barrier((own[-1], *others))
        return own + [send(each, beside) for each in own], others

    middle, piece = call(
        pack_kernel, [block, (pair * rows + PIECE_ROWS, lanes)], [tile], [base, moved, passed, types]
    )
    backward, _ = lax.optimization_barrier((backward, piece))
    stored = call(turn_kernel, [(steps // 2,) + block] * 2, [tile], [backward])
    pieces, stored = exchange(piece, *stored)
    leaving, *pieces = lax.optimization_barrier((stored[0], *pieces))
    arrived = [send(leaving, {2: 0})]
    middle, piece, kept, total, factor = call(
        early_kernel,
        [block, half, block, block, (fields.shape[0], 3 * planes, rows, lanes)],
        work,
        [taps, weights, base, middle, *pieces, *stored],
    )
    own_types, piece = lax.optimization_barrier((own_types, piece))
    pieces, (across_types,) = exchange(piece, send(own_types, {2: 0}))
    leaving, *pieces = lax.optimization_barrier((stored[1], *pieces))
    arrived.append(send(leaving, {2: 0}))
    middle, piece, beside_kept, beside_total = call(
        mid_kernel,
        [block, half, block, block],
        work,
        [taps, weights, across_types, middle, *pieces, factor, *stored],
    )
    pieces, _ = exchange(piece)
    beside_total = send(beside_total, beside)
    held = planes * (orients // n_sec)
    handoff, share, to_pair, to_across, to_corner = call(
        functools.partial(late_kernel, last),
        [(planes, orients, cells)]
        + [(held, cells)] * 2
        + [(held + pair * orients, cells), (pair * orients, cells)],
        work + [inner, pltpu.VMEM((orients, cells), jnp.float32)],
        [taps, weights, middle, *pieces, factor, kept, beside_kept, total, beside_total, *arrived, *stored],
    )
    to_pair = send(to_pair, beside)
    to_across = send(to_across, (2, 0, 3, 1))
    to_corner = send(to_corner, (3, 2, 1, 0))
    handoff, density = call(
        functools.partial(finish_kernel, n_sec * steps),
        [(1,) + handoff.shape, (planes, orients // n_sec, cells)],
        [],
        [handoff, share, to_pair, to_across, to_corner],
    )
    return handoff, density


def pairs_fit(n_sec, planes, steps, orients, cells, kinds):
    return (
        n_sec == TICKS + 1 == 4
        and planes == steps
        and planes % 2 == 0
        and 2 * orients == 2 * CZ == cells // 2 == 128
        and 2 * kinds * planes == OWN_KINDS and steps % 2 == 0
        and GROUP < 2 * planes
    )


def solution(mesh):
    in_specs = (
        P("sec", "gx", None, None),
        P("sec", "gx", None, None),
        P(None, "gx", None),
        P("sec", None),
        P(),
        P(),
        P(),
        P(),
        P(),
    )
    out_specs = (P("sec", "gx", None, None), P("gx", "sec", None))

    def body(incoming, backward, fields, *rest):
        steps, planes, orients, cells = backward.shape
        fits = pairs_fit(mesh.shape["sec"], planes, steps, orients, cells, fields.shape[0])
        return (paired if fits else per_device)(incoming, backward, fields, *rest)

    return jax.shard_map(body, mesh=mesh, in_specs=in_specs, out_specs=out_specs, check_vma=False)
```

```python
import functools

import jax
import jax.numpy as jnp
from jax import lax
from jax.experimental import pallas as pl
from jax.experimental.pallas import tpu as pltpu
from jax.sharding import PartitionSpec as P

TICKS = 3
CZ = 64
GROUP = 6
FIELD_ROWS = 32
TAP_ROWS = 8
OWN_KINDS, FIRST_KINDS = 24, 25
LEAD = 1
VMEM_BYTES = 16 * 2**20
WHOLE_VMEM_BYTES = 62 * 2**20
IN_VMEM = pl.BlockSpec(memory_space=pltpu.VMEM)


def padded_2(block, sides, width):
    for axis, dim in sides:
        count = lax.axis_size(axis)
        forward = [(i, i + 1) for i in range(count - 1)]
        forward.append((count - 1, 0))
        backward = [(target, source) for source, target in forward]
        low = lax.ppermute(
            lax.slice_in_dim(block, block.shape[dim] - width, None, axis=dim), axis, forward
        )
        high = lax.ppermute(lax.slice_in_dim(block, 0, width, axis=dim), axis, backward)
        block = jnp.concatenate([low, block, high], axis=dim)
    return block


def from_behind(array, axis, by):
    length = lax.axis_size(axis)
    pairs = [(i, i + by) for i in range(length) if 0 <= i + by < length]
    return lax.ppermute(array, axis, pairs)


def boltzmann(fields, kinds):
    selector = kinds == jnp.arange(fields.shape[0], dtype=jnp.int32)
    chosen = jnp.sum(jnp.where(selector[:, None, None], fields, jnp.zeros_like(fields)), axis=0)
    return jnp.exp(-chosen)


def column(taps, which):
    return taps[which][None, :, None]


def advance_padded(padded, factor, axial_taps, lateral_taps, depth_taps, kernel):
    along_x = (
        column(axial_taps, 0) * padded[:-2]
        + column(axial_taps, 1) * padded[1:-1]
        + column(axial_taps, 2) * padded[2:]
    )
    along_y = (
        column(lateral_taps, 0) * jnp.roll(along_x, CZ, axis=2)
        + column(lateral_taps, 1) * along_x
        + column(lateral_taps, 2) * jnp.roll(along_x, -CZ, axis=2)
    )
    depth_pos = (jnp.arange(along_y.shape[2], dtype=jnp.int32) % CZ)[None, None, :]
    behind = jnp.where(
        depth_pos == 0, jnp.roll(along_y, -(CZ - 1), axis=2), jnp.roll(along_y, 1, axis=2)
    )
    ahead = jnp.where(
        depth_pos == CZ - 1, jnp.roll(along_y, CZ - 1, axis=2), jnp.roll(along_y, -1, axis=2)
    )
    along_z = (
        column(depth_taps, 0) * behind
        + column(depth_taps, 1) * along_y
        + column(depth_taps, 2) * ahead
    )
    blended = jnp.einsum(
        "uv,xvc->xuc",
        kernel,
        along_z,
        precision=lax.Precision.HIGHEST,
        preferred_element_type=jnp.float32,
    )
    return blended * factor[:, None, :]


def per_device(
    incoming,
    backward,
    fields,
    block_types,
    axial_taps,
    lateral_taps,
    depth_taps,
    bend_diagonal,
    bend_coupling,
):
    kernel = jnp.diag(bend_diagonal) + bend_coupling
    steps_each = block_types.shape[1]
    planes = incoming.shape[1]
    start = incoming[0]
    first_section = lax.axis_index("sec") == 0
    wide_fields = padded_2(fields, (("gx", 1),), steps_each)
    factors = [boltzmann(wide_fields, block_types[0, position]) for position in range(steps_each)]
    current = start
    outgoing = start
    accumulated = jnp.zeros(start.shape, jnp.float32)
    for tick_index in range(TICKS):
        final_tick = tick_index + 1 == TICKS
        extended = padded_2(current, (("gx", 0),), steps_each)
        for position in range(steps_each):
            margin = steps_each - position - 1
            offset = steps_each - margin
            factor = factors[position][offset : offset + planes + 2 * margin]
            extended = advance_padded(
                extended, factor, axial_taps, lateral_taps, depth_taps, kernel
            )
            if final_tick:
                accumulated = accumulated + extended[margin : margin + planes] * backward[
                    position
                ].astype(jnp.float32)
        outgoing = extended
        if not final_tick:
            shifted = from_behind(outgoing, "sec", 1)
            current = jnp.where(first_section, start, shifted)
    reduced = lax.psum_scatter(accumulated, "sec", scatter_dimension=1, tiled=True)
    density = reduced / (lax.axis_size("sec") * steps_each)
    return (outgoing[None], density)


def to_tile(plane, scratch):
    half = plane.shape[1] // 2
    scratch[...] = jnp.concatenate([plane[:, :half], plane[:, half:]], axis=0).T
    return reorder(scratch)


def reorder(scratch):
    rows = scratch.shape[0]
    return jnp.concatenate(
        [scratch[pl.ds(yl * CZ + zl, 8, stride=8), :] for yl in range(rows // CZ) for zl in range(CZ // 8)], axis=0
    )


def from_tile(tile, scratch):
    rows = tile.shape[0]
    for yl in range(rows // CZ):
        for zl in range(CZ // 8):
            at = (yl * (CZ // 8) + zl) * 8
            scratch[pl.ds(yl * CZ + zl, 8, stride=8), :] = tile[at : at + 8]
    turned = scratch[...].T
    half = turned.shape[0] // 2
    return jnp.concatenate([turned[:half], turned[half:]], axis=1)


def stencil(behind, here, ahead, taps):
    a = here + taps[0] * behind + taps[1] * ahead
    low, high = a[:CZ], a[CZ:]
    low_turned = pltpu.roll(low, a.shape[1] // 2, 1)
    high_turned = pltpu.roll(high, a.shape[1] // 2, 1)
    out = []
    for b in (
        low + taps[2] * high_turned + taps[3] * high,
        high + taps[2] * low + taps[3] * low_turned,
    ):
        back = jnp.concatenate([pltpu.roll(b[-8:], 1, 0), b[:-8]], axis=0)
        front = jnp.concatenate([b[8:], pltpu.roll(b[:8], 7, 0)], axis=0)
        out.append(b + taps[4] * back + taps[5] * front)
    return jnp.concatenate(out, axis=0)


def position():
    sec = lax.axis_index("sec")
    return sec, lax.rem(sec, 2)


def launch_kernel(*refs):
    sources, (lead, bundle) = refs[:9], refs[9:11]
    scratch, copies, sems = refs[11], refs[12:21], refs[21]
    moves = [
        pltpu.make_async_copy(source.at[pl.ds(0, copy.shape[0])], copy, sems.at[i])
        for i, (source, copy) in enumerate(zip(sources, copies))
    ]
    for move in moves:
        move.start()
    incoming, stored, fields, kinds, axial, lateral, depth, diagonal, coupling = copies
    for move in moves[2:]:
        move.wait()
    rows = scratch.shape[0]
    orients = rows // 2
    ratios = [each[w : w + 1] / each[1:2] for each in (axial, lateral, depth) for w in (0, 2)]
    for i, ratio in enumerate(ratios + ratios[:2]):
        bundle[i : i + 1] = jnp.concatenate([ratio, ratio], axis=1)
    square = (orients, orients)
    same = lax.broadcasted_iota(jnp.int32, square, 0) == lax.broadcasted_iota(jnp.int32, square, 1)
    kernel = jnp.where(same, diagonal[...], 0.0) + coupling[...]
    kernel = kernel * (axial[1:2] * lateral[1:2] * depth[1:2])
    upper = jnp.concatenate([kernel, jnp.zeros_like(kernel)], axis=1)
    bundle[TAP_ROWS : TAP_ROWS + rows] = jnp.concatenate([upper, pltpu.roll(upper, orients, 1)], axis=0).T
    line = kinds[...].astype(jnp.float32)
    line = jnp.concatenate([line, jnp.zeros((1, rows - line.shape[1]), jnp.float32)], axis=1)
    types = line
    planes = incoming.shape[1]
    at = TAP_ROWS + rows
    bundle[at : at + FIELD_ROWS] = jnp.zeros((FIELD_ROWS, rows), jnp.float32)
    for kind in range(fields.shape[0]):
        for i in range(planes):
            line = fields[kind, i : i + 1, :]
            here = at + (kind * planes + i) * 2
            bundle[here : here + 1] = line[:, :rows]
            bundle[here + 1 : here + 2] = line[:, rows:]
    bundle[at + OWN_KINDS : at + OWN_KINDS + 1] = types
    moves[0].wait()
    for i in range(planes):
        here = at + FIELD_ROWS + i * rows
        bundle[here : here + rows] = to_tile(incoming[0, i], scratch)
    moves[1].wait()
    for step in range(LEAD):
        for i in range(planes):
            here = (step * planes + i) * orients
            lead[here : here + orients] = stored[step, i].astype(jnp.float32)
    lead[lead.shape[0] - 8 :] = jnp.broadcast_to(jnp.concatenate([types, types], axis=1), (8, lead.shape[1]))


def launch(incoming, backward, fields, kinds, axial, lateral, depth, diagonal, coupling):
    planes, orients, cells = backward.shape[1:]
    rows = 2 * orients
    operands = [incoming, backward, fields, kinds, axial, lateral, depth, diagonal.reshape(1, -1), coupling]
    shapes = [(LEAD * planes * orients + 8, cells), (TAP_ROWS + rows + FIELD_ROWS + planes * rows, rows)]
    taken = [(LEAD,) + each.shape[1:] if i == 1 else each.shape for i, each in enumerate(operands)]
    return pl.pallas_call(
        launch_kernel,
        in_specs=[pl.BlockSpec(memory_space=pltpu.HBM)] * len(operands),
        out_specs=[IN_VMEM] * len(shapes),
        out_shape=[jax.ShapeDtypeStruct(shape, jnp.float32) for shape in shapes],
        scratch_shapes=[pltpu.VMEM((rows, rows), jnp.float32)]
        + [pltpu.VMEM(shape, each.dtype) for shape, each in zip(taken, operands)]
        + [pltpu.SemaphoreType.DMA((len(operands),))],
        compiler_params=pltpu.CompilerParams(vmem_limit_bytes=WHOLE_VMEM_BYTES),
    )(*operands)


def turn_kernel(backward, lead, early, late, out, across, scratch):
    orients = scratch.shape[0] // 2
    across[...] = lead[lead.shape[0] - 8 :, : scratch.shape[1]]
    for target, begin in ((early, 0), (late, LEAD)):
        for step in range(target.shape[0]):
            for i in range(target.shape[1]):
                target[step, i] = to_tile(backward[begin + step, i].astype(jnp.float32), scratch)
    for step in range(out.shape[0]):
        for i in range(out.shape[1]):
            here = (step * out.shape[1] + i) * orients
            out[step, i] = to_tile(lead[here : here + orients], scratch)


def unpack_kernel(bundle, out, taps, weights):
    rows = taps.shape[1]
    taps[...] = bundle[:TAP_ROWS]
    twice = bundle[TAP_ROWS : TAP_ROWS + rows]
    coarse = twice.astype(jnp.bfloat16)
    fine = (twice - coarse.astype(jnp.float32)).astype(jnp.bfloat16)
    weights[...] = jnp.concatenate(
        [jnp.concatenate([coarse, fine], axis=1), jnp.concatenate([coarse, jnp.zeros_like(fine)], axis=1)], axis=0
    )
    at = out.shape[0] - FIELD_ROWS
    lines = TAP_ROWS + rows
    out[at:] = bundle[lines : lines + FIELD_ROWS]
    out[:at] = bundle[lines + FIELD_ROWS :]


def pack_kernel(base, moved, passed, types, out, scratch):
    sec, odd = position()
    rows = scratch.shape[0]
    at = out.shape[0] - FIELD_ROWS
    out[at:] = base[at:]
    out[at + FIRST_KINDS : at + FIRST_KINDS + 1] = jnp.where(
        sec == 0, base[at + OWN_KINDS : at + OWN_KINDS + 1], types[:1]
    )

    @pl.when(sec == 0)
    def _():
        out[:at] = base[:at]

    def fill(source):
        for i in range(source.shape[0]):
            out[i * rows : (i + 1) * rows] = to_tile(source[i], scratch)

    pl.when(odd == 1)(lambda: fill(moved))
    pl.when((sec > 0) & (odd == 0))(lambda: fill(passed))


def scalars_of(row, count):
    lane = lax.broadcasted_iota(jnp.int32, row.shape, 1)
    return [jnp.sum(jnp.where(lane == i, row, 0.0)).astype(jnp.int32) for i in range(count)]


def places(odd, planes, reach, blocks):
    return [reach + block * planes + planes // 2 * core for core in (odd, 1 - odd) for block in blocks]


def run_steps(kinds, taps, weights, count, slab, other, first, second, factor, offset, after):
    tap = [taps[i : i + 1, :] for i in range(6)]
    extent, rows, lanes = slab.shape
    buffers = (slab, other)

    def blend(source, at, packed):
        for i in range(GROUP):
            e = stencil(source[at + i - 1], source[at + i], source[at + i + 1], tap)
            coarse = e.astype(jnp.bfloat16)
            packed[i * rows : (i + 1) * rows, :lanes] = coarse
            packed[i * rows : (i + 1) * rows, lanes:] = (e - coarse.astype(jnp.float32)).astype(jnp.bfloat16)

    def mix(target, at, packed, kind):
        product = jnp.dot(packed[...], weights[...], preferred_element_type=jnp.float32)
        product = product[:, :lanes] + product[:, lanes:]
        for i in range(GROUP):
            target[at + i] = product[i * rows : (i + 1) * rows] * factor[kind, at + i + offset]

    for step in range(count):
        source, target = buffers[step % 2], buffers[1 - step % 2]
        begin, width = step + 1, extent - 2 * step - 2
        groups = -(-width // GROUP)
        kind = kinds[step]

        def at(i, begin=begin, width=width):
            return jnp.minimum(begin + i * GROUP, begin + width - GROUP)

        blend(source, at(0), first)
        if groups > 1:

            def body(i, carry, source=source, target=target, at=at, kind=kind):
                blend(source, at(2 * i + 1), second)
                mix(target, at(2 * i), first, kind)
                blend(source, at(2 * i + 2), first)
                mix(target, at(2 * i + 1), second, kind)
                return carry

            lax.fori_loop(0, (groups - 1) // 2, body, 0)
        if groups % 2 == 0:
            blend(source, at(groups - 1), second)
            mix(target, at(groups - 2), first, kind)
            mix(target, at(groups - 1), second, kind)
        else:
            mix(target, at(groups - 1), first, kind)
        after(step, target)


def spread_factor(columns, factor, starts, width):
    rows, lanes = factor.shape[2:]
    pair = factor.shape[1] // len(starts)
    right = (lax.broadcasted_iota(jnp.int32, (rows, lanes), 1) >= lanes // 2).astype(jnp.int32)
    for piece, start in enumerate(starts):
        for kind in range(factor.shape[0]):
            for i in range(pair):
                at = piece * width + (kind * pair + i) * 2
                factor[kind, start + i] = jnp.take_along_axis(columns, right + at, axis=1, mode="promise_in_bounds")


def early_kernel(taps, weights, across, *refs):
    pieces, stored, (middle, half_out, kept, total, factor) = refs[:5], refs[5:7], refs[7:12]
    slab, other, first, second, scratch = refs[12:]
    sec, odd = position()
    planes, rows = middle.shape[:2]
    pair = planes // 2
    reach = (slab.shape[0] - planes) // 2
    mine, others = (planes * (1 + core) for core in (odd, 1 - odd))
    starts = [reach, reach - mine, reach + mine, reach - others, reach + others]
    for piece, start in zip(pieces, starts):
        for i in range(planes):
            slab[start + i] = piece[i * rows : (i + 1) * rows]
    at = planes * rows
    steps = LEAD + stored[1].shape[0]
    own_kinds, first_kinds = (pieces[0][at + row : at + row + 1] for row in (OWN_KINDS, FIRST_KINDS))
    beside_kinds, beside_first = (pieces[3][at + row : at + row + 1] for row in (OWN_KINDS, FIRST_KINDS))
    kinds = scalars_of(jnp.where((sec == 1) | (sec == 2), beside_first, first_kinds), steps)
    kinds += scalars_of(jnp.where((sec == 1) | (sec == 2), own_kinds, beside_kinds), steps)
    last_kinds = jnp.where(sec == 0, across[:1], own_kinds)
    half_out[pair * rows :] = jnp.broadcast_to(last_kinds, (8, rows))
    width = 2 * planes * factor.shape[0]
    lines = [piece[at : at + width] for piece in pieces]
    lines.append(jnp.zeros((rows - width * len(pieces), rows), jnp.float32))
    scratch[...] = jnp.exp(-jnp.concatenate(lines, axis=0)).T
    spread_factor(reorder(scratch), factor, starts, width)
    total[...] = jnp.zeros(total.shape, jnp.float32)
    kept[...] = jnp.zeros(kept.shape, jnp.float32)

    def after(step, state):
        @pl.when(sec == step // steps)
        def _():
            j = step % steps
            source = stored[0][j] if j < LEAD else stored[1][j - LEAD]
            total[...] += state[reach : reach + planes] * source
            if j + 1 == steps:
                kept[...] = state[reach : reach + planes]

    run_steps(kinds, taps, weights, reach, slab, other, first, second, factor, 0, after)
    state = (slab, other)[reach % 2]
    middle[...] = state[reach : reach + planes]
    for i in range(pair):
        half_out[i * rows : (i + 1) * rows] = state[reach + pair * odd + i]


def late_kernel(blocks, last, taps, weights, middle, *refs):
    pieces, refs = refs[: 2 * len(blocks)], refs[2 * len(blocks) :]
    factor, kept, total_in, total_beside, series, stored = refs[0], refs[1], refs[2], refs[3], refs[4:6], refs[6:8]
    handoff, share, to_pair, to_across, to_corner = refs[8:13]
    slab, other, first, second, scratch, total, saved, whole = refs[13:]
    sec, odd = position()
    planes, rows = middle.shape[:2]
    pair = planes // 2
    reach = (slab.shape[0] - planes) // 2
    begun = (factor.shape[1] - planes) // 2
    even, uneven = (jnp.where(odd == core, pieces[0][pair * rows :], pieces[len(blocks)][pair * rows :]) for core in (0, 1))
    kinds = scalars_of(jnp.where(sec < 2, even, uneven)[:1], reach)
    slab[reach : reach + planes] = middle[...]
    for piece, start in zip(pieces, places(odd, planes, reach, blocks)):
        for i in range(pair):
            slab[start + i] = piece[i * rows : (i + 1) * rows]
    total[...] = jnp.zeros(total.shape, jnp.float32)

    @pl.when(sec == 0)
    def _():
        total[...] = total_in[...] + total_beside[...]

    saved[...] = kept[...]

    def after(step, state):
        for where, source in ((sec == 0, series), (sec == last, stored)):

            @pl.when(where)
            def _(source=source):
                part = source[0][step] if step < LEAD else source[1][step - LEAD]
                total[...] += state[reach : reach + planes] * part

    run_steps(kinds, taps, weights, reach, slab, other, first, second, factor, begun - reach, after)
    state = (slab, other)[reach % 2]

    @pl.when(sec == last)
    def _():
        saved[...] = state[reach : reach + planes]

    orients = handoff.shape[1]
    count = orients // (last + 1)
    held = planes * count
    to_corner[...] = jnp.zeros(to_corner.shape, jnp.float32)
    for i in range(planes):
        handoff[i] = from_tile(saved[i], scratch)
        whole[...] = from_tile(total[i], scratch)
        for piece, who in (
            (share, sec),
            (to_pair, sec + 1 - 2 * odd),
            (to_across, jnp.where(sec == 0, 2, 1)),
            (to_corner, last - sec),
        ):
            piece[i * count : (i + 1) * count] = whole[pl.ds(pl.multiple_of(who * count, count), count)]
    for i in range(pair):
        to_across[held + i * orients : held + (i + 1) * orients] = from_tile(state[reach + pair * odd + i], scratch)

    @pl.when(sec == 1)
    def _():
        to_corner[...] = to_across[held:]


def finish_kernel(contour, handoff_in, share, to_pair, to_across, to_corner, handoff, density):
    sec = lax.axis_index("sec")
    planes, count = density.shape[:2]
    held = planes * count
    corner = jnp.where(sec == 2, 0.0, to_corner[:held])
    total = (share[...] + to_pair[...] + to_across[:held] + corner) / contour
    for i in range(planes):
        density[i] = total[i * count : (i + 1) * count]
    handoff[0] = handoff_in[...]

    @pl.when(sec == 2)
    def _():
        orients = handoff.shape[2]
        pair = planes // 2
        for i in range(pair):
            handoff[0, i] = to_across[held + i * orients : held + (i + 1) * orients]
            handoff[0, pair + i] = to_corner[i * orients : (i + 1) * orients]


def call(kernel, out_shape, scratch, operands, dtypes=None):
    return pl.pallas_call(
        kernel,
        in_specs=[IN_VMEM] * len(operands),
        out_specs=[IN_VMEM] * len(out_shape),
        out_shape=[jax.ShapeDtypeStruct(shape, (dtypes or {}).get(i, jnp.float32)) for i, shape in enumerate(out_shape)],
        scratch_shapes=scratch,
        compiler_params=pltpu.CompilerParams(vmem_limit_bytes=VMEM_BYTES),
    )(*operands)


def paired(incoming, backward, fields, block_types, axial_taps, lateral_taps, depth_taps, bend_diagonal, bend_coupling):
    n_sec, n_gx = lax.axis_size("sec"), lax.axis_size("gx")
    steps, planes, orients, cells = backward.shape
    pair = planes // 2
    reach = (TICKS - 1) * steps, steps
    near = (1, -1)
    rows = 2 * orients
    lanes = cells // 2
    last = n_sec - 1

    def send(array, by_sec, even=0, odd=0):
        by_sec = by_sec.items() if isinstance(by_sec, dict) else enumerate(by_sec)
        pairs = [
            (s * n_gx + g, t * n_gx + (g + (odd if s % 2 else even)) % n_gx) for s, t in by_sec for g in range(n_gx)
        ]
        return lax.ppermute(array, ("sec", "gx"), pairs)

    same, beside = (0, 1, 2, 3), (1, 0, 3, 2)
    moved = send(incoming[0], {0: 1, 1: 3})
    lead, bundle = launch(
        incoming, backward, fields, block_types, axial_taps, lateral_taps, depth_taps, bend_diagonal, bend_coupling
    )
    types = jnp.pad(block_types.astype(jnp.float32), ((0, 7), (0, lanes - steps)))
    types = send(types, {1: 3})
    lead = send(lead, {2: 0})
    size = planes * rows + FIELD_ROWS
    base, taps, weights = call(
        unpack_kernel, [(size, lanes), (TAP_ROWS, lanes), (2 * rows, 2 * lanes)], [], [bundle], {2: jnp.bfloat16}
    )
    moved, base, types = lax.optimization_barrier((moved, base, types))
    passed = send(moved, {3: 2})

    tile = pltpu.VMEM((rows, lanes), jnp.float32)
    packed = pltpu.VMEM((GROUP * rows, 2 * lanes), jnp.bfloat16)
    inner = pltpu.VMEM((planes, rows, lanes), jnp.float32)

    def work(extent):
        slab = pltpu.VMEM((planes + 2 * extent, rows, lanes), jnp.float32)
        return [slab, slab, packed, packed, tile]

    (piece,) = call(pack_kernel, [(size, lanes)], [tile], [base, moved, passed, types])
    own = [send(piece, same, shift, 2 * shift) for shift in near]
    backward, _ = lax.optimization_barrier((backward, piece))
    *stored, lead, across = call(
        turn_kernel,
        [(count, planes, rows, lanes) for count in (LEAD, steps - LEAD, LEAD)] + [(8, lanes)],
        [tile],
        [backward, lead],
    )
    own[-1], *stored = lax.optimization_barrier((own[-1], *stored))
    swapped = [send(each, beside) for each in own]
    late_stored, *swapped = lax.optimization_barrier((stored[1], *swapped))
    late_last = send(late_stored, {2: 0})
    middle, piece, kept, total, factor = call(
        early_kernel,
        [(planes, rows, lanes), (pair * rows + 8, lanes), (planes, rows, lanes), (planes, rows, lanes)]
        + [(fields.shape[0], planes + 2 * reach[0], rows, lanes)],
        work(reach[0]),
        [taps, weights, across, piece, *own, *swapped, *stored],
    )
    own = [send(piece, same, shift, shift) for shift in near]
    beside_total = send(total, beside)
    swapped = [send(each, beside) for each in own]
    held = planes * (orients // n_sec)
    handoff, share, to_pair, to_across, to_corner = call(
        functools.partial(late_kernel, tuple(-shift for shift in near), last),
        [(planes, orients, cells)]
        + [(held, cells)] * 2
        + [(held + pair * orients, cells), (pair * orients, cells)],
        work(reach[1]) + [inner, inner, pltpu.VMEM((orients, cells), jnp.float32)],
        [taps, weights, middle, *own, *swapped, factor, kept, total, beside_total]
        + [lead, late_last, *stored],
    )
    to_pair = send(to_pair, beside)
    to_across = send(to_across, (2, 0, 3, 1))
    to_corner = send(to_corner, (3, 2, 1, 0))
    handoff, density = call(
        functools.partial(finish_kernel, n_sec * steps),
        [(1,) + handoff.shape, (planes, orients // n_sec, cells)],
        [],
        [handoff, share, to_pair, to_across, to_corner],
    )
    return handoff, density


def pairs_fit(n_sec, planes, steps, orients, cells, kinds):
    return (
        n_sec == TICKS + 1 == 4
        and planes == steps
        and planes % 2 == 0
        and 2 * orients == 2 * CZ == cells // 2 == 128
        and 2 * kinds * planes <= OWN_KINDS and 10 * kinds * planes <= 2 * orients
        and GROUP < 2 * planes
    )


def solution(mesh):
    in_specs = (
        P("sec", "gx", None, None),
        P("sec", "gx", None, None),
        P(None, "gx", None),
        P("sec", None),
        P(),
        P(),
        P(),
        P(),
        P(),
    )
    out_specs = (P("sec", "gx", None, None), P("gx", "sec", None))

    def body(incoming, backward, fields, *rest):
        steps, planes, orients, cells = backward.shape
        fits = pairs_fit(mesh.shape["sec"], planes, steps, orients, cells, fields.shape[0])
        return (paired if fits else per_device)(incoming, backward, fields, *rest)

    return jax.shard_map(body, mesh=mesh, in_specs=in_specs, out_specs=out_specs, check_vma=False)
```

```python
import functools

import jax
import jax.numpy as jnp
from jax import lax
from jax.experimental import pallas as pl
from jax.experimental.pallas import tpu as pltpu
from jax.sharding import PartitionSpec as P

TICKS = 3
CZ = 64
GROUP = 6
FIELD_ROWS = 32
TAP_ROWS = 8
OWN_KINDS, FIRST_KINDS = 24, 25
LEAD = 1
VMEM_BYTES = 16 * 2**20
WHOLE_VMEM_BYTES = 62 * 2**20
IN_VMEM = pl.BlockSpec(memory_space=pltpu.VMEM)


def padded_2(block, sides, width):
    for axis, dim in sides:
        count = lax.axis_size(axis)
        forward = [(i, i + 1) for i in range(count - 1)]
        forward.append((count - 1, 0))
        backward = [(target, source) for source, target in forward]
        low = lax.ppermute(
            lax.slice_in_dim(block, block.shape[dim] - width, None, axis=dim), axis, forward
        )
        high = lax.ppermute(lax.slice_in_dim(block, 0, width, axis=dim), axis, backward)
        block = jnp.concatenate([low, block, high], axis=dim)
    return block


def from_behind(array, axis, by):
    length = lax.axis_size(axis)
    pairs = [(i, i + by) for i in range(length) if 0 <= i + by < length]
    return lax.ppermute(array, axis, pairs)


def boltzmann(fields, kinds):
    selector = kinds == jnp.arange(fields.shape[0], dtype=jnp.int32)
    chosen = jnp.sum(jnp.where(selector[:, None, None], fields, jnp.zeros_like(fields)), axis=0)
    return jnp.exp(-chosen)


def column(taps, which):
    return taps[which][None, :, None]


def advance_padded(padded, factor, axial_taps, lateral_taps, depth_taps, kernel):
    along_x = (
        column(axial_taps, 0) * padded[:-2]
        + column(axial_taps, 1) * padded[1:-1]
        + column(axial_taps, 2) * padded[2:]
    )
    along_y = (
        column(lateral_taps, 0) * jnp.roll(along_x, CZ, axis=2)
        + column(lateral_taps, 1) * along_x
        + column(lateral_taps, 2) * jnp.roll(along_x, -CZ, axis=2)
    )
    depth_pos = (jnp.arange(along_y.shape[2], dtype=jnp.int32) % CZ)[None, None, :]
    behind = jnp.where(
        depth_pos == 0, jnp.roll(along_y, -(CZ - 1), axis=2), jnp.roll(along_y, 1, axis=2)
    )
    ahead = jnp.where(
        depth_pos == CZ - 1, jnp.roll(along_y, CZ - 1, axis=2), jnp.roll(along_y, -1, axis=2)
    )
    along_z = (
        column(depth_taps, 0) * behind
        + column(depth_taps, 1) * along_y
        + column(depth_taps, 2) * ahead
    )
    blended = jnp.einsum(
        "uv,xvc->xuc",
        kernel,
        along_z,
        precision=lax.Precision.HIGHEST,
        preferred_element_type=jnp.float32,
    )
    return blended * factor[:, None, :]


def per_device(
    incoming,
    backward,
    fields,
    block_types,
    axial_taps,
    lateral_taps,
    depth_taps,
    bend_diagonal,
    bend_coupling,
):
    kernel = jnp.diag(bend_diagonal) + bend_coupling
    steps_each = block_types.shape[1]
    planes = incoming.shape[1]
    start = incoming[0]
    first_section = lax.axis_index("sec") == 0
    wide_fields = padded_2(fields, (("gx", 1),), steps_each)
    factors = [boltzmann(wide_fields, block_types[0, position]) for position in range(steps_each)]
    current = start
    outgoing = start
    accumulated = jnp.zeros(start.shape, jnp.float32)
    for tick_index in range(TICKS):
        final_tick = tick_index + 1 == TICKS
        extended = padded_2(current, (("gx", 0),), steps_each)
        for position in range(steps_each):
            margin = steps_each - position - 1
            offset = steps_each - margin
            factor = factors[position][offset : offset + planes + 2 * margin]
            extended = advance_padded(
                extended, factor, axial_taps, lateral_taps, depth_taps, kernel
            )
            if final_tick:
                accumulated = accumulated + extended[margin : margin + planes] * backward[
                    position
                ].astype(jnp.float32)
        outgoing = extended
        if not final_tick:
            shifted = from_behind(outgoing, "sec", 1)
            current = jnp.where(first_section, start, shifted)
    reduced = lax.psum_scatter(accumulated, "sec", scatter_dimension=1, tiled=True)
    density = reduced / (lax.axis_size("sec") * steps_each)
    return (outgoing[None], density)


def to_tile(plane, scratch):
    half = plane.shape[1] // 2
    scratch[...] = jnp.concatenate([plane[:, :half], plane[:, half:]], axis=0).T
    return reorder(scratch)


def reorder(scratch):
    rows = scratch.shape[0]
    return jnp.concatenate(
        [scratch[pl.ds(yl * CZ + zl, 8, stride=8), :] for yl in range(rows // CZ) for zl in range(CZ // 8)], axis=0
    )


def from_tile(tile, scratch):
    rows = tile.shape[0]
    for yl in range(rows // CZ):
        for zl in range(CZ // 8):
            at = (yl * (CZ // 8) + zl) * 8
            scratch[pl.ds(yl * CZ + zl, 8, stride=8), :] = tile[at : at + 8]
    turned = scratch[...].T
    half = turned.shape[0] // 2
    return jnp.concatenate([turned[:half], turned[half:]], axis=1)


def stencil(behind, here, ahead, taps):
    a = here + taps[0] * behind + taps[1] * ahead
    low, high = a[:CZ], a[CZ:]
    low_turned = pltpu.roll(low, a.shape[1] // 2, 1)
    high_turned = pltpu.roll(high, a.shape[1] // 2, 1)
    out = []
    for b in (
        low + taps[2] * high_turned + taps[3] * high,
        high + taps[2] * low + taps[3] * low_turned,
    ):
        back = jnp.concatenate([pltpu.roll(b[-8:], 1, 0), b[:-8]], axis=0)
        front = jnp.concatenate([b[8:], pltpu.roll(b[:8], 7, 0)], axis=0)
        out.append(b + taps[4] * back + taps[5] * front)
    return jnp.concatenate(out, axis=0)


def position():
    sec = lax.axis_index("sec")
    return sec, lax.rem(sec, 2)


def launch_kernel(*refs):
    sources, (lead, bundle) = refs[:9], refs[9:11]
    scratch, copies, sems = refs[11], refs[12:21], refs[21]
    moves = [
        pltpu.make_async_copy(source.at[pl.ds(0, copy.shape[0])], copy, sems.at[i])
        for i, (source, copy) in enumerate(zip(sources, copies))
    ]
    for move in moves:
        move.start()
    incoming, stored, fields, kinds, axial, lateral, depth, diagonal, coupling = copies
    for move in moves[2:]:
        move.wait()
    rows = scratch.shape[0]
    orients = rows // 2
    ratios = [each[w : w + 1] / each[1:2] for each in (axial, lateral, depth) for w in (0, 2)]
    for i, ratio in enumerate(ratios + ratios[:2]):
        bundle[i : i + 1] = jnp.concatenate([ratio, ratio], axis=1)
    square = (orients, orients)
    same = lax.broadcasted_iota(jnp.int32, square, 0) == lax.broadcasted_iota(jnp.int32, square, 1)
    kernel = jnp.where(same, diagonal[...], 0.0) + coupling[...]
    kernel = kernel * (axial[1:2] * lateral[1:2] * depth[1:2])
    upper = jnp.concatenate([kernel, jnp.zeros_like(kernel)], axis=1)
    bundle[TAP_ROWS : TAP_ROWS + rows] = jnp.concatenate([upper, pltpu.roll(upper, orients, 1)], axis=0).T
    line = kinds[...].astype(jnp.float32)
    line = jnp.concatenate([line, jnp.zeros((1, rows - line.shape[1]), jnp.float32)], axis=1)
    types = line
    planes = incoming.shape[1]
    at = TAP_ROWS + rows
    bundle[at : at + FIELD_ROWS] = jnp.zeros((FIELD_ROWS, rows), jnp.float32)
    for kind in range(fields.shape[0]):
        for i in range(planes):
            line = fields[kind, i : i + 1, :]
            here = at + (kind * planes + i) * 2
            bundle[here : here + 1] = line[:, :rows]
            bundle[here + 1 : here + 2] = line[:, rows:]
    bundle[at + OWN_KINDS : at + OWN_KINDS + 1] = types
    moves[0].wait()
    for i in range(planes):
        here = at + FIELD_ROWS + i * rows
        bundle[here : here + rows] = to_tile(incoming[0, i], scratch)
    moves[1].wait()
    for step in range(LEAD):
        for i in range(planes):
            here = (step * planes + i) * orients
            lead[here : here + orients] = stored[step, i].astype(jnp.float32)
    lead[lead.shape[0] - 8 :] = jnp.broadcast_to(jnp.concatenate([types, types], axis=1), (8, lead.shape[1]))


def launch(incoming, backward, fields, kinds, axial, lateral, depth, diagonal, coupling):
    planes, orients, cells = backward.shape[1:]
    rows = 2 * orients
    operands = [incoming, backward, fields, kinds, axial, lateral, depth, diagonal.reshape(1, -1), coupling]
    shapes = [(LEAD * planes * orients + 8, cells), (TAP_ROWS + rows + FIELD_ROWS + planes * rows, rows)]
    taken = [(LEAD,) + each.shape[1:] if i == 1 else each.shape for i, each in enumerate(operands)]
    return pl.pallas_call(
        launch_kernel,
        in_specs=[pl.BlockSpec(memory_space=pltpu.HBM)] * len(operands),
        out_specs=[IN_VMEM] * len(shapes),
        out_shape=[jax.ShapeDtypeStruct(shape, jnp.float32) for shape in shapes],
        scratch_shapes=[pltpu.VMEM((rows, rows), jnp.float32)]
        + [pltpu.VMEM(shape, each.dtype) for shape, each in zip(taken, operands)]
        + [pltpu.SemaphoreType.DMA((len(operands),))],
        compiler_params=pltpu.CompilerParams(vmem_limit_bytes=WHOLE_VMEM_BYTES),
    )(*operands)


def turn_kernel(backward, lead, early, late, out, across, scratch):
    orients = scratch.shape[0] // 2
    across[...] = lead[lead.shape[0] - 8 :, : scratch.shape[1]]
    for target, begin in ((early, 0), (late, LEAD)):
        for step in range(target.shape[0]):
            for i in range(target.shape[1]):
                target[step, i] = to_tile(backward[begin + step, i].astype(jnp.float32), scratch)
    for step in range(out.shape[0]):
        for i in range(out.shape[1]):
            here = (step * out.shape[1] + i) * orients
            out[step, i] = to_tile(lead[here : here + orients], scratch)


def unpack_kernel(bundle, out, taps, weights):
    rows = taps.shape[1]
    taps[...] = bundle[:TAP_ROWS]
    twice = bundle[TAP_ROWS : TAP_ROWS + rows]
    coarse = twice.astype(jnp.bfloat16)
    fine = (twice - coarse.astype(jnp.float32)).astype(jnp.bfloat16)
    weights[...] = jnp.concatenate(
        [jnp.concatenate([coarse, fine], axis=1), jnp.concatenate([coarse, jnp.zeros_like(fine)], axis=1)], axis=0
    )
    at = out.shape[0] - FIELD_ROWS
    lines = TAP_ROWS + rows
    out[at:] = bundle[lines : lines + FIELD_ROWS]
    out[:at] = bundle[lines + FIELD_ROWS :]


def pack_kernel(base, moved, passed, types, out, scratch):
    sec, odd = position()
    rows = scratch.shape[0]
    at = out.shape[0] - FIELD_ROWS
    out[at:] = base[at:]
    out[at + FIRST_KINDS : at + FIRST_KINDS + 1] = jnp.where(
        sec == 0, base[at + OWN_KINDS : at + OWN_KINDS + 1], types[:1]
    )

    @pl.when(sec == 0)
    def _():
        out[:at] = base[:at]

    def fill(source):
        for i in range(source.shape[0]):
            out[i * rows : (i + 1) * rows] = to_tile(source[i], scratch)

    pl.when(odd == 1)(lambda: fill(moved))
    pl.when((sec > 0) & (odd == 0))(lambda: fill(passed))


def scalars_of(row, count):
    lane = lax.broadcasted_iota(jnp.int32, row.shape, 1)
    return [jnp.sum(jnp.where(lane == i, row, 0.0)).astype(jnp.int32) for i in range(count)]


def places(odd, planes, reach, blocks):
    return [reach + block * planes + planes // 2 * core for core in (odd, 1 - odd) for block in blocks]


def run_steps(kinds, taps, weights, count, slab, other, first, second, factor, offset, after):
    tap = [taps[i : i + 1, :] for i in range(6)]
    extent, rows, lanes = slab.shape
    buffers = (slab, other)

    def blend(source, at, packed):
        for i in range(GROUP):
            e = stencil(source[at + i - 1], source[at + i], source[at + i + 1], tap)
            coarse = e.astype(jnp.bfloat16)
            packed[i * rows : (i + 1) * rows, :lanes] = coarse
            packed[i * rows : (i + 1) * rows, lanes:] = (e - coarse.astype(jnp.float32)).astype(jnp.bfloat16)

    def mix(target, at, packed, kind):
        product = jnp.dot(packed[...], weights[...], preferred_element_type=jnp.float32)
        product = product[:, :lanes] + product[:, lanes:]
        for i in range(GROUP):
            target[at + i] = product[i * rows : (i + 1) * rows] * factor[kind, at + i + offset]

    for step in range(count):
        source, target = buffers[step % 2], buffers[1 - step % 2]
        begin, width = step + 1, extent - 2 * step - 2
        groups = -(-width // GROUP)
        kind = kinds[step]

        def at(i, begin=begin, width=width):
            return jnp.minimum(begin + i * GROUP, begin + width - GROUP)

        blend(source, at(0), first)
        if groups > 1:

            def body(i, carry, source=source, target=target, at=at, kind=kind):
                blend(source, at(2 * i + 1), second)
                mix(target, at(2 * i), first, kind)
                blend(source, at(2 * i + 2), first)
                mix(target, at(2 * i + 1), second, kind)
                return carry

            lax.fori_loop(0, (groups - 1) // 2, body, 0)
        if groups % 2 == 0:
            blend(source, at(groups - 1), second)
            mix(target, at(groups - 2), first, kind)
            mix(target, at(groups - 1), second, kind)
        else:
            mix(target, at(groups - 1), first, kind)
        after(step, target)


def spread_factor(columns, factor, starts, width):
    rows, lanes = factor.shape[2:]
    pair = width // (2 * factor.shape[0])
    right = (lax.broadcasted_iota(jnp.int32, (rows, lanes), 1) >= lanes // 2).astype(jnp.int32)
    for piece, start in enumerate(starts):
        for kind in range(factor.shape[0]):
            for i in range(pair):
                at = piece * width + (kind * pair + i) * 2
                factor[kind, start + i] = jnp.take_along_axis(columns, right + at, axis=1, mode="promise_in_bounds")


def slab_starts(planes, reach):
    odd = position()[1]
    mine, others = (planes * (1 + core) for core in (odd, 1 - odd))
    return [reach, reach - mine, reach + mine, reach - others, reach + others]


def fill_factor(pieces, starts, factor, scratch):
    rows = scratch.shape[0]
    planes = (pieces[0].shape[0] - FIELD_ROWS) // rows
    width = 2 * planes * factor.shape[0]
    lines = [piece[planes * rows : planes * rows + width] for piece in pieces]
    lines.append(jnp.zeros((rows - width * len(pieces), rows), jnp.float32))
    scratch[...] = jnp.exp(-jnp.concatenate(lines, axis=0)).T
    spread_factor(reorder(scratch), factor, starts, width)


def factor_kernel(*refs):
    pieces, factor, scratch = refs[:3], refs[3], refs[4]
    planes = (pieces[0].shape[0] - FIELD_ROWS) // scratch.shape[0]
    fill_factor(pieces, slab_starts(planes, (factor.shape[1] - planes) // 2)[:3], factor, scratch)


def early_kernel(taps, weights, across, *refs):
    pieces, stored, (middle, half_out, kept, total, factor) = refs[:5], refs[5:7], refs[8:13]
    slab, other, first, second, scratch = refs[13:]
    sec, odd = position()
    planes, rows = middle.shape[:2]
    pair = planes // 2
    reach = (slab.shape[0] - planes) // 2
    starts = slab_starts(planes, reach)
    for piece, start in zip(pieces, starts):
        for i in range(planes):
            slab[start + i] = piece[i * rows : (i + 1) * rows]
    at = planes * rows
    steps = LEAD + stored[1].shape[0]
    own_kinds, first_kinds = (pieces[0][at + row : at + row + 1] for row in (OWN_KINDS, FIRST_KINDS))
    beside_kinds, beside_first = (pieces[3][at + row : at + row + 1] for row in (OWN_KINDS, FIRST_KINDS))
    kinds = scalars_of(jnp.where((sec == 1) | (sec == 2), beside_first, first_kinds), steps)
    kinds += scalars_of(jnp.where((sec == 1) | (sec == 2), own_kinds, beside_kinds), steps)
    last_kinds = jnp.where(sec == 0, across[:1], own_kinds)
    half_out[pair * rows :] = jnp.broadcast_to(last_kinds, (8, rows))
    fill_factor(pieces[3:], starts[3:], factor, scratch)
    total[...] = jnp.zeros(total.shape, jnp.float32)
    kept[...] = jnp.zeros(kept.shape, jnp.float32)

    def after(step, state):
        @pl.when(sec == step // steps)
        def _():
            j = step % steps
            source = stored[0][j] if j < LEAD else stored[1][j - LEAD]
            total[...] += state[reach : reach + planes] * source
            if j + 1 == steps:
                kept[...] = state[reach : reach + planes]

    run_steps(kinds, taps, weights, reach, slab, other, first, second, factor, 0, after)
    state = (slab, other)[reach % 2]
    middle[...] = state[reach : reach + planes]
    for i in range(pair):
        half_out[i * rows : (i + 1) * rows] = state[reach + pair * odd + i]


def late_kernel(blocks, last, taps, weights, middle, *refs):
    pieces, refs = refs[: 2 * len(blocks)], refs[2 * len(blocks) :]
    factor, kept, total_in, total_beside, series, stored = refs[0], refs[1], refs[2], refs[3], refs[4:6], refs[6:8]
    handoff, share, to_pair, to_across, to_corner = refs[8:13]
    slab, other, first, second, scratch, total, saved, whole = refs[13:]
    sec, odd = position()
    planes, rows = middle.shape[:2]
    pair = planes // 2
    reach = (slab.shape[0] - planes) // 2
    begun = (factor.shape[1] - planes) // 2
    even, uneven = (jnp.where(odd == core, pieces[0][pair * rows :], pieces[len(blocks)][pair * rows :]) for core in (0, 1))
    kinds = scalars_of(jnp.where(sec < 2, even, uneven)[:1], reach)
    slab[reach : reach + planes] = middle[...]
    for piece, start in zip(pieces, places(odd, planes, reach, blocks)):
        for i in range(pair):
            slab[start + i] = piece[i * rows : (i + 1) * rows]
    total[...] = jnp.zeros(total.shape, jnp.float32)

    @pl.when(sec == 0)
    def _():
        total[...] = total_in[...] + total_beside[...]

    saved[...] = kept[...]

    def after(step, state):
        for where, source in ((sec == 0, series), (sec == last, stored)):

            @pl.when(where)
            def _(source=source):
                part = source[0][step] if step < LEAD else source[1][step - LEAD]
                total[...] += state[reach : reach + planes] * part

    run_steps(kinds, taps, weights, reach, slab, other, first, second, factor, begun - reach, after)
    state = (slab, other)[reach % 2]

    @pl.when(sec == last)
    def _():
        saved[...] = state[reach : reach + planes]

    orients = handoff.shape[1]
    count = orients // (last + 1)
    held = planes * count
    to_corner[...] = jnp.zeros(to_corner.shape, jnp.float32)
    for i in range(planes):
        handoff[i] = from_tile(saved[i], scratch)
        whole[...] = from_tile(total[i], scratch)
        for piece, who in (
            (share, sec),
            (to_pair, sec + 1 - 2 * odd),
            (to_across, jnp.where(sec == 0, 2, 1)),
            (to_corner, last - sec),
        ):
            piece[i * count : (i + 1) * count] = whole[pl.ds(pl.multiple_of(who * count, count), count)]
    for i in range(pair):
        to_across[held + i * orients : held + (i + 1) * orients] = from_tile(state[reach + pair * odd + i], scratch)

    @pl.when(sec == 1)
    def _():
        to_corner[...] = to_across[held:]


def finish_kernel(contour, handoff_in, share, to_pair, to_across, to_corner, handoff, density):
    sec = lax.axis_index("sec")
    planes, count = density.shape[:2]
    held = planes * count
    corner = jnp.where(sec == 2, 0.0, to_corner[:held])
    total = (share[...] + to_pair[...] + to_across[:held] + corner) / contour
    for i in range(planes):
        density[i] = total[i * count : (i + 1) * count]
    handoff[0] = handoff_in[...]

    @pl.when(sec == 2)
    def _():
        orients = handoff.shape[2]
        pair = planes // 2
        for i in range(pair):
            handoff[0, i] = to_across[held + i * orients : held + (i + 1) * orients]
            handoff[0, pair + i] = to_corner[i * orients : (i + 1) * orients]


def call(kernel, out_shape, scratch, operands, dtypes=None, aliases=None, cost=None):
    return pl.pallas_call(
        kernel,
        in_specs=[IN_VMEM] * len(operands),
        out_specs=[IN_VMEM] * len(out_shape),
        out_shape=[jax.ShapeDtypeStruct(shape, (dtypes or {}).get(i, jnp.float32)) for i, shape in enumerate(out_shape)],
        scratch_shapes=scratch,
        input_output_aliases=aliases or {},
        cost_estimate=cost,
        compiler_params=pltpu.CompilerParams(vmem_limit_bytes=VMEM_BYTES),
    )(*operands)


def paired(incoming, backward, fields, block_types, axial_taps, lateral_taps, depth_taps, bend_diagonal, bend_coupling):
    n_sec, n_gx = lax.axis_size("sec"), lax.axis_size("gx")
    steps, planes, orients, cells = backward.shape
    pair = planes // 2
    reach = (TICKS - 1) * steps, steps
    near = (1, -1)
    rows = 2 * orients
    lanes = cells // 2
    last = n_sec - 1

    def send(array, by_sec, even=0, odd=0):
        by_sec = by_sec.items() if isinstance(by_sec, dict) else enumerate(by_sec)
        pairs = [
            (s * n_gx + g, t * n_gx + (g + (odd if s % 2 else even)) % n_gx) for s, t in by_sec for g in range(n_gx)
        ]
        return lax.ppermute(array, ("sec", "gx"), pairs)

    same, beside = (0, 1, 2, 3), (1, 0, 3, 2)
    moved = send(incoming[0], {0: 1, 1: 3})
    lead, bundle = launch(
        incoming, backward, fields, block_types, axial_taps, lateral_taps, depth_taps, bend_diagonal, bend_coupling
    )
    types = jnp.pad(block_types.astype(jnp.float32), ((0, 7), (0, lanes - steps)))
    types = send(types, {1: 3})
    lead = send(lead, {2: 0})
    size = planes * rows + FIELD_ROWS
    base, taps, weights = call(
        unpack_kernel, [(size, lanes), (TAP_ROWS, lanes), (2 * rows, 2 * lanes)], [], [bundle], {2: jnp.bfloat16}
    )
    moved, base, types = lax.optimization_barrier((moved, base, types))
    passed = send(moved, {3: 2})

    tile = pltpu.VMEM((rows, lanes), jnp.float32)
    packed = pltpu.VMEM((GROUP * rows, 2 * lanes), jnp.bfloat16)
    inner = pltpu.VMEM((planes, rows, lanes), jnp.float32)

    def work(extent):
        slab = pltpu.VMEM((planes + 2 * extent, rows, lanes), jnp.float32)
        return [slab, slab, packed, packed, tile]

    (piece,) = call(pack_kernel, [(size, lanes)], [tile], [base, moved, passed, types])
    own = [send(piece, same, shift, 2 * shift) for shift in near]
    backward, _ = lax.optimization_barrier((backward, piece))
    *stored, lead, across = call(
        turn_kernel,
        [(count, planes, rows, lanes) for count in (LEAD, steps - LEAD, LEAD)] + [(8, lanes)],
        [tile],
        [backward, lead],
    )
    own[-1], *stored = lax.optimization_barrier((own[-1], *stored))
    swapped = [send(each, beside) for each in own]
    table = (fields.shape[0], planes + 2 * reach[0], rows, lanes)
    known, swapped[1] = lax.optimization_barrier((piece, swapped[1]))
    (factor,) = call(factor_kernel, [table], [tile], [known, *own])
    late_stored, factor, *swapped = lax.optimization_barrier((stored[1], factor, *swapped))
    late_last = send(late_stored, {2: 0})
    middle, piece, kept, total, factor = call(
        early_kernel,
        [(planes, rows, lanes), (pair * rows + 8, lanes), (planes, rows, lanes), (planes, rows, lanes)]
        + [table],
        work(reach[0]),
        [taps, weights, across, piece, *own, *swapped, *stored, factor],
        aliases={10: 4},
    )
    own = [send(piece, same, shift, shift) for shift in near]
    beside_total = send(total, beside)
    swapped = [send(each, beside) for each in own]
    held = planes * (orients // n_sec)
    handoff, share, to_pair, to_across, to_corner = call(
        functools.partial(late_kernel, tuple(-shift for shift in near), last),
        [(planes, orients, cells)]
        + [(held, cells)] * 2
        + [(held + pair * orients, cells), (pair * orients, cells)],
        work(reach[1]) + [inner, inner, pltpu.VMEM((orients, cells), jnp.float32)],
        [taps, weights, middle, *own, *swapped, factor, kept, total, beside_total]
        + [lead, late_last, *stored],
    )
    to_pair = send(to_pair, beside)
    to_across = send(to_across, (2, 0, 3, 1))
    to_corner = send(to_corner, (3, 2, 1, 0))
    handoff, density = call(
        functools.partial(finish_kernel, n_sec * steps),
        [(1,) + handoff.shape, (planes, orients // n_sec, cells)],
        [],
        [handoff, share, to_pair, to_across, to_corner],
    )
    return handoff, density


def pairs_fit(n_sec, planes, steps, orients, cells, kinds):
    return (
        n_sec == TICKS + 1 == 4
        and planes == steps
        and planes % 2 == 0
        and 2 * orients == 2 * CZ == cells // 2 == 128
        and 2 * kinds * planes <= OWN_KINDS and 10 * kinds * planes <= 2 * orients
        and GROUP < 2 * planes
    )


def solution(mesh):
    in_specs = (
        P("sec", "gx", None, None),
        P("sec", "gx", None, None),
        P(None, "gx", None),
        P("sec", None),
        P(),
        P(),
        P(),
        P(),
        P(),
    )
    out_specs = (P("sec", "gx", None, None), P("gx", "sec", None))

    def body(incoming, backward, fields, *rest):
        steps, planes, orients, cells = backward.shape
        fits = pairs_fit(mesh.shape["sec"], planes, steps, orients, cells, fields.shape[0])
        return (paired if fits else per_device)(incoming, backward, fields, *rest)

    return jax.shard_map(body, mesh=mesh, in_specs=in_specs, out_specs=out_specs, check_vma=False)
```

```python
import functools

import jax
import jax.numpy as jnp
from jax import lax
from jax.experimental import pallas as pl
from jax.experimental.pallas import tpu as pltpu
from jax.sharding import PartitionSpec as P

TICKS = 3
CZ = 64
GROUP = 6
FIELD_ROWS = 32
TAP_ROWS = 8
OWN_KINDS, FIRST_KINDS = 24, 25
LEAD = 1
VMEM_BYTES = 16 * 2**20
WHOLE_VMEM_BYTES = 62 * 2**20
IN_VMEM = pl.BlockSpec(memory_space=pltpu.VMEM)


def padded_2(block, sides, width):
    for axis, dim in sides:
        count = lax.axis_size(axis)
        forward = [(i, i + 1) for i in range(count - 1)]
        forward.append((count - 1, 0))
        backward = [(target, source) for source, target in forward]
        low = lax.ppermute(
            lax.slice_in_dim(block, block.shape[dim] - width, None, axis=dim), axis, forward
        )
        high = lax.ppermute(lax.slice_in_dim(block, 0, width, axis=dim), axis, backward)
        block = jnp.concatenate([low, block, high], axis=dim)
    return block


def from_behind(array, axis, by):
    length = lax.axis_size(axis)
    pairs = [(i, i + by) for i in range(length) if 0 <= i + by < length]
    return lax.ppermute(array, axis, pairs)


def boltzmann(fields, kinds):
    selector = kinds == jnp.arange(fields.shape[0], dtype=jnp.int32)
    chosen = jnp.sum(jnp.where(selector[:, None, None], fields, jnp.zeros_like(fields)), axis=0)
    return jnp.exp(-chosen)


def column(taps, which):
    return taps[which][None, :, None]


def advance_padded(padded, factor, axial_taps, lateral_taps, depth_taps, kernel):
    along_x = (
        column(axial_taps, 0) * padded[:-2]
        + column(axial_taps, 1) * padded[1:-1]
        + column(axial_taps, 2) * padded[2:]
    )
    along_y = (
        column(lateral_taps, 0) * jnp.roll(along_x, CZ, axis=2)
        + column(lateral_taps, 1) * along_x
        + column(lateral_taps, 2) * jnp.roll(along_x, -CZ, axis=2)
    )
    depth_pos = (jnp.arange(along_y.shape[2], dtype=jnp.int32) % CZ)[None, None, :]
    behind = jnp.where(
        depth_pos == 0, jnp.roll(along_y, -(CZ - 1), axis=2), jnp.roll(along_y, 1, axis=2)
    )
    ahead = jnp.where(
        depth_pos == CZ - 1, jnp.roll(along_y, CZ - 1, axis=2), jnp.roll(along_y, -1, axis=2)
    )
    along_z = (
        column(depth_taps, 0) * behind
        + column(depth_taps, 1) * along_y
        + column(depth_taps, 2) * ahead
    )
    blended = jnp.einsum(
        "uv,xvc->xuc",
        kernel,
        along_z,
        precision=lax.Precision.HIGHEST,
        preferred_element_type=jnp.float32,
    )
    return blended * factor[:, None, :]


def per_device(
    incoming,
    backward,
    fields,
    block_types,
    axial_taps,
    lateral_taps,
    depth_taps,
    bend_diagonal,
    bend_coupling,
):
    kernel = jnp.diag(bend_diagonal) + bend_coupling
    steps_each = block_types.shape[1]
    planes = incoming.shape[1]
    start = incoming[0]
    first_section = lax.axis_index("sec") == 0
    wide_fields = padded_2(fields, (("gx", 1),), steps_each)
    factors = [boltzmann(wide_fields, block_types[0, position]) for position in range(steps_each)]
    current = start
    outgoing = start
    accumulated = jnp.zeros(start.shape, jnp.float32)
    for tick_index in range(TICKS):
        final_tick = tick_index + 1 == TICKS
        extended = padded_2(current, (("gx", 0),), steps_each)
        for position in range(steps_each):
            margin = steps_each - position - 1
            offset = steps_each - margin
            factor = factors[position][offset : offset + planes + 2 * margin]
            extended = advance_padded(
                extended, factor, axial_taps, lateral_taps, depth_taps, kernel
            )
            if final_tick:
                accumulated = accumulated + extended[margin : margin + planes] * backward[
                    position
                ].astype(jnp.float32)
        outgoing = extended
        if not final_tick:
            shifted = from_behind(outgoing, "sec", 1)
            current = jnp.where(first_section, start, shifted)
    reduced = lax.psum_scatter(accumulated, "sec", scatter_dimension=1, tiled=True)
    density = reduced / (lax.axis_size("sec") * steps_each)
    return (outgoing[None], density)


def to_tile(plane, scratch):
    half = plane.shape[1] // 2
    scratch[...] = jnp.concatenate([plane[:, :half], plane[:, half:]], axis=0).T
    return reorder(scratch)


def reorder(scratch):
    rows = scratch.shape[0]
    return jnp.concatenate(
        [scratch[pl.ds(yl * CZ + zl, 8, stride=8), :] for yl in range(rows // CZ) for zl in range(CZ // 8)], axis=0
    )


def from_tile(tile, scratch):
    rows = tile.shape[0]
    for yl in range(rows // CZ):
        for zl in range(CZ // 8):
            at = (yl * (CZ // 8) + zl) * 8
            scratch[pl.ds(yl * CZ + zl, 8, stride=8), :] = tile[at : at + 8]
    turned = scratch[...].T
    half = turned.shape[0] // 2
    return jnp.concatenate([turned[:half], turned[half:]], axis=1)


def stencil(behind, here, ahead, taps):
    a = here + taps[0] * behind + taps[1] * ahead
    low, high = a[:CZ], a[CZ:]
    low_turned = pltpu.roll(low, a.shape[1] // 2, 1)
    high_turned = pltpu.roll(high, a.shape[1] // 2, 1)
    out = []
    for b in (
        low + taps[2] * high_turned + taps[3] * high,
        high + taps[2] * low + taps[3] * low_turned,
    ):
        back = jnp.concatenate([pltpu.roll(b[-8:], 1, 0), b[:-8]], axis=0)
        front = jnp.concatenate([b[8:], pltpu.roll(b[:8], 7, 0)], axis=0)
        out.append(b + taps[4] * back + taps[5] * front)
    return jnp.concatenate(out, axis=0)


def position():
    sec = lax.axis_index("sec")
    return sec, lax.rem(sec, 2)


def launch_kernel(*refs):
    sources, (lead, bundle) = refs[:9], refs[9:11]
    scratch, copies, sems = refs[11], refs[12:21], refs[21]
    moves = [
        pltpu.make_async_copy(source.at[pl.ds(0, copy.shape[0])], copy, sems.at[i])
        for i, (source, copy) in enumerate(zip(sources, copies))
    ]
    for move in moves:
        move.start()
    incoming, stored, fields, kinds, axial, lateral, depth, diagonal, coupling = copies
    for move in moves[2:]:
        move.wait()
    rows = scratch.shape[0]
    orients = rows // 2
    ratios = [each[w : w + 1] / each[1:2] for each in (axial, lateral, depth) for w in (0, 2)]
    for i, ratio in enumerate(ratios + ratios[:2]):
        bundle[i : i + 1] = jnp.concatenate([ratio, ratio], axis=1)
    square = (orients, orients)
    same = lax.broadcasted_iota(jnp.int32, square, 0) == lax.broadcasted_iota(jnp.int32, square, 1)
    kernel = jnp.where(same, diagonal[...], 0.0) + coupling[...]
    kernel = kernel * (axial[1:2] * lateral[1:2] * depth[1:2])
    upper = jnp.concatenate([kernel, jnp.zeros_like(kernel)], axis=1)
    bundle[TAP_ROWS : TAP_ROWS + rows] = jnp.concatenate([upper, pltpu.roll(upper, orients, 1)], axis=0).T
    line = kinds[...].astype(jnp.float32)
    line = jnp.concatenate([line, jnp.zeros((1, rows - line.shape[1]), jnp.float32)], axis=1)
    types = line
    planes = incoming.shape[1]
    at = TAP_ROWS + rows
    bundle[at : at + FIELD_ROWS] = jnp.zeros((FIELD_ROWS, rows), jnp.float32)
    for kind in range(fields.shape[0]):
        for i in range(planes):
            line = fields[kind, i : i + 1, :]
            here = at + (kind * planes + i) * 2
            bundle[here : here + 1] = line[:, :rows]
            bundle[here + 1 : here + 2] = line[:, rows:]
    bundle[at + OWN_KINDS : at + OWN_KINDS + 1] = types
    moves[0].wait()
    for i in range(planes):
        here = at + FIELD_ROWS + i * rows
        bundle[here : here + rows] = to_tile(incoming[0, i], scratch)
    moves[1].wait()
    for step in range(LEAD):
        for i in range(planes):
            here = (step * planes + i) * orients
            lead[here : here + orients] = stored[step, i].astype(jnp.float32)
    lead[lead.shape[0] - 8 :] = jnp.broadcast_to(jnp.concatenate([types, types], axis=1), (8, lead.shape[1]))


def launch(incoming, backward, fields, kinds, axial, lateral, depth, diagonal, coupling):
    planes, orients, cells = backward.shape[1:]
    rows = 2 * orients
    operands = [incoming, backward, fields, kinds, axial, lateral, depth, diagonal.reshape(1, -1), coupling]
    shapes = [(LEAD * planes * orients + 8, cells), (TAP_ROWS + rows + FIELD_ROWS + planes * rows, rows)]
    taken = [(LEAD,) + each.shape[1:] if i == 1 else each.shape for i, each in enumerate(operands)]
    return pl.pallas_call(
        launch_kernel,
        in_specs=[pl.BlockSpec(memory_space=pltpu.HBM)] * len(operands),
        out_specs=[IN_VMEM] * len(shapes),
        out_shape=[jax.ShapeDtypeStruct(shape, jnp.float32) for shape in shapes],
        scratch_shapes=[pltpu.VMEM((rows, rows), jnp.float32)]
        + [pltpu.VMEM(shape, each.dtype) for shape, each in zip(taken, operands)]
        + [pltpu.SemaphoreType.DMA((len(operands),))],
        compiler_params=pltpu.CompilerParams(vmem_limit_bytes=WHOLE_VMEM_BYTES),
    )(*operands)


def turn_kernel(backward, lead, early, late, out, across, scratch):
    orients = scratch.shape[0] // 2
    across[...] = lead[lead.shape[0] - 8 :, : scratch.shape[1]]
    for target, begin in ((early, 0), (late, LEAD)):
        for step in range(target.shape[0]):
            for i in range(target.shape[1]):
                target[step, i] = to_tile(backward[begin + step, i].astype(jnp.float32), scratch)
    for step in range(out.shape[0]):
        for i in range(out.shape[1]):
            here = (step * out.shape[1] + i) * orients
            out[step, i] = to_tile(lead[here : here + orients], scratch)


def unpack_kernel(bundle, out, taps, weights):
    rows = taps.shape[1]
    taps[...] = bundle[:TAP_ROWS]
    twice = bundle[TAP_ROWS : TAP_ROWS + rows]
    coarse = twice.astype(jnp.bfloat16)
    fine = (twice - coarse.astype(jnp.float32)).astype(jnp.bfloat16)
    weights[...] = jnp.concatenate(
        [jnp.concatenate([coarse, fine], axis=1), jnp.concatenate([coarse, jnp.zeros_like(fine)], axis=1)], axis=0
    )
    at = out.shape[0] - FIELD_ROWS
    lines = TAP_ROWS + rows
    out[at:] = bundle[lines : lines + FIELD_ROWS]
    out[:at] = bundle[lines + FIELD_ROWS :]


def pack_kernel(base, moved, passed, types, out, scratch):
    sec, odd = position()
    rows = scratch.shape[0]
    at = out.shape[0] - FIELD_ROWS
    out[at:] = base[at:]
    out[at + FIRST_KINDS : at + FIRST_KINDS + 1] = jnp.where(
        sec == 0, base[at + OWN_KINDS : at + OWN_KINDS + 1], types[:1]
    )

    @pl.when(sec == 0)
    def _():
        out[:at] = base[:at]

    def fill(source):
        for i in range(source.shape[0]):
            out[i * rows : (i + 1) * rows] = to_tile(source[i], scratch)

    pl.when(odd == 1)(lambda: fill(moved))
    pl.when((sec > 0) & (odd == 0))(lambda: fill(passed))


def scalars_of(row, count):
    lane = lax.broadcasted_iota(jnp.int32, row.shape, 1)
    return [jnp.sum(jnp.where(lane == i, row, 0.0)).astype(jnp.int32) for i in range(count)]


def places(odd, planes, reach, blocks):
    return [reach + block * planes + planes // 2 * core for core in (odd, 1 - odd) for block in blocks]


def run_steps(kinds, taps, weights, count, slab, other, first, second, factor, offset, after):
    tap = [taps[i : i + 1, :] for i in range(6)]
    extent, rows, lanes = slab.shape
    buffers = (slab, other)

    def blend(source, at, packed):
        for i in range(GROUP):
            e = stencil(source[at + i - 1], source[at + i], source[at + i + 1], tap)
            coarse = e.astype(jnp.bfloat16)
            packed[i * rows : (i + 1) * rows, :lanes] = coarse
            packed[i * rows : (i + 1) * rows, lanes:] = (e - coarse.astype(jnp.float32)).astype(jnp.bfloat16)

    def mix(target, at, packed, kind):
        product = jnp.dot(packed[...], weights[...], preferred_element_type=jnp.float32)
        product = product[:, :lanes] + product[:, lanes:]
        for i in range(GROUP):
            target[at + i] = product[i * rows : (i + 1) * rows] * factor[kind, at + i + offset]

    for step in range(count):
        source, target = buffers[step % 2], buffers[1 - step % 2]
        begin, width = step + 1, extent - 2 * step - 2
        groups = -(-width // GROUP)
        kind = kinds[step]

        def at(i, begin=begin, width=width):
            return jnp.minimum(begin + i * GROUP, begin + width - GROUP)

        blend(source, at(0), first)
        if groups > 1:

            def body(i, carry, source=source, target=target, at=at, kind=kind):
                blend(source, at(2 * i + 1), second)
                mix(target, at(2 * i), first, kind)
                blend(source, at(2 * i + 2), first)
                mix(target, at(2 * i + 1), second, kind)
                return carry

            lax.fori_loop(0, (groups - 1) // 2, body, 0)
        if groups % 2 == 0:
            blend(source, at(groups - 1), second)
            mix(target, at(groups - 2), first, kind)
            mix(target, at(groups - 1), second, kind)
        else:
            mix(target, at(groups - 1), first, kind)
        after(step, target)


def spread_factor(columns, factor, starts, width):
    rows, lanes = factor.shape[2:]
    pair = width // (2 * factor.shape[0])
    right = (lax.broadcasted_iota(jnp.int32, (rows, lanes), 1) >= lanes // 2).astype(jnp.int32)
    for piece, start in enumerate(starts):
        for kind in range(factor.shape[0]):
            for i in range(pair):
                at = piece * width + (kind * pair + i) * 2
                factor[kind, start + i] = jnp.take_along_axis(columns, right + at, axis=1, mode="promise_in_bounds")


def slab_starts(planes, reach):
    odd = position()[1]
    mine, others = (planes * (1 + core) for core in (odd, 1 - odd))
    return [reach, reach + mine, reach - mine, reach + others, reach - others]


def fill_factor(pieces, starts, factor, scratch):
    rows = scratch.shape[0]
    planes = (pieces[0].shape[0] - FIELD_ROWS) // rows
    width = 2 * planes * factor.shape[0]
    lines = [piece[planes * rows : planes * rows + width] for piece in pieces]
    lines.append(jnp.zeros((rows - width * len(pieces), rows), jnp.float32))
    scratch[...] = jnp.exp(-jnp.concatenate(lines, axis=0)).T
    spread_factor(reorder(scratch), factor, starts, width)


def factor_kernel(*refs):
    pieces, factor, scratch = refs[:3], refs[3], refs[4]
    planes = (pieces[0].shape[0] - FIELD_ROWS) // scratch.shape[0]
    fill_factor(pieces, slab_starts(planes, (factor.shape[1] - planes) // 2)[:3], factor, scratch)


def early_kernel(taps, weights, across, *refs):
    pieces, stored, (middle, half_out, kept, total, factor) = refs[:5], refs[5:7], refs[8:13]
    slab, other, first, second, scratch = refs[13:]
    sec, odd = position()
    planes, rows = middle.shape[:2]
    pair = planes // 2
    reach = (slab.shape[0] - planes) // 2
    starts = slab_starts(planes, reach)
    for piece, start in zip(pieces, starts):
        for i in range(planes):
            slab[start + i] = piece[i * rows : (i + 1) * rows]
    at = planes * rows
    steps = LEAD + stored[1].shape[0]
    own_kinds, first_kinds = (pieces[0][at + row : at + row + 1] for row in (OWN_KINDS, FIRST_KINDS))
    beside_kinds, beside_first = (pieces[3][at + row : at + row + 1] for row in (OWN_KINDS, FIRST_KINDS))
    kinds = scalars_of(jnp.where((sec == 1) | (sec == 2), beside_first, first_kinds), steps)
    kinds += scalars_of(jnp.where((sec == 1) | (sec == 2), own_kinds, beside_kinds), steps)
    last_kinds = jnp.where(sec == 0, across[:1], own_kinds)
    half_out[pair * rows :] = jnp.broadcast_to(last_kinds, (8, rows))
    fill_factor(pieces[3:], starts[3:], factor, scratch)
    total[...] = jnp.zeros(total.shape, jnp.float32)
    kept[...] = jnp.zeros(kept.shape, jnp.float32)

    def after(step, state):
        @pl.when(sec == step // steps)
        def _():
            j = step % steps
            source = stored[0][j] if j < LEAD else stored[1][j - LEAD]
            total[...] += state[reach : reach + planes] * source
            if j + 1 == steps:
                kept[...] = state[reach : reach + planes]

    run_steps(kinds, taps, weights, reach, slab, other, first, second, factor, 0, after)
    state = (slab, other)[reach % 2]
    middle[...] = state[reach : reach + planes]
    for i in range(pair):
        half_out[i * rows : (i + 1) * rows] = state[reach + pair * odd + i]


def late_kernel(blocks, last, taps, weights, middle, *refs):
    pieces, refs = refs[: 2 * len(blocks)], refs[2 * len(blocks) :]
    factor, kept, total_in, total_beside, series, stored = refs[0], refs[1], refs[2], refs[3], refs[4:6], refs[6:8]
    handoff, share, to_pair, to_across, to_corner = refs[8:13]
    slab, other, first, second, scratch, total, saved, whole = refs[13:]
    sec, odd = position()
    planes, rows = middle.shape[:2]
    pair = planes // 2
    reach = (slab.shape[0] - planes) // 2
    begun = (factor.shape[1] - planes) // 2
    even, uneven = (jnp.where(odd == core, pieces[0][pair * rows :], pieces[len(blocks)][pair * rows :]) for core in (0, 1))
    kinds = scalars_of(jnp.where(sec < 2, even, uneven)[:1], reach)
    slab[reach : reach + planes] = middle[...]
    for piece, start in zip(pieces, places(odd, planes, reach, blocks)):
        for i in range(pair):
            slab[start + i] = piece[i * rows : (i + 1) * rows]
    total[...] = jnp.zeros(total.shape, jnp.float32)

    @pl.when(sec == 0)
    def _():
        total[...] = total_in[...] + total_beside[...]

    saved[...] = kept[...]

    def after(step, state):
        for where, source in ((sec == 0, series), (sec == last, stored)):

            @pl.when(where)
            def _(source=source):
                part = source[0][step] if step < LEAD else source[1][step - LEAD]
                total[...] += state[reach : reach + planes] * part

    run_steps(kinds, taps, weights, reach, slab, other, first, second, factor, begun - reach, after)
    state = (slab, other)[reach % 2]

    @pl.when(sec == last)
    def _():
        saved[...] = state[reach : reach + planes]

    orients = handoff.shape[1]
    count = orients // (last + 1)
    held = planes * count
    to_corner[...] = jnp.zeros(to_corner.shape, jnp.float32)
    for i in range(planes):
        handoff[i] = from_tile(saved[i], scratch)
        whole[...] = from_tile(total[i], scratch)
        for piece, who in (
            (share, sec),
            (to_pair, sec + 1 - 2 * odd),
            (to_across, jnp.where(sec == 0, 2, 1)),
            (to_corner, last - sec),
        ):
            piece[i * count : (i + 1) * count] = whole[pl.ds(pl.multiple_of(who * count, count), count)]
    for i in range(pair):
        to_across[held + i * orients : held + (i + 1) * orients] = from_tile(state[reach + pair * odd + i], scratch)

    @pl.when(sec == 1)
    def _():
        to_corner[...] = to_across[held:]


def finish_kernel(contour, handoff_in, share, to_pair, to_across, to_corner, handoff, density):
    sec = lax.axis_index("sec")
    planes, count = density.shape[:2]
    held = planes * count
    corner = jnp.where(sec == 2, 0.0, to_corner[:held])
    total = (share[...] + to_pair[...] + to_across[:held] + corner) / contour
    for i in range(planes):
        density[i] = total[i * count : (i + 1) * count]
    handoff[0] = handoff_in[...]

    @pl.when(sec == 2)
    def _():
        orients = handoff.shape[2]
        pair = planes // 2
        for i in range(pair):
            handoff[0, i] = to_across[held + i * orients : held + (i + 1) * orients]
            handoff[0, pair + i] = to_corner[i * orients : (i + 1) * orients]


def call(kernel, out_shape, scratch, operands, dtypes=None, aliases=None, cost=None):
    return pl.pallas_call(
        kernel,
        in_specs=[IN_VMEM] * len(operands),
        out_specs=[IN_VMEM] * len(out_shape),
        out_shape=[jax.ShapeDtypeStruct(shape, (dtypes or {}).get(i, jnp.float32)) for i, shape in enumerate(out_shape)],
        scratch_shapes=scratch,
        input_output_aliases=aliases or {},
        cost_estimate=cost,
        compiler_params=pltpu.CompilerParams(vmem_limit_bytes=VMEM_BYTES),
    )(*operands)


def paired(incoming, backward, fields, block_types, axial_taps, lateral_taps, depth_taps, bend_diagonal, bend_coupling):
    n_sec, n_gx = lax.axis_size("sec"), lax.axis_size("gx")
    steps, planes, orients, cells = backward.shape
    pair = planes // 2
    reach = (TICKS - 1) * steps, steps
    near = (-1, 1)
    rows = 2 * orients
    lanes = cells // 2
    last = n_sec - 1

    def send(array, by_sec, even=0, odd=0):
        by_sec = by_sec.items() if isinstance(by_sec, dict) else enumerate(by_sec)
        pairs = [
            (s * n_gx + g, t * n_gx + (g + (odd if s % 2 else even)) % n_gx) for s, t in by_sec for g in range(n_gx)
        ]
        return lax.ppermute(array, ("sec", "gx"), pairs)

    same, beside = (0, 1, 2, 3), (1, 0, 3, 2)
    moved = send(incoming[0], {0: 1, 1: 3})
    lead, bundle = launch(
        incoming, backward, fields, block_types, axial_taps, lateral_taps, depth_taps, bend_diagonal, bend_coupling
    )
    types = jnp.pad(block_types.astype(jnp.float32), ((0, 7), (0, lanes - steps)))
    types = send(types, {1: 3})
    lead = send(lead, {2: 0})
    size = planes * rows + FIELD_ROWS
    base, taps, weights = call(
        unpack_kernel, [(size, lanes), (TAP_ROWS, lanes), (2 * rows, 2 * lanes)], [], [bundle], {2: jnp.bfloat16}
    )
    moved, base, types = lax.optimization_barrier((moved, base, types))
    passed = send(moved, {3: 2})

    tile = pltpu.VMEM((rows, lanes), jnp.float32)
    packed = pltpu.VMEM((GROUP * rows, 2 * lanes), jnp.bfloat16)
    inner = pltpu.VMEM((planes, rows, lanes), jnp.float32)

    def work(extent):
        slab = pltpu.VMEM((planes + 2 * extent, rows, lanes), jnp.float32)
        return [slab, slab, packed, packed, tile]

    (piece,) = call(pack_kernel, [(size, lanes)], [tile], [base, moved, passed, types])
    own = [send(piece, same, shift, 2 * shift) for shift in near]
    backward, _ = lax.optimization_barrier((backward, piece))
    *stored, lead, across = call(
        turn_kernel,
        [(count, planes, rows, lanes) for count in (LEAD, steps - LEAD, LEAD)] + [(8, lanes)],
        [tile],
        [backward, lead],
    )
    own[-1], *stored = lax.optimization_barrier((own[-1], *stored))
    swapped = [send(each, beside) for each in own]
    table = (fields.shape[0], planes + 2 * reach[0], rows, lanes)
    known, swapped[1] = lax.optimization_barrier((piece, swapped[1]))
    (factor,) = call(factor_kernel, [table], [tile], [known, *own])
    late_stored, factor, *swapped = lax.optimization_barrier((stored[1], factor, *swapped))
    late_last = send(late_stored, {2: 0})
    middle, piece, kept, total, factor = call(
        early_kernel,
        [(planes, rows, lanes), (pair * rows + 8, lanes), (planes, rows, lanes), (planes, rows, lanes)]
        + [table],
        work(reach[0]),
        [taps, weights, across, piece, *own, *swapped, *stored, factor],
        aliases={10: 4},
    )
    own = [send(piece, same, shift, shift) for shift in near]
    beside_total = send(total, beside)
    swapped = [send(each, beside) for each in own]
    held = planes * (orients // n_sec)
    handoff, share, to_pair, to_across, to_corner = call(
        functools.partial(late_kernel, tuple(-shift for shift in near), last),
        [(planes, orients, cells)]
        + [(held, cells)] * 2
        + [(held + pair * orients, cells), (pair * orients, cells)],
        work(reach[1]) + [inner, inner, pltpu.VMEM((orients, cells), jnp.float32)],
        [taps, weights, middle, *own, *swapped, factor, kept, total, beside_total]
        + [lead, late_last, *stored],
    )
    to_pair = send(to_pair, beside)
    to_across = send(to_across, (2, 0, 3, 1))
    to_corner = send(to_corner, (3, 2, 1, 0))
    handoff, density = call(
        functools.partial(finish_kernel, n_sec * steps),
        [(1,) + handoff.shape, (planes, orients // n_sec, cells)],
        [],
        [handoff, share, to_pair, to_across, to_corner],
    )
    return handoff, density


def pairs_fit(n_sec, planes, steps, orients, cells, kinds):
    return (
        n_sec == TICKS + 1 == 4
        and planes == steps
        and planes % 2 == 0
        and 2 * orients == 2 * CZ == cells // 2 == 128
        and 2 * kinds * planes <= OWN_KINDS and 10 * kinds * planes <= 2 * orients
        and GROUP < 2 * planes
    )


def solution(mesh):
    in_specs = (
        P("sec", "gx", None, None),
        P("sec", "gx", None, None),
        P(None, "gx", None),
        P("sec", None),
        P(),
        P(),
        P(),
        P(),
        P(),
    )
    out_specs = (P("sec", "gx", None, None), P("gx", "sec", None))

    def body(incoming, backward, fields, *rest):
        steps, planes, orients, cells = backward.shape
        fits = pairs_fit(mesh.shape["sec"], planes, steps, orients, cells, fields.shape[0])
        return (paired if fits else per_device)(incoming, backward, fields, *rest)

    return jax.shard_map(body, mesh=mesh, in_specs=in_specs, out_specs=out_specs, check_vma=False)
```

```python
import functools

import jax
import jax.numpy as jnp
from jax import lax
from jax.experimental import pallas as pl
from jax.experimental.pallas import tpu as pltpu
from jax.sharding import PartitionSpec as P

TICKS = 3
CZ = 64
GROUP = 6
FIELD_ROWS = 32
TAP_ROWS = 8
OWN_KINDS, FIRST_KINDS = 24, 25
VMEM_BYTES = 16 * 2**20
WHOLE_VMEM_BYTES = 62 * 2**20
IN_VMEM = pl.BlockSpec(memory_space=pltpu.VMEM)


def padded_2(block, sides, width):
    for axis, dim in sides:
        count = lax.axis_size(axis)
        forward = [(i, i + 1) for i in range(count - 1)]
        forward.append((count - 1, 0))
        backward = [(target, source) for source, target in forward]
        low = lax.ppermute(
            lax.slice_in_dim(block, block.shape[dim] - width, None, axis=dim), axis, forward
        )
        high = lax.ppermute(lax.slice_in_dim(block, 0, width, axis=dim), axis, backward)
        block = jnp.concatenate([low, block, high], axis=dim)
    return block


def from_behind(array, axis, by):
    length = lax.axis_size(axis)
    pairs = [(i, i + by) for i in range(length) if 0 <= i + by < length]
    return lax.ppermute(array, axis, pairs)


def boltzmann(fields, kinds):
    selector = kinds == jnp.arange(fields.shape[0], dtype=jnp.int32)
    chosen = jnp.sum(jnp.where(selector[:, None, None], fields, jnp.zeros_like(fields)), axis=0)
    return jnp.exp(-chosen)


def column(taps, which):
    return taps[which][None, :, None]


def advance_padded(padded, factor, axial_taps, lateral_taps, depth_taps, kernel):
    along_x = (
        column(axial_taps, 0) * padded[:-2]
        + column(axial_taps, 1) * padded[1:-1]
        + column(axial_taps, 2) * padded[2:]
    )
    along_y = (
        column(lateral_taps, 0) * jnp.roll(along_x, CZ, axis=2)
        + column(lateral_taps, 1) * along_x
        + column(lateral_taps, 2) * jnp.roll(along_x, -CZ, axis=2)
    )
    depth_pos = (jnp.arange(along_y.shape[2], dtype=jnp.int32) % CZ)[None, None, :]
    behind = jnp.where(
        depth_pos == 0, jnp.roll(along_y, -(CZ - 1), axis=2), jnp.roll(along_y, 1, axis=2)
    )
    ahead = jnp.where(
        depth_pos == CZ - 1, jnp.roll(along_y, CZ - 1, axis=2), jnp.roll(along_y, -1, axis=2)
    )
    along_z = (
        column(depth_taps, 0) * behind
        + column(depth_taps, 1) * along_y
        + column(depth_taps, 2) * ahead
    )
    blended = jnp.einsum(
        "uv,xvc->xuc",
        kernel,
        along_z,
        precision=lax.Precision.HIGHEST,
        preferred_element_type=jnp.float32,
    )
    return blended * factor[:, None, :]


def per_device(
    incoming,
    backward,
    fields,
    block_types,
    axial_taps,
    lateral_taps,
    depth_taps,
    bend_diagonal,
    bend_coupling,
):
    kernel = jnp.diag(bend_diagonal) + bend_coupling
    steps_each = block_types.shape[1]
    planes = incoming.shape[1]
    start = incoming[0]
    first_section = lax.axis_index("sec") == 0
    wide_fields = padded_2(fields, (("gx", 1),), steps_each)
    factors = [boltzmann(wide_fields, block_types[0, position]) for position in range(steps_each)]
    current = start
    outgoing = start
    accumulated = jnp.zeros(start.shape, jnp.float32)
    for tick_index in range(TICKS):
        final_tick = tick_index + 1 == TICKS
        extended = padded_2(current, (("gx", 0),), steps_each)
        for position in range(steps_each):
            margin = steps_each - position - 1
            offset = steps_each - margin
            factor = factors[position][offset : offset + planes + 2 * margin]
            extended = advance_padded(
                extended, factor, axial_taps, lateral_taps, depth_taps, kernel
            )
            if final_tick:
                accumulated = accumulated + extended[margin : margin + planes] * backward[
                    position
                ].astype(jnp.float32)
        outgoing = extended
        if not final_tick:
            shifted = from_behind(outgoing, "sec", 1)
            current = jnp.where(first_section, start, shifted)
    reduced = lax.psum_scatter(accumulated, "sec", scatter_dimension=1, tiled=True)
    density = reduced / (lax.axis_size("sec") * steps_each)
    return (outgoing[None], density)


def to_tile(plane, scratch):
    half = plane.shape[1] // 2
    scratch[...] = jnp.concatenate([plane[:, :half], plane[:, half:]], axis=0).T
    return reorder(scratch)


def reorder(scratch):
    rows = scratch.shape[0]
    return jnp.concatenate(
        [scratch[pl.ds(yl * CZ + zl, 8, stride=8), :] for yl in range(rows // CZ) for zl in range(CZ // 8)], axis=0
    )


def from_tile(tile, scratch):
    rows = tile.shape[0]
    for yl in range(rows // CZ):
        for zl in range(CZ // 8):
            at = (yl * (CZ // 8) + zl) * 8
            scratch[pl.ds(yl * CZ + zl, 8, stride=8), :] = tile[at : at + 8]
    turned = scratch[...].T
    half = turned.shape[0] // 2
    return jnp.concatenate([turned[:half], turned[half:]], axis=1)


def stencil(behind, here, ahead, taps):
    a = here + taps[0] * behind + taps[1] * ahead
    low, high = a[:CZ], a[CZ:]
    low_turned = pltpu.roll(low, a.shape[1] // 2, 1)
    high_turned = pltpu.roll(high, a.shape[1] // 2, 1)
    out = []
    for b in (
        low + taps[2] * high_turned + taps[3] * high,
        high + taps[2] * low + taps[3] * low_turned,
    ):
        back = jnp.concatenate([pltpu.roll(b[-8:], 1, 0), b[:-8]], axis=0)
        front = jnp.concatenate([b[8:], pltpu.roll(b[:8], 7, 0)], axis=0)
        out.append(b + taps[4] * back + taps[5] * front)
    return jnp.concatenate(out, axis=0)


def position():
    sec = lax.axis_index("sec")
    return sec, lax.rem(sec, 2)


def launch_kernel(*refs):
    sources, bundle, scratch, copies, sems = refs[:8], refs[8], refs[9], refs[10:18], refs[18]
    moves = [pltpu.make_async_copy(s, c, sems.at[i]) for i, (s, c) in enumerate(zip(sources, copies))]
    for move in moves:
        move.start()
    incoming, fields, kinds, axial, lateral, depth, diagonal, coupling = copies
    for move in moves[1:]:
        move.wait()
    rows = scratch.shape[0]
    orients = rows // 2
    ratios = [each[w : w + 1] / each[1:2] for each in (axial, lateral, depth) for w in (0, 2)]
    for i, ratio in enumerate(ratios + ratios[:2]):
        bundle[i : i + 1] = jnp.concatenate([ratio, ratio], axis=1)
    square = (orients, orients)
    same = lax.broadcasted_iota(jnp.int32, square, 0) == lax.broadcasted_iota(jnp.int32, square, 1)
    kernel = jnp.where(same, diagonal[...], 0.0) + coupling[...]
    kernel = kernel * (axial[1:2] * lateral[1:2] * depth[1:2])
    upper = jnp.concatenate([kernel, jnp.zeros_like(kernel)], axis=1)
    bundle[TAP_ROWS : TAP_ROWS + rows] = jnp.concatenate([upper, pltpu.roll(upper, orients, 1)], axis=0).T
    line = kinds[...].astype(jnp.float32)
    line = jnp.concatenate([line, jnp.zeros((1, rows - line.shape[1]), jnp.float32)], axis=1)
    types = line
    planes = incoming.shape[1]
    at = TAP_ROWS + rows
    bundle[at : at + FIELD_ROWS] = jnp.zeros((FIELD_ROWS, rows), jnp.float32)
    for kind in range(fields.shape[0]):
        for i in range(planes):
            line = fields[kind, i : i + 1, :]
            here = at + (kind * planes + i) * 2
            bundle[here : here + 1] = line[:, :rows]
            bundle[here + 1 : here + 2] = line[:, rows:]
    bundle[at + OWN_KINDS : at + OWN_KINDS + 1] = types
    moves[0].wait()
    for i in range(planes):
        here = at + FIELD_ROWS + i * rows
        bundle[here : here + rows] = to_tile(incoming[0, i], scratch)


def launch(incoming, fields, kinds, axial, lateral, depth, diagonal, coupling):
    planes, orients, cells = incoming.shape[1:]
    rows = 2 * orients
    operands = [incoming, fields, kinds, axial, lateral, depth, diagonal.reshape(1, -1), coupling]
    return pl.pallas_call(
        launch_kernel,
        in_specs=[pl.BlockSpec(memory_space=pltpu.HBM)] * len(operands),
        out_specs=IN_VMEM,
        out_shape=jax.ShapeDtypeStruct((TAP_ROWS + rows + FIELD_ROWS + planes * rows, rows), jnp.float32),
        scratch_shapes=[pltpu.VMEM((rows, rows), jnp.float32)]
        + [pltpu.VMEM(each.shape, each.dtype) for each in operands]
        + [pltpu.SemaphoreType.DMA((len(operands),))],
        compiler_params=pltpu.CompilerParams(vmem_limit_bytes=WHOLE_VMEM_BYTES),
    )(*operands)


def turn_kernel(backward, out, scratch):
    for step in range(out.shape[0]):
        for i in range(out.shape[1]):
            out[step, i] = to_tile(backward[step, i].astype(jnp.float32), scratch)


def unpack_kernel(bundle, out, taps, weights):
    rows = taps.shape[1]
    taps[...] = bundle[:TAP_ROWS]
    twice = bundle[TAP_ROWS : TAP_ROWS + rows]
    coarse = twice.astype(jnp.bfloat16)
    fine = (twice - coarse.astype(jnp.float32)).astype(jnp.bfloat16)
    weights[...] = jnp.concatenate(
        [jnp.concatenate([coarse, fine], axis=1), jnp.concatenate([coarse, jnp.zeros_like(fine)], axis=1)], axis=0
    )
    at = out.shape[0] - FIELD_ROWS
    lines = TAP_ROWS + rows
    out[at:] = bundle[lines : lines + FIELD_ROWS]
    out[:at] = bundle[lines + FIELD_ROWS :]


def pack_kernel(base, moved, passed, types, out, scratch):
    sec, odd = position()
    rows = scratch.shape[0]
    at = out.shape[0] - FIELD_ROWS
    out[at:] = base[at:]
    out[at + FIRST_KINDS : at + FIRST_KINDS + 1] = jnp.where(
        sec == 0, base[at + OWN_KINDS : at + OWN_KINDS + 1], types[:1]
    )

    @pl.when(sec == 0)
    def _():
        out[:at] = base[:at]

    def fill(source):
        for i in range(source.shape[0]):
            out[i * rows : (i + 1) * rows] = to_tile(source[i], scratch)

    pl.when(odd == 1)(lambda: fill(moved))
    pl.when((sec > 0) & (odd == 0))(lambda: fill(passed))


def scalars_of(row, count):
    lane = lax.broadcasted_iota(jnp.int32, row.shape, 1)
    return [jnp.sum(jnp.where(lane == i, row, 0.0)).astype(jnp.int32) for i in range(count)]


def places(odd, planes, reach, blocks):
    return [reach + block * planes + planes // 2 * core for core in (odd, 1 - odd) for block in blocks]


def run_steps(kinds, taps, weights, count, slab, other, first, second, factor, offset, after):
    tap = [taps[i : i + 1, :] for i in range(6)]
    extent, rows, lanes = slab.shape
    buffers = (slab, other)

    def blend(source, at, packed):
        for i in range(GROUP):
            e = stencil(source[at + i - 1], source[at + i], source[at + i + 1], tap)
            coarse = e.astype(jnp.bfloat16)
            packed[i * rows : (i + 1) * rows, :lanes] = coarse
            packed[i * rows : (i + 1) * rows, lanes:] = (e - coarse.astype(jnp.float32)).astype(jnp.bfloat16)

    def mix(target, at, packed, kind):
        product = jnp.dot(packed[...], weights[...], preferred_element_type=jnp.float32)
        product = product[:, :lanes] + product[:, lanes:]
        for i in range(GROUP):
            target[at + i] = product[i * rows : (i + 1) * rows] * factor[kind, at + i + offset]

    for step in range(count):
        source, target = buffers[step % 2], buffers[1 - step % 2]
        begin, width = step + 1, extent - 2 * step - 2
        groups = -(-width // GROUP)
        kind = kinds[step]

        def at(i, begin=begin, width=width):
            return jnp.minimum(begin + i * GROUP, begin + width - GROUP)

        blend(source, at(0), first)
        if groups > 1:

            def body(i, carry, source=source, target=target, at=at, kind=kind):
                blend(source, at(2 * i + 1), second)
                mix(target, at(2 * i), first, kind)
                blend(source, at(2 * i + 2), first)
                mix(target, at(2 * i + 1), second, kind)
                return carry

            lax.fori_loop(0, (groups - 1) // 2, body, 0)
        if groups % 2 == 0:
            blend(source, at(groups - 1), second)
            mix(target, at(groups - 2), first, kind)
            mix(target, at(groups - 1), second, kind)
        else:
            mix(target, at(groups - 1), first, kind)
        after(step, target)


def spread_factor(columns, factor, starts, width):
    rows, lanes = factor.shape[2:]
    pair = width // (2 * factor.shape[0])
    right = (lax.broadcasted_iota(jnp.int32, (rows, lanes), 1) >= lanes // 2).astype(jnp.int32)
    for piece, start in enumerate(starts):
        for kind in range(factor.shape[0]):
            for i in range(pair):
                at = piece * width + (kind * pair + i) * 2
                factor[kind, start + i] = jnp.take_along_axis(columns, right + at, axis=1, mode="promise_in_bounds")


def slab_starts(planes, reach):
    odd = position()[1]
    mine, others = (planes * (1 + core) for core in (odd, 1 - odd))
    return [reach, reach + mine, reach - mine, reach + others, reach - others]


def fill_factor(pieces, starts, factor, scratch):
    rows = scratch.shape[0]
    planes = (pieces[0].shape[0] - FIELD_ROWS) // rows
    width = 2 * planes * factor.shape[0]
    lines = [piece[planes * rows : planes * rows + width] for piece in pieces]
    lines.append(jnp.zeros((rows - width * len(pieces), rows), jnp.float32))
    scratch[...] = jnp.exp(-jnp.concatenate(lines, axis=0)).T
    spread_factor(reorder(scratch), factor, starts, width)


def factor_kernel(*refs):
    pieces, factor, scratch = refs[:3], refs[3], refs[4]
    planes = (pieces[0].shape[0] - FIELD_ROWS) // scratch.shape[0]
    fill_factor(pieces, slab_starts(planes, (factor.shape[1] - planes) // 2)[:3], factor, scratch)


def early_kernel(taps, weights, across, *refs):
    pieces, stored, (middle, half_out, kept, total, factor) = refs[:5], refs[5], refs[7:12]
    slab, other, first, second, scratch = refs[12:]
    sec, odd = position()
    planes, rows = middle.shape[:2]
    pair = planes // 2
    reach = (slab.shape[0] - planes) // 2
    starts = slab_starts(planes, reach)
    for piece, start in zip(pieces, starts):
        for i in range(planes):
            slab[start + i] = piece[i * rows : (i + 1) * rows]
    at = planes * rows
    steps = stored.shape[0]
    own_kinds, first_kinds = (pieces[0][at + row : at + row + 1] for row in (OWN_KINDS, FIRST_KINDS))
    beside_kinds, beside_first = (pieces[3][at + row : at + row + 1] for row in (OWN_KINDS, FIRST_KINDS))
    kinds = scalars_of(jnp.where((sec == 1) | (sec == 2), beside_first, first_kinds), steps)
    kinds += scalars_of(jnp.where((sec == 1) | (sec == 2), own_kinds, beside_kinds), steps)
    last_kinds = jnp.where(sec == 0, across[:1], own_kinds)
    half_out[pair * rows :] = jnp.broadcast_to(last_kinds, (8, rows))
    fill_factor(pieces[3:], starts[3:], factor, scratch)
    total[...] = jnp.zeros(total.shape, jnp.float32)
    kept[...] = jnp.zeros(kept.shape, jnp.float32)

    def after(step, state):
        @pl.when(sec == step // steps)
        def _():
            total[...] += state[reach : reach + planes] * stored[step % steps]
            if (step + 1) % steps == 0:
                kept[...] = state[reach : reach + planes]

    run_steps(kinds, taps, weights, reach, slab, other, first, second, factor, 0, after)
    state = (slab, other)[reach % 2]
    middle[...] = state[reach : reach + planes]
    for i in range(pair):
        half_out[i * rows : (i + 1) * rows] = state[reach + pair * odd + i]


def late_kernel(blocks, last, taps, weights, middle, *refs):
    pieces, refs = refs[: 2 * len(blocks)], refs[2 * len(blocks) :]
    factor, kept, total_in, total_beside, series, stored = refs[:6]
    handoff, share, to_pair, to_across, to_corner = refs[6:11]
    slab, other, first, second, scratch, total, saved, whole = refs[11:]
    sec, odd = position()
    planes, rows = middle.shape[:2]
    pair = planes // 2
    reach = (slab.shape[0] - planes) // 2
    begun = (factor.shape[1] - planes) // 2
    even, uneven = (jnp.where(odd == core, pieces[0][pair * rows :], pieces[len(blocks)][pair * rows :]) for core in (0, 1))
    kinds = scalars_of(jnp.where(sec < 2, even, uneven)[:1], reach)
    slab[reach : reach + planes] = middle[...]
    for piece, start in zip(pieces, places(odd, planes, reach, blocks)):
        for i in range(pair):
            slab[start + i] = piece[i * rows : (i + 1) * rows]
    total[...] = jnp.zeros(total.shape, jnp.float32)

    @pl.when(sec == 0)
    def _():
        total[...] = total_in[...] + total_beside[...]

    saved[...] = kept[...]

    def after(step, state):
        for where, source in ((sec == 0, series), (sec == last, stored)):

            @pl.when(where)
            def _(source=source):
                total[...] += state[reach : reach + planes] * source[step]

    run_steps(kinds, taps, weights, reach, slab, other, first, second, factor, begun - reach, after)
    state = (slab, other)[reach % 2]

    @pl.when(sec == last)
    def _():
        saved[...] = state[reach : reach + planes]

    orients = handoff.shape[1]
    count = orients // (last + 1)
    held = planes * count
    to_corner[...] = jnp.zeros(to_corner.shape, jnp.float32)
    for i in range(planes):
        handoff[i] = from_tile(saved[i], scratch)
        whole[...] = from_tile(total[i], scratch)
        for piece, who in (
            (share, sec),
            (to_pair, sec + 1 - 2 * odd),
            (to_across, jnp.where(sec == 0, 2, 1)),
            (to_corner, last - sec),
        ):
            piece[i * count : (i + 1) * count] = whole[pl.ds(pl.multiple_of(who * count, count), count)]
    for i in range(pair):
        to_across[held + i * orients : held + (i + 1) * orients] = from_tile(state[reach + pair * odd + i], scratch)

    @pl.when(sec == 1)
    def _():
        to_corner[...] = to_across[held:]


def finish_kernel(contour, handoff_in, share, to_pair, to_across, to_corner, handoff, density):
    sec = lax.axis_index("sec")
    planes, count = density.shape[:2]
    held = planes * count
    corner = jnp.where(sec == 2, 0.0, to_corner[:held])
    total = (share[...] + to_pair[...] + to_across[:held] + corner) / contour
    for i in range(planes):
        density[i] = total[i * count : (i + 1) * count]
    handoff[0] = handoff_in[...]

    @pl.when(sec == 2)
    def _():
        orients = handoff.shape[2]
        pair = planes // 2
        for i in range(pair):
            handoff[0, i] = to_across[held + i * orients : held + (i + 1) * orients]
            handoff[0, pair + i] = to_corner[i * orients : (i + 1) * orients]


def call(kernel, out_shape, scratch, operands, dtypes=None, aliases=None, cost=None):
    return pl.pallas_call(
        kernel,
        in_specs=[IN_VMEM] * len(operands),
        out_specs=[IN_VMEM] * len(out_shape),
        out_shape=[jax.ShapeDtypeStruct(shape, (dtypes or {}).get(i, jnp.float32)) for i, shape in enumerate(out_shape)],
        scratch_shapes=scratch,
        input_output_aliases=aliases or {},
        cost_estimate=cost,
        compiler_params=pltpu.CompilerParams(vmem_limit_bytes=VMEM_BYTES),
    )(*operands)


def paired(incoming, backward, fields, block_types, axial_taps, lateral_taps, depth_taps, bend_diagonal, bend_coupling):
    n_sec, n_gx = lax.axis_size("sec"), lax.axis_size("gx")
    steps, planes, orients, cells = backward.shape
    pair = planes // 2
    reach = (TICKS - 1) * steps, steps
    near = (-1, 1)
    rows = 2 * orients
    lanes = cells // 2
    last = n_sec - 1

    def send(array, by_sec, even=0, odd=0):
        by_sec = by_sec.items() if isinstance(by_sec, dict) else enumerate(by_sec)
        pairs = [
            (s * n_gx + g, t * n_gx + (g + (odd if s % 2 else even)) % n_gx) for s, t in by_sec for g in range(n_gx)
        ]
        return lax.ppermute(array, ("sec", "gx"), pairs)

    same, beside = (0, 1, 2, 3), (1, 0, 3, 2)
    moved = send(incoming[0], {0: 1, 1: 3})
    bundle = launch(
        incoming, fields, block_types, axial_taps, lateral_taps, depth_taps, bend_diagonal, bend_coupling
    )
    own_types = jnp.pad(block_types.astype(jnp.float32), ((0, 7), (0, lanes - steps)))
    types = send(own_types, {1: 3})
    size = planes * rows + FIELD_ROWS
    base, taps, weights = call(
        unpack_kernel, [(size, lanes), (TAP_ROWS, lanes), (2 * rows, 2 * lanes)], [], [bundle], {2: jnp.bfloat16}
    )
    moved, base, types = lax.optimization_barrier((moved, base, types))
    passed = send(moved, {3: 2})

    tile = pltpu.VMEM((rows, lanes), jnp.float32)
    packed = pltpu.VMEM((GROUP * rows, 2 * lanes), jnp.bfloat16)
    inner = pltpu.VMEM((planes, rows, lanes), jnp.float32)

    def work(extent):
        slab = pltpu.VMEM((planes + 2 * extent, rows, lanes), jnp.float32)
        return [slab, slab, packed, packed, tile]

    (piece,) = call(pack_kernel, [(size, lanes)], [tile], [base, moved, passed, types])
    own = [send(piece, same, shift, 2 * shift) for shift in near]
    backward, own_types, _ = lax.optimization_barrier((backward, own_types, piece))
    across_types = send(own_types, {2: 0})
    (stored,) = call(turn_kernel, [(steps, planes, rows, lanes)], [tile], [backward])
    own[-1], stored, across_types = lax.optimization_barrier((own[-1], stored, across_types))
    swapped = [send(each, beside) for each in own]
    table = (fields.shape[0], planes + 2 * reach[0], rows, lanes)
    known, swapped[1] = lax.optimization_barrier((piece, swapped[1]))
    (factor,) = call(factor_kernel, [table], [tile], [known, *own])
    late_stored, factor, *swapped = lax.optimization_barrier((stored, factor, *swapped))
    late_last = send(late_stored, {2: 0})
    middle, piece, kept, total, factor = call(
        early_kernel,
        [(planes, rows, lanes), (pair * rows + 8, lanes), (planes, rows, lanes), (planes, rows, lanes)]
        + [table],
        work(reach[0]),
        [taps, weights, across_types, piece, *own, *swapped, stored, factor],
        aliases={9: 4},
    )
    own = [send(piece, same, shift, shift) for shift in near]
    beside_total = send(total, beside)
    swapped = [send(each, beside) for each in own]
    held = planes * (orients // n_sec)
    handoff, share, to_pair, to_across, to_corner = call(
        functools.partial(late_kernel, tuple(-shift for shift in near), last),
        [(planes, orients, cells)]
        + [(held, cells)] * 2
        + [(held + pair * orients, cells), (pair * orients, cells)],
        work(reach[1]) + [inner, inner, pltpu.VMEM((orients, cells), jnp.float32)],
        [taps, weights, middle, *own, *swapped, factor, kept, total, beside_total]
        + [late_last, stored],
    )
    to_pair = send(to_pair, beside)
    to_across = send(to_across, (2, 0, 3, 1))
    to_corner = send(to_corner, (3, 2, 1, 0))
    handoff, density = call(
        functools.partial(finish_kernel, n_sec * steps),
        [(1,) + handoff.shape, (planes, orients // n_sec, cells)],
        [],
        [handoff, share, to_pair, to_across, to_corner],
    )
    return handoff, density


def pairs_fit(n_sec, planes, steps, orients, cells, kinds):
    return (
        n_sec == TICKS + 1 == 4
        and planes == steps
        and planes % 2 == 0
        and 2 * orients == 2 * CZ == cells // 2 == 128
        and 2 * kinds * planes <= OWN_KINDS and 10 * kinds * planes <= 2 * orients
        and GROUP < 2 * planes
    )


def solution(mesh):
    in_specs = (
        P("sec", "gx", None, None),
        P("sec", "gx", None, None),
        P(None, "gx", None),
        P("sec", None),
        P(),
        P(),
        P(),
        P(),
        P(),
    )
    out_specs = (P("sec", "gx", None, None), P("gx", "sec", None))

    def body(incoming, backward, fields, *rest):
        steps, planes, orients, cells = backward.shape
        fits = pairs_fit(mesh.shape["sec"], planes, steps, orients, cells, fields.shape[0])
        return (paired if fits else per_device)(incoming, backward, fields, *rest)

    return jax.shard_map(body, mesh=mesh, in_specs=in_specs, out_specs=out_specs, check_vma=False)
```

```python
import functools

import jax
import jax.numpy as jnp
from jax import lax
from jax.experimental import pallas as pl
from jax.experimental.pallas import tpu as pltpu
from jax.sharding import PartitionSpec as P

TICKS = 3
CZ = 64
GROUP = 6
FIELD_ROWS = 32
TAP_ROWS = 8
OWN_KINDS, FIRST_KINDS = 24, 25
VMEM_BYTES = 16 * 2**20
WHOLE_VMEM_BYTES = 62 * 2**20
IN_VMEM = pl.BlockSpec(memory_space=pltpu.VMEM)


def padded_2(block, sides, width):
    for axis, dim in sides:
        count = lax.axis_size(axis)
        forward = [(i, i + 1) for i in range(count - 1)]
        forward.append((count - 1, 0))
        backward = [(target, source) for source, target in forward]
        low = lax.ppermute(
            lax.slice_in_dim(block, block.shape[dim] - width, None, axis=dim), axis, forward
        )
        high = lax.ppermute(lax.slice_in_dim(block, 0, width, axis=dim), axis, backward)
        block = jnp.concatenate([low, block, high], axis=dim)
    return block


def from_behind(array, axis, by):
    length = lax.axis_size(axis)
    pairs = [(i, i + by) for i in range(length) if 0 <= i + by < length]
    return lax.ppermute(array, axis, pairs)


def boltzmann(fields, kinds):
    selector = kinds == jnp.arange(fields.shape[0], dtype=jnp.int32)
    chosen = jnp.sum(jnp.where(selector[:, None, None], fields, jnp.zeros_like(fields)), axis=0)
    return jnp.exp(-chosen)


def column(taps, which):
    return taps[which][None, :, None]


def advance_padded(padded, factor, axial_taps, lateral_taps, depth_taps, kernel):
    along_x = (
        column(axial_taps, 0) * padded[:-2]
        + column(axial_taps, 1) * padded[1:-1]
        + column(axial_taps, 2) * padded[2:]
    )
    along_y = (
        column(lateral_taps, 0) * jnp.roll(along_x, CZ, axis=2)
        + column(lateral_taps, 1) * along_x
        + column(lateral_taps, 2) * jnp.roll(along_x, -CZ, axis=2)
    )
    depth_pos = (jnp.arange(along_y.shape[2], dtype=jnp.int32) % CZ)[None, None, :]
    behind = jnp.where(
        depth_pos == 0, jnp.roll(along_y, -(CZ - 1), axis=2), jnp.roll(along_y, 1, axis=2)
    )
    ahead = jnp.where(
        depth_pos == CZ - 1, jnp.roll(along_y, CZ - 1, axis=2), jnp.roll(along_y, -1, axis=2)
    )
    along_z = (
        column(depth_taps, 0) * behind
        + column(depth_taps, 1) * along_y
        + column(depth_taps, 2) * ahead
    )
    blended = jnp.einsum(
        "uv,xvc->xuc",
        kernel,
        along_z,
        precision=lax.Precision.HIGHEST,
        preferred_element_type=jnp.float32,
    )
    return blended * factor[:, None, :]


def per_device(
    incoming,
    backward,
    fields,
    block_types,
    axial_taps,
    lateral_taps,
    depth_taps,
    bend_diagonal,
    bend_coupling,
):
    kernel = jnp.diag(bend_diagonal) + bend_coupling
    steps_each = block_types.shape[1]
    planes = incoming.shape[1]
    start = incoming[0]
    first_section = lax.axis_index("sec") == 0
    wide_fields = padded_2(fields, (("gx", 1),), steps_each)
    factors = [boltzmann(wide_fields, block_types[0, position]) for position in range(steps_each)]
    current = start
    outgoing = start
    accumulated = jnp.zeros(start.shape, jnp.float32)
    for tick_index in range(TICKS):
        final_tick = tick_index + 1 == TICKS
        extended = padded_2(current, (("gx", 0),), steps_each)
        for position in range(steps_each):
            margin = steps_each - position - 1
            offset = steps_each - margin
            factor = factors[position][offset : offset + planes + 2 * margin]
            extended = advance_padded(
                extended, factor, axial_taps, lateral_taps, depth_taps, kernel
            )
            if final_tick:
                accumulated = accumulated + extended[margin : margin + planes] * backward[
                    position
                ].astype(jnp.float32)
        outgoing = extended
        if not final_tick:
            shifted = from_behind(outgoing, "sec", 1)
            current = jnp.where(first_section, start, shifted)
    reduced = lax.psum_scatter(accumulated, "sec", scatter_dimension=1, tiled=True)
    density = reduced / (lax.axis_size("sec") * steps_each)
    return (outgoing[None], density)


def to_tile(plane, scratch):
    half = plane.shape[1] // 2
    scratch[...] = jnp.concatenate([plane[:, :half], plane[:, half:]], axis=0).T
    return reorder(scratch)


def reorder(scratch):
    rows = scratch.shape[0]
    return jnp.concatenate(
        [scratch[pl.ds(yl * CZ + zl, 8, stride=8), :] for yl in range(rows // CZ) for zl in range(CZ // 8)], axis=0
    )


def from_tile(tile, scratch):
    rows = tile.shape[0]
    for yl in range(rows // CZ):
        for zl in range(CZ // 8):
            at = (yl * (CZ // 8) + zl) * 8
            scratch[pl.ds(yl * CZ + zl, 8, stride=8), :] = tile[at : at + 8]
    turned = scratch[...].T
    half = turned.shape[0] // 2
    return jnp.concatenate([turned[:half], turned[half:]], axis=1)


def stencil(behind, here, ahead, taps):
    a = here + taps[0] * behind + taps[1] * ahead
    low, high = a[:CZ], a[CZ:]
    low_turned = pltpu.roll(low, a.shape[1] // 2, 1)
    high_turned = pltpu.roll(high, a.shape[1] // 2, 1)
    out = []
    for b in (
        low + taps[2] * high_turned + taps[3] * high,
        high + taps[2] * low + taps[3] * low_turned,
    ):
        back = jnp.concatenate([pltpu.roll(b[-8:], 1, 0), b[:-8]], axis=0)
        front = jnp.concatenate([b[8:], pltpu.roll(b[:8], 7, 0)], axis=0)
        out.append(b + taps[4] * back + taps[5] * front)
    return jnp.concatenate(out, axis=0)


def position():
    sec = lax.axis_index("sec")
    return sec, lax.rem(sec, 2)


def launch_kernel(*refs):
    sources, bundle, scratch, copies, sems = refs[:8], refs[8], refs[9], refs[10:18], refs[18]
    moves = [pltpu.make_async_copy(s, c, sems.at[i]) for i, (s, c) in enumerate(zip(sources, copies))]
    for move in moves:
        move.start()
    incoming, fields, kinds, axial, lateral, depth, diagonal, coupling = copies
    for move in moves[1:]:
        move.wait()
    rows = scratch.shape[0]
    orients = rows // 2
    ratios = [each[w : w + 1] / each[1:2] for each in (axial, lateral, depth) for w in (0, 2)]
    for i, ratio in enumerate(ratios + ratios[:2]):
        bundle[i : i + 1] = jnp.concatenate([ratio, ratio], axis=1)
    square = (orients, orients)
    same = lax.broadcasted_iota(jnp.int32, square, 0) == lax.broadcasted_iota(jnp.int32, square, 1)
    kernel = jnp.where(same, diagonal[...], 0.0) + coupling[...]
    kernel = kernel * (axial[1:2] * lateral[1:2] * depth[1:2])
    upper = jnp.concatenate([kernel, jnp.zeros_like(kernel)], axis=1)
    bundle[TAP_ROWS : TAP_ROWS + rows] = jnp.concatenate([upper, pltpu.roll(upper, orients, 1)], axis=0).T
    line = kinds[...].astype(jnp.float32)
    line = jnp.concatenate([line, jnp.zeros((1, rows - line.shape[1]), jnp.float32)], axis=1)
    types = line
    planes = incoming.shape[1]
    at = TAP_ROWS + rows
    bundle[at : at + FIELD_ROWS] = jnp.zeros((FIELD_ROWS, rows), jnp.float32)
    for kind in range(fields.shape[0]):
        for i in range(planes):
            line = fields[kind, i : i + 1, :]
            here = at + (kind * planes + i) * 2
            bundle[here : here + 1] = line[:, :rows]
            bundle[here + 1 : here + 2] = line[:, rows:]
    bundle[at + OWN_KINDS : at + OWN_KINDS + 1] = types
    moves[0].wait()
    for i in range(planes):
        here = at + FIELD_ROWS + i * rows
        bundle[here : here + rows] = to_tile(incoming[0, i], scratch)


def launch(incoming, fields, kinds, axial, lateral, depth, diagonal, coupling):
    planes, orients, cells = incoming.shape[1:]
    rows = 2 * orients
    operands = [incoming, fields, kinds, axial, lateral, depth, diagonal.reshape(1, -1), coupling]
    return pl.pallas_call(
        launch_kernel,
        in_specs=[pl.BlockSpec(memory_space=pltpu.HBM)] * len(operands),
        out_specs=IN_VMEM,
        out_shape=jax.ShapeDtypeStruct((TAP_ROWS + rows + FIELD_ROWS + planes * rows, rows), jnp.float32),
        scratch_shapes=[pltpu.VMEM((rows, rows), jnp.float32)]
        + [pltpu.VMEM(each.shape, each.dtype) for each in operands]
        + [pltpu.SemaphoreType.DMA((len(operands),))],
        compiler_params=pltpu.CompilerParams(vmem_limit_bytes=WHOLE_VMEM_BYTES),
    )(*operands)


def turn_kernel(backward, out, scratch):
    for step in range(out.shape[0]):
        for i in range(out.shape[1]):
            out[step, i] = to_tile(backward[step, i].astype(jnp.float32), scratch)


def unpack_kernel(bundle, out, taps, weights):
    rows = taps.shape[1]
    taps[...] = bundle[:TAP_ROWS]
    twice = bundle[TAP_ROWS : TAP_ROWS + rows]
    coarse = twice.astype(jnp.bfloat16)
    fine = (twice - coarse.astype(jnp.float32)).astype(jnp.bfloat16)
    weights[...] = jnp.concatenate(
        [jnp.concatenate([coarse, fine], axis=1), jnp.concatenate([coarse, jnp.zeros_like(fine)], axis=1)], axis=0
    )
    at = out.shape[0] - FIELD_ROWS
    lines = TAP_ROWS + rows
    out[at:] = bundle[lines : lines + FIELD_ROWS]
    out[:at] = bundle[lines + FIELD_ROWS :]


def pack_kernel(base, moved, passed, types, out, scratch):
    sec, odd = position()
    rows = scratch.shape[0]
    at = out.shape[0] - FIELD_ROWS
    out[at:] = base[at:]
    out[at + FIRST_KINDS : at + FIRST_KINDS + 1] = jnp.where(
        sec == 0, base[at + OWN_KINDS : at + OWN_KINDS + 1], types[:1]
    )

    @pl.when(sec == 0)
    def _():
        out[:at] = base[:at]

    def fill(source):
        for i in range(source.shape[0]):
            out[i * rows : (i + 1) * rows] = to_tile(source[i], scratch)

    pl.when(odd == 1)(lambda: fill(moved))
    pl.when((sec > 0) & (odd == 0))(lambda: fill(passed))


def scalars_of(row, count):
    lane = lax.broadcasted_iota(jnp.int32, row.shape, 1)
    return [jnp.sum(jnp.where(lane == i, row, 0.0)).astype(jnp.int32) for i in range(count)]


def places(odd, planes, reach, blocks):
    return [reach + block * planes + planes // 2 * core for core in (odd, 1 - odd) for block in blocks]


def run_steps(kinds, taps, weights, count, slab, other, first, second, factor, offset, after):
    tap = [taps[i : i + 1, :] for i in range(6)]
    extent, rows, lanes = slab.shape
    buffers = (slab, other)

    def blend(source, at, packed):
        for i in range(GROUP):
            e = stencil(source[at + i - 1], source[at + i], source[at + i + 1], tap)
            coarse = e.astype(jnp.bfloat16)
            packed[i * rows : (i + 1) * rows, :lanes] = coarse
            packed[i * rows : (i + 1) * rows, lanes:] = (e - coarse.astype(jnp.float32)).astype(jnp.bfloat16)

    def mix(target, at, packed, kind):
        product = jnp.dot(packed[...], weights[...], preferred_element_type=jnp.float32)
        product = product[:, :lanes] + product[:, lanes:]
        for i in range(GROUP):
            target[at + i] = product[i * rows : (i + 1) * rows] * factor[kind, at + i + offset]

    for step in range(count):
        source, target = buffers[step % 2], buffers[1 - step % 2]
        begin, width = step + 1, extent - 2 * step - 2
        groups = -(-width // GROUP)
        kind = kinds[step]

        def at(i, begin=begin, width=width):
            return jnp.minimum(begin + i * GROUP, begin + width - GROUP)

        blend(source, at(0), first)
        if groups > 1:

            def body(i, carry, source=source, target=target, at=at, kind=kind):
                blend(source, at(2 * i + 1), second)
                mix(target, at(2 * i), first, kind)
                blend(source, at(2 * i + 2), first)
                mix(target, at(2 * i + 1), second, kind)
                return carry

            lax.fori_loop(0, (groups - 1) // 2, body, 0)
        if groups % 2 == 0:
            blend(source, at(groups - 1), second)
            mix(target, at(groups - 2), first, kind)
            mix(target, at(groups - 1), second, kind)
        else:
            mix(target, at(groups - 1), first, kind)
        after(step, target)


def spread_factor(columns, factor, starts, width):
    rows, lanes = factor.shape[2:]
    pair = width // (2 * factor.shape[0])
    right = (lax.broadcasted_iota(jnp.int32, (rows, lanes), 1) >= lanes // 2).astype(jnp.int32)
    for piece, start in enumerate(starts):
        for kind in range(factor.shape[0]):
            for i in range(pair):
                at = piece * width + (kind * pair + i) * 2
                factor[kind, start + i] = jnp.take_along_axis(columns, right + at, axis=1, mode="promise_in_bounds")


def slab_starts(planes, reach):
    odd = position()[1]
    mine, others = (planes * (1 + core) for core in (odd, 1 - odd))
    return [reach, reach + mine, reach - mine, reach + others, reach - others]


def fill_factor(pieces, starts, factor, scratch):
    rows = scratch.shape[0]
    planes = (pieces[0].shape[0] - FIELD_ROWS) // rows
    width = 2 * planes * factor.shape[0]
    lines = [piece[planes * rows : planes * rows + width] for piece in pieces]
    lines.append(jnp.zeros((rows - width * len(pieces), rows), jnp.float32))
    scratch[...] = jnp.exp(-jnp.concatenate(lines, axis=0)).T
    spread_factor(reorder(scratch), factor, starts, width)


def factor_kernel(*refs):
    pieces, factor, scratch = refs[:3], refs[3], refs[4]
    planes = (pieces[0].shape[0] - FIELD_ROWS) // scratch.shape[0]
    fill_factor(pieces, slab_starts(planes, (factor.shape[1] - planes) // 2)[:3], factor, scratch)


def early_kernel(taps, weights, across, *refs):
    pieces, stored, (middle, half_out, kept, total, factor) = refs[:5], refs[5], refs[7:12]
    slab, other, first, second, scratch = refs[12:]
    sec, odd = position()
    planes, rows = middle.shape[:2]
    pair = planes // 2
    reach = (slab.shape[0] - planes) // 2
    starts = slab_starts(planes, reach)
    for piece, start in zip(pieces, starts):
        for i in range(planes):
            slab[start + i] = piece[i * rows : (i + 1) * rows]
    at = planes * rows
    steps = stored.shape[0]
    own_kinds, first_kinds = (pieces[0][at + row : at + row + 1] for row in (OWN_KINDS, FIRST_KINDS))
    beside_kinds, beside_first = (pieces[3][at + row : at + row + 1] for row in (OWN_KINDS, FIRST_KINDS))
    kinds = scalars_of(jnp.where((sec == 1) | (sec == 2), beside_first, first_kinds), steps)
    kinds += scalars_of(jnp.where((sec == 1) | (sec == 2), own_kinds, beside_kinds), steps)
    last_kinds = jnp.where(sec == 0, across[:1], own_kinds)
    half_out[pair * rows :] = jnp.broadcast_to(last_kinds, (8, rows))
    fill_factor(pieces[3:], starts[3:], factor, scratch)
    total[...] = jnp.zeros(total.shape, jnp.float32)
    kept[...] = jnp.zeros(kept.shape, jnp.float32)

    def after(step, state):
        @pl.when(sec == step // steps)
        def _():
            total[...] += state[reach : reach + planes] * stored[step % steps]
            if (step + 1) % steps == 0:
                kept[...] = state[reach : reach + planes]

    run_steps(kinds, taps, weights, reach, slab, other, first, second, factor, 0, after)
    state = (slab, other)[reach % 2]
    middle[...] = state[reach : reach + planes]
    for i in range(pair):
        half_out[i * rows : (i + 1) * rows] = state[reach + pair * odd + i]


def late_kernel(blocks, last, taps, weights, middle, *refs):
    pieces, refs = refs[: 2 * len(blocks)], refs[2 * len(blocks) :]
    factor, kept, total_in, total_beside, series, stored = refs[:6]
    handoff, share, to_pair, to_across, to_corner = refs[6:11]
    slab, other, first, second, scratch, total, saved, whole = refs[11:]
    sec, odd = position()
    planes, rows = middle.shape[:2]
    pair = planes // 2
    reach = (slab.shape[0] - planes) // 2
    begun = (factor.shape[1] - planes) // 2
    even, uneven = (jnp.where(odd == core, pieces[0][pair * rows :], pieces[len(blocks)][pair * rows :]) for core in (0, 1))
    kinds = scalars_of(jnp.where(sec < 2, even, uneven)[:1], reach)
    slab[reach : reach + planes] = middle[...]
    for piece, start in zip(pieces, places(odd, planes, reach, blocks)):
        for i in range(pair):
            slab[start + i] = piece[i * rows : (i + 1) * rows]
    total[...] = jnp.zeros(total.shape, jnp.float32)

    @pl.when(sec == 0)
    def _():
        total[...] = total_in[...] + total_beside[...]

    saved[...] = kept[...]

    def after(step, state):
        for where, source in ((sec == 0, series), (sec == last, stored)):

            @pl.when(where)
            def _(source=source):
                total[...] += state[reach : reach + planes] * source[step]

    run_steps(kinds, taps, weights, reach, slab, other, first, second, factor, begun - reach, after)
    state = (slab, other)[reach % 2]

    @pl.when(sec == last)
    def _():
        saved[...] = state[reach : reach + planes]

    orients = handoff.shape[1]
    count = orients // (last + 1)
    held = planes * count
    to_corner[...] = jnp.zeros(to_corner.shape, jnp.float32)
    for i in range(planes):
        handoff[i] = from_tile(saved[i], scratch)
        whole[...] = from_tile(total[i], scratch)
        for piece, who in (
            (share, sec),
            (to_pair, sec + 1 - 2 * odd),
            (to_across, jnp.where(sec == 0, 2, 1)),
            (to_corner, last - sec),
        ):
            piece[i * count : (i + 1) * count] = whole[pl.ds(pl.multiple_of(who * count, count), count)]
    few = planes // 4
    for i in range(few):
        to_across[held + i * orients : held + (i + 1) * orients] = from_tile(state[reach + i], scratch)

    @pl.when(sec == 1)
    def _():
        for i in range(few, planes):
            to_corner[(i - few) * orients : (i - few + 1) * orients] = from_tile(state[reach + i], scratch)


def finish_kernel(contour, handoff_in, share, to_pair, to_across, to_corner, handoff, density):
    sec = lax.axis_index("sec")
    planes, count = density.shape[:2]
    held = planes * count
    corner = jnp.where(sec == 2, 0.0, to_corner[:held])
    total = (share[...] + to_pair[...] + to_across[:held] + corner) / contour
    for i in range(planes):
        density[i] = total[i * count : (i + 1) * count]
    handoff[0] = handoff_in[...]

    @pl.when(sec == 2)
    def _():
        orients = handoff.shape[2]
        few = planes // 4
        for i in range(few):
            handoff[0, i] = to_across[held + i * orients : held + (i + 1) * orients]
        for i in range(few, planes):
            handoff[0, i] = to_corner[(i - few) * orients : (i - few + 1) * orients]


def call(kernel, out_shape, scratch, operands, dtypes=None, aliases=None, cost=None):
    return pl.pallas_call(
        kernel,
        in_specs=[IN_VMEM] * len(operands),
        out_specs=[IN_VMEM] * len(out_shape),
        out_shape=[jax.ShapeDtypeStruct(shape, (dtypes or {}).get(i, jnp.float32)) for i, shape in enumerate(out_shape)],
        scratch_shapes=scratch,
        input_output_aliases=aliases or {},
        cost_estimate=cost,
        compiler_params=pltpu.CompilerParams(vmem_limit_bytes=VMEM_BYTES),
    )(*operands)


def paired(incoming, backward, fields, block_types, axial_taps, lateral_taps, depth_taps, bend_diagonal, bend_coupling):
    n_sec, n_gx = lax.axis_size("sec"), lax.axis_size("gx")
    steps, planes, orients, cells = backward.shape
    pair = planes // 2
    reach = (TICKS - 1) * steps, steps
    near = (-1, 1)
    rows = 2 * orients
    lanes = cells // 2
    last = n_sec - 1

    def send(array, by_sec, even=0, odd=0):
        by_sec = by_sec.items() if isinstance(by_sec, dict) else enumerate(by_sec)
        pairs = [
            (s * n_gx + g, t * n_gx + (g + (odd if s % 2 else even)) % n_gx) for s, t in by_sec for g in range(n_gx)
        ]
        return lax.ppermute(array, ("sec", "gx"), pairs)

    same, beside = (0, 1, 2, 3), (1, 0, 3, 2)
    moved = send(incoming[0], {0: 1, 1: 3})
    bundle = launch(
        incoming, fields, block_types, axial_taps, lateral_taps, depth_taps, bend_diagonal, bend_coupling
    )
    own_types = jnp.pad(block_types.astype(jnp.float32), ((0, 7), (0, lanes - steps)))
    types = send(own_types, {1: 3})
    size = planes * rows + FIELD_ROWS
    base, taps, weights = call(
        unpack_kernel, [(size, lanes), (TAP_ROWS, lanes), (2 * rows, 2 * lanes)], [], [bundle], {2: jnp.bfloat16}
    )
    moved, base, types = lax.optimization_barrier((moved, base, types))
    passed = send(moved, {3: 2})

    tile = pltpu.VMEM((rows, lanes), jnp.float32)
    packed = pltpu.VMEM((GROUP * rows, 2 * lanes), jnp.bfloat16)
    inner = pltpu.VMEM((planes, rows, lanes), jnp.float32)

    def work(extent):
        slab = pltpu.VMEM((planes + 2 * extent, rows, lanes), jnp.float32)
        return [slab, slab, packed, packed, tile]

    (piece,) = call(pack_kernel, [(size, lanes)], [tile], [base, moved, passed, types])
    own = [send(piece, same, shift, 2 * shift) for shift in near]
    backward, own_types, _ = lax.optimization_barrier((backward, own_types, piece))
    across_types = send(own_types, {2: 0})
    (stored,) = call(turn_kernel, [(steps, planes, rows, lanes)], [tile], [backward])
    own[-1], stored, across_types = lax.optimization_barrier((own[-1], stored, across_types))
    swapped = [send(each, beside) for each in own]
    table = (fields.shape[0], planes + 2 * reach[0], rows, lanes)
    known, swapped[1] = lax.optimization_barrier((piece, swapped[1]))
    (factor,) = call(factor_kernel, [table], [tile], [known, *own])
    late_stored, factor, *swapped = lax.optimization_barrier((stored, factor, *swapped))
    late_last = send(late_stored, {2: 0})
    middle, piece, kept, total, factor = call(
        early_kernel,
        [(planes, rows, lanes), (pair * rows + 8, lanes), (planes, rows, lanes), (planes, rows, lanes)]
        + [table],
        work(reach[0]),
        [taps, weights, across_types, piece, *own, *swapped, stored, factor],
        aliases={9: 4},
    )
    own = [send(piece, same, shift, shift) for shift in near]
    beside_total = send(total, beside)
    swapped = [send(each, beside) for each in own]
    held = planes * (orients // n_sec)
    handoff, share, to_pair, to_across, to_corner = call(
        functools.partial(late_kernel, tuple(-shift for shift in near), last),
        [(planes, orients, cells)]
        + [(held, cells)] * 2
        + [(held + planes // 4 * orients, cells), ((planes - planes // 4) * orients, cells)],
        work(reach[1]) + [inner, inner, pltpu.VMEM((orients, cells), jnp.float32)],
        [taps, weights, middle, *own, *swapped, factor, kept, total, beside_total]
        + [late_last, stored],
    )
    to_pair = send(to_pair, beside)
    to_across = send(to_across, (2, 0, 3, 1))
    to_corner = send(to_corner, (3, 2, 1, 0))
    handoff, density = call(
        functools.partial(finish_kernel, n_sec * steps),
        [(1,) + handoff.shape, (planes, orients // n_sec, cells)],
        [],
        [handoff, share, to_pair, to_across, to_corner],
    )
    return handoff, density


def pairs_fit(n_sec, planes, steps, orients, cells, kinds):
    return (
        n_sec == TICKS + 1 == 4
        and planes == steps
        and planes % 4 == 0
        and 2 * orients == 2 * CZ == cells // 2 == 128
        and 2 * kinds * planes <= OWN_KINDS and 10 * kinds * planes <= 2 * orients
        and GROUP < 2 * planes
    )


def solution(mesh):
    in_specs = (
        P("sec", "gx", None, None),
        P("sec", "gx", None, None),
        P(None, "gx", None),
        P("sec", None),
        P(),
        P(),
        P(),
        P(),
        P(),
    )
    out_specs = (P("sec", "gx", None, None), P("gx", "sec", None))

    def body(incoming, backward, fields, *rest):
        steps, planes, orients, cells = backward.shape
        fits = pairs_fit(mesh.shape["sec"], planes, steps, orients, cells, fields.shape[0])
        return (paired if fits else per_device)(incoming, backward, fields, *rest)

    return jax.shard_map(body, mesh=mesh, in_specs=in_specs, out_specs=out_specs, check_vma=False)
```

```python
import functools

import jax
import jax.numpy as jnp
from jax import lax
from jax.experimental import pallas as pl
from jax.experimental.pallas import tpu as pltpu
from jax.sharding import PartitionSpec as P

TICKS = 3
CZ = 64
GROUP = 6
FIELD_ROWS = 32
TAP_ROWS = 8
OWN_KINDS, FIRST_KINDS = 24, 25
VMEM_BYTES = 16 * 2**20
WHOLE_VMEM_BYTES = 62 * 2**20
IN_VMEM = pl.BlockSpec(memory_space=pltpu.VMEM)


def padded_2(block, sides, width):
    for axis, dim in sides:
        count = lax.axis_size(axis)
        forward = [(i, i + 1) for i in range(count - 1)]
        forward.append((count - 1, 0))
        backward = [(target, source) for source, target in forward]
        low = lax.ppermute(
            lax.slice_in_dim(block, block.shape[dim] - width, None, axis=dim), axis, forward
        )
        high = lax.ppermute(lax.slice_in_dim(block, 0, width, axis=dim), axis, backward)
        block = jnp.concatenate([low, block, high], axis=dim)
    return block


def from_behind(array, axis, by):
    length = lax.axis_size(axis)
    pairs = [(i, i + by) for i in range(length) if 0 <= i + by < length]
    return lax.ppermute(array, axis, pairs)


def boltzmann(fields, kinds):
    selector = kinds == jnp.arange(fields.shape[0], dtype=jnp.int32)
    chosen = jnp.sum(jnp.where(selector[:, None, None], fields, jnp.zeros_like(fields)), axis=0)
    return jnp.exp(-chosen)


def column(taps, which):
    return taps[which][None, :, None]


def advance_padded(padded, factor, axial_taps, lateral_taps, depth_taps, kernel):
    along_x = (
        column(axial_taps, 0) * padded[:-2]
        + column(axial_taps, 1) * padded[1:-1]
        + column(axial_taps, 2) * padded[2:]
    )
    along_y = (
        column(lateral_taps, 0) * jnp.roll(along_x, CZ, axis=2)
        + column(lateral_taps, 1) * along_x
        + column(lateral_taps, 2) * jnp.roll(along_x, -CZ, axis=2)
    )
    depth_pos = (jnp.arange(along_y.shape[2], dtype=jnp.int32) % CZ)[None, None, :]
    behind = jnp.where(
        depth_pos == 0, jnp.roll(along_y, -(CZ - 1), axis=2), jnp.roll(along_y, 1, axis=2)
    )
    ahead = jnp.where(
        depth_pos == CZ - 1, jnp.roll(along_y, CZ - 1, axis=2), jnp.roll(along_y, -1, axis=2)
    )
    along_z = (
        column(depth_taps, 0) * behind
        + column(depth_taps, 1) * along_y
        + column(depth_taps, 2) * ahead
    )
    blended = jnp.einsum(
        "uv,xvc->xuc",
        kernel,
        along_z,
        precision=lax.Precision.HIGHEST,
        preferred_element_type=jnp.float32,
    )
    return blended * factor[:, None, :]


def per_device(
    incoming,
    backward,
    fields,
    block_types,
    axial_taps,
    lateral_taps,
    depth_taps,
    bend_diagonal,
    bend_coupling,
):
    kernel = jnp.diag(bend_diagonal) + bend_coupling
    steps_each = block_types.shape[1]
    planes = incoming.shape[1]
    start = incoming[0]
    first_section = lax.axis_index("sec") == 0
    wide_fields = padded_2(fields, (("gx", 1),), steps_each)
    factors = [boltzmann(wide_fields, block_types[0, position]) for position in range(steps_each)]
    current = start
    outgoing = start
    accumulated = jnp.zeros(start.shape, jnp.float32)
    for tick_index in range(TICKS):
        final_tick = tick_index + 1 == TICKS
        extended = padded_2(current, (("gx", 0),), steps_each)
        for position in range(steps_each):
            margin = steps_each - position - 1
            offset = steps_each - margin
            factor = factors[position][offset : offset + planes + 2 * margin]
            extended = advance_padded(
                extended, factor, axial_taps, lateral_taps, depth_taps, kernel
            )
            if final_tick:
                accumulated = accumulated + extended[margin : margin + planes] * backward[
                    position
                ].astype(jnp.float32)
        outgoing = extended
        if not final_tick:
            shifted = from_behind(outgoing, "sec", 1)
            current = jnp.where(first_section, start, shifted)
    reduced = lax.psum_scatter(accumulated, "sec", scatter_dimension=1, tiled=True)
    density = reduced / (lax.axis_size("sec") * steps_each)
    return (outgoing[None], density)


def to_tile(plane, scratch):
    half = plane.shape[1] // 2
    scratch[...] = jnp.concatenate([plane[:, :half], plane[:, half:]], axis=0).T
    return reorder(scratch)


def reorder(scratch):
    rows = scratch.shape[0]
    return jnp.concatenate(
        [scratch[pl.ds(yl * CZ + zl, 8, stride=8), :] for yl in range(rows // CZ) for zl in range(CZ // 8)], axis=0
    )


def from_tile(tile, scratch):
    rows = tile.shape[0]
    for yl in range(rows // CZ):
        for zl in range(CZ // 8):
            at = (yl * (CZ // 8) + zl) * 8
            scratch[pl.ds(yl * CZ + zl, 8, stride=8), :] = tile[at : at + 8]
    turned = scratch[...].T
    half = turned.shape[0] // 2
    return jnp.concatenate([turned[:half], turned[half:]], axis=1)


def stencil(behind, here, ahead, taps):
    a = here + taps[0] * behind + taps[1] * ahead
    low, high = a[:CZ], a[CZ:]
    low_turned = pltpu.roll(low, a.shape[1] // 2, 1)
    high_turned = pltpu.roll(high, a.shape[1] // 2, 1)
    out = []
    for b in (
        low + taps[2] * high_turned + taps[3] * high,
        high + taps[2] * low + taps[3] * low_turned,
    ):
        back = jnp.concatenate([pltpu.roll(b[-8:], 1, 0), b[:-8]], axis=0)
        front = jnp.concatenate([b[8:], pltpu.roll(b[:8], 7, 0)], axis=0)
        out.append(b + taps[4] * back + taps[5] * front)
    return jnp.concatenate(out, axis=0)


def position():
    sec = lax.axis_index("sec")
    return sec, lax.rem(sec, 2)


def launch_kernel(*refs):
    sources, bundle, scratch, copies, sems = refs[:8], refs[8], refs[9], refs[10:18], refs[18]
    moves = [pltpu.make_async_copy(s, c, sems.at[i]) for i, (s, c) in enumerate(zip(sources, copies))]
    for move in moves:
        move.start()
    incoming, fields, kinds, axial, lateral, depth, diagonal, coupling = copies
    for move in moves[1:]:
        move.wait()
    rows = scratch.shape[0]
    orients = rows // 2
    ratios = [each[w : w + 1] / each[1:2] for each in (axial, lateral, depth) for w in (0, 2)]
    for i, ratio in enumerate(ratios + ratios[:2]):
        bundle[i : i + 1] = jnp.concatenate([ratio, ratio], axis=1)
    square = (orients, orients)
    same = lax.broadcasted_iota(jnp.int32, square, 0) == lax.broadcasted_iota(jnp.int32, square, 1)
    kernel = jnp.where(same, diagonal[...], 0.0) + coupling[...]
    kernel = kernel * (axial[1:2] * lateral[1:2] * depth[1:2])
    upper = jnp.concatenate([kernel, jnp.zeros_like(kernel)], axis=1)
    bundle[TAP_ROWS : TAP_ROWS + rows] = jnp.concatenate([upper, pltpu.roll(upper, orients, 1)], axis=0).T
    line = kinds[...].astype(jnp.float32)
    line = jnp.concatenate([line, jnp.zeros((1, rows - line.shape[1]), jnp.float32)], axis=1)
    types = line
    planes = incoming.shape[1]
    at = TAP_ROWS + rows
    bundle[at : at + FIELD_ROWS] = jnp.zeros((FIELD_ROWS, rows), jnp.float32)
    for kind in range(fields.shape[0]):
        for i in range(planes):
            line = fields[kind, i : i + 1, :]
            here = at + (kind * planes + i) * 2
            bundle[here : here + 1] = line[:, :rows]
            bundle[here + 1 : here + 2] = line[:, rows:]
    bundle[at + OWN_KINDS : at + OWN_KINDS + 1] = types
    moves[0].wait()
    for i in range(planes):
        here = at + FIELD_ROWS + i * rows
        bundle[here : here + rows] = to_tile(incoming[0, i], scratch)


def launch(incoming, fields, kinds, axial, lateral, depth, diagonal, coupling):
    planes, orients, cells = incoming.shape[1:]
    rows = 2 * orients
    operands = [incoming, fields, kinds, axial, lateral, depth, diagonal.reshape(1, -1), coupling]
    return pl.pallas_call(
        launch_kernel,
        in_specs=[pl.BlockSpec(memory_space=pltpu.HBM)] * len(operands),
        out_specs=IN_VMEM,
        out_shape=jax.ShapeDtypeStruct((TAP_ROWS + rows + FIELD_ROWS + planes * rows, rows), jnp.float32),
        scratch_shapes=[pltpu.VMEM((rows, rows), jnp.float32)]
        + [pltpu.VMEM(each.shape, each.dtype) for each in operands]
        + [pltpu.SemaphoreType.DMA((len(operands),))],
        compiler_params=pltpu.CompilerParams(vmem_limit_bytes=WHOLE_VMEM_BYTES),
    )(*operands)


def turn_kernel(backward, out, scratch):
    for step in range(out.shape[0]):
        for i in range(out.shape[1]):
            out[step, i] = to_tile(backward[step, i].astype(jnp.float32), scratch)


def unpack_kernel(bundle, out, taps, weights):
    rows = taps.shape[1]
    taps[...] = bundle[:TAP_ROWS]
    twice = bundle[TAP_ROWS : TAP_ROWS + rows]
    coarse = twice.astype(jnp.bfloat16)
    fine = (twice - coarse.astype(jnp.float32)).astype(jnp.bfloat16)
    weights[...] = jnp.concatenate(
        [jnp.concatenate([coarse, fine], axis=1), jnp.concatenate([coarse, jnp.zeros_like(fine)], axis=1)], axis=0
    )
    at = out.shape[0] - FIELD_ROWS
    lines = TAP_ROWS + rows
    out[at:] = bundle[lines : lines + FIELD_ROWS]
    out[:at] = bundle[lines + FIELD_ROWS :]


def pack_kernel(base, moved, passed, types, out, scratch):
    sec, odd = position()
    rows = scratch.shape[0]
    at = out.shape[0] - FIELD_ROWS
    out[at:] = base[at:]
    out[at + FIRST_KINDS : at + FIRST_KINDS + 1] = jnp.where(
        sec == 0, base[at + OWN_KINDS : at + OWN_KINDS + 1], types[:1]
    )

    @pl.when(sec == 0)
    def _():
        out[:at] = base[:at]

    def fill(source):
        for i in range(source.shape[0]):
            out[i * rows : (i + 1) * rows] = to_tile(source[i], scratch)

    pl.when(odd == 1)(lambda: fill(moved))
    pl.when((sec > 0) & (odd == 0))(lambda: fill(passed))


def scalars_of(row, count):
    lane = lax.broadcasted_iota(jnp.int32, row.shape, 1)
    return [jnp.sum(jnp.where(lane == i, row, 0.0)).astype(jnp.int32) for i in range(count)]


def places(odd, planes, reach, blocks):
    return [reach + block * planes + planes // 2 * core for core in (odd, 1 - odd) for block in blocks]


def run_steps(kinds, taps, weights, count, slab, other, first, second, factor, offset, after):
    tap = [taps[i : i + 1, :] for i in range(6)]
    extent, rows, lanes = slab.shape
    buffers = (slab, other)

    def blend(source, at, packed):
        for i in range(GROUP):
            e = stencil(source[at + i - 1], source[at + i], source[at + i + 1], tap)
            coarse = e.astype(jnp.bfloat16)
            packed[i * rows : (i + 1) * rows, :lanes] = coarse
            packed[i * rows : (i + 1) * rows, lanes:] = (e - coarse.astype(jnp.float32)).astype(jnp.bfloat16)

    def mix(target, at, packed, kind):
        product = jnp.dot(packed[...], weights[...], preferred_element_type=jnp.float32)
        product = product[:, :lanes] + product[:, lanes:]
        for i in range(GROUP):
            target[at + i] = product[i * rows : (i + 1) * rows] * factor[kind, at + i + offset]

    for step in range(count):
        source, target = buffers[step % 2], buffers[1 - step % 2]
        begin, width = step + 1, extent - 2 * step - 2
        groups = -(-width // GROUP)
        kind = kinds[step]

        def at(i, begin=begin, width=width):
            return jnp.minimum(begin + i * GROUP, begin + width - GROUP)

        blend(source, at(0), first)
        if groups > 1:

            def body(i, carry, source=source, target=target, at=at, kind=kind):
                blend(source, at(2 * i + 1), second)
                mix(target, at(2 * i), first, kind)
                blend(source, at(2 * i + 2), first)
                mix(target, at(2 * i + 1), second, kind)
                return carry

            lax.fori_loop(0, (groups - 1) // 2, body, 0)
        if groups % 2 == 0:
            blend(source, at(groups - 1), second)
            mix(target, at(groups - 2), first, kind)
            mix(target, at(groups - 1), second, kind)
        else:
            mix(target, at(groups - 1), first, kind)
        after(step, target)


def spread_factor(columns, factor, starts, width):
    rows, lanes = factor.shape[2:]
    pair = width // (2 * factor.shape[0])
    right = (lax.broadcasted_iota(jnp.int32, (rows, lanes), 1) >= lanes // 2).astype(jnp.int32)
    for piece, start in enumerate(starts):
        for kind in range(factor.shape[0]):
            for i in range(pair):
                at = piece * width + (kind * pair + i) * 2
                factor[kind, start + i] = jnp.take_along_axis(columns, right + at, axis=1, mode="promise_in_bounds")


def slab_starts(planes, reach):
    odd = position()[1]
    mine, others = (planes * (1 + core) for core in (odd, 1 - odd))
    return [reach, reach + mine, reach - mine, reach + others, reach - others]


def fill_factor(pieces, starts, factor, scratch):
    rows = scratch.shape[0]
    planes = (pieces[0].shape[0] - FIELD_ROWS) // rows
    width = 2 * planes * factor.shape[0]
    lines = [piece[planes * rows : planes * rows + width] for piece in pieces]
    lines.append(jnp.zeros((rows - width * len(pieces), rows), jnp.float32))
    scratch[...] = jnp.exp(-jnp.concatenate(lines, axis=0)).T
    spread_factor(reorder(scratch), factor, starts, width)


def factor_kernel(*refs):
    pieces, factor, scratch = refs[:3], refs[3], refs[4]
    planes = (pieces[0].shape[0] - FIELD_ROWS) // scratch.shape[0]
    fill_factor(pieces, slab_starts(planes, (factor.shape[1] - planes) // 2)[:3], factor, scratch)


def early_kernel(taps, weights, across, *refs):
    pieces, stored, (middle, half_out, kept, total, factor) = refs[:5], refs[5], refs[7:12]
    slab, other, first, second, scratch = refs[12:]
    sec, odd = position()
    planes, rows = middle.shape[:2]
    pair = planes // 2
    reach = (slab.shape[0] - planes) // 2
    starts = slab_starts(planes, reach)
    for piece, start in zip(pieces, starts):
        for i in range(planes):
            slab[start + i] = piece[i * rows : (i + 1) * rows]
    at = planes * rows
    steps = stored.shape[0]
    own_kinds, first_kinds = (pieces[0][at + row : at + row + 1] for row in (OWN_KINDS, FIRST_KINDS))
    beside_kinds, beside_first = (pieces[3][at + row : at + row + 1] for row in (OWN_KINDS, FIRST_KINDS))
    kinds = scalars_of(jnp.where((sec == 1) | (sec == 2), beside_first, first_kinds), steps)
    kinds += scalars_of(jnp.where((sec == 1) | (sec == 2), own_kinds, beside_kinds), steps)
    last_kinds = jnp.where(sec == 0, across[:1], own_kinds)
    half_out[pair * rows :] = jnp.broadcast_to(last_kinds, (8, rows))
    fill_factor(pieces[3:], starts[3:], factor, scratch)
    total[...] = jnp.zeros(total.shape, jnp.float32)
    kept[...] = jnp.zeros(kept.shape, jnp.float32)

    def after(step, state):
        @pl.when(sec == step // steps)
        def _():
            total[...] += state[reach : reach + planes] * stored[step % steps]
            if (step + 1) % steps == 0:
                kept[...] = state[reach : reach + planes]

    run_steps(kinds, taps, weights, reach, slab, other, first, second, factor, 0, after)
    state = (slab, other)[reach % 2]
    middle[...] = state[reach : reach + planes]
    for i in range(pair):
        half_out[i * rows : (i + 1) * rows] = state[reach + pair * odd + i]


def late_kernel(blocks, last, taps, weights, middle, *refs):
    pieces, refs = refs[: 2 * len(blocks)], refs[2 * len(blocks) :]
    factor, kept, total_in, total_beside, series, stored = refs[:6]
    handoff, share, to_pair, to_across, to_corner = refs[6:11]
    slab, other, first, second, scratch, total, saved, whole = refs[11:]
    sec, odd = position()
    planes, rows = middle.shape[:2]
    pair = planes // 2
    reach = (slab.shape[0] - planes) // 2
    begun = (factor.shape[1] - planes) // 2
    even, uneven = (jnp.where(odd == core, pieces[0][pair * rows :], pieces[len(blocks)][pair * rows :]) for core in (0, 1))
    kinds = scalars_of(jnp.where(sec < 2, even, uneven)[:1], reach)
    slab[reach : reach + planes] = middle[...]
    for piece, start in zip(pieces, places(odd, planes, reach, blocks)):
        for i in range(pair):
            slab[start + i] = piece[i * rows : (i + 1) * rows]
    total[...] = jnp.zeros(total.shape, jnp.float32)

    @pl.when(sec == 0)
    def _():
        total[...] = total_in[...] + total_beside[...]

    saved[...] = kept[...]

    def after(step, state):
        for where, source in ((sec == 0, series), (sec == last, stored)):

            @pl.when(where)
            def _(source=source):
                total[...] += state[reach : reach + planes] * source[step]

    run_steps(kinds, taps, weights, reach, slab, other, first, second, factor, begun - reach, after)
    state = (slab, other)[reach % 2]

    @pl.when(sec == last)
    def _():
        saved[...] = state[reach : reach + planes]

    orients = handoff.shape[1]
    count = orients // (last + 1)
    held = planes * count
    to_corner[...] = jnp.zeros(to_corner.shape, jnp.float32)
    for i in range(planes):
        handoff[i] = from_tile(saved[i], scratch)
        whole[...] = from_tile(total[i], scratch)
        for piece, who in (
            (share, sec),
            (to_pair, sec + 1 - 2 * odd),
            (to_across, jnp.where(sec == 0, 2, 1)),
            (to_corner, last - sec),
        ):
            piece[i * count : (i + 1) * count] = whole[pl.ds(pl.multiple_of(who * count, count), count)]
    for i in range(pair):
        to_across[held + i * orients : held + (i + 1) * orients] = from_tile(state[reach + pair * odd + i], scratch)

    @pl.when(sec == 1)
    def _():
        to_corner[...] = to_across[held:]


def finish_kernel(contour, handoff_in, share, to_pair, to_across, to_corner, handoff, density):
    sec = lax.axis_index("sec")
    planes, count = density.shape[:2]
    held = planes * count
    corner = jnp.where(sec == 2, 0.0, to_corner[:held])
    total = (share[...] + to_pair[...] + to_across[:held] + corner) / contour
    for i in range(planes):
        density[i] = total[i * count : (i + 1) * count]
    handoff[0] = handoff_in[...]

    @pl.when(sec == 2)
    def _():
        orients = handoff.shape[2]
        pair = planes // 2
        for i in range(pair):
            handoff[0, i] = to_across[held + i * orients : held + (i + 1) * orients]
            handoff[0, pair + i] = to_corner[i * orients : (i + 1) * orients]


def call(kernel, out_shape, scratch, operands, dtypes=None, aliases=None, cost=None):
    return pl.pallas_call(
        kernel,
        in_specs=[IN_VMEM] * len(operands),
        out_specs=[IN_VMEM] * len(out_shape),
        out_shape=[jax.ShapeDtypeStruct(shape, (dtypes or {}).get(i, jnp.float32)) for i, shape in enumerate(out_shape)],
        scratch_shapes=scratch,
        input_output_aliases=aliases or {},
        cost_estimate=cost,
        compiler_params=pltpu.CompilerParams(vmem_limit_bytes=VMEM_BYTES),
    )(*operands)


def paired(incoming, backward, fields, block_types, axial_taps, lateral_taps, depth_taps, bend_diagonal, bend_coupling):
    n_sec, n_gx = lax.axis_size("sec"), lax.axis_size("gx")
    steps, planes, orients, cells = backward.shape
    pair = planes // 2
    reach = (TICKS - 1) * steps, steps
    near = (-1, 1)
    rows = 2 * orients
    lanes = cells // 2
    last = n_sec - 1

    def send(array, by_sec, even=0, odd=0):
        by_sec = by_sec.items() if isinstance(by_sec, dict) else enumerate(by_sec)
        pairs = [
            (s * n_gx + g, t * n_gx + (g + (odd if s % 2 else even)) % n_gx) for s, t in by_sec for g in range(n_gx)
        ]
        return lax.ppermute(array, ("sec", "gx"), pairs)

    same, beside = (0, 1, 2, 3), (1, 0, 3, 2)
    moved = send(incoming[0], {0: 1, 1: 3})
    bundle = launch(
        incoming, fields, block_types, axial_taps, lateral_taps, depth_taps, bend_diagonal, bend_coupling
    )
    own_types = jnp.pad(block_types.astype(jnp.float32), ((0, 7), (0, lanes - steps)))
    types = send(own_types, {1: 3})
    size = planes * rows + FIELD_ROWS
    base, taps, weights = call(
        unpack_kernel, [(size, lanes), (TAP_ROWS, lanes), (2 * rows, 2 * lanes)], [], [bundle], {2: jnp.bfloat16}
    )
    moved, base, types = lax.optimization_barrier((moved, base, types))
    passed = send(moved, {3: 2})

    tile = pltpu.VMEM((rows, lanes), jnp.float32)
    packed = pltpu.VMEM((GROUP * rows, 2 * lanes), jnp.bfloat16)
    inner = pltpu.VMEM((planes, rows, lanes), jnp.float32)

    def work(extent):
        slab = pltpu.VMEM((planes + 2 * extent, rows, lanes), jnp.float32)
        return [slab, slab, packed, packed, tile]

    (piece,) = call(pack_kernel, [(size, lanes)], [tile], [base, moved, passed, types])
    own = [send(piece, same, shift, 2 * shift) for shift in near]
    backward, own_types, _ = lax.optimization_barrier((backward, own_types, piece))
    across_types = send(own_types, {2: 0})
    (stored,) = call(turn_kernel, [(steps, planes, rows, lanes)], [tile], [backward])
    own[-1], stored, across_types = lax.optimization_barrier((own[-1], stored, across_types))
    swapped = [send(each, beside) for each in own]
    table = (fields.shape[0], planes + 2 * reach[0], rows, lanes)
    (factor,) = call(factor_kernel, [table], [tile], [piece, *own])
    late_stored, factor, *swapped = lax.optimization_barrier((stored, factor, *swapped))
    late_last = send(late_stored, {2: 0})
    middle, piece, kept, total, factor = call(
        early_kernel,
        [(planes, rows, lanes), (pair * rows + 8, lanes), (planes, rows, lanes), (planes, rows, lanes)]
        + [table],
        work(reach[0]),
        [taps, weights, across_types, piece, *own, *swapped, stored, factor],
        aliases={9: 4},
    )
    own = [send(piece, same, shift, shift) for shift in near]
    beside_total = send(total, beside)
    swapped = [send(each, beside) for each in own]
    held = planes * (orients // n_sec)
    handoff, share, to_pair, to_across, to_corner = call(
        functools.partial(late_kernel, tuple(-shift for shift in near), last),
        [(planes, orients, cells)]
        + [(held, cells)] * 2
        + [(held + pair * orients, cells), (pair * orients, cells)],
        work(reach[1]) + [inner, inner, pltpu.VMEM((orients, cells), jnp.float32)],
        [taps, weights, middle, *own, *swapped, factor, kept, total, beside_total]
        + [late_last, stored],
    )
    to_pair = send(to_pair, beside)
    to_across = send(to_across, (2, 0, 3, 1))
    to_corner = send(to_corner, (3, 2, 1, 0))
    handoff, density = call(
        functools.partial(finish_kernel, n_sec * steps),
        [(1,) + handoff.shape, (planes, orients // n_sec, cells)],
        [],
        [handoff, share, to_pair, to_across, to_corner],
    )
    return handoff, density


def pairs_fit(n_sec, planes, steps, orients, cells, kinds):
    return (
        n_sec == TICKS + 1 == 4
        and planes == steps
        and planes % 2 == 0
        and 2 * orients == 2 * CZ == cells // 2 == 128
        and 2 * kinds * planes <= OWN_KINDS and 10 * kinds * planes <= 2 * orients
        and GROUP < 2 * planes
    )


def solution(mesh):
    in_specs = (
        P("sec", "gx", None, None),
        P("sec", "gx", None, None),
        P(None, "gx", None),
        P("sec", None),
        P(),
        P(),
        P(),
        P(),
        P(),
    )
    out_specs = (P("sec", "gx", None, None), P("gx", "sec", None))

    def body(incoming, backward, fields, *rest):
        steps, planes, orients, cells = backward.shape
        fits = pairs_fit(mesh.shape["sec"], planes, steps, orients, cells, fields.shape[0])
        return (paired if fits else per_device)(incoming, backward, fields, *rest)

    return jax.shard_map(body, mesh=mesh, in_specs=in_specs, out_specs=out_specs, check_vma=False)
```
